32 devices in a mesh: blk: 16 (over z, x, core), src: 2 (over y).
Axes of the slice: x: 2, y: 2, z: 4, core: 2. Of those that a mesh axis runs over, the one named last changes fastest.
Arguments:
- raw_records: float32 [512, 10240], P('blk', 'src'), may hold values from -6 to 6
- fir_taps: float32 [64], replicated, may hold values from -0.75 to 0.75
- alive_mask: int32 [512], P('blk'), may hold values 0 or 1
- source_index: int32 [16, 2], P('blk'), may hold values from 0 to 31
Outputs:
- correlations: bfloat16 [32, 512, 512], P('src', 'blk')
The draws below stay inside these ranges and needn't reach their ends.
All inputs are finite; a program needn't handle non-finite values. No bound on the sum of `alive_mask` on one device may be relied on, other than what follows from the above.
Results may differ from the reference program's by a relative error of at most 0.0053.
Values sent between devices are 32-bit elements; how exact they have to be, the bound alone decides.
No kernel may reach another device: no remote copies, remote signals or barrier semaphores. Data moves between devices by JAX's collectives and lax.ppermute only.
A program may use at most 128 MiB of HBM per device.

```python
import math
import jax
import jax.numpy as jnp
from jax import lax

VS = 2
S = 512
NFFT = 1024
LAGS = 512
TAPS = 64
DEC = 20
HALF = 64
RAW = 10240
CB = 32
BLOCKS = 16
CHANNELS = 512
NSRC = 32


def touch_ends(drawn, rng, smallest, high):
    extent = drawn.shape
    index_at = [jax.random.randint(jax.random.fold_in(rng, axis), (), 0, extent[axis]) for axis in range(len(extent))]
    drawn = drawn.at[tuple(index_at)].set(smallest)
    longest = extent.index(max(extent))
    index_at[longest] = (index_at[longest] + 1) % extent[longest]
    return drawn.at[tuple(index_at)].set(high)


def shard_levels(key, shape, pieces, smallest, high):
    factor_of = 1.0
    for axis_at, blocks in pieces:
        steps = jax.random.uniform(jax.random.fold_in(jax.random.fold_in(key, 6), axis_at), (blocks,), jnp.float32, smallest / len(pieces), high / len(pieces))
        factor_of = factor_of * jnp.repeat(jnp.exp(steps), shape[axis_at] // blocks).reshape((-1,) + (1,) * (len(shape) - 1 - axis_at))
    return factor_of


def noise(rng, extent, width, most, cuts=(), kind=jnp.bfloat16):
    values = width * jax.random.normal(rng, extent, jnp.float32)
    if cuts:
        values = values * shard_levels(rng, extent, cuts, -0.22, 0.18)
    return jnp.clip(values, -most, most).astype(kind)


def setup_inputs(seed: int = 0) -> dict:
    arg_keys = jax.random.split(jax.random.key(seed), 5)
    return {
        "raw_records": noise(arg_keys[0], (CHANNELS, RAW), 1.0, 6.0, ((0, 16), (1, 2)), jnp.float32),
        "fir_taps": noise(arg_keys[1], (TAPS,), TAPS ** -0.5, 0.75, (), jnp.float32),
        "alive_mask": touch_ends((jax.random.randint(arg_keys[2], (CHANNELS,), 0, 8) < 7).astype(jnp.int32), jax.random.fold_in(arg_keys[2], 1), 0, 1),
        "source_index": touch_ends(jax.random.randint(arg_keys[3], (BLOCKS, VS), 0, CB), jax.random.fold_in(arg_keys[3], 1), 0, CB - 1).astype(jnp.int32),
    }


def decimate(records, fir_taps, out_count):
    tap_groups = -(-TAPS // DEC)
    needed = DEC * (out_count + tap_groups - 1)
    padded = jnp.pad(records, ((0, 0), (0, DEC * tap_groups)))[:, :needed]
    sample_blocks = padded.reshape(padded.shape[0], out_count + tap_groups - 1, DEC)
    tap_rows = jnp.pad(fir_taps, (0, tap_groups * DEC - TAPS)).reshape(tap_groups, DEC)
    filtered = jnp.zeros((padded.shape[0], out_count), jnp.float32)
    for tap_group in range(tap_groups):
        filtered = filtered + jnp.einsum('cnm,m->cn', sample_blocks[:, tap_group:tap_group + out_count], tap_rows[tap_group], precision=lax.Precision.HIGHEST)
    return filtered

def forward_table():
    sample_times = jnp.arange(S, dtype=jnp.int32)[:, None]
    bin_index = jnp.arange(NFFT // 2, dtype=jnp.int32)[None, :]
    phases = 2.0 * math.pi / NFFT * (sample_times * bin_index % NFFT).astype(jnp.float32)
    return jnp.concatenate([jnp.cos(phases), -jnp.sin(phases)], axis=1)

def band_table():
    half_bins = NFFT // 2
    row_bins = jnp.arange(half_bins, dtype=jnp.int32)[:, None]
    col_bins = jnp.arange(half_bins, dtype=jnp.int32)[None, :]
    band_mask = (jnp.abs(row_bins - col_bins) <= HALF).astype(jnp.float32)
    return (band_mask, lax.optimization_barrier(jnp.sum(band_mask, axis=0)))

def whiten(series, alive_rows):
    spectrum = jnp.dot(series, forward_table(), precision=lax.Precision.HIGHEST)
    half_bins = spectrum.shape[1] // 2
    real_part = spectrum[:, :half_bins]
    imag_part = spectrum[:, half_bins:]
    power_bins = real_part * real_part + imag_part * imag_part
    band_mask, band_count = band_table()
    smooth = jnp.dot(power_bins, band_mask, precision=lax.Precision.HIGHEST) / band_count
    inverse_amp = alive_rows[:, None] / jnp.sqrt(smooth + 1e-06)
    return spectrum * jnp.concatenate([inverse_amp, inverse_amp], axis=1)

def lag_table():
    half_bins = NFFT // 2
    bin_index = jnp.arange(half_bins, dtype=jnp.int32)[:, None]
    lag_shift = jnp.arange(LAGS, dtype=jnp.int32)[None, :] - LAGS // 2
    phases = 2.0 * math.pi / NFFT * (bin_index * lag_shift % NFFT).astype(jnp.float32)
    bin_weight = jnp.where(bin_index == 0, 0.5, 1.0).astype(jnp.float32) / math.sqrt(half_bins)
    return jnp.concatenate([bin_weight * jnp.cos(phases), -bin_weight * jnp.sin(phases)], axis=0).astype(jnp.bfloat16)

def reference(raw_records, fir_taps, alive_mask, source_index):
    series = decimate(raw_records, fir_taps, S)
    spectra = whiten(series, alive_mask.astype(jnp.float32))
    offsets = (jnp.arange(BLOCKS, dtype=jnp.int32) * CB)[:, None]
    source_channel = source_index.astype(jnp.int32) + offsets
    lag_weights = lag_table().astype(jnp.float32)
    half_bins = NFFT // 2
    receivers = jnp.arange(CHANNELS, dtype=jnp.int32)

    def group_corr(group_channels):
        sources = spectra[group_channels]
        src_re = sources[:, None, :half_bins]
        src_im = sources[:, None, half_bins:]
        rec_re = spectra[None, :, :half_bins]
        rec_im = spectra[None, :, half_bins:]
        cross_spec = jnp.concatenate([src_re * rec_re + src_im * rec_im, src_re * rec_im - src_im * rec_re], axis=2).astype(jnp.bfloat16)
        flat_cross = cross_spec.reshape(VS * CHANNELS, 2 * half_bins).astype(jnp.float32)
        lagged = jnp.dot(flat_cross, lag_weights, preferred_element_type=jnp.float32).reshape(VS, CHANNELS, LAGS)
        self_pair = receivers[None, :] == group_channels[:, None]
        return jnp.where(self_pair[:, :, None], 0.0, lagged).astype(jnp.bfloat16)
    stacked = lax.map(group_corr, source_channel)
    return stacked.reshape(NSRC, CHANNELS, LAGS)
```

```python
import math

import jax
import jax.numpy as jnp
import numpy as np
from jax import lax
from jax.experimental import pallas as pl
from jax.experimental.pallas import tpu as pltpu
from jax.sharding import PartitionSpec as P

S = 512
NFFT = 1024
BINS = NFFT // 2
LAGS = 512
TAPS = 64
DEC = 20
HALF = 64
LANES = 128
SUBLANES = 8
CHUNK = 640
CHUNK_OUT = CHUNK // DEC
VMEM_LIMIT = 48 * 1024 * 1024


def forward_table():
    phases = 2.0 * math.pi / NFFT * (np.outer(np.arange(S), np.arange(BINS)) % NFFT)
    return np.concatenate([np.cos(phases), -np.sin(phases)], axis=1).astype(np.float32)


def split_table(table):
    high = table.astype(jnp.bfloat16)
    low = (table - high.astype(np.float32)).astype(jnp.bfloat16)
    return high, low


def band_table():
    bins = np.arange(BINS)
    return (np.abs(bins[:, None] - bins[None, :]) <= HALF).astype(jnp.bfloat16)


def lag_table():
    bins = np.arange(BINS)[:, None]
    shift = np.arange(LAGS)[None, :] - LAGS // 2
    phases = 2.0 * math.pi / NFFT * (bins * shift % NFFT)
    weight = np.where(bins == 0, 0.5, 1.0) / math.sqrt(BINS)
    table = np.concatenate([weight * np.cos(phases), -weight * np.sin(phases)], axis=0)
    return table.astype(np.float32).astype(jnp.bfloat16)


def split(value):
    high = value.astype(jnp.bfloat16)
    return high, (value - high.astype(jnp.float32)).astype(jnp.bfloat16)


def dot(a, b):
    return jnp.dot(a, b, preferred_element_type=jnp.float32)


def dot_t(a, b):
    return lax.dot_general(a, b, (((1,), (1,)), ((), ())), preferred_element_type=jnp.float32)


def decimate_kernel(raw_ref, taps_ref, out_ref):
    rows = raw_ref.shape[0]
    chunks = raw_ref.shape[1] // CHUNK
    taps = jnp.broadcast_to(taps_ref[...], (SUBLANES, TAPS))
    eight = jnp.concatenate([taps, jnp.zeros((SUBLANES, CHUNK - TAPS), jnp.float32)], axis=1)
    for _ in range(2):
        eight = pltpu.roll(eight, 0, 1, stride=DEC // 2, stride_axis=0)
    wrapped = jnp.concatenate(
        [eight]
        + [pltpu.roll(eight, DEC * at, 1) for at in range(SUBLANES, CHUNK_OUT, SUBLANES)],
        axis=0,
    )
    lane = lax.broadcasted_iota(jnp.int32, (CHUNK_OUT, CHUNK), 1)
    row = lax.broadcasted_iota(jnp.int32, (CHUNK_OUT, CHUNK), 0)
    main = jnp.where(lane >= DEC * row, wrapped, 0.0)
    rim = wrapped - main
    gap = jnp.zeros((LANES - 2 * CHUNK_OUT, CHUNK), jnp.float32)
    weights_hi, weights_lo = split(jnp.concatenate([main, gap, rim], axis=0))
    stacked = jnp.concatenate(
        [raw_ref[:, CHUNK * j : CHUNK * (j + 1)] for j in range(chunks)], axis=0
    )
    raw_hi, raw_lo = split(stacked)
    both = dot_t(raw_hi, jnp.concatenate([weights_hi, weights_lo], axis=0))
    result = both[:, :LANES] + both[:, LANES:] + dot_t(raw_lo, weights_hi)
    part = [result[rows * j : rows * (j + 1)] for j in range(chunks)]
    per_tile = LANES // CHUNK_OUT
    col = lax.broadcasted_iota(jnp.int32, (rows, LANES), 1)
    is_main = col < LANES // 2
    tiles = -(-chunks // per_tile)
    for tile in range(tiles):
        first = tile * per_tile
        total = jnp.where(is_main, part[first], 0.0)
        for step in range(1, min(per_tile, chunks - first)):
            total = total + pltpu.roll(part[first + step], CHUNK_OUT * step, 1)
        if first + per_tile < chunks:
            total = total + jnp.where(is_main, 0.0, part[first + per_tile])
        out_ref[:, LANES * tile : LANES * (tile + 1)] = total
    out_ref[:, LANES * tiles :] = jnp.where(is_main, 0.0, part[0])


def whiten(series, alive, fwd_hi_ref, fwd_lo_ref, band_ref):
    rows = series.shape[0]
    high, low = split(series)
    first = dot(jnp.concatenate([high, low], axis=0), fwd_hi_ref[...])
    spectrum = first[:rows] + first[rows:] + dot(high, fwd_lo_ref[...])
    real_part = spectrum[:, :BINS]
    imag_part = spectrum[:, BINS:]
    power = real_part * real_part + imag_part * imag_part
    power_hi, rest = split(power)
    power_mid, power_lo = split(power - power_hi.astype(jnp.float32))
    banded = dot(jnp.concatenate([power_hi, power_mid, power_lo], axis=0), band_ref[...])
    total = banded[:rows] + banded[rows : 2 * rows] + banded[2 * rows :]
    bins = lax.broadcasted_iota(jnp.int32, (1, BINS), 1)
    count = jnp.minimum(bins + HALF, BINS - 1) - jnp.maximum(bins - HALF, 0) + 1
    smooth = total / count.astype(jnp.float32)
    factor = alive / jnp.sqrt(smooth + 1e-06)
    return real_part * factor, imag_part * factor


def spectra_kernel(paired, ids_ref, picks_ref, alive_ref, *refs):
    if paired:
        mine_ref, other_ref, fwd_hi_ref, fwd_lo_ref, band_ref, spectra_ref, payload_ref = refs
        is_first = ids_ref[1] == 0
        mine, other = mine_ref[...], other_ref[...]
        early = jnp.where(is_first, mine, other)
        late = jnp.where(is_first, other, mine)
        half = S // 2
        seam = early[:, half - LANES : half] + late[:, half:]
        series = jnp.concatenate([early[:, : half - LANES], seam, late[:, :half]], axis=1)
    else:
        series_ref, fwd_hi_ref, fwd_lo_ref, band_ref, spectra_ref, payload_ref = refs
        series = series_ref[...]
    rows = series.shape[0]
    diagonal = lax.broadcasted_iota(jnp.int32, (rows, rows), 0) == lax.broadcasted_iota(
        jnp.int32, (rows, rows), 1
    )
    alive_rows = jnp.broadcast_to(alive_ref[...].astype(jnp.float32), (rows, rows))
    alive = jnp.sum(jnp.where(diagonal, alive_rows, 0.0), axis=1, keepdims=True)
    real_part, imag_part = whiten(series, alive, fwd_hi_ref, fwd_lo_ref, band_ref)
    spectra_ref[:, :BINS] = real_part
    spectra_ref[:, BINS:] = imag_part
    tiles = NFFT // LANES
    for slot in range(picks_ref.shape[1]):
        picked = spectra_ref[pl.ds(picks_ref[0, slot], 1), :]
        for tile in range(tiles):
            payload_ref[slot * tiles + tile : slot * tiles + tile + 1, :] = picked[
                :, LANES * tile : LANES * (tile + 1)
            ]


def correlate_kernel(group, ids_ref, picks_ref, spectra_ref, sources_ref, lag_ref, out_ref, cross_ref):
    rows = spectra_ref.shape[0]
    slots = picks_ref.shape[1]
    tiles = NFFT // LANES
    half = tiles // 2
    own = ids_ref[0]
    base = ids_ref[1] * group
    for block in range(group):
        place = jnp.bitwise_xor(base + block, own)
        for slot in range(slots):
            source = block * slots + slot
            for tile in range(half):
                at = slot * tiles + tile
                src_re = sources_ref[place, at : at + 1, :]
                src_im = sources_ref[place, at + half : at + half + 1, :]
                rec_re = spectra_ref[:, LANES * tile : LANES * (tile + 1)]
                rec_im = spectra_ref[:, BINS + LANES * tile : BINS + LANES * (tile + 1)]
                cross_re = src_re * rec_re + src_im * rec_im
                cross_im = src_re * rec_im - src_im * rec_re
                where = pl.ds(rows * source, rows)
                cross_ref[where, LANES * tile : LANES * (tile + 1)] = cross_re.astype(jnp.bfloat16)
                cross_ref[where, BINS + LANES * tile : BINS + LANES * (tile + 1)] = cross_im.astype(
                    jnp.bfloat16
                )
    lagged = dot(cross_ref[...], lag_ref[...])
    for source in range(group * slots):
        out_ref[source] = lagged[rows * source : rows * (source + 1)].astype(jnp.bfloat16)

    @pl.when((own >= base) & (own < base + group))
    def _():
        channel = lax.broadcasted_iota(jnp.int32, (rows, LAGS), 0)
        for slot in range(slots):
            source = (own - base) * slots + slot
            kept = out_ref[source].astype(jnp.float32)
            out_ref[source] = jnp.where(channel == picks_ref[0, slot], 0.0, kept).astype(
                jnp.bfloat16
            )


SMEM = pl.BlockSpec(memory_space=pltpu.SMEM)
VMEM = pl.BlockSpec(memory_space=pltpu.VMEM)
PARAMS = pltpu.CompilerParams(vmem_limit_bytes=VMEM_LIMIT)


def local(raw_records, fir_taps, alive_mask, source_index):
    src_count = lax.axis_size("src")
    blk_count = lax.axis_size("blk")
    rows, raw_count = raw_records.shape
    slots = source_index.shape[1]
    group = blk_count // src_count
    out_count = raw_count // DEC
    width = -(-out_count // LANES) * LANES + LANES
    ids = jnp.stack([lax.axis_index("blk"), lax.axis_index("src")]).astype(jnp.int32)
    forward_hi, forward_lo = split_table(forward_table())

    with jax.named_scope("decimate"):
        decimated = pl.pallas_call(
            decimate_kernel,
            out_shape=jax.ShapeDtypeStruct((rows, width), jnp.float32),
            in_specs=[VMEM, VMEM],
            out_specs=VMEM,
            compiler_params=PARAMS,
        )(raw_records, fir_taps.reshape(1, TAPS))

    paired = src_count == 2 and out_count % LANES == 0
    with jax.named_scope("regroup"):
        if paired:
            pieces = (decimated, lax.ppermute(decimated, "src", [(0, 1), (1, 0)]))
        else:
            shards = lax.all_gather(decimated, "src", axis=0)
            series = shards[:, :, :out_count]
            rims = jnp.pad(shards[1:, :, width - 3 :], ((0, 1), (0, 0), (out_count - 3, 0)))
            series = (series + rims).transpose(1, 0, 2).reshape(rows, S)
            pieces = (series,)

    with jax.named_scope("spectra"):
        spectra, payload = pl.pallas_call(
            lambda *refs: spectra_kernel(paired, *refs),
            out_shape=(
                jax.ShapeDtypeStruct((rows, NFFT), jnp.float32),
                jax.ShapeDtypeStruct((slots * NFFT // LANES, LANES), jnp.float32),
            ),
            in_specs=[SMEM, SMEM] + [VMEM] * (4 + len(pieces)),
            out_specs=(VMEM, VMEM),
            compiler_params=PARAMS,
        )(
            ids,
            source_index,
            alive_mask.reshape(1, rows),
            *pieces,
            jnp.asarray(forward_hi),
            jnp.asarray(forward_lo),
            jnp.asarray(band_table()),
        )

    with jax.named_scope("gather_sources"):
        sources = payload[None]
        step = 1
        while step < blk_count:
            arrived = lax.ppermute(sources, "blk", [(b, b ^ step) for b in range(blk_count)])
            sources = jnp.concatenate([sources, arrived], axis=0)
            step *= 2

    with jax.named_scope("correlate"):
        return pl.pallas_call(
            lambda *refs: correlate_kernel(group, *refs),
            out_shape=jax.ShapeDtypeStruct((group * slots, rows, LAGS), jnp.bfloat16),
            in_specs=[SMEM, SMEM, VMEM, VMEM, VMEM],
            out_specs=VMEM,
            scratch_shapes=[pltpu.VMEM((group * slots * rows, NFFT), jnp.bfloat16)],
            compiler_params=PARAMS,
        )(ids, source_index, spectra, sources, jnp.asarray(lag_table()))


def solution(mesh):
    in_specs = (P("blk", "src"), P(), P("blk"), P("blk", None))
    out_specs = P("src", "blk", None)
    return jax.shard_map(local, mesh=mesh, in_specs=in_specs, out_specs=out_specs, check_vma=False)
```

```python
import math

import jax
import jax.numpy as jnp
import numpy as np
from jax import lax
from jax.experimental import pallas as pl
from jax.experimental.pallas import tpu as pltpu
from jax.sharding import PartitionSpec as P

S = 512
NFFT = 1024
BINS = NFFT // 2
LAGS = 512
TAPS = 64
DEC = 20
HALF = 64
LANES = 128
SUBLANES = 8
EDGE = (TAPS - 1) // DEC
CHUNK = 640
CHUNK_OUT = CHUNK // DEC
VMEM_LIMIT = 48 * 1024 * 1024


def forward_table():
    phases = 2.0 * math.pi / NFFT * (np.outer(np.arange(S), np.arange(BINS)) % NFFT)
    return np.concatenate([np.cos(phases), -np.sin(phases)], axis=1).astype(np.float32)


def split_table(table):
    high = table.astype(jnp.bfloat16)
    low = (table - high.astype(np.float32)).astype(jnp.bfloat16)
    return high, low


def band_table():
    bins = np.arange(BINS)
    return (np.abs(bins[:, None] - bins[None, :]) <= HALF).astype(jnp.bfloat16)


def lag_table():
    bins = np.arange(BINS)[:, None]
    shift = np.arange(LAGS)[None, :] - LAGS // 2
    phases = 2.0 * math.pi / NFFT * (bins * shift % NFFT)
    weight = np.where(bins == 0, 0.5, 1.0) / math.sqrt(BINS)
    table = np.concatenate([weight * np.cos(phases), -weight * np.sin(phases)], axis=0)
    return table.astype(np.float32).astype(jnp.bfloat16)


def split(value):
    high = value.astype(jnp.bfloat16)
    return high, (value - high.astype(jnp.float32)).astype(jnp.bfloat16)


def dot(a, b):
    return jnp.dot(a, b, preferred_element_type=jnp.float32)


def dot_t(a, b):
    return lax.dot_general(a, b, (((1,), (1,)), ((), ())), preferred_element_type=jnp.float32)


def decimate_kernel(raw_hbm, taps_hbm, out_ref, raw_ref, taps_ref, sems):
    rows = raw_hbm.shape[0]
    chunks = raw_hbm.shape[1] // CHUNK
    taps_copy = pltpu.make_async_copy(taps_hbm, taps_ref, sems.at[chunks])
    taps_copy.start()
    copies = []
    for j in range(chunks):
        copies.append(
            pltpu.make_async_copy(
                raw_hbm.at[:, CHUNK * j : CHUNK * (j + 1)],
                raw_ref.at[rows * j : rows * (j + 1), :],
                sems.at[j],
            )
        )
        copies[-1].start()
    taps_copy.wait()
    taps = jnp.broadcast_to(taps_ref[...], (SUBLANES, TAPS))
    eight = jnp.concatenate([taps, jnp.zeros((SUBLANES, CHUNK - TAPS), jnp.float32)], axis=1)
    for _ in range(2):
        eight = pltpu.roll(eight, 0, 1, stride=DEC // 2, stride_axis=0)
    wrapped = jnp.concatenate(
        [eight]
        + [pltpu.roll(eight, DEC * at, 1) for at in range(SUBLANES, CHUNK_OUT, SUBLANES)],
        axis=0,
    )
    lane = lax.broadcasted_iota(jnp.int32, (CHUNK_OUT, CHUNK), 1)
    row = lax.broadcasted_iota(jnp.int32, (CHUNK_OUT, CHUNK), 0)
    main = jnp.where(lane >= DEC * row, wrapped, 0.0)
    rim = wrapped - main
    gap = jnp.zeros((LANES - 2 * CHUNK_OUT, CHUNK), jnp.float32)
    weights_hi, weights_lo = split(jnp.concatenate([main, gap, rim], axis=0))
    for copy in copies:
        copy.wait()
    raw_hi, raw_lo = split(raw_ref[...])
    both = dot_t(raw_hi, jnp.concatenate([weights_hi, weights_lo], axis=0))
    result = both[:, :LANES] + both[:, LANES:] + dot_t(raw_lo, weights_hi)
    part = [result[rows * j : rows * (j + 1)] for j in range(chunks)]
    per_tile = LANES // CHUNK_OUT
    col = lax.broadcasted_iota(jnp.int32, (rows, LANES), 1)
    is_main = col < LANES // 2
    tiles = -(-chunks // per_tile)
    for tile in range(tiles):
        first = tile * per_tile
        total = jnp.where(is_main, part[first], 0.0)
        for step in range(1, min(per_tile, chunks - first)):
            total = total + pltpu.roll(part[first + step], CHUNK_OUT * step, 1)
        if first + per_tile < chunks:
            total = total + jnp.where(is_main, 0.0, part[first + per_tile])
        out_ref[:, LANES * tile : LANES * (tile + 1)] = total
    out_ref[:, LANES * tiles :] = jnp.where(is_main, 0.0, part[0])


def copy_all(pairs, sems):
    copies = [
        pltpu.make_async_copy(source, target, sems.at[at])
        for at, (source, target) in enumerate(pairs)
    ]
    for copy in copies:
        copy.start()
    return copies


def prepare_kernel(
    series_ref, alive_hbm, picks_hbm, fwd_hi_hbm, fwd_lo_hbm, band_hbm, edge_hbm, *refs
):
    paired = len(refs) > 11
    partial_ref, band_ref, alive_out, picks_out = refs[:4]
    refs = refs[4:]
    if paired:
        other_hi, other_lo, edge_out = refs[:3]
        refs = refs[3:]
    fwd_hi, fwd_lo, alive_ref, picks_ref, edge_ref, sems = refs[:6]
    rows, depth = series_ref.shape
    if paired:
        count = depth - LANES
        here = lax.axis_index("src")
        own = pl.ds(pl.multiple_of(count * here, LANES), depth)
        rest = pl.ds(pl.multiple_of(LANES + count * (1 - here), LANES), count)
        pairs = [
            (fwd_hi_hbm.at[own], fwd_hi),
            (fwd_lo_hbm.at[own], fwd_lo),
            (alive_hbm, alive_ref),
            (picks_hbm, picks_ref),
            (edge_hbm, edge_ref),
            (fwd_hi_hbm.at[rest], other_hi),
            (fwd_lo_hbm.at[rest], other_lo),
            (band_hbm, band_ref),
        ]
    else:
        pairs = [
            (fwd_hi_hbm.at[LANES:], fwd_hi),
            (fwd_lo_hbm.at[LANES:], fwd_lo),
            (alive_hbm, alive_ref),
            (picks_hbm, picks_ref),
            (band_hbm, band_ref),
        ]
    copies = copy_all(pairs, sems)
    for copy in copies[:5]:
        copy.wait()
    if paired:
        own_series = jnp.concatenate(
            [series_ref[:, depth - LANES :], series_ref[:, : depth - LANES]], axis=1
        )
        edge_out[...] = jnp.where(here == 0, edge_ref[...], 0.0)
    else:
        own_series = series_ref[...]
    high, low = split(own_series)
    first = dot(jnp.concatenate([high, low], axis=0), fwd_hi[...])
    partial_ref[...] = first[:rows] + first[rows:] + dot(high, fwd_lo[...])
    diagonal = lax.broadcasted_iota(jnp.int32, (rows, rows), 0) == lax.broadcasted_iota(
        jnp.int32, (rows, rows), 1
    )
    alive_rows = jnp.broadcast_to(alive_ref[...].astype(jnp.float32), (rows, rows))
    alive = jnp.sum(jnp.where(diagonal, alive_rows, 0.0), axis=1, keepdims=True)
    alive_out[...] = jnp.broadcast_to(alive, (rows, LANES))
    channel = lax.broadcasted_iota(jnp.int32, (rows, LANES), 0)
    for slot in range(picks_ref.shape[1]):
        pick = jnp.broadcast_to(picks_ref[:, slot : slot + 1], (rows, LANES))
        picks_out[slot] = jnp.where(channel == pick, 1.0, 0.0)
    for copy in copies[5:]:
        copy.wait()


def spectra_kernel(partial_ref, band_ref, alive_ref, picks_ref, *refs):
    spectrum = partial_ref[...]
    rows = spectrum.shape[0]
    if len(refs) > 2:
        other_ref, other_hi, other_lo, edge_ref = refs[:4]
        count = other_ref.shape[1] - LANES
        high, low = split(other_ref[:, :count])
        first = dot(jnp.concatenate([high, low], axis=0), other_hi[...])
        spectrum = spectrum + (first[:rows] + first[rows:] + dot(high, other_lo[...]))
        for at in range(EDGE):
            late = other_ref[:, count + LANES - EDGE + at : count + LANES - EDGE + at + 1]
            spectrum = spectrum + late * edge_ref[at : at + 1, :]
    spectra_ref, payload_ref = refs[-2:]
    real_part = spectrum[:, :BINS]
    imag_part = spectrum[:, BINS:]
    power = real_part * real_part + imag_part * imag_part
    power_hi, rest = split(power)
    power_mid, power_lo = split(power - power_hi.astype(jnp.float32))
    banded = dot(jnp.concatenate([power_hi, power_mid, power_lo], axis=0), band_ref[...])
    total = banded[:rows] + banded[rows : 2 * rows] + banded[2 * rows :]
    bins = lax.broadcasted_iota(jnp.int32, (1, BINS), 1)
    count = jnp.minimum(bins + HALF, BINS - 1) - jnp.maximum(bins - HALF, 0) + 1
    smooth = total / count.astype(jnp.float32)
    factor = alive_ref[:, :1] / jnp.sqrt(smooth + 1e-06)
    tiles = NFFT // LANES
    for tile in range(tiles):
        span = slice(LANES * tile, LANES * (tile + 1))
        start = LANES * (tile % (tiles // 2))
        value = spectrum[:, span] * factor[:, start : start + LANES]
        spectra_ref[:, span] = value
        for slot in range(picks_ref.shape[0]):
            at = slot * tiles + tile
            payload_ref[at : at + 1, :] = jnp.sum(
                value * picks_ref[slot], axis=0, keepdims=True
            )


def correlate_kernel(group, spectra_ref, sources_ref, picks_ref, lag_ref, out_hbm, cross_ref, out_ref, sems):
    rows = spectra_ref.shape[0]
    slots = picks_ref.shape[0]
    tiles = NFFT // LANES
    half = tiles // 2
    own = lax.axis_index("blk")
    base = lax.axis_index("src") * group
    per_part = max(1, (group * slots) // 4)
    copies = []
    for part in range(group * slots // per_part):
        first = part * per_part
        for source in range(first, first + per_part):
            block, slot = divmod(source, slots)
            is_own = jnp.where(own == base + block, 1.0, 0.0)
            keep = 1.0 - is_own * picks_ref[slot]
            for tile in range(half):
                at = slot * tiles + tile
                src_re = sources_ref[base + block, at : at + 1, :] * keep
                src_im = sources_ref[base + block, at + half : at + half + 1, :] * keep
                re = slice(LANES * tile, LANES * (tile + 1))
                im = slice(BINS + LANES * tile, BINS + LANES * (tile + 1))
                rec_re, rec_im = spectra_ref[:, re], spectra_ref[:, im]
                where = slice(rows * source, rows * (source + 1))
                cross_ref[where, re] = (src_re * rec_re + src_im * rec_im).astype(jnp.bfloat16)
                cross_ref[where, im] = (src_re * rec_im - src_im * rec_re).astype(jnp.bfloat16)
        lagged = dot(cross_ref[rows * first : rows * (first + per_part), :], lag_ref[...])
        for source in range(first, first + per_part):
            at = source - first
            out_ref[source] = lagged[rows * at : rows * (at + 1)].astype(jnp.bfloat16)
        span = pl.ds(first, per_part)
        copies.append(pltpu.make_async_copy(out_ref.at[span], out_hbm.at[span], sems.at[part]))
        copies[-1].start()
    for copy in copies:
        copy.wait()


ANY = pl.BlockSpec(memory_space=pl.ANY)
VMEM = pl.BlockSpec(memory_space=pltpu.VMEM)
PARAMS = pltpu.CompilerParams(vmem_limit_bytes=VMEM_LIMIT)


def shaped(*shape, dtype=jnp.float32):
    return jax.ShapeDtypeStruct(shape, dtype)


def local(raw_records, fir_taps, alive_mask, source_index):
    src_count = lax.axis_size("src")
    blk_count = lax.axis_size("blk")
    rows, raw_count = raw_records.shape
    slots = source_index.shape[1]
    group = blk_count // src_count
    out_count = raw_count // DEC
    width = -(-out_count // LANES) * LANES + LANES
    chunks = raw_count // CHUNK
    paired = src_count == 2 and out_count % LANES == 0
    forward = forward_table()
    forward_hi, forward_lo = split_table(np.pad(forward, ((LANES, 0), (0, 0))))
    edge = np.pad(forward[out_count - EDGE : out_count], ((0, SUBLANES - EDGE), (0, 0)))
    bf16 = jnp.bfloat16

    with jax.named_scope("decimate"):
        decimated = pl.pallas_call(
            decimate_kernel,
            out_shape=shaped(rows, width),
            in_specs=[ANY, ANY],
            out_specs=VMEM,
            scratch_shapes=[
                pltpu.VMEM((rows * chunks, CHUNK), jnp.float32),
                pltpu.VMEM((1, TAPS), jnp.float32),
                pltpu.SemaphoreType.DMA((chunks + 1,)),
            ],
            compiler_params=PARAMS,
        )(raw_records, fir_taps.reshape(1, TAPS))

    with jax.named_scope("regroup"):
        if paired:
            series = decimated
            depth = width
            other = lax.ppermute(decimated, "src", [(0, 1), (1, 0)])
        else:
            shards = lax.all_gather(decimated, "src", axis=0)
            rims = jnp.pad(
                shards[1:, :, width - EDGE :], ((0, 1), (0, 0), (out_count - EDGE, 0))
            )
            series = shards[:, :, :out_count] + rims
            series = series.transpose(1, 0, 2).reshape(rows, S)
            depth = S

    with jax.named_scope("prepare"):
        out_shape = [
            shaped(rows, NFFT),
            shaped(BINS, BINS, dtype=bf16),
            shaped(rows, LANES),
            shaped(slots, rows, LANES),
        ]
        if paired:
            out_shape += [shaped(out_count, NFFT, dtype=bf16)] * 2 + [shaped(SUBLANES, NFFT)]
        partial, band, alive, picks, *others = pl.pallas_call(
            prepare_kernel,
            out_shape=out_shape,
            in_specs=[VMEM] + [ANY] * 6,
            out_specs=[VMEM] * len(out_shape),
            scratch_shapes=[
                pltpu.VMEM((depth, NFFT), bf16),
                pltpu.VMEM((depth, NFFT), bf16),
                pltpu.VMEM((1, rows), jnp.int32),
                pltpu.VMEM((1, slots), jnp.int32),
                pltpu.VMEM((SUBLANES, NFFT), jnp.float32),
                pltpu.SemaphoreType.DMA((8,)),
            ],
            compiler_params=PARAMS,
            cost_estimate=pl.CostEstimate(
                flops=6 * rows * depth * NFFT, bytes_accessed=6 * S * NFFT, transcendentals=0
            ),
        )(
            series,
            alive_mask.reshape(1, rows),
            source_index,
            jnp.asarray(forward_hi),
            jnp.asarray(forward_lo),
            jnp.asarray(band_table()),
            jnp.asarray(edge),
        )

    with jax.named_scope("spectra"):
        operands = [partial, band, alive, picks]
        if paired:
            operands += [other] + others
        spectra, payload = pl.pallas_call(
            spectra_kernel,
            out_shape=(shaped(rows, NFFT), shaped(slots * NFFT // LANES, LANES)),
            in_specs=[VMEM] * len(operands),
            out_specs=(VMEM, VMEM),
            compiler_params=PARAMS,
        )(*operands)

    with jax.named_scope("gather_sources"):
        copies = jnp.broadcast_to(payload[None], (blk_count,) + payload.shape)
        sources = lax.all_to_all(copies, "blk", split_axis=0, concat_axis=0, tiled=True)

    with jax.named_scope("correlate"):
        total = group * slots
        return pl.pallas_call(
            lambda *refs: correlate_kernel(group, *refs),
            out_shape=shaped(total, rows, LAGS, dtype=bf16),
            in_specs=[VMEM] * 4,
            out_specs=ANY,
            scratch_shapes=[
                pltpu.VMEM((total * rows, NFFT), bf16),
                pltpu.VMEM((total, rows, LAGS), bf16),
                pltpu.SemaphoreType.DMA((4,)),
            ],
            compiler_params=PARAMS,
        )(spectra, sources, picks, jnp.asarray(lag_table()))


def solution(mesh):
    in_specs = (P("blk", "src"), P(), P("blk"), P("blk", None))
    out_specs = P("src", "blk", None)
    return jax.shard_map(local, mesh=mesh, in_specs=in_specs, out_specs=out_specs, check_vma=False)
```

```python
import math

import jax
import jax.numpy as jnp
import numpy as np
from jax import lax
from jax.experimental import pallas as pl
from jax.experimental.pallas import tpu as pltpu
from jax.sharding import PartitionSpec as P

S = 512
NFFT = 1024
BINS = NFFT // 2
LAGS = 512
TAPS = 64
DEC = 20
HALF = 64
LANES = 128
SUBLANES = 8
PAYLOAD = 4
EDGE = (TAPS - 1) // DEC
CHUNK = 640
CHUNK_OUT = CHUNK // DEC
VMEM_LIMIT = 48 * 1024 * 1024


def forward_table():
    phases = 2.0 * math.pi / NFFT * (np.outer(np.arange(S), np.arange(BINS)) % NFFT)
    return np.concatenate([np.cos(phases), -np.sin(phases)], axis=1).astype(np.float32)


def split_table(table):
    high = table.astype(jnp.bfloat16)
    low = (table - high.astype(np.float32)).astype(jnp.bfloat16)
    return high, low


def band_table():
    bins = np.arange(BINS)
    return (np.abs(bins[:, None] - bins[None, :]) <= HALF).astype(jnp.bfloat16)


def lag_table():
    bins = np.arange(BINS)[:, None]
    shift = np.arange(LAGS)[None, :] - LAGS // 2
    phases = 2.0 * math.pi / NFFT * (bins * shift % NFFT)
    weight = np.where(bins == 0, 0.5, 1.0) / math.sqrt(BINS)
    table = np.concatenate([weight * np.cos(phases), -weight * np.sin(phases)], axis=0)
    return table.astype(np.float32).astype(jnp.bfloat16)


def split(value):
    high = value.astype(jnp.bfloat16)
    return high, (value - high.astype(jnp.float32)).astype(jnp.bfloat16)


def dot(a, b):
    return jnp.dot(a, b, preferred_element_type=jnp.float32)


def dot_t(a, b):
    return lax.dot_general(a, b, (((1,), (1,)), ((), ())), preferred_element_type=jnp.float32)


def column(row):
    count = row.shape[1]
    at = [lax.broadcasted_iota(jnp.int32, (count, count), axis) for axis in range(2)]
    rows = jnp.broadcast_to(row, (count, count))
    return jnp.sum(jnp.where(at[0] == at[1], rows, 0.0), axis=1, keepdims=True)


def start_copies(pairs, sems):
    copies = [
        pltpu.make_async_copy(source, target, sems.at[at])
        for at, (source, target) in enumerate(pairs)
    ]
    for copy in copies:
        copy.start()
    return copies


def decimate_kernel(
    raw_hbm, taps_hbm, alive_hbm, picks_hbm, out_ref, payload_ref, raw_ref, taps_ref, alive_ref, picks_ref, sems
):
    rows = raw_hbm.shape[0]
    chunks = raw_hbm.shape[1] // CHUNK
    pairs = [(taps_hbm, taps_ref)]
    for j in range(chunks):
        span = slice(CHUNK * j, CHUNK * (j + 1))
        pairs.append((raw_hbm.at[:, span], raw_ref.at[rows * j : rows * (j + 1), :]))
    pairs += [(alive_hbm, alive_ref), (picks_hbm, picks_ref)]
    copies = start_copies(pairs, sems)
    copies[0].wait()
    taps = jnp.broadcast_to(taps_ref[...], (SUBLANES, TAPS))
    eight = jnp.concatenate([taps, jnp.zeros((SUBLANES, CHUNK - TAPS), jnp.float32)], axis=1)
    for _ in range(2):
        eight = pltpu.roll(eight, 0, 1, stride=DEC // 2, stride_axis=0)
    wrapped = jnp.concatenate(
        [eight]
        + [pltpu.roll(eight, DEC * at, 1) for at in range(SUBLANES, CHUNK_OUT, SUBLANES)],
        axis=0,
    )
    lane = lax.broadcasted_iota(jnp.int32, (CHUNK_OUT, CHUNK), 1)
    row = lax.broadcasted_iota(jnp.int32, (CHUNK_OUT, CHUNK), 0)
    main = jnp.where(lane >= DEC * row, wrapped, 0.0)
    rim = wrapped - main
    gap = jnp.zeros((LANES - 2 * CHUNK_OUT, CHUNK), jnp.float32)
    weights_hi, weights_lo = split(jnp.concatenate([main, gap, rim], axis=0))
    for copy in copies[1:]:
        copy.wait()
    raw_hi, raw_lo = split(raw_ref[...])
    both = dot_t(raw_hi, jnp.concatenate([weights_hi, weights_lo], axis=0))
    result = both[:, :LANES] + both[:, LANES:] + dot_t(raw_lo, weights_hi)
    part = [result[rows * j : rows * (j + 1)] for j in range(chunks)]
    per_tile = LANES // CHUNK_OUT
    col = lax.broadcasted_iota(jnp.int32, (rows, LANES), 1)
    is_main = col < LANES // 2
    tiles = -(-chunks // per_tile)
    results = []
    for tile in range(tiles):
        first = tile * per_tile
        total = jnp.where(is_main, part[first], 0.0)
        for step in range(1, min(per_tile, chunks - first)):
            total = total + pltpu.roll(part[first + step], CHUNK_OUT * step, 1)
        if first + per_tile < chunks:
            total = total + jnp.where(is_main, 0.0, part[first + per_tile])
        results.append(total)
    results.append(jnp.where(is_main, 0.0, part[0]))
    channel = lax.broadcasted_iota(jnp.int32, (rows, LANES), 0)
    alive = jnp.broadcast_to(column(alive_ref[...].astype(jnp.float32)), (rows, LANES))
    for slot in range(picks_ref.shape[1]):
        picked = channel == jnp.broadcast_to(picks_ref[:, slot : slot + 1], (rows, LANES))
        for at, value in enumerate(results + [alive]):
            row = slot * (tiles + 2) + at
            payload_ref[row : row + 1, :] = jnp.sum(
                jnp.where(picked, value, 0.0), axis=0, keepdims=True
            )
    for tile, value in enumerate(results):
        out_ref[:, LANES * tile : LANES * (tile + 1)] = value


def transform(series, table_hi, table_lo):
    rows = series.shape[0]
    high, low = split(series)
    first = dot(jnp.concatenate([high, low], axis=0), table_hi)
    return first[:rows] + first[rows:] + dot(high, table_lo)


def shard_transform(shard_ref, at, hi_ref, lo_ref):
    count = shard_ref.shape[1] - LANES
    span = pl.ds(pl.multiple_of(count * at, LANES), count + LANES)
    series = jnp.concatenate([shard_ref[:, count:], shard_ref[:, :count]], axis=1)
    return transform(series, hi_ref[span, :], lo_ref[span, :])


def whitening(spectrum, alive, band):
    rows = spectrum.shape[0]
    real_part = spectrum[:, :BINS]
    imag_part = spectrum[:, BINS:]
    power = real_part * real_part + imag_part * imag_part
    power_hi, rest = split(power)
    power_mid, power_lo = split(power - power_hi.astype(jnp.float32))
    banded = dot(jnp.concatenate([power_hi, power_mid, power_lo], axis=0), band)
    total = banded[:rows] + banded[rows : 2 * rows] + banded[2 * rows :]
    bins = lax.broadcasted_iota(jnp.int32, (1, BINS), 1)
    count = jnp.minimum(bins + HALF, BINS - 1) - jnp.maximum(bins - HALF, 0) + 1
    factor = alive / jnp.sqrt(total / count.astype(jnp.float32) + 1e-06)
    return real_part * factor, imag_part * factor


def prepare_kernel(
    series_ref, alive_hbm, picks_hbm, fwd_hi_hbm, fwd_lo_hbm, band_hbm,
    partial_ref, hi_ref, lo_ref, band_ref, alive_out, picks_out, alive_ref, picks_ref, sems,
):
    copies = start_copies(
        [
            (fwd_hi_hbm, hi_ref),
            (fwd_lo_hbm, lo_ref),
            (alive_hbm, alive_ref),
            (picks_hbm, picks_ref),
            (band_hbm, band_ref),
        ],
        sems,
    )
    for copy in copies:
        copy.wait()
    rows, depth = series_ref.shape
    if depth == S:
        partial_ref[...] = transform(series_ref[...], hi_ref[LANES:, :], lo_ref[LANES:, :])
    else:
        partial_ref[...] = shard_transform(series_ref, lax.axis_index("src"), hi_ref, lo_ref)
    alive_out[...] = jnp.broadcast_to(
        column(alive_ref[...].astype(jnp.float32)), (rows, LANES)
    )
    channel = lax.broadcasted_iota(jnp.int32, (rows, LANES), 0)
    for slot in range(picks_ref.shape[1]):
        pick = jnp.broadcast_to(picks_ref[:, slot : slot + 1], (rows, LANES))
        picks_out[slot] = jnp.where(channel == pick, 1.0, 0.0)


def spectra_kernel(partial_ref, band_ref, alive_ref, *refs):
    spectrum = partial_ref[...]
    spectra_ref = refs[-1]
    if len(refs) > 1:
        other_ref, hi_ref, lo_ref = refs[:3]
        there = 1 - lax.axis_index("src")
        spectrum = spectrum + shard_transform(other_ref, there, hi_ref, lo_ref)
    real_part, imag_part = whitening(spectrum, alive_ref[:, :1], band_ref[...])
    spectra_ref[:, :BINS] = real_part
    spectra_ref[:, BINS:] = imag_part


def correlate_kernel(
    slots, spectra_ref, sources_ref, picks_ref, hi_ref, lo_ref, band_ref, lag_ref, out_hbm,
    source_ref, cross_ref, out_ref, sems,
):
    rows = spectra_ref.shape[0]
    group = out_ref.shape[0] // slots
    half = BINS // LANES
    own = lax.axis_index("blk")
    base = lax.axis_index("src") * group
    stride = 2 * slots * PAYLOAD
    first_row = base * stride

    def entry(half_at, at):
        return jnp.concatenate(
            [
                sources_ref[
                    pl.ds(first_row + (half_at * slots + slot) * PAYLOAD + at, group, stride=stride), :
                ]
                for slot in range(slots)
            ],
            axis=0,
        )

    series = jnp.concatenate(
        [entry(0, 0), entry(0, 1) + entry(1, 2), entry(1, 0), entry(1, 1)], axis=1
    )
    spectrum = transform(series, hi_ref[LANES:, :], lo_ref[LANES:, :])
    real_part, imag_part = whitening(spectrum, entry(0, 3)[:, :1], band_ref[...])
    source_ref[:, :BINS] = real_part
    source_ref[:, BINS:] = imag_part
    per_part = max(1, (group * slots) // 4)
    copies = []
    for part in range(group * slots // per_part):
        first = part * per_part
        for source in range(first, first + per_part):
            block, slot = divmod(source, slots)
            is_own = jnp.where(own == base + block, 1.0, 0.0)
            keep = 1.0 - is_own * picks_ref[slot]
            at = slot * group + block
            for tile in range(half):
                re = slice(LANES * tile, LANES * (tile + 1))
                im = slice(BINS + LANES * tile, BINS + LANES * (tile + 1))
                src_re = source_ref[at : at + 1, re] * keep
                src_im = source_ref[at : at + 1, im] * keep
                rec_re, rec_im = spectra_ref[:, re], spectra_ref[:, im]
                where = slice(rows * source, rows * (source + 1))
                cross_ref[where, re] = (src_re * rec_re + src_im * rec_im).astype(jnp.bfloat16)
                cross_ref[where, im] = (src_re * rec_im - src_im * rec_re).astype(jnp.bfloat16)
        lagged = dot(cross_ref[rows * first : rows * (first + per_part), :], lag_ref[...])
        for source in range(first, first + per_part):
            at = source - first
            out_ref[source] = lagged[rows * at : rows * (at + 1)].astype(jnp.bfloat16)
        span = pl.ds(first, per_part)
        copies.append(pltpu.make_async_copy(out_ref.at[span], out_hbm.at[span], sems.at[part]))
        copies[-1].start()
    for copy in copies:
        copy.wait()


HBM = pl.BlockSpec(memory_space=pltpu.HBM)
VMEM = pl.BlockSpec(memory_space=pltpu.VMEM)
PARAMS = pltpu.CompilerParams(vmem_limit_bytes=VMEM_LIMIT)


def in_hbm(*arrays):
    return [pltpu.with_memory_space_constraint(array, pltpu.HBM) for array in arrays]


def shaped(*shape, dtype=jnp.float32):
    return jax.ShapeDtypeStruct(shape, dtype)


def local(raw_records, fir_taps, alive_mask, source_index):
    src_count = lax.axis_size("src")
    blk_count = lax.axis_size("blk")
    rows, raw_count = raw_records.shape
    slots = source_index.shape[1]
    group = blk_count // src_count
    out_count = raw_count // DEC
    width = -(-out_count // LANES) * LANES + LANES
    chunks = raw_count // CHUNK
    paired = src_count == 2 and 2 * out_count == S
    bf16 = jnp.bfloat16
    forward_hi, forward_lo = split_table(np.pad(forward_table(), ((LANES, 0), (0, 0))))
    alive_row = alive_mask.reshape(1, rows)

    with jax.named_scope("decimate"):
        payload_rows = width // LANES + 1
        decimated, payload = pl.pallas_call(
            decimate_kernel,
            out_shape=(shaped(rows, width), shaped(slots * payload_rows, LANES)),
            in_specs=[HBM] * 4,
            out_specs=(VMEM, VMEM),
            scratch_shapes=[
                pltpu.VMEM((rows * chunks, CHUNK), jnp.float32),
                pltpu.VMEM((1, TAPS), jnp.float32),
                pltpu.VMEM((1, rows), jnp.int32),
                pltpu.VMEM((1, slots), jnp.int32),
                pltpu.SemaphoreType.DMA((chunks + 3,)),
            ],
            compiler_params=PARAMS,
        )(*in_hbm(raw_records, fir_taps.reshape(1, TAPS), alive_row, source_index))

    def whole(shards):
        rims = jnp.pad(shards[1:, :, width - EDGE :], ((0, 1), (0, 0), (out_count - EDGE, 0)))
        series = shards[:, :, :out_count] + rims
        return series.transpose(1, 0, 2).reshape(shards.shape[1], S)

    with jax.named_scope("gather_sources"):
        gathered = lax.all_gather(payload, ("blk", "src"), axis=0, tiled=True)
        if not paired:
            shards = gathered.reshape(blk_count, src_count, slots, payload_rows, LANES)
            lives = shards[:, :1, :, payload_rows - 1 :]
            shards = shards[:, :, :, : payload_rows - 1].transpose(1, 0, 2, 3, 4)
            series = whole(shards.reshape(src_count, blk_count * slots, width))
            series = series.reshape(blk_count, slots, 2, S // 2 // LANES, LANES)
            series = jnp.pad(series, ((0, 0), (0, 0), (0, 0), (0, 1), (0, 0)))
            lives = jnp.broadcast_to(lives, (blk_count, 2, slots, 1, LANES))
            gathered = jnp.concatenate([series.transpose(0, 2, 1, 3, 4), lives], axis=3)
            gathered = gathered.reshape(blk_count * 2 * slots * PAYLOAD, LANES)

    with jax.named_scope("regroup"):
        if paired:
            series = decimated
            other = lax.ppermute(decimated, "src", [(0, 1), (1, 0)])
        else:
            series = whole(lax.all_gather(decimated, "src", axis=0))

    with jax.named_scope("prepare"):
        out_shape = (
            shaped(rows, NFFT),
            shaped(S + LANES, NFFT, dtype=bf16),
            shaped(S + LANES, NFFT, dtype=bf16),
            shaped(BINS, BINS, dtype=bf16),
            shaped(rows, LANES),
            shaped(slots, rows, LANES),
        )
        partial, table_hi, table_lo, band, alive, picks = pl.pallas_call(
            prepare_kernel,
            out_shape=out_shape,
            in_specs=[VMEM] + [HBM] * 5,
            out_specs=(VMEM,) * len(out_shape),
            scratch_shapes=[
                pltpu.VMEM((1, rows), jnp.int32),
                pltpu.VMEM((1, slots), jnp.int32),
                pltpu.SemaphoreType.DMA((5,)),
            ],
            compiler_params=PARAMS,
            cost_estimate=pl.CostEstimate(
                flops=6 * rows * S * NFFT, bytes_accessed=6 * S * NFFT, transcendentals=0
            ),
        )(
            series,
            *in_hbm(
                alive_row,
                source_index,
                jnp.asarray(forward_hi),
                jnp.asarray(forward_lo),
                jnp.asarray(band_table()),
            ),
        )

    with jax.named_scope("spectra"):
        operands = [partial, band, alive]
        if paired:
            operands += [other, table_hi, table_lo]
        spectra = pl.pallas_call(
            spectra_kernel,
            out_shape=shaped(rows, NFFT),
            in_specs=[VMEM] * len(operands),
            out_specs=VMEM,
            compiler_params=PARAMS,
        )(*operands)

    with jax.named_scope("correlate"):
        total = group * slots
        return pl.pallas_call(
            lambda *refs: correlate_kernel(slots, *refs),
            out_shape=shaped(total, rows, LAGS, dtype=bf16),
            in_specs=[VMEM] * 7,
            out_specs=HBM,
            scratch_shapes=[
                pltpu.VMEM((total, NFFT), jnp.float32),
                pltpu.VMEM((total * rows, NFFT), bf16),
                pltpu.VMEM((total, rows, LAGS), bf16),
                pltpu.SemaphoreType.DMA((4,)),
            ],
            compiler_params=PARAMS,
        )(spectra, gathered, picks, table_hi, table_lo, band, jnp.asarray(lag_table()))


def solution(mesh):
    in_specs = (P("blk", "src"), P(), P("blk"), P("blk", None))
    out_specs = P("src", "blk", None)
    return jax.shard_map(local, mesh=mesh, in_specs=in_specs, out_specs=out_specs, check_vma=False)
```

```python
import math

import jax
import jax.numpy as jnp
import numpy as np
from jax import lax
from jax.experimental import pallas as pl
from jax.experimental.pallas import tpu as pltpu
from jax.sharding import PartitionSpec as P

S = 512
NFFT = 1024
BINS = NFFT // 2
LAGS = 512
TAPS = 64
DEC = 20
HALF = 64
LANES = 128
SUBLANES = 8
DIRECT_STEPS = 3
EDGE = (TAPS - 1) // DEC
CHUNK = 640
CHUNK_OUT = CHUNK // DEC
VMEM_LIMIT = 48 * 1024 * 1024


def forward_table():
    phases = 2.0 * math.pi / NFFT * (np.outer(np.arange(S), np.arange(BINS)) % NFFT)
    return np.concatenate([np.cos(phases), -np.sin(phases)], axis=1).astype(np.float32)


def split_table(table):
    high = table.astype(jnp.bfloat16)
    low = (table - high.astype(np.float32)).astype(jnp.bfloat16)
    return high, low


def band_table():
    bins = np.arange(BINS)
    return (np.abs(bins[:, None] - bins[None, :]) <= HALF).astype(jnp.bfloat16)


def lag_table():
    bins = np.arange(BINS)[:, None]
    shift = np.arange(LAGS)[None, :] - LAGS // 2
    phases = 2.0 * math.pi / NFFT * (bins * shift % NFFT)
    weight = np.where(bins == 0, 0.5, 1.0) / math.sqrt(BINS)
    table = np.concatenate([weight * np.cos(phases), -weight * np.sin(phases)], axis=0)
    return table.astype(np.float32).astype(jnp.bfloat16)


def split(value):
    high = value.astype(jnp.bfloat16)
    return high, (value - high.astype(jnp.float32)).astype(jnp.bfloat16)


def dot(a, b):
    return jnp.dot(a, b, preferred_element_type=jnp.float32)


def dot_t(a, b):
    return lax.dot_general(a, b, (((1,), (1,)), ((), ())), preferred_element_type=jnp.float32)


def column(row):
    count = row.shape[1]
    at = [lax.broadcasted_iota(jnp.int32, (count, count), axis) for axis in range(2)]
    rows = jnp.broadcast_to(row, (count, count))
    return jnp.sum(jnp.where(at[0] == at[1], rows, 0.0), axis=1, keepdims=True)


def start_copies(pairs, sems):
    copies = [
        pltpu.make_async_copy(source, target, sems.at[at])
        for at, (source, target) in enumerate(pairs)
    ]
    for copy in copies:
        copy.start()
    return copies


def decimate_kernel(raw_hbm, taps_hbm, out_ref, raw_ref, taps_ref, sems):
    rows = raw_hbm.shape[0]
    chunks = raw_hbm.shape[1] // CHUNK
    pairs = [(taps_hbm, taps_ref)]
    for j in range(chunks):
        span = slice(CHUNK * j, CHUNK * (j + 1))
        pairs.append((raw_hbm.at[:, span], raw_ref.at[rows * j : rows * (j + 1), :]))
    copies = start_copies(pairs, sems)
    copies[0].wait()
    taps = jnp.broadcast_to(taps_ref[...], (SUBLANES, TAPS))
    eight = jnp.concatenate([taps, jnp.zeros((SUBLANES, CHUNK - TAPS), jnp.float32)], axis=1)
    for _ in range(2):
        eight = pltpu.roll(eight, 0, 1, stride=DEC // 2, stride_axis=0)
    wrapped = jnp.concatenate(
        [eight]
        + [pltpu.roll(eight, DEC * at, 1) for at in range(SUBLANES, CHUNK_OUT, SUBLANES)],
        axis=0,
    )
    lane = lax.broadcasted_iota(jnp.int32, (CHUNK_OUT, CHUNK), 1)
    row = lax.broadcasted_iota(jnp.int32, (CHUNK_OUT, CHUNK), 0)
    main = jnp.where(lane >= DEC * row, wrapped, 0.0)
    rim = wrapped - main
    gap = jnp.zeros((LANES - 2 * CHUNK_OUT, CHUNK), jnp.float32)
    weights_hi, weights_lo = split(jnp.concatenate([main, gap, rim], axis=0))
    for copy in copies[1:]:
        copy.wait()
    raw_hi, raw_lo = split(raw_ref[...])
    both = dot_t(raw_hi, jnp.concatenate([weights_hi, weights_lo], axis=0))
    result = both[:, :LANES] + both[:, LANES:] + dot_t(raw_lo, weights_hi)
    part = [result[rows * j : rows * (j + 1)] for j in range(chunks)]
    per_tile = LANES // CHUNK_OUT
    col = lax.broadcasted_iota(jnp.int32, (rows, LANES), 1)
    is_main = col < LANES // 2
    tiles = -(-chunks // per_tile)
    for tile in range(tiles):
        first = tile * per_tile
        total = jnp.where(is_main, part[first], 0.0)
        for step in range(1, min(per_tile, chunks - first)):
            total = total + pltpu.roll(part[first + step], CHUNK_OUT * step, 1)
        if first + per_tile < chunks:
            total = total + jnp.where(is_main, 0.0, part[first + per_tile])
        out_ref[:, LANES * tile : LANES * (tile + 1)] = total
    out_ref[:, LANES * tiles :] = jnp.where(is_main, 0.0, part[0])


def transform(series, table_hi, table_lo):
    rows = series.shape[0]
    high, low = split(series)
    first = dot(jnp.concatenate([high, low], axis=0), table_hi)
    return first[:rows] + first[rows:] + dot(high, table_lo)


def shard_transform(shard_ref, at, hi_ref, lo_ref):
    count = shard_ref.shape[1] - LANES
    span = pl.ds(pl.multiple_of(count * at, LANES), count + LANES)
    series = jnp.concatenate([shard_ref[:, count:], shard_ref[:, :count]], axis=1)
    return transform(series, hi_ref[span, :], lo_ref[span, :])


def whitening(spectrum, alive, band):
    rows = spectrum.shape[0]
    real_part = spectrum[:, :BINS]
    imag_part = spectrum[:, BINS:]
    power = real_part * real_part + imag_part * imag_part
    power_hi, rest = split(power)
    power_mid, power_lo = split(power - power_hi.astype(jnp.float32))
    banded = dot(jnp.concatenate([power_hi, power_mid, power_lo], axis=0), band)
    total = banded[:rows] + banded[rows : 2 * rows] + banded[2 * rows :]
    bins = lax.broadcasted_iota(jnp.int32, (1, BINS), 1)
    count = jnp.minimum(bins + HALF, BINS - 1) - jnp.maximum(bins - HALF, 0) + 1
    factor = alive / jnp.sqrt(total / count.astype(jnp.float32) + 1e-06)
    return real_part * factor, imag_part * factor


def prepare_kernel(
    series_ref, alive_hbm, picks_hbm, fwd_hi_hbm, fwd_lo_hbm, band_hbm,
    partial_ref, hi_ref, lo_ref, band_ref, alive_out, picks_out, alive_ref, picks_ref, sems,
):
    copies = start_copies(
        [
            (fwd_hi_hbm, hi_ref),
            (fwd_lo_hbm, lo_ref),
            (alive_hbm, alive_ref),
            (picks_hbm, picks_ref),
            (band_hbm, band_ref),
        ],
        sems,
    )
    for copy in copies:
        copy.wait()
    rows, depth = series_ref.shape
    if depth == S:
        partial_ref[...] = transform(series_ref[...], hi_ref[LANES:, :], lo_ref[LANES:, :])
    else:
        partial_ref[...] = shard_transform(series_ref, lax.axis_index("src"), hi_ref, lo_ref)
    alive_out[...] = jnp.broadcast_to(
        column(alive_ref[...].astype(jnp.float32)), (rows, LANES)
    )
    channel = lax.broadcasted_iota(jnp.int32, (rows, LANES), 0)
    for slot in range(picks_ref.shape[1]):
        pick = jnp.broadcast_to(picks_ref[:, slot : slot + 1], (rows, LANES))
        picks_out[slot] = jnp.where(channel == pick, 1.0, 0.0)


def spectra_kernel(partial_ref, band_ref, alive_ref, picks_ref, *refs):
    spectrum = partial_ref[...]
    spectra_ref, payload_ref = refs[-2:]
    if len(refs) > 2:
        other_ref, hi_ref, lo_ref = refs[:3]
        there = 1 - lax.axis_index("src")
        spectrum = spectrum + shard_transform(other_ref, there, hi_ref, lo_ref)
    whitened = whitening(spectrum, alive_ref[:, :1], band_ref[...])
    tiles = NFFT // LANES
    for tile in range(tiles):
        at = LANES * (tile % (tiles // 2))
        value = whitened[tile // (tiles // 2)][:, at : at + LANES]
        spectra_ref[:, LANES * tile : LANES * (tile + 1)] = value
        for slot in range(picks_ref.shape[0]):
            row = slot * tiles + tile
            payload_ref[0, row : row + 1, :] = jnp.sum(
                value * picks_ref[slot], axis=0, keepdims=True
            )


def correlate_kernel(
    group, direct, spectra_ref, picks_ref, lag_ref, *refs
):
    out_hbm, source_ref, cross_ref, out_ref, sems = refs[-5:]
    rows = spectra_ref.shape[0]
    slots = picks_ref.shape[0]
    tiles = NFFT // LANES
    half = tiles // 2
    own = lax.axis_index("blk")
    base = lax.axis_index("src") * group
    if direct:
        core = own & 1
        for at, ref in enumerate(refs[:-5]):
            source_ref[2 * at : 2 * at + 2] = ref[...]

    def place_of(block):
        relative = (base + block) ^ own
        if not direct:
            return relative
        chip = relative >> 1
        by_even = (chip == 3) | (chip == 5)
        step = jnp.where((chip == 2) | (chip == 6), 2, jnp.where(chip == 7, 3, 1))
        sender = jnp.where(by_even, 0, 1)
        entry = jnp.where(sender == core, step, step + DIRECT_STEPS)
        order = ((base + block) & 1) ^ sender
        return jnp.where(chip == 0, relative, 2 * entry + order)

    sources = source_ref if direct else refs[0]
    per_part = max(1, (group * slots) // 4)
    copies = []
    for part in range(group * slots // per_part):
        first = part * per_part
        for source in range(first, first + per_part):
            block, slot = divmod(source, slots)
            place = place_of(block)
            is_own = jnp.where(own == base + block, 1.0, 0.0)
            keep = 1.0 - is_own * picks_ref[slot]
            for tile in range(half):
                at = slot * tiles + tile
                re = slice(LANES * tile, LANES * (tile + 1))
                im = slice(BINS + LANES * tile, BINS + LANES * (tile + 1))
                src_re = sources[place, at : at + 1, :] * keep
                src_im = sources[place, at + half : at + half + 1, :] * keep
                rec_re, rec_im = spectra_ref[:, re], spectra_ref[:, im]
                where = slice(rows * source, rows * (source + 1))
                cross_ref[where, re] = (src_re * rec_re + src_im * rec_im).astype(jnp.bfloat16)
                cross_ref[where, im] = (src_re * rec_im - src_im * rec_re).astype(jnp.bfloat16)
        lagged = dot(cross_ref[rows * first : rows * (first + per_part), :], lag_ref[...])
        for source in range(first, first + per_part):
            at = source - first
            out_ref[source] = lagged[rows * at : rows * (at + 1)].astype(jnp.bfloat16)
        span = pl.ds(first, per_part)
        copies.append(pltpu.make_async_copy(out_ref.at[span], out_hbm.at[span], sems.at[part]))
        copies[-1].start()
    for copy in copies:
        copy.wait()


HBM = pl.BlockSpec(memory_space=pltpu.HBM)
VMEM = pl.BlockSpec(memory_space=pltpu.VMEM)
PARAMS = pltpu.CompilerParams(vmem_limit_bytes=VMEM_LIMIT)


def in_hbm(*arrays):
    return [pltpu.with_memory_space_constraint(array, pltpu.HBM) for array in arrays]


def shaped(*shape, dtype=jnp.float32):
    return jax.ShapeDtypeStruct(shape, dtype)


def gather_doubling(payload, blk_count):
    step = 1
    while step < blk_count:
        arrived = lax.ppermute(payload, "blk", [(b, b ^ step) for b in range(blk_count)])
        payload = jnp.concatenate([payload, arrived], axis=0)
        step *= 2
    return payload


def gather_direct(payload, blk_count, src_count):
    half = blk_count // src_count
    own = lax.ppermute(payload, "blk", [(b, b ^ 1) for b in range(blk_count)])
    pair = jnp.concatenate([payload, own], axis=0)
    home = {0: (6, None, None), 1: (2, 4, None)}
    away = {0: (10, None, None), 1: (8, 12, 14)}
    received = []
    for step in range(DIRECT_STEPS):
        moves = []
        for b in range(blk_count):
            for s in range(src_count):
                at_home = b // half == s
                mask = (home if at_home else away)[b % 2][step]
                if mask is not None:
                    to = (b ^ mask) * src_count + (s if at_home else 1 - s)
                    moves.append((b * src_count + s, to))
        received.append(lax.ppermute(pair, ("blk", "src"), moves))
    twins = []
    for step, array in enumerate(received):
        moves = [(b, b ^ 1) for b in range(blk_count) if away[b % 2][step] is not None]
        twins.append(lax.ppermute(array, "blk", moves))
    return [pair] + received + twins


def local(raw_records, fir_taps, alive_mask, source_index):
    src_count = lax.axis_size("src")
    blk_count = lax.axis_size("blk")
    rows, raw_count = raw_records.shape
    slots = source_index.shape[1]
    group = blk_count // src_count
    out_count = raw_count // DEC
    width = -(-out_count // LANES) * LANES + LANES
    chunks = raw_count // CHUNK
    paired = src_count == 2 and 2 * out_count == S
    bf16 = jnp.bfloat16
    forward_hi, forward_lo = split_table(np.pad(forward_table(), ((LANES, 0), (0, 0))))
    alive_row = alive_mask.reshape(1, rows)

    with jax.named_scope("decimate"):
        decimated = pl.pallas_call(
            decimate_kernel,
            out_shape=shaped(rows, width),
            in_specs=[HBM] * 2,
            out_specs=VMEM,
            scratch_shapes=[
                pltpu.VMEM((rows * chunks, CHUNK), jnp.float32),
                pltpu.VMEM((1, TAPS), jnp.float32),
                pltpu.SemaphoreType.DMA((chunks + 1,)),
            ],
            compiler_params=PARAMS,
        )(*in_hbm(raw_records, fir_taps.reshape(1, TAPS)))

    def whole(shards):
        rims = jnp.pad(shards[1:, :, width - EDGE :], ((0, 1), (0, 0), (out_count - EDGE, 0)))
        series = shards[:, :, :out_count] + rims
        return series.transpose(1, 0, 2).reshape(shards.shape[1], S)

    with jax.named_scope("regroup"):
        if paired:
            series = decimated
            other = lax.ppermute(decimated, "src", [(0, 1), (1, 0)])
        else:
            series = whole(lax.all_gather(decimated, "src", axis=0))

    with jax.named_scope("prepare"):
        out_shape = (
            shaped(rows, NFFT),
            shaped(S + LANES, NFFT, dtype=bf16),
            shaped(S + LANES, NFFT, dtype=bf16),
            shaped(BINS, BINS, dtype=bf16),
            shaped(rows, LANES),
            shaped(slots, rows, LANES),
        )
        partial, table_hi, table_lo, band, alive, picks = pl.pallas_call(
            prepare_kernel,
            out_shape=out_shape,
            in_specs=[VMEM] + [HBM] * 5,
            out_specs=(VMEM,) * len(out_shape),
            scratch_shapes=[
                pltpu.VMEM((1, rows), jnp.int32),
                pltpu.VMEM((1, slots), jnp.int32),
                pltpu.SemaphoreType.DMA((5,)),
            ],
            compiler_params=PARAMS,
            cost_estimate=pl.CostEstimate(
                flops=6 * rows * S * NFFT, bytes_accessed=6 * S * NFFT, transcendentals=0
            ),
        )(
            series,
            *in_hbm(
                alive_row,
                source_index,
                jnp.asarray(forward_hi),
                jnp.asarray(forward_lo),
                jnp.asarray(band_table()),
            ),
        )

    with jax.named_scope("spectra"):
        operands = [partial, band, alive, picks]
        if paired:
            operands += [other, table_hi, table_lo]
        spectra, payload = pl.pallas_call(
            spectra_kernel,
            out_shape=(shaped(rows, NFFT), shaped(1, slots * NFFT // LANES, LANES)),
            in_specs=[VMEM] * len(operands),
            out_specs=(VMEM, VMEM),
            compiler_params=PARAMS,
        )(*operands)

    with jax.named_scope("gather_sources"):
        direct = paired and group == 8
        if direct:
            payloads = gather_direct(payload, blk_count, src_count)
        else:
            payloads = [gather_doubling(payload, blk_count)]

    with jax.named_scope("correlate"):
        total = group * slots
        held = sum(array.shape[0] for array in payloads)
        return pl.pallas_call(
            lambda *refs: correlate_kernel(group, direct, *refs),
            out_shape=shaped(total, rows, LAGS, dtype=bf16),
            in_specs=[VMEM] * (3 + len(payloads)),
            out_specs=HBM,
            scratch_shapes=[
                pltpu.VMEM((held,) + payload.shape[1:], jnp.float32),
                pltpu.VMEM((total * rows, NFFT), bf16),
                pltpu.VMEM((total, rows, LAGS), bf16),
                pltpu.SemaphoreType.DMA((4,)),
            ],
            compiler_params=PARAMS,
        )(spectra, picks, jnp.asarray(lag_table()), *payloads)


def solution(mesh):
    in_specs = (P("blk", "src"), P(), P("blk"), P("blk", None))
    out_specs = P("src", "blk", None)
    return jax.shard_map(local, mesh=mesh, in_specs=in_specs, out_specs=out_specs, check_vma=False)
```

```python
import math

import jax
import jax.numpy as jnp
import numpy as np
from jax import lax
from jax.experimental import pallas as pl
from jax.experimental.pallas import tpu as pltpu
from jax.sharding import PartitionSpec as P

S = 512
NFFT = 1024
BINS = NFFT // 2
LAGS = 512
TAPS = 64
DEC = 20
HALF = 64
LANES = 128
SUBLANES = 8
PAYLOAD = 4
EDGE = (TAPS - 1) // DEC
CHUNK = 640
CHUNK_OUT = CHUNK // DEC
VMEM_LIMIT = 48 * 1024 * 1024


def forward_table():
    phases = 2.0 * math.pi / NFFT * (np.outer(np.arange(S), np.arange(BINS)) % NFFT)
    return np.concatenate([np.cos(phases), -np.sin(phases)], axis=1).astype(np.float32)


def split_table(table):
    high = table.astype(jnp.bfloat16)
    low = (table - high.astype(np.float32)).astype(jnp.bfloat16)
    return high, low


def band_table():
    bins = np.arange(BINS)
    return (np.abs(bins[:, None] - bins[None, :]) <= HALF).astype(jnp.bfloat16)


def lag_table():
    bins = np.arange(BINS)[:, None]
    shift = np.arange(LAGS)[None, :] - LAGS // 2
    phases = 2.0 * math.pi / NFFT * (bins * shift % NFFT)
    weight = np.where(bins == 0, 0.5, 1.0) / math.sqrt(BINS)
    table = np.concatenate([weight * np.cos(phases), -weight * np.sin(phases)], axis=0)
    return table.astype(np.float32).astype(jnp.bfloat16)


def split(value):
    high = value.astype(jnp.bfloat16)
    return high, (value - high.astype(jnp.float32)).astype(jnp.bfloat16)


def dot(a, b):
    return jnp.dot(a, b, preferred_element_type=jnp.float32)


def dot_t(a, b):
    return lax.dot_general(a, b, (((1,), (1,)), ((), ())), preferred_element_type=jnp.float32)


def column(row):
    count = row.shape[1]
    at = [lax.broadcasted_iota(jnp.int32, (count, count), axis) for axis in range(2)]
    rows = jnp.broadcast_to(row, (count, count))
    return jnp.sum(jnp.where(at[0] == at[1], rows, 0.0), axis=1, keepdims=True)


def start_copies(pairs, sems):
    copies = [
        pltpu.make_async_copy(source, target, sems.at[at])
        for at, (source, target) in enumerate(pairs)
    ]
    for copy in copies:
        copy.start()
    return copies


def decimate_kernel(
    raw_hbm, taps_hbm, alive_hbm, picks_hbm, out_ref, payload_ref, raw_ref, taps_ref, alive_ref, picks_ref, sems
):
    rows = raw_hbm.shape[0]
    chunks = raw_hbm.shape[1] // CHUNK
    pairs = [(taps_hbm, taps_ref)]
    for j in range(chunks):
        span = slice(CHUNK * j, CHUNK * (j + 1))
        pairs.append((raw_hbm.at[:, span], raw_ref.at[rows * j : rows * (j + 1), :]))
    pairs += [(alive_hbm, alive_ref), (picks_hbm, picks_ref)]
    copies = start_copies(pairs, sems)
    copies[0].wait()
    taps = jnp.broadcast_to(taps_ref[...], (SUBLANES, TAPS))
    eight = jnp.concatenate([taps, jnp.zeros((SUBLANES, CHUNK - TAPS), jnp.float32)], axis=1)
    for _ in range(2):
        eight = pltpu.roll(eight, 0, 1, stride=DEC // 2, stride_axis=0)
    wrapped = jnp.concatenate(
        [eight]
        + [pltpu.roll(eight, DEC * at, 1) for at in range(SUBLANES, CHUNK_OUT, SUBLANES)],
        axis=0,
    )
    lane = lax.broadcasted_iota(jnp.int32, (CHUNK_OUT, CHUNK), 1)
    row = lax.broadcasted_iota(jnp.int32, (CHUNK_OUT, CHUNK), 0)
    main = jnp.where(lane >= DEC * row, wrapped, 0.0)
    rim = wrapped - main
    gap = jnp.zeros((LANES - 2 * CHUNK_OUT, CHUNK), jnp.float32)
    weights_hi, weights_lo = split(jnp.concatenate([main, gap, rim], axis=0))
    for copy in copies[1:]:
        copy.wait()
    raw_hi, raw_lo = split(raw_ref[...])
    both = dot_t(raw_hi, jnp.concatenate([weights_hi, weights_lo], axis=0))
    result = both[:, :LANES] + both[:, LANES:] + dot_t(raw_lo, weights_hi)
    part = [result[rows * j : rows * (j + 1)] for j in range(chunks)]
    per_tile = LANES // CHUNK_OUT
    col = lax.broadcasted_iota(jnp.int32, (rows, LANES), 1)
    is_main = col < LANES // 2
    tiles = -(-chunks // per_tile)
    results = []
    for tile in range(tiles):
        first = tile * per_tile
        total = jnp.where(is_main, part[first], 0.0)
        for step in range(1, min(per_tile, chunks - first)):
            total = total + pltpu.roll(part[first + step], CHUNK_OUT * step, 1)
        if first + per_tile < chunks:
            total = total + jnp.where(is_main, 0.0, part[first + per_tile])
        results.append(total)
    results.append(jnp.where(is_main, 0.0, part[0]))
    channel = lax.broadcasted_iota(jnp.int32, (rows, LANES), 0)
    alive = jnp.broadcast_to(column(alive_ref[...].astype(jnp.float32)), (rows, LANES))
    for slot in range(picks_ref.shape[1]):
        picked = channel == jnp.broadcast_to(picks_ref[:, slot : slot + 1], (rows, LANES))
        for at, value in enumerate(results + [alive]):
            row = slot * (tiles + 2) + at
            payload_ref[row : row + 1, :] = jnp.sum(
                jnp.where(picked, value, 0.0), axis=0, keepdims=True
            )
    for tile, value in enumerate(results):
        out_ref[:, LANES * tile : LANES * (tile + 1)] = value


def transform(series, table_hi, table_lo):
    rows = series.shape[0]
    high, low = split(series)
    first = dot(jnp.concatenate([high, low], axis=0), table_hi)
    return first[:rows] + first[rows:] + dot(high, table_lo)


def shard_transform(shard_ref, at, hi_ref, lo_ref):
    count = shard_ref.shape[1] - LANES
    span = pl.ds(pl.multiple_of(count * at, LANES), count + LANES)
    series = jnp.concatenate([shard_ref[:, count:], shard_ref[:, :count]], axis=1)
    return transform(series, hi_ref[span, :], lo_ref[span, :])


def whitening(spectrum, alive, band):
    rows = spectrum.shape[0]
    real_part = spectrum[:, :BINS]
    imag_part = spectrum[:, BINS:]
    power = real_part * real_part + imag_part * imag_part
    power_hi, rest = split(power)
    power_mid, power_lo = split(power - power_hi.astype(jnp.float32))
    banded = dot(jnp.concatenate([power_hi, power_mid, power_lo], axis=0), band)
    total = banded[:rows] + banded[rows : 2 * rows] + banded[2 * rows :]
    bins = lax.broadcasted_iota(jnp.int32, (1, BINS), 1)
    count = jnp.minimum(bins + HALF, BINS - 1) - jnp.maximum(bins - HALF, 0) + 1
    factor = alive / jnp.sqrt(total / count.astype(jnp.float32) + 1e-06)
    return real_part * factor, imag_part * factor


def prepare_kernel(
    series_ref, alive_hbm, picks_hbm, fwd_hi_hbm, fwd_lo_hbm, band_hbm,
    partial_ref, hi_ref, lo_ref, band_ref, alive_out, picks_out, alive_ref, picks_ref, sems,
):
    copies = start_copies(
        [
            (fwd_hi_hbm, hi_ref),
            (fwd_lo_hbm, lo_ref),
            (alive_hbm, alive_ref),
            (picks_hbm, picks_ref),
            (band_hbm, band_ref),
        ],
        sems,
    )
    for copy in copies:
        copy.wait()
    rows, depth = series_ref.shape
    if depth == S:
        partial_ref[...] = transform(series_ref[...], hi_ref[LANES:, :], lo_ref[LANES:, :])
    else:
        partial_ref[...] = shard_transform(series_ref, lax.axis_index("src"), hi_ref, lo_ref)
    alive_out[...] = jnp.broadcast_to(
        column(alive_ref[...].astype(jnp.float32)), (rows, LANES)
    )
    channel = lax.broadcasted_iota(jnp.int32, (rows, LANES), 0)
    for slot in range(picks_ref.shape[1]):
        pick = jnp.broadcast_to(picks_ref[:, slot : slot + 1], (rows, LANES))
        picks_out[slot] = jnp.where(channel == pick, 1.0, 0.0)


def spectra_kernel(partial_ref, band_ref, alive_ref, *refs):
    spectrum = partial_ref[...]
    spectra_ref = refs[-1]
    if len(refs) > 1:
        other_ref, hi_ref, lo_ref = refs[:3]
        there = 1 - lax.axis_index("src")
        spectrum = spectrum + shard_transform(other_ref, there, hi_ref, lo_ref)
    real_part, imag_part = whitening(spectrum, alive_ref[:, :1], band_ref[...])
    spectra_ref[:, :BINS] = real_part
    spectra_ref[:, BINS:] = imag_part


def correlate_kernel(
    slots, spectra_ref, sources_ref, picks_ref, hi_ref, lo_ref, band_ref, lag_ref, out_hbm,
    source_ref, cross_ref, out_ref, sems,
):
    rows = spectra_ref.shape[0]
    group = out_ref.shape[0] // slots
    half = BINS // LANES
    own = lax.axis_index("blk")
    base = lax.axis_index("src") * group
    stride = 2 * slots * PAYLOAD
    first_row = base * stride

    def entry(half_at, at):
        return jnp.concatenate(
            [
                sources_ref[
                    pl.ds(first_row + (half_at * slots + slot) * PAYLOAD + at, group, stride=stride), :
                ]
                for slot in range(slots)
            ],
            axis=0,
        )

    series = jnp.concatenate(
        [entry(0, 0), entry(0, 1) + entry(1, 2), entry(1, 0), entry(1, 1)], axis=1
    )
    spectrum = transform(series, hi_ref[LANES:, :], lo_ref[LANES:, :])
    real_part, imag_part = whitening(spectrum, entry(0, 3)[:, :1], band_ref[...])
    source_ref[:, :BINS] = real_part
    source_ref[:, BINS:] = imag_part
    per_part = max(1, (group * slots) // 4)
    copies = []
    for part in range(group * slots // per_part):
        first = part * per_part
        for source in range(first, first + per_part):
            block, slot = divmod(source, slots)
            is_own = jnp.where(own == base + block, 1.0, 0.0)
            keep = 1.0 - is_own * picks_ref[slot]
            at = slot * group + block
            for tile in range(half):
                re = slice(LANES * tile, LANES * (tile + 1))
                im = slice(BINS + LANES * tile, BINS + LANES * (tile + 1))
                src_re = source_ref[at : at + 1, re] * keep
                src_im = source_ref[at : at + 1, im] * keep
                rec_re, rec_im = spectra_ref[:, re], spectra_ref[:, im]
                where = slice(rows * source, rows * (source + 1))
                cross_ref[where, re] = (src_re * rec_re + src_im * rec_im).astype(jnp.bfloat16)
                cross_ref[where, im] = (src_re * rec_im - src_im * rec_re).astype(jnp.bfloat16)
        lagged = dot(cross_ref[rows * first : rows * (first + per_part), :], lag_ref[...])
        for source in range(first, first + per_part):
            at = source - first
            out_ref[source] = lagged[rows * at : rows * (at + 1)].astype(jnp.bfloat16)
        span = pl.ds(first, per_part)
        copies.append(pltpu.make_async_copy(out_ref.at[span], out_hbm.at[span], sems.at[part]))
        copies[-1].start()
    for copy in copies:
        copy.wait()


HBM = pl.BlockSpec(memory_space=pltpu.HBM)
VMEM = pl.BlockSpec(memory_space=pltpu.VMEM)
PARAMS = pltpu.CompilerParams(vmem_limit_bytes=VMEM_LIMIT)


def in_hbm(*arrays):
    return [pltpu.with_memory_space_constraint(array, pltpu.HBM) for array in arrays]


def shaped(*shape, dtype=jnp.float32):
    return jax.ShapeDtypeStruct(shape, dtype)


def local(raw_records, fir_taps, alive_mask, source_index):
    src_count = lax.axis_size("src")
    blk_count = lax.axis_size("blk")
    rows, raw_count = raw_records.shape
    slots = source_index.shape[1]
    group = blk_count // src_count
    out_count = raw_count // DEC
    width = -(-out_count // LANES) * LANES + LANES
    chunks = raw_count // CHUNK
    paired = src_count == 2 and 2 * out_count == S
    bf16 = jnp.bfloat16
    forward_hi, forward_lo = split_table(np.pad(forward_table(), ((LANES, 0), (0, 0))))
    alive_row = alive_mask.reshape(1, rows)

    with jax.named_scope("decimate"):
        payload_rows = width // LANES + 1
        decimated, payload = pl.pallas_call(
            decimate_kernel,
            out_shape=(shaped(rows, width), shaped(slots * payload_rows, LANES)),
            in_specs=[HBM] * 4,
            out_specs=(VMEM, VMEM),
            scratch_shapes=[
                pltpu.VMEM((rows * chunks, CHUNK), jnp.float32),
                pltpu.VMEM((1, TAPS), jnp.float32),
                pltpu.VMEM((1, rows), jnp.int32),
                pltpu.VMEM((1, slots), jnp.int32),
                pltpu.SemaphoreType.DMA((chunks + 3,)),
            ],
            compiler_params=PARAMS,
        )(*in_hbm(raw_records, fir_taps.reshape(1, TAPS), alive_row, source_index))

    def whole(shards):
        rims = jnp.pad(shards[1:, :, width - EDGE :], ((0, 1), (0, 0), (out_count - EDGE, 0)))
        series = shards[:, :, :out_count] + rims
        return series.transpose(1, 0, 2).reshape(shards.shape[1], S)

    with jax.named_scope("gather_sources"):
        device_count = blk_count * src_count
        copies = jnp.broadcast_to(payload[None], (device_count,) + payload.shape)
        gathered = lax.all_to_all(copies, ("blk", "src"), split_axis=0, concat_axis=0, tiled=True)
        gathered = gathered.reshape(device_count * payload.shape[0], LANES)
        if not paired:
            shards = gathered.reshape(blk_count, src_count, slots, payload_rows, LANES)
            lives = shards[:, :1, :, payload_rows - 1 :]
            shards = shards[:, :, :, : payload_rows - 1].transpose(1, 0, 2, 3, 4)
            series = whole(shards.reshape(src_count, blk_count * slots, width))
            series = series.reshape(blk_count, slots, 2, S // 2 // LANES, LANES)
            series = jnp.pad(series, ((0, 0), (0, 0), (0, 0), (0, 1), (0, 0)))
            lives = jnp.broadcast_to(lives, (blk_count, 2, slots, 1, LANES))
            gathered = jnp.concatenate([series.transpose(0, 2, 1, 3, 4), lives], axis=3)
            gathered = gathered.reshape(blk_count * 2 * slots * PAYLOAD, LANES)

    with jax.named_scope("regroup"):
        if paired:
            series = decimated
            other = lax.ppermute(decimated, "src", [(0, 1), (1, 0)])
        else:
            series = whole(lax.all_gather(decimated, "src", axis=0))

    with jax.named_scope("prepare"):
        out_shape = (
            shaped(rows, NFFT),
            shaped(S + LANES, NFFT, dtype=bf16),
            shaped(S + LANES, NFFT, dtype=bf16),
            shaped(BINS, BINS, dtype=bf16),
            shaped(rows, LANES),
            shaped(slots, rows, LANES),
        )
        partial, table_hi, table_lo, band, alive, picks = pl.pallas_call(
            prepare_kernel,
            out_shape=out_shape,
            in_specs=[VMEM] + [HBM] * 5,
            out_specs=(VMEM,) * len(out_shape),
            scratch_shapes=[
                pltpu.VMEM((1, rows), jnp.int32),
                pltpu.VMEM((1, slots), jnp.int32),
                pltpu.SemaphoreType.DMA((5,)),
            ],
            compiler_params=PARAMS,
            cost_estimate=pl.CostEstimate(
                flops=6 * rows * S * NFFT, bytes_accessed=6 * S * NFFT, transcendentals=0
            ),
        )(
            series,
            *in_hbm(
                alive_row,
                source_index,
                jnp.asarray(forward_hi),
                jnp.asarray(forward_lo),
                jnp.asarray(band_table()),
            ),
        )

    with jax.named_scope("spectra"):
        operands = [partial, band, alive]
        if paired:
            operands += [other, table_hi, table_lo]
        spectra = pl.pallas_call(
            spectra_kernel,
            out_shape=shaped(rows, NFFT),
            in_specs=[VMEM] * len(operands),
            out_specs=VMEM,
            compiler_params=PARAMS,
        )(*operands)

    with jax.named_scope("correlate"):
        total = group * slots
        return pl.pallas_call(
            lambda *refs: correlate_kernel(slots, *refs),
            out_shape=shaped(total, rows, LAGS, dtype=bf16),
            in_specs=[VMEM] * 7,
            out_specs=HBM,
            scratch_shapes=[
                pltpu.VMEM((total, NFFT), jnp.float32),
                pltpu.VMEM((total * rows, NFFT), bf16),
                pltpu.VMEM((total, rows, LAGS), bf16),
                pltpu.SemaphoreType.DMA((4,)),
            ],
            compiler_params=PARAMS,
        )(spectra, gathered, picks, table_hi, table_lo, band, jnp.asarray(lag_table()))


def solution(mesh):
    in_specs = (P("blk", "src"), P(), P("blk"), P("blk", None))
    out_specs = P("src", "blk", None)
    return jax.shard_map(local, mesh=mesh, in_specs=in_specs, out_specs=out_specs, check_vma=False)
```

```python
import math

import jax
import jax.numpy as jnp
import numpy as np
from jax import lax
from jax.experimental import pallas as pl
from jax.experimental.pallas import tpu as pltpu
from jax.sharding import PartitionSpec as P

S = 512
NFFT = 1024
BINS = NFFT // 2
LAGS = 512
TAPS = 64
DEC = 20
HALF = 64
LANES = 128
SUBLANES = 8
EDGE = (TAPS - 1) // DEC
CHUNK = 640
CHUNK_OUT = CHUNK // DEC
VMEM_LIMIT = 48 * 1024 * 1024


def forward_table():
    phases = 2.0 * math.pi / NFFT * (np.outer(np.arange(S), np.arange(BINS)) % NFFT)
    return np.concatenate([np.cos(phases), -np.sin(phases)], axis=1).astype(np.float32)


def split_table(table):
    high = table.astype(jnp.bfloat16)
    low = (table - high.astype(np.float32)).astype(jnp.bfloat16)
    return high, low


def band_table():
    bins = np.arange(BINS)
    return (np.abs(bins[:, None] - bins[None, :]) <= HALF).astype(jnp.bfloat16)


def lag_table():
    bins = np.arange(BINS)[:, None]
    shift = np.arange(LAGS)[None, :] - LAGS // 2
    phases = 2.0 * math.pi / NFFT * (bins * shift % NFFT)
    weight = np.where(bins == 0, 0.5, 1.0) / math.sqrt(BINS)
    table = np.concatenate([weight * np.cos(phases), -weight * np.sin(phases)], axis=0)
    return table.astype(np.float32).astype(jnp.bfloat16)


def split(value):
    high = value.astype(jnp.bfloat16)
    return high, (value - high.astype(jnp.float32)).astype(jnp.bfloat16)


def dot(a, b):
    return jnp.dot(a, b, preferred_element_type=jnp.float32)


def dot_t(a, b):
    return lax.dot_general(a, b, (((1,), (1,)), ((), ())), preferred_element_type=jnp.float32)


def column(row):
    count = row.shape[1]
    at = [lax.broadcasted_iota(jnp.int32, (count, count), axis) for axis in range(2)]
    rows = jnp.broadcast_to(row, (count, count))
    return jnp.sum(jnp.where(at[0] == at[1], rows, 0.0), axis=1, keepdims=True)


def start_copies(pairs, sems):
    copies = [
        pltpu.make_async_copy(source, target, sems.at[at])
        for at, (source, target) in enumerate(pairs)
    ]
    for copy in copies:
        copy.start()
    return copies


def decimate_kernel(
    raw_hbm, taps_hbm, alive_hbm, picks_hbm, out_ref, pieces_ref, raw_ref, taps_ref, alive_ref, picks_ref, sems
):
    rows = raw_hbm.shape[0]
    chunks = raw_hbm.shape[1] // CHUNK
    pairs = [(taps_hbm, taps_ref)]
    for j in range(chunks):
        span = slice(CHUNK * j, CHUNK * (j + 1))
        pairs.append((raw_hbm.at[:, span], raw_ref.at[rows * j : rows * (j + 1), :]))
    pairs += [(alive_hbm, alive_ref), (picks_hbm, picks_ref)]
    copies = start_copies(pairs, sems)
    copies[0].wait()
    taps = jnp.broadcast_to(taps_ref[...], (SUBLANES, TAPS))
    eight = jnp.concatenate([taps, jnp.zeros((SUBLANES, CHUNK - TAPS), jnp.float32)], axis=1)
    for _ in range(2):
        eight = pltpu.roll(eight, 0, 1, stride=DEC // 2, stride_axis=0)
    wrapped = jnp.concatenate(
        [eight]
        + [pltpu.roll(eight, DEC * at, 1) for at in range(SUBLANES, CHUNK_OUT, SUBLANES)],
        axis=0,
    )
    lane = lax.broadcasted_iota(jnp.int32, (CHUNK_OUT, CHUNK), 1)
    row = lax.broadcasted_iota(jnp.int32, (CHUNK_OUT, CHUNK), 0)
    main = jnp.where(lane >= DEC * row, wrapped, 0.0)
    rim = wrapped - main
    gap = jnp.zeros((LANES - 2 * CHUNK_OUT, CHUNK), jnp.float32)
    weights_hi, weights_lo = split(jnp.concatenate([main, gap, rim], axis=0))
    for copy in copies[1:]:
        copy.wait()
    raw_hi, raw_lo = split(raw_ref[...])
    both = dot_t(raw_hi, jnp.concatenate([weights_hi, weights_lo], axis=0))
    result = both[:, :LANES] + both[:, LANES:] + dot_t(raw_lo, weights_hi)
    part = [result[rows * j : rows * (j + 1)] for j in range(chunks)]
    per_tile = LANES // CHUNK_OUT
    col = lax.broadcasted_iota(jnp.int32, (rows, LANES), 1)
    is_main = col < LANES // 2
    tiles = -(-chunks // per_tile)
    results = []
    for tile in range(tiles):
        first = tile * per_tile
        total = jnp.where(is_main, part[first], 0.0)
        for step in range(1, min(per_tile, chunks - first)):
            total = total + pltpu.roll(part[first + step], CHUNK_OUT * step, 1)
        if first + per_tile < chunks:
            total = total + jnp.where(is_main, 0.0, part[first + per_tile])
        results.append(total)
    results.append(jnp.where(is_main, 0.0, part[0]))
    channel = lax.broadcasted_iota(jnp.int32, (rows, LANES), 0)
    alive = jnp.broadcast_to(column(alive_ref[...].astype(jnp.float32)), (rows, LANES))
    piece = []
    rims = jnp.zeros((1, LANES), jnp.float32)
    for slot in range(picks_ref.shape[1]):
        picked = channel == jnp.broadcast_to(picks_ref[:, slot : slot + 1], (rows, LANES))
        lives = jnp.where(picked, alive, 0.0)
        source = [jnp.sum(lives * value, axis=0, keepdims=True) for value in results]
        piece += source[:-1]
        rims = rims + pltpu.roll(source[-1], LANES - EDGE * slot if slot else 0, 1)
    piece.append(rims)
    for device in range(pieces_ref.shape[0]):
        for at, value in enumerate(piece):
            pieces_ref[device, :, LANES * at : LANES * (at + 1)] = value
    for tile, value in enumerate(results):
        out_ref[:, LANES * tile : LANES * (tile + 1)] = value


def transform(series, table_hi, table_lo):
    rows = series.shape[0]
    high, low = split(series)
    first = dot(jnp.concatenate([high, low], axis=0), table_hi)
    return first[:rows] + first[rows:] + dot(high, table_lo)


def shard_transform(shard_ref, at, hi_ref, lo_ref):
    count = shard_ref.shape[1] - LANES
    span = pl.ds(pl.multiple_of(count * at, LANES), count + LANES)
    series = jnp.concatenate([shard_ref[:, count:], shard_ref[:, :count]], axis=1)
    return transform(series, hi_ref[span, :], lo_ref[span, :])


def whitening(spectrum, alive, band):
    rows = spectrum.shape[0]
    real_part = spectrum[:, :BINS]
    imag_part = spectrum[:, BINS:]
    power = real_part * real_part + imag_part * imag_part
    power_hi, rest = split(power)
    power_mid, power_lo = split(power - power_hi.astype(jnp.float32))
    banded = dot(jnp.concatenate([power_hi, power_mid, power_lo], axis=0), band)
    total = banded[:rows] + banded[rows : 2 * rows] + banded[2 * rows :]
    bins = lax.broadcasted_iota(jnp.int32, (1, BINS), 1)
    count = jnp.minimum(bins + HALF, BINS - 1) - jnp.maximum(bins - HALF, 0) + 1
    factor = alive / jnp.sqrt(total / count.astype(jnp.float32) + 1e-06)
    return real_part * factor, imag_part * factor


def prepare_kernel(
    series_ref, alive_hbm, picks_hbm, fwd_hi_hbm, fwd_lo_hbm, band_hbm, lag_hbm,
    partial_ref, hi_ref, lo_ref, band_ref, lag_ref, alive_out, picks_out, alive_ref, picks_ref, sems,
):
    copies = start_copies(
        [
            (fwd_hi_hbm, hi_ref),
            (fwd_lo_hbm, lo_ref),
            (alive_hbm, alive_ref),
            (picks_hbm, picks_ref),
            (band_hbm, band_ref),
            (lag_hbm, lag_ref),
        ],
        sems,
    )
    for copy in copies[:4]:
        copy.wait()
    rows, depth = series_ref.shape
    if depth == S:
        partial_ref[...] = transform(series_ref[...], hi_ref[LANES:, :], lo_ref[LANES:, :])
    else:
        partial_ref[...] = shard_transform(series_ref, lax.axis_index("src"), hi_ref, lo_ref)
    alive_out[...] = jnp.broadcast_to(
        column(alive_ref[...].astype(jnp.float32)), (rows, LANES)
    )
    channel = lax.broadcasted_iota(jnp.int32, (rows, LANES), 0)
    for slot in range(picks_ref.shape[1]):
        pick = jnp.broadcast_to(picks_ref[:, slot : slot + 1], (rows, LANES))
        picks_out[slot] = jnp.where(channel == pick, 1.0, 0.0)
    for copy in copies[4:]:
        copy.wait()


def spectra_kernel(partial_ref, band_ref, alive_ref, *refs):
    spectrum = partial_ref[...]
    spectra_ref = refs[-1]
    if len(refs) > 1:
        other_ref, hi_ref, lo_ref = refs[:3]
        there = 1 - lax.axis_index("src")
        spectrum = spectrum + shard_transform(other_ref, there, hi_ref, lo_ref)
    real_part, imag_part = whitening(spectrum, alive_ref[:, :1], band_ref[...])
    spectra_ref[:, :BINS] = real_part
    spectra_ref[:, BINS:] = imag_part


def correlate_kernel(
    slots, spectra_ref, sources_ref, picks_ref, hi_ref, lo_ref, band_ref, lag_ref, out_hbm,
    series_ref, rims_ref, source_ref, cross_ref, out_ref, sems,
):
    rows = spectra_ref.shape[0]
    group = out_ref.shape[0] // slots
    half = BINS // LANES
    own = lax.axis_index("blk")
    base = lax.axis_index("src") * group
    tiles = S // 2 // LANES
    for slot in range(slots):
        for block in range(group):
            row = slice(slot * group + block, slot * group + block + 1)
            at = 2 * (base + block)
            for tile in range(tiles):
                span = slice(LANES * (slot * tiles + tile), LANES * (slot * tiles + tile + 1))
                early = slice(LANES * tile, LANES * (tile + 1))
                late = slice(S // 2 + LANES * tile, S // 2 + LANES * (tile + 1))
                series_ref[row, early] = sources_ref[at, :, span]
                series_ref[row, late] = sources_ref[at + 1, :, span]
            rims_ref[row, :] = sources_ref[at + 1, :, LANES * slots * tiles :]
    rims = jnp.concatenate(
        [
            pltpu.roll(rims_ref[slot * group : (slot + 1) * group, :], EDGE * slot, 1)
            for slot in range(slots)
        ],
        axis=0,
    )
    lane = lax.broadcasted_iota(jnp.int32, rims.shape, 1)
    seam = slice(S // 2 - LANES, S // 2)
    series_ref[:, seam] = series_ref[:, seam] + jnp.where(lane >= LANES - EDGE, rims, 0.0)
    series = series_ref[...]
    spectrum = transform(series, hi_ref[LANES:, :], lo_ref[LANES:, :])
    real_part, imag_part = whitening(spectrum, 1.0, band_ref[...])
    source_ref[:, :BINS] = real_part
    source_ref[:, BINS:] = imag_part
    per_part = max(1, (group * slots) // 4)
    copies = []
    for part in range(group * slots // per_part):
        first = part * per_part
        for source in range(first, first + per_part):
            block, slot = divmod(source, slots)
            is_own = jnp.where(own == base + block, 1.0, 0.0)
            keep = 1.0 - is_own * picks_ref[slot]
            at = slot * group + block
            for tile in range(half):
                re = slice(LANES * tile, LANES * (tile + 1))
                im = slice(BINS + LANES * tile, BINS + LANES * (tile + 1))
                src_re = source_ref[at : at + 1, re] * keep
                src_im = source_ref[at : at + 1, im] * keep
                rec_re, rec_im = spectra_ref[:, re], spectra_ref[:, im]
                where = slice(rows * source, rows * (source + 1))
                cross_ref[where, re] = (src_re * rec_re + src_im * rec_im).astype(jnp.bfloat16)
                cross_ref[where, im] = (src_re * rec_im - src_im * rec_re).astype(jnp.bfloat16)
        lagged = dot(cross_ref[rows * first : rows * (first + per_part), :], lag_ref[...])
        for source in range(first, first + per_part):
            at = source - first
            out_ref[source] = lagged[rows * at : rows * (at + 1)].astype(jnp.bfloat16)
        span = pl.ds(first, per_part)
        copies.append(pltpu.make_async_copy(out_ref.at[span], out_hbm.at[span], sems.at[part]))
        copies[-1].start()
    for copy in copies:
        copy.wait()


HBM = pl.BlockSpec(memory_space=pltpu.HBM)
VMEM = pl.BlockSpec(memory_space=pltpu.VMEM)
PARAMS = pltpu.CompilerParams(vmem_limit_bytes=VMEM_LIMIT)


def in_hbm(*arrays):
    return [pltpu.with_memory_space_constraint(array, pltpu.HBM) for array in arrays]


def shaped(*shape, dtype=jnp.float32):
    return jax.ShapeDtypeStruct(shape, dtype)


def local(raw_records, fir_taps, alive_mask, source_index):
    src_count = lax.axis_size("src")
    blk_count = lax.axis_size("blk")
    rows, raw_count = raw_records.shape
    slots = source_index.shape[1]
    group = blk_count // src_count
    out_count = raw_count // DEC
    width = -(-out_count // LANES) * LANES + LANES
    chunks = raw_count // CHUNK
    paired = src_count == 2 and 2 * out_count == S
    bf16 = jnp.bfloat16
    forward_hi, forward_lo = split_table(np.pad(forward_table(), ((LANES, 0), (0, 0))))
    alive_row = alive_mask.reshape(1, rows)

    with jax.named_scope("decimate"):
        device_count = blk_count * src_count
        main = slots * (width - LANES)
        decimated, pieces = pl.pallas_call(
            decimate_kernel,
            out_shape=(shaped(rows, width), shaped(device_count, 1, main + LANES)),
            in_specs=[HBM] * 4,
            out_specs=(VMEM, VMEM),
            scratch_shapes=[
                pltpu.VMEM((rows * chunks, CHUNK), jnp.float32),
                pltpu.VMEM((1, TAPS), jnp.float32),
                pltpu.VMEM((1, rows), jnp.int32),
                pltpu.VMEM((1, slots), jnp.int32),
                pltpu.SemaphoreType.DMA((chunks + 3,)),
            ],
            compiler_params=PARAMS,
        )(*in_hbm(raw_records, fir_taps.reshape(1, TAPS), alive_row, source_index))

    def whole(shards):
        rims = jnp.pad(shards[1:, :, width - EDGE :], ((0, 1), (0, 0), (out_count - EDGE, 0)))
        series = shards[:, :, :out_count] + rims
        return series.transpose(1, 0, 2).reshape(shards.shape[1], S)

    with jax.named_scope("gather_sources"):
        gathered = lax.all_to_all(pieces, ("blk", "src"), split_axis=0, concat_axis=0, tiled=True)
        if not paired:
            shards = gathered.reshape(blk_count, src_count, main + LANES)
            shards = shards.transpose(1, 0, 2)
            rims = [shards[:, :, main + LANES - EDGE * (slot + 1) :] for slot in range(slots)]
            rims = jnp.stack([rim[:, :, :EDGE] for rim in rims], axis=2)
            rims = jnp.pad(rims, ((0, 0), (0, 0), (0, 0), (LANES - EDGE, 0)))
            series = shards[:, :, :main].reshape(src_count, blk_count, slots, width - LANES)
            series = jnp.concatenate([series, rims], axis=3)
            series = whole(series.reshape(src_count, blk_count * slots, width))
            series = series.reshape(blk_count, slots, 2, S // 2).transpose(0, 2, 1, 3)
            series = series.reshape(blk_count * 2, 1, slots * S // 2)
            gathered = jnp.pad(series, ((0, 0), (0, 0), (0, LANES)))

    with jax.named_scope("regroup"):
        if paired:
            series = decimated
            other = lax.ppermute(decimated, "src", [(0, 1), (1, 0)])
        else:
            series = whole(lax.all_gather(decimated, "src", axis=0))

    with jax.named_scope("prepare"):
        out_shape = (
            shaped(rows, NFFT),
            shaped(S + LANES, NFFT, dtype=bf16),
            shaped(S + LANES, NFFT, dtype=bf16),
            shaped(BINS, BINS, dtype=bf16),
            shaped(NFFT, LAGS, dtype=bf16),
            shaped(rows, LANES),
            shaped(slots, rows, LANES),
        )
        partial, table_hi, table_lo, band, lag, alive, picks = pl.pallas_call(
            prepare_kernel,
            out_shape=out_shape,
            in_specs=[VMEM] + [HBM] * 6,
            out_specs=(VMEM,) * len(out_shape),
            scratch_shapes=[
                pltpu.VMEM((1, rows), jnp.int32),
                pltpu.VMEM((1, slots), jnp.int32),
                pltpu.SemaphoreType.DMA((6,)),
            ],
            compiler_params=PARAMS,
            cost_estimate=pl.CostEstimate(
                flops=6 * rows * S * NFFT, bytes_accessed=6 * S * NFFT, transcendentals=0
            ),
        )(
            series,
            *in_hbm(
                alive_row,
                source_index,
                jnp.asarray(forward_hi),
                jnp.asarray(forward_lo),
                jnp.asarray(band_table()),
                jnp.asarray(lag_table()),
            ),
        )

    with jax.named_scope("spectra"):
        operands = [partial, band, alive]
        if paired:
            operands += [other, table_hi, table_lo]
        spectra = pl.pallas_call(
            spectra_kernel,
            out_shape=shaped(rows, NFFT),
            in_specs=[VMEM] * len(operands),
            out_specs=VMEM,
            compiler_params=PARAMS,
        )(*operands)

    with jax.named_scope("correlate"):
        total = group * slots
        return pl.pallas_call(
            lambda *refs: correlate_kernel(slots, *refs),
            out_shape=shaped(total, rows, LAGS, dtype=bf16),
            in_specs=[VMEM] * 7,
            out_specs=HBM,
            scratch_shapes=[
                pltpu.VMEM((total, S), jnp.float32),
                pltpu.VMEM((total, LANES), jnp.float32),
                pltpu.VMEM((total, NFFT), jnp.float32),
                pltpu.VMEM((total * rows, NFFT), bf16),
                pltpu.VMEM((total, rows, LAGS), bf16),
                pltpu.SemaphoreType.DMA((4,)),
            ],
            compiler_params=PARAMS,
        )(spectra, gathered, picks, table_hi, table_lo, band, lag)


def solution(mesh):
    in_specs = (P("blk", "src"), P(), P("blk"), P("blk", None))
    out_specs = P("src", "blk", None)
    return jax.shard_map(local, mesh=mesh, in_specs=in_specs, out_specs=out_specs, check_vma=False)
```

```python
import math

import jax
import jax.numpy as jnp
import numpy as np
from jax import lax
from jax.experimental import pallas as pl
from jax.experimental.pallas import tpu as pltpu
from jax.sharding import PartitionSpec as P

S = 512
NFFT = 1024
BINS = NFFT // 2
LAGS = 512
TAPS = 64
DEC = 20
HALF = 64
LANES = 128
SUBLANES = 8
EDGE = (TAPS - 1) // DEC
CHUNK = 640
CHUNK_OUT = CHUNK // DEC
VMEM_LIMIT = 48 * 1024 * 1024


def forward_table():
    phases = 2.0 * math.pi / NFFT * (np.outer(np.arange(S), np.arange(BINS)) % NFFT)
    return np.concatenate([np.cos(phases), -np.sin(phases)], axis=1).astype(np.float32)


def split_table(table):
    high = table.astype(jnp.bfloat16)
    low = (table - high.astype(np.float32)).astype(jnp.bfloat16)
    return high, low


def band_table():
    bins = np.arange(3 * LANES)[:, None] - LANES
    return (np.abs(bins - np.arange(LANES)[None, :]) <= HALF).astype(jnp.bfloat16)


def lag_table():
    bins = np.arange(BINS)[:, None]
    shift = np.arange(LAGS)[None, :] - LAGS // 2
    phases = 2.0 * math.pi / NFFT * (bins * shift % NFFT)
    weight = np.where(bins == 0, 0.5, 1.0) / math.sqrt(BINS)
    table = np.concatenate([weight * np.cos(phases), -weight * np.sin(phases)], axis=0)
    return table.astype(np.float32).astype(jnp.bfloat16)


def split(value):
    high = value.astype(jnp.bfloat16)
    return high, (value - high.astype(jnp.float32)).astype(jnp.bfloat16)


def dot(a, b):
    return jnp.dot(a, b, preferred_element_type=jnp.float32)


def dot_t(a, b):
    return lax.dot_general(a, b, (((1,), (1,)), ((), ())), preferred_element_type=jnp.float32)


def column(row):
    count = row.shape[1]
    at = [lax.broadcasted_iota(jnp.int32, (count, count), axis) for axis in range(2)]
    rows = jnp.broadcast_to(row, (count, count))
    return jnp.sum(jnp.where(at[0] == at[1], rows, 0.0), axis=1, keepdims=True)


def start_copies(pairs, sems):
    copies = [
        pltpu.make_async_copy(source, target, sems.at[at])
        for at, (source, target) in enumerate(pairs)
    ]
    for copy in copies:
        copy.start()
    return copies


def decimate_kernel(
    raw_hbm, taps_hbm, alive_hbm, picks_hbm, out_ref, pieces_hbm,
    raw_ref, taps_ref, alive_ref, picks_ref, source_ref, pieces_ref, sems,
):
    rows = raw_hbm.shape[0]
    chunks = raw_hbm.shape[1] // CHUNK
    slots = picks_ref.shape[1]
    pairs = [(taps_hbm, taps_ref), (picks_hbm, picks_ref), (alive_hbm, alive_ref)]
    for j in range(chunks):
        span = slice(CHUNK * j, CHUNK * (j + 1))
        pairs.append((raw_hbm.at[:, span], raw_ref.at[rows * j : rows * (j + 1), :]))
    copies = start_copies(pairs, sems)
    copies[0].wait()
    taps = jnp.broadcast_to(taps_ref[...], (SUBLANES, TAPS))
    eight = jnp.concatenate([taps, jnp.zeros((SUBLANES, CHUNK - TAPS), jnp.float32)], axis=1)
    for _ in range(2):
        eight = pltpu.roll(eight, 0, 1, stride=DEC // 2, stride_axis=0)
    wrapped = jnp.concatenate(
        [eight]
        + [pltpu.roll(eight, DEC * at, 1) for at in range(SUBLANES, CHUNK_OUT, SUBLANES)],
        axis=0,
    )
    lane = lax.broadcasted_iota(jnp.int32, (CHUNK_OUT, CHUNK), 1)
    row = lax.broadcasted_iota(jnp.int32, (CHUNK_OUT, CHUNK), 0)
    main = jnp.where(lane >= DEC * row, wrapped, 0.0)
    rim = wrapped - main
    gap = jnp.zeros((LANES - 2 * CHUNK_OUT, CHUNK), jnp.float32)
    weights_hi, weights_lo = split(jnp.concatenate([main, gap, rim], axis=0))
    weights = jnp.concatenate([weights_hi, weights_lo], axis=0)

    def filtered(stacked):
        count = stacked.shape[0] // chunks
        high, low = split(stacked)
        both = dot_t(high, weights)
        result = both[:, :LANES] + both[:, LANES:] + dot_t(low, weights_hi)
        part = [result[count * j : count * (j + 1)] for j in range(chunks)]
        per_tile = LANES // CHUNK_OUT
        is_main = lax.broadcasted_iota(jnp.int32, (count, LANES), 1) < LANES // 2
        tiles = []
        for first in range(0, chunks, per_tile):
            total = jnp.where(is_main, part[first], 0.0)
            for step in range(1, min(per_tile, chunks - first)):
                total = total + pltpu.roll(part[first + step], CHUNK_OUT * step, 1)
            if first + per_tile < chunks:
                total = total + jnp.where(is_main, 0.0, part[first + per_tile])
            tiles.append(total)
        return tiles + [jnp.where(is_main, 0.0, part[0])]

    for copy in copies[1:]:
        copy.wait()
    source_ref[...] = jnp.zeros_like(source_ref)
    for slot in range(slots):
        pick = picks_ref[0, slot]
        alive = alive_ref[0, pick].astype(jnp.float32)
        for j in range(chunks):
            at = SUBLANES * j + slot
            source_ref[at : at + 1, :] = raw_ref[pl.ds(rows * j + pick, 1), :] * alive
    sources = filtered(source_ref[...])
    rims = jnp.zeros((1, LANES), jnp.float32)
    for slot in range(slots):
        late = sources[-1][slot : slot + 1]
        rims = rims + pltpu.roll(late, LANES - EDGE * slot if slot else 0, 1)
    piece = [tile[slot : slot + 1] for slot in range(slots) for tile in sources[:-1]] + [rims]
    for device in range(pieces_ref.shape[0]):
        for at, value in enumerate(piece):
            pieces_ref[device, :, LANES * at : LANES * (at + 1)] = value
    sending = pltpu.make_async_copy(pieces_ref, pieces_hbm, sems.at[0])
    sending.start()
    for at, value in enumerate(filtered(raw_ref[...])):
        out_ref[:, LANES * at : LANES * (at + 1)] = value
    sending.wait()


def transform(series, table_hi, table_lo):
    rows = series.shape[0]
    high, low = split(series)
    first = dot(jnp.concatenate([high, low], axis=0), table_hi)
    return first[:rows] + first[rows:] + dot(high, table_lo)


def shard_transform(shard_ref, at, hi_ref, lo_ref):
    count = shard_ref.shape[1] - LANES
    main = pl.ds(pl.multiple_of(count * at, LANES), count)
    edge = pl.ds(pl.multiple_of(jnp.maximum(count * at - LANES, 0), LANES), LANES)
    rim = jnp.where(at > 0, shard_ref[:, count:], 0.0)
    series = jnp.concatenate([shard_ref[:, :count], rim], axis=1)
    tables = [
        jnp.concatenate([ref[main, :], ref[edge, :]], axis=0) for ref in (hi_ref, lo_ref)
    ]
    return transform(series, *tables)


def whitening(spectrum, alive, band):
    rows = spectrum.shape[0]
    real_part = spectrum[:, :BINS]
    imag_part = spectrum[:, BINS:]
    power = real_part * real_part + imag_part * imag_part
    tiles = BINS // LANES
    power_hi, rest = split(power)
    power_mid, power_lo = split(power - power_hi.astype(jnp.float32))
    stacked = []
    for part in (power_hi, power_mid, power_lo):
        zero = jnp.zeros((rows, LANES), part.dtype)
        wide = jnp.concatenate([zero, part, zero], axis=1)
        stacked += [wide[:, LANES * tile : LANES * (tile + 3)] for tile in range(tiles)]
    banded = dot(jnp.concatenate(stacked, axis=0), band)
    step = rows * tiles
    summed = banded[:step] + banded[step : 2 * step] + banded[2 * step :]
    total = jnp.concatenate(
        [summed[rows * tile : rows * (tile + 1)] for tile in range(tiles)], axis=1
    )
    bins = lax.broadcasted_iota(jnp.int32, (1, BINS), 1)
    count = jnp.minimum(bins + HALF, BINS - 1) - jnp.maximum(bins - HALF, 0) + 1
    factor = alive / jnp.sqrt(total / count.astype(jnp.float32) + 1e-06)
    return real_part * factor, imag_part * factor


def prepare_kernel(
    series_ref, alive_hbm, picks_hbm, fwd_hi_hbm, fwd_lo_hbm, band_hbm, lag_hbm,
    partial_ref, hi_ref, lo_ref, band_ref, lag_ref, alive_out, picks_out, alive_ref, picks_ref, sems,
):
    copies = start_copies(
        [
            (fwd_hi_hbm, hi_ref),
            (fwd_lo_hbm, lo_ref),
            (alive_hbm, alive_ref),
            (picks_hbm, picks_ref),
            (band_hbm, band_ref),
            (lag_hbm, lag_ref),
        ],
        sems,
    )
    for copy in copies[:4]:
        copy.wait()
    rows, depth = series_ref.shape
    if depth == S:
        partial_ref[...] = transform(series_ref[...], hi_ref[...], lo_ref[...])
    else:
        partial_ref[...] = shard_transform(series_ref, lax.axis_index("src"), hi_ref, lo_ref)
    alive_out[...] = jnp.broadcast_to(
        column(alive_ref[...].astype(jnp.float32)), (rows, LANES)
    )
    channel = lax.broadcasted_iota(jnp.int32, (rows, LANES), 0)
    for slot in range(picks_ref.shape[1]):
        pick = jnp.broadcast_to(picks_ref[:, slot : slot + 1], (rows, LANES))
        picks_out[slot] = jnp.where(channel == pick, 1.0, 0.0)
    for copy in copies[4:]:
        copy.wait()


def spectra_kernel(partial_ref, band_ref, alive_ref, *refs):
    spectrum = partial_ref[...]
    spectra_ref = refs[-1]
    if len(refs) > 1:
        other_ref, hi_ref, lo_ref = refs[:3]
        there = 1 - lax.axis_index("src")
        spectrum = spectrum + shard_transform(other_ref, there, hi_ref, lo_ref)
    real_part, imag_part = whitening(spectrum, alive_ref[:, :1], band_ref[...])
    spectra_ref[:, :BINS] = real_part
    spectra_ref[:, BINS:] = imag_part


def correlate_kernel(
    slots, spectra_ref, picks_ref, hi_ref, lo_ref, band_ref, lag_ref, *refs
):
    pieces = refs[:-7]
    out_hbm, series_ref, rims_ref, source_ref, cross_ref, out_ref, sems = refs[-7:]
    rows = spectra_ref.shape[0]
    group = out_ref.shape[0] // slots
    half = BINS // LANES
    own = lax.axis_index("blk")
    base = lax.axis_index("src") * group
    tiles = S // 2 // LANES

    def read(block, at, span):
        if len(pieces) == 1:
            return pieces[0][2 * (base + block) + at, :, span]
        entry = 2 * ((base + block) >> 1) + at
        same = ((base + block) & 1) == (own & 1)
        return jnp.where(same, pieces[0][entry, :, span], pieces[1][entry, :, span])

    for slot in range(slots):
        for block in range(group):
            row = slice(slot * group + block, slot * group + block + 1)
            for tile in range(tiles):
                span = slice(LANES * (slot * tiles + tile), LANES * (slot * tiles + tile + 1))
                early = slice(LANES * tile, LANES * (tile + 1))
                late = slice(S // 2 + LANES * tile, S // 2 + LANES * (tile + 1))
                series_ref[row, early] = read(block, 0, span)
                series_ref[row, late] = read(block, 1, span)
            rims_ref[row, :] = read(block, 1, slice(LANES * slots * tiles, None))
    rims = jnp.concatenate(
        [
            pltpu.roll(rims_ref[slot * group : (slot + 1) * group, :], EDGE * slot, 1)
            for slot in range(slots)
        ],
        axis=0,
    )
    lane = lax.broadcasted_iota(jnp.int32, rims.shape, 1)
    seam = slice(S // 2 - LANES, S // 2)
    series_ref[:, seam] = series_ref[:, seam] + jnp.where(lane >= LANES - EDGE, rims, 0.0)
    series = series_ref[...]
    spectrum = transform(series, hi_ref[...], lo_ref[...])
    real_part, imag_part = whitening(spectrum, 1.0, band_ref[...])
    source_ref[:, :BINS] = real_part
    source_ref[:, BINS:] = imag_part
    per_part = max(1, (group * slots) // 4)
    copies = []
    for part in range(group * slots // per_part):
        first = part * per_part
        for source in range(first, first + per_part):
            block, slot = divmod(source, slots)
            is_own = jnp.where(own == base + block, 1.0, 0.0)
            keep = 1.0 - is_own * picks_ref[slot]
            at = slot * group + block
            for tile in range(half):
                re = slice(LANES * tile, LANES * (tile + 1))
                im = slice(BINS + LANES * tile, BINS + LANES * (tile + 1))
                src_re = source_ref[at : at + 1, re] * keep
                src_im = source_ref[at : at + 1, im] * keep
                rec_re, rec_im = spectra_ref[:, re], spectra_ref[:, im]
                where = slice(rows * source, rows * (source + 1))
                cross_ref[where, re] = (src_re * rec_re + src_im * rec_im).astype(jnp.bfloat16)
                cross_ref[where, im] = (src_re * rec_im - src_im * rec_re).astype(jnp.bfloat16)
        lagged = dot(cross_ref[rows * first : rows * (first + per_part), :], lag_ref[...])
        for source in range(first, first + per_part):
            at = source - first
            out_ref[source] = lagged[rows * at : rows * (at + 1)].astype(jnp.bfloat16)
        span = pl.ds(first, per_part)
        copies.append(pltpu.make_async_copy(out_ref.at[span], out_hbm.at[span], sems.at[part]))
        copies[-1].start()
    for copy in copies:
        copy.wait()


HBM = pl.BlockSpec(memory_space=pltpu.HBM)
VMEM = pl.BlockSpec(memory_space=pltpu.VMEM)
PARAMS = pltpu.CompilerParams(vmem_limit_bytes=VMEM_LIMIT)


def in_hbm(*arrays):
    return [pltpu.with_memory_space_constraint(array, pltpu.HBM) for array in arrays]


def shaped(*shape, dtype=jnp.float32):
    return jax.ShapeDtypeStruct(shape, dtype)


def local(raw_records, fir_taps, alive_mask, source_index):
    src_count = lax.axis_size("src")
    blk_count = lax.axis_size("blk")
    rows, raw_count = raw_records.shape
    slots = source_index.shape[1]
    group = blk_count // src_count
    out_count = raw_count // DEC
    width = -(-out_count // LANES) * LANES + LANES
    chunks = raw_count // CHUNK
    paired = src_count == 2 and 2 * out_count == S
    bf16 = jnp.bfloat16
    forward_hi, forward_lo = split_table(forward_table())
    alive_row = alive_mask.reshape(1, rows)

    with jax.named_scope("decimate"):
        members = [
            [b * src_count + s for b in range(core, blk_count, 2) for s in range(src_count)]
            for core in range(2)
        ]
        member_count = len(members[0]) if paired else blk_count * src_count
        main = slots * (width - LANES)
        decimated, pieces = pl.pallas_call(
            decimate_kernel,
            out_shape=(shaped(rows, width), shaped(member_count, 1, main + LANES)),
            in_specs=[HBM] * 4,
            out_specs=(VMEM, HBM),
            scratch_shapes=[
                pltpu.VMEM((rows * chunks, CHUNK), jnp.float32),
                pltpu.VMEM((1, TAPS), jnp.float32),
                pltpu.SMEM((1, rows), jnp.int32),
                pltpu.SMEM((1, slots), jnp.int32),
                pltpu.VMEM((SUBLANES * chunks, CHUNK), jnp.float32),
                pltpu.VMEM((member_count, 1, main + LANES), jnp.float32),
                pltpu.SemaphoreType.DMA((chunks + 3,)),
            ],
            compiler_params=PARAMS,
        )(*in_hbm(raw_records, fir_taps.reshape(1, TAPS), alive_row, source_index))

    def whole(shards):
        rims = jnp.pad(shards[1:, :, width - EDGE :], ((0, 1), (0, 0), (out_count - EDGE, 0)))
        series = shards[:, :, :out_count] + rims
        return series.transpose(1, 0, 2).reshape(shards.shape[1], S)

    with jax.named_scope("gather_sources"):
        gathered = lax.all_to_all(
            pieces,
            ("blk", "src"),
            split_axis=0,
            concat_axis=0,
            tiled=True,
            axis_index_groups=members if paired else None,
        )
        if paired:
            twin = lax.ppermute(gathered, "blk", [(b, b ^ 1) for b in range(blk_count)])
            gathered = (gathered, twin)
        else:
            shards = gathered.reshape(blk_count, src_count, main + LANES)
            shards = shards.transpose(1, 0, 2)
            rims = [shards[:, :, main + LANES - EDGE * (slot + 1) :] for slot in range(slots)]
            rims = jnp.stack([rim[:, :, :EDGE] for rim in rims], axis=2)
            rims = jnp.pad(rims, ((0, 0), (0, 0), (0, 0), (LANES - EDGE, 0)))
            series = shards[:, :, :main].reshape(src_count, blk_count, slots, width - LANES)
            series = jnp.concatenate([series, rims], axis=3)
            series = whole(series.reshape(src_count, blk_count * slots, width))
            series = series.reshape(blk_count, slots, 2, S // 2).transpose(0, 2, 1, 3)
            series = series.reshape(blk_count * 2, 1, slots * S // 2)
            gathered = (jnp.pad(series, ((0, 0), (0, 0), (0, LANES))),)

    with jax.named_scope("regroup"):
        if paired:
            series = decimated
            other = lax.ppermute(decimated, "src", [(0, 1), (1, 0)])
        else:
            series = whole(lax.all_gather(decimated, "src", axis=0))

    with jax.named_scope("prepare"):
        out_shape = (
            shaped(rows, NFFT),
            shaped(S, NFFT, dtype=bf16),
            shaped(S, NFFT, dtype=bf16),
            shaped(3 * LANES, LANES, dtype=bf16),
            shaped(NFFT, LAGS, dtype=bf16),
            shaped(rows, LANES),
            shaped(slots, rows, LANES),
        )
        partial, table_hi, table_lo, band, lag, alive, picks = pl.pallas_call(
            prepare_kernel,
            out_shape=out_shape,
            in_specs=[VMEM] + [HBM] * 6,
            out_specs=(VMEM,) * len(out_shape),
            scratch_shapes=[
                pltpu.VMEM((1, rows), jnp.int32),
                pltpu.VMEM((1, slots), jnp.int32),
                pltpu.SemaphoreType.DMA((6,)),
            ],
            compiler_params=PARAMS,
            cost_estimate=pl.CostEstimate(
                flops=6 * rows * S * NFFT, bytes_accessed=6 * S * NFFT, transcendentals=0
            ),
        )(
            series,
            *in_hbm(
                alive_row,
                source_index,
                jnp.asarray(forward_hi),
                jnp.asarray(forward_lo),
                jnp.asarray(band_table()),
                jnp.asarray(lag_table()),
            ),
        )

    with jax.named_scope("spectra"):
        operands = [partial, band, alive]
        if paired:
            operands += [other, table_hi, table_lo]
        spectra = pl.pallas_call(
            spectra_kernel,
            out_shape=shaped(rows, NFFT),
            in_specs=[VMEM] * len(operands),
            out_specs=VMEM,
            compiler_params=PARAMS,
        )(*operands)

    with jax.named_scope("correlate"):
        total = group * slots
        return pl.pallas_call(
            lambda *refs: correlate_kernel(slots, *refs),
            out_shape=shaped(total, rows, LAGS, dtype=bf16),
            in_specs=[VMEM] * (6 + len(gathered)),
            out_specs=HBM,
            scratch_shapes=[
                pltpu.VMEM((total, S), jnp.float32),
                pltpu.VMEM((total, LANES), jnp.float32),
                pltpu.VMEM((total, NFFT), jnp.float32),
                pltpu.VMEM((total * rows, NFFT), bf16),
                pltpu.VMEM((total, rows, LAGS), bf16),
                pltpu.SemaphoreType.DMA((4,)),
            ],
            compiler_params=PARAMS,
        )(spectra, picks, table_hi, table_lo, band, lag, *gathered)


def solution(mesh):
    in_specs = (P("blk", "src"), P(), P("blk"), P("blk", None))
    out_specs = P("src", "blk", None)
    return jax.shard_map(local, mesh=mesh, in_specs=in_specs, out_specs=out_specs, check_vma=False)
```

```python
import math

import jax
import jax.numpy as jnp
import numpy as np
from jax import lax
from jax.experimental import pallas as pl
from jax.experimental.pallas import tpu as pltpu
from jax.sharding import PartitionSpec as P

S = 512
NFFT = 1024
BINS = NFFT // 2
LAGS = 512
TAPS = 64
DEC = 20
HALF = 64
LANES = 128
SUBLANES = 8
PARTS = 2
EDGE = (TAPS - 1) // DEC
CHUNK = 640
CHUNK_OUT = CHUNK // DEC
VMEM_LIMIT = 48 * 1024 * 1024


def forward_table():
    phases = 2.0 * math.pi / NFFT * (np.outer(np.arange(S), np.arange(BINS)) % NFFT)
    return np.concatenate([np.cos(phases), -np.sin(phases)], axis=1).astype(np.float32)


def split_table(table):
    high = table.astype(jnp.bfloat16)
    low = (table - high.astype(np.float32)).astype(jnp.bfloat16)
    return high, low


def band_table():
    bins = np.arange(3 * LANES)[:, None] - LANES
    return (np.abs(bins - np.arange(LANES)[None, :]) <= HALF).astype(jnp.bfloat16)


def lag_table():
    bins = np.arange(BINS)[:, None]
    shift = np.arange(LAGS)[None, :] - LAGS // 2
    phases = 2.0 * math.pi / NFFT * (bins * shift % NFFT)
    weight = np.where(bins == 0, 0.5, 1.0) / math.sqrt(BINS)
    table = np.concatenate([weight * np.cos(phases), -weight * np.sin(phases)], axis=0)
    return table.astype(np.float32).astype(jnp.bfloat16)


def split(value):
    high = value.astype(jnp.bfloat16)
    return high, (value - high.astype(jnp.float32)).astype(jnp.bfloat16)


def dot(a, b):
    return jnp.dot(a, b, preferred_element_type=jnp.float32)


def dot_t(a, b):
    return lax.dot_general(a, b, (((1,), (1,)), ((), ())), preferred_element_type=jnp.float32)


def column(row):
    count = row.shape[1]
    at = [lax.broadcasted_iota(jnp.int32, (count, count), axis) for axis in range(2)]
    rows = jnp.broadcast_to(row, (count, count))
    return jnp.sum(jnp.where(at[0] == at[1], rows, 0.0), axis=1, keepdims=True)


def start_copies(pairs, sems):
    copies = [
        pltpu.make_async_copy(source, target, sems.at[at])
        for at, (source, target) in enumerate(pairs)
    ]
    for copy in copies:
        copy.start()
    return copies


def decimate_kernel(
    raw_hbm, taps_hbm, alive_hbm, picks_hbm, out_ref, pieces_hbm,
    raw_ref, taps_ref, alive_ref, picks_ref, source_ref, pieces_ref, sems,
):
    rows = raw_hbm.shape[0]
    chunks = raw_hbm.shape[1] // CHUNK
    slots = picks_ref.shape[1]
    pairs = [(taps_hbm, taps_ref), (picks_hbm, picks_ref), (alive_hbm, alive_ref)]
    for j in range(chunks):
        span = slice(CHUNK * j, CHUNK * (j + 1))
        pairs.append((raw_hbm.at[:, span], raw_ref.at[rows * j : rows * (j + 1), :]))
    copies = start_copies(pairs, sems)
    copies[0].wait()
    taps = jnp.broadcast_to(taps_ref[...], (SUBLANES, TAPS))
    eight = jnp.concatenate([taps, jnp.zeros((SUBLANES, CHUNK - TAPS), jnp.float32)], axis=1)
    for _ in range(2):
        eight = pltpu.roll(eight, 0, 1, stride=DEC // 2, stride_axis=0)
    wrapped = jnp.concatenate(
        [eight]
        + [pltpu.roll(eight, DEC * at, 1) for at in range(SUBLANES, CHUNK_OUT, SUBLANES)],
        axis=0,
    )
    lane = lax.broadcasted_iota(jnp.int32, (CHUNK_OUT, CHUNK), 1)
    row = lax.broadcasted_iota(jnp.int32, (CHUNK_OUT, CHUNK), 0)
    main = jnp.where(lane >= DEC * row, wrapped, 0.0)
    rim = wrapped - main
    gap = jnp.zeros((LANES - 2 * CHUNK_OUT, CHUNK), jnp.float32)
    weights_hi, weights_lo = split(jnp.concatenate([main, gap, rim], axis=0))
    weights = jnp.concatenate([weights_hi, weights_lo], axis=0)

    def filtered(stacked):
        count = stacked.shape[0] // chunks
        high, low = split(stacked)
        both = dot_t(high, weights)
        result = both[:, :LANES] + both[:, LANES:] + dot_t(low, weights_hi)
        part = [result[count * j : count * (j + 1)] for j in range(chunks)]
        per_tile = LANES // CHUNK_OUT
        is_main = lax.broadcasted_iota(jnp.int32, (count, LANES), 1) < LANES // 2
        tiles = []
        for first in range(0, chunks, per_tile):
            total = jnp.where(is_main, part[first], 0.0)
            for step in range(1, min(per_tile, chunks - first)):
                total = total + pltpu.roll(part[first + step], CHUNK_OUT * step, 1)
            if first + per_tile < chunks:
                total = total + jnp.where(is_main, 0.0, part[first + per_tile])
            tiles.append(total)
        return tiles + [jnp.where(is_main, 0.0, part[0])]

    for copy in copies[1:]:
        copy.wait()
    source_ref[...] = jnp.zeros_like(source_ref)
    for slot in range(slots):
        pick = picks_ref[0, slot]
        alive = alive_ref[0, pick].astype(jnp.float32)
        for j in range(chunks):
            at = SUBLANES * j + slot
            source_ref[at : at + 1, :] = raw_ref[pl.ds(rows * j + pick, 1), :] * alive
    sources = filtered(source_ref[...])
    rims = jnp.zeros((1, LANES), jnp.float32)
    for slot in range(slots):
        late = sources[-1][slot : slot + 1]
        rims = rims + pltpu.roll(late, LANES - EDGE * slot if slot else 0, 1)
    piece = [tile[slot : slot + 1] for slot in range(slots) for tile in sources[:-1]] + [rims]
    for device in range(pieces_ref.shape[0]):
        for at, value in enumerate(piece):
            pieces_ref[device, :, LANES * at : LANES * (at + 1)] = value
    sending = pltpu.make_async_copy(pieces_ref, pieces_hbm, sems.at[0])
    sending.start()
    for at, value in enumerate(filtered(raw_ref[...])):
        out_ref[:, LANES * at : LANES * (at + 1)] = value
    sending.wait()


def transform(series, table_hi, table_lo):
    rows = series.shape[0]
    high, low = split(series)
    first = dot(jnp.concatenate([high, low], axis=0), table_hi)
    return first[:rows] + first[rows:] + dot(high, table_lo)


def shard_transform(shard_ref, at, hi_ref, lo_ref):
    count = shard_ref.shape[1] - LANES
    main = pl.ds(pl.multiple_of(count * at, LANES), count)
    edge = pl.ds(pl.multiple_of(jnp.maximum(count * at - LANES, 0), LANES), LANES)
    rim = jnp.where(at > 0, shard_ref[:, count:], 0.0)
    series = jnp.concatenate([shard_ref[:, :count], rim], axis=1)
    tables = [
        jnp.concatenate([ref[main, :], ref[edge, :]], axis=0) for ref in (hi_ref, lo_ref)
    ]
    return transform(series, *tables)


def whitening(spectrum, alive, band):
    rows = spectrum.shape[0]
    real_part = spectrum[:, :BINS]
    imag_part = spectrum[:, BINS:]
    power = real_part * real_part + imag_part * imag_part
    tiles = BINS // LANES
    power_hi, rest = split(power)
    power_mid, power_lo = split(power - power_hi.astype(jnp.float32))
    stacked = []
    for part in (power_hi, power_mid, power_lo):
        zero = jnp.zeros((rows, LANES), part.dtype)
        wide = jnp.concatenate([zero, part, zero], axis=1)
        stacked += [wide[:, LANES * tile : LANES * (tile + 3)] for tile in range(tiles)]
    banded = dot(jnp.concatenate(stacked, axis=0), band)
    step = rows * tiles
    summed = banded[:step] + banded[step : 2 * step] + banded[2 * step :]
    total = jnp.concatenate(
        [summed[rows * tile : rows * (tile + 1)] for tile in range(tiles)], axis=1
    )
    bins = lax.broadcasted_iota(jnp.int32, (1, BINS), 1)
    count = jnp.minimum(bins + HALF, BINS - 1) - jnp.maximum(bins - HALF, 0) + 1
    factor = alive / jnp.sqrt(total / count.astype(jnp.float32) + 1e-06)
    return real_part * factor, imag_part * factor


def prepare_kernel(
    series_ref, alive_hbm, picks_hbm, fwd_hi_hbm, fwd_lo_hbm, band_hbm, lag_hbm,
    partial_ref, hi_ref, lo_ref, band_ref, lag_ref, alive_out, picks_out, alive_ref, picks_ref, sems,
):
    copies = start_copies(
        [
            (fwd_hi_hbm, hi_ref),
            (fwd_lo_hbm, lo_ref),
            (alive_hbm, alive_ref),
            (picks_hbm, picks_ref),
            (band_hbm, band_ref),
            (lag_hbm, lag_ref),
        ],
        sems,
    )
    for copy in copies[:4]:
        copy.wait()
    rows, depth = series_ref.shape
    if depth == S:
        partial_ref[...] = transform(series_ref[...], hi_ref[...], lo_ref[...])
    else:
        partial_ref[...] = shard_transform(series_ref, lax.axis_index("src"), hi_ref, lo_ref)
    alive_out[...] = jnp.broadcast_to(
        column(alive_ref[...].astype(jnp.float32)), (rows, LANES)
    )
    channel = lax.broadcasted_iota(jnp.int32, (rows, LANES), 0)
    for slot in range(picks_ref.shape[1]):
        pick = jnp.broadcast_to(picks_ref[:, slot : slot + 1], (rows, LANES))
        picks_out[slot] = jnp.where(channel == pick, 1.0, 0.0)
    for copy in copies[4:]:
        copy.wait()


def spectra_kernel(partial_ref, band_ref, alive_ref, *refs):
    spectrum = partial_ref[...]
    spectra_ref = refs[-1]
    if len(refs) > 1:
        other_ref, hi_ref, lo_ref = refs[:3]
        there = 1 - lax.axis_index("src")
        spectrum = spectrum + shard_transform(other_ref, there, hi_ref, lo_ref)
    real_part, imag_part = whitening(spectrum, alive_ref[:, :1], band_ref[...])
    spectra_ref[:, :BINS] = real_part
    spectra_ref[:, BINS:] = imag_part


def correlate_kernel(
    slots, spectra_ref, pieces_ref, picks_ref, hi_ref, lo_ref, band_ref, lag_ref, out_hbm,
    series_ref, rims_ref, source_ref, cross_ref, out_ref, sems,
):
    rows = spectra_ref.shape[0]
    group = out_ref.shape[0] // slots
    half = BINS // LANES
    own = lax.axis_index("blk")
    base = lax.axis_index("src") * group
    tiles = S // 2 // LANES

    for slot in range(slots):
        for block in range(group):
            row = slice(slot * group + block, slot * group + block + 1)
            at = 2 * (base + block)
            for tile in range(tiles):
                span = slice(LANES * (slot * tiles + tile), LANES * (slot * tiles + tile + 1))
                early = slice(LANES * tile, LANES * (tile + 1))
                late = slice(S // 2 + LANES * tile, S // 2 + LANES * (tile + 1))
                series_ref[row, early] = pieces_ref[at, :, span]
                series_ref[row, late] = pieces_ref[at + 1, :, span]
            rims_ref[row, :] = pieces_ref[at + 1, :, LANES * slots * tiles :]
    rims = jnp.concatenate(
        [
            pltpu.roll(rims_ref[slot * group : (slot + 1) * group, :], EDGE * slot, 1)
            for slot in range(slots)
        ],
        axis=0,
    )
    lane = lax.broadcasted_iota(jnp.int32, rims.shape, 1)
    seam = slice(S // 2 - LANES, S // 2)
    series_ref[:, seam] = series_ref[:, seam] + jnp.where(lane >= LANES - EDGE, rims, 0.0)
    series = series_ref[...]
    spectrum = transform(series, hi_ref[...], lo_ref[...])
    real_part, imag_part = whitening(spectrum, 1.0, band_ref[...])
    source_ref[:, :BINS] = real_part
    source_ref[:, BINS:] = imag_part
    per_part = max(1, (group * slots) // PARTS)
    copies = []
    for part in range(group * slots // per_part):
        first = part * per_part
        for source in range(first, first + per_part):
            block, slot = divmod(source, slots)
            at = slot * group + block
            for tile in range(half):
                re = slice(LANES * tile, LANES * (tile + 1))
                im = slice(BINS + LANES * tile, BINS + LANES * (tile + 1))
                src_re, src_im = source_ref[at : at + 1, re], source_ref[at : at + 1, im]
                rec_re, rec_im = spectra_ref[:, re], spectra_ref[:, im]
                where = slice(rows * source, rows * (source + 1))
                cross_ref[where, re] = (src_re * rec_re + src_im * rec_im).astype(jnp.bfloat16)
                cross_ref[where, im] = (src_re * rec_im - src_im * rec_re).astype(jnp.bfloat16)
        lagged = dot(cross_ref[rows * first : rows * (first + per_part), :], lag_ref[...])
        for source in range(first, first + per_part):
            block, slot = divmod(source, slots)
            keep = 1.0 - jnp.where(own == base + block, 1.0, 0.0) * picks_ref[slot]
            at = source - first
            kept = lagged[rows * at : rows * (at + 1)] * jnp.concatenate(
                [keep] * (LAGS // LANES), axis=1
            )
            out_ref[source] = kept.astype(jnp.bfloat16)
        span = pl.ds(first, per_part)
        copies.append(pltpu.make_async_copy(out_ref.at[span], out_hbm.at[span], sems.at[part]))
        copies[-1].start()
    for copy in copies:
        copy.wait()


HBM = pl.BlockSpec(memory_space=pltpu.HBM)
VMEM = pl.BlockSpec(memory_space=pltpu.VMEM)
PARAMS = pltpu.CompilerParams(vmem_limit_bytes=VMEM_LIMIT)


def in_hbm(*arrays):
    return [pltpu.with_memory_space_constraint(array, pltpu.HBM) for array in arrays]


def shaped(*shape, dtype=jnp.float32):
    return jax.ShapeDtypeStruct(shape, dtype)


def local(raw_records, fir_taps, alive_mask, source_index):
    src_count = lax.axis_size("src")
    blk_count = lax.axis_size("blk")
    rows, raw_count = raw_records.shape
    slots = source_index.shape[1]
    group = blk_count // src_count
    out_count = raw_count // DEC
    width = -(-out_count // LANES) * LANES + LANES
    chunks = raw_count // CHUNK
    paired = src_count == 2 and 2 * out_count == S
    bf16 = jnp.bfloat16
    forward_hi, forward_lo = split_table(forward_table())
    alive_row = alive_mask.reshape(1, rows)

    with jax.named_scope("decimate"):
        device_count = blk_count * src_count
        main = slots * (width - LANES)
        decimated, pieces = pl.pallas_call(
            decimate_kernel,
            out_shape=(shaped(rows, width), shaped(device_count, 1, main + LANES)),
            in_specs=[HBM] * 4,
            out_specs=(VMEM, HBM),
            scratch_shapes=[
                pltpu.VMEM((rows * chunks, CHUNK), jnp.float32),
                pltpu.VMEM((1, TAPS), jnp.float32),
                pltpu.SMEM((1, rows), jnp.int32),
                pltpu.SMEM((1, slots), jnp.int32),
                pltpu.VMEM((SUBLANES * chunks, CHUNK), jnp.float32),
                pltpu.VMEM((device_count, 1, main + LANES), jnp.float32),
                pltpu.SemaphoreType.DMA((chunks + 3,)),
            ],
            compiler_params=PARAMS,
        )(*in_hbm(raw_records, fir_taps.reshape(1, TAPS), alive_row, source_index))

    def whole(shards):
        rims = jnp.pad(shards[1:, :, width - EDGE :], ((0, 1), (0, 0), (out_count - EDGE, 0)))
        series = shards[:, :, :out_count] + rims
        return series.transpose(1, 0, 2).reshape(shards.shape[1], S)

    with jax.named_scope("gather_sources"):
        gathered = lax.all_to_all(pieces, ("blk", "src"), split_axis=0, concat_axis=0, tiled=True)
        if not paired:
            shards = gathered.reshape(blk_count, src_count, main + LANES)
            shards = shards.transpose(1, 0, 2)
            rims = [shards[:, :, main + LANES - EDGE * (slot + 1) :] for slot in range(slots)]
            rims = jnp.stack([rim[:, :, :EDGE] for rim in rims], axis=2)
            rims = jnp.pad(rims, ((0, 0), (0, 0), (0, 0), (LANES - EDGE, 0)))
            series = shards[:, :, :main].reshape(src_count, blk_count, slots, width - LANES)
            series = jnp.concatenate([series, rims], axis=3)
            series = whole(series.reshape(src_count, blk_count * slots, width))
            series = series.reshape(blk_count, slots, 2, S // 2).transpose(0, 2, 1, 3)
            series = series.reshape(blk_count * 2, 1, slots * S // 2)
            gathered = jnp.pad(series, ((0, 0), (0, 0), (0, LANES)))

    with jax.named_scope("regroup"):
        if paired:
            series = decimated
            other = lax.ppermute(decimated, "src", [(0, 1), (1, 0)])
        else:
            series = whole(lax.all_gather(decimated, "src", axis=0))

    with jax.named_scope("prepare"):
        out_shape = (
            shaped(rows, NFFT),
            shaped(S, NFFT, dtype=bf16),
            shaped(S, NFFT, dtype=bf16),
            shaped(3 * LANES, LANES, dtype=bf16),
            shaped(NFFT, LAGS, dtype=bf16),
            shaped(rows, LANES),
            shaped(slots, rows, LANES),
        )
        partial, table_hi, table_lo, band, lag, alive, picks = pl.pallas_call(
            prepare_kernel,
            out_shape=out_shape,
            in_specs=[VMEM] + [HBM] * 6,
            out_specs=(VMEM,) * len(out_shape),
            scratch_shapes=[
                pltpu.VMEM((1, rows), jnp.int32),
                pltpu.VMEM((1, slots), jnp.int32),
                pltpu.SemaphoreType.DMA((6,)),
            ],
            compiler_params=PARAMS,
            cost_estimate=pl.CostEstimate(
                flops=6 * rows * S * NFFT, bytes_accessed=6 * S * NFFT, transcendentals=0
            ),
        )(
            series,
            *in_hbm(
                alive_row,
                source_index,
                jnp.asarray(forward_hi),
                jnp.asarray(forward_lo),
                jnp.asarray(band_table()),
                jnp.asarray(lag_table()),
            ),
        )

    with jax.named_scope("spectra"):
        operands = [partial, band, alive]
        if paired:
            operands += [other, table_hi, table_lo]
        spectra = pl.pallas_call(
            spectra_kernel,
            out_shape=shaped(rows, NFFT),
            in_specs=[VMEM] * len(operands),
            out_specs=VMEM,
            compiler_params=PARAMS,
        )(*operands)

    with jax.named_scope("correlate"):
        total = group * slots
        return pl.pallas_call(
            lambda *refs: correlate_kernel(slots, *refs),
            out_shape=shaped(total, rows, LAGS, dtype=bf16),
            in_specs=[VMEM] * 7,
            out_specs=HBM,
            scratch_shapes=[
                pltpu.VMEM((total, S), jnp.float32),
                pltpu.VMEM((total, LANES), jnp.float32),
                pltpu.VMEM((total, NFFT), jnp.float32),
                pltpu.VMEM((total * rows, NFFT), bf16),
                pltpu.VMEM((total, rows, LAGS), bf16),
                pltpu.SemaphoreType.DMA((PARTS,)),
            ],
            compiler_params=PARAMS,
        )(spectra, gathered, picks, table_hi, table_lo, band, lag)


def solution(mesh):
    in_specs = (P("blk", "src"), P(), P("blk"), P("blk", None))
    out_specs = P("src", "blk", None)
    return jax.shard_map(local, mesh=mesh, in_specs=in_specs, out_specs=out_specs, check_vma=False)
```

```python
import math

import jax
import jax.numpy as jnp
import numpy as np
from jax import lax
from jax.experimental import pallas as pl
from jax.experimental.pallas import tpu as pltpu
from jax.sharding import PartitionSpec as P

S = 512
NFFT = 1024
BINS = NFFT // 2
LAGS = 512
TAPS = 64
DEC = 20
HALF = 64
LANES = 128
SUBLANES = 8
PARTS = 2
EDGE = (TAPS - 1) // DEC
CHUNK = 640
CHUNK_OUT = CHUNK // DEC
VMEM_LIMIT = 48 * 1024 * 1024


def forward_table():
    phases = 2.0 * math.pi / NFFT * (np.outer(np.arange(S // 2), np.arange(BINS)) % NFFT)
    return np.concatenate([np.cos(phases), -np.sin(phases)], axis=1).astype(np.float32)


def split_table(table):
    high = table.astype(jnp.bfloat16)
    low = (table - high.astype(np.float32)).astype(jnp.bfloat16)
    return high, low


def band_table():
    bins = np.arange(3 * LANES)[:, None] - LANES
    return (np.abs(bins - np.arange(LANES)[None, :]) <= HALF).astype(jnp.bfloat16)


def lag_table():
    bins = np.arange(BINS)[:, None]
    shift = np.arange(LAGS)[None, :] - LAGS // 2
    phases = 2.0 * math.pi / NFFT * (bins * shift % NFFT)
    weight = np.where(bins == 0, 0.5, 1.0) / math.sqrt(BINS)
    table = np.concatenate([weight * np.cos(phases), -weight * np.sin(phases)], axis=0)
    return table.astype(np.float32).astype(jnp.bfloat16)


def split(value):
    high = value.astype(jnp.bfloat16)
    return high, (value - high.astype(jnp.float32)).astype(jnp.bfloat16)


def dot(a, b):
    return jnp.dot(a, b, preferred_element_type=jnp.float32)


def column(row):
    count = row.shape[1]
    at = [lax.broadcasted_iota(jnp.int32, (count, count), axis) for axis in range(2)]
    rows = jnp.broadcast_to(row, (count, count))
    return jnp.sum(jnp.where(at[0] == at[1], rows, 0.0), axis=1, keepdims=True)


def start_copies(pairs, sems):
    copies = [
        pltpu.make_async_copy(source, target, sems.at[at])
        for at, (source, target) in enumerate(pairs)
    ]
    for copy in copies:
        copy.start()
    return copies


def decimate_kernel(
    raw_hbm, taps_hbm, alive_hbm, picks_hbm, out_ref, pieces_hbm,
    raw_ref, taps_ref, alive_ref, picks_ref, source_ref, pieces_ref, sems,
):
    rows = raw_hbm.shape[0]
    chunks = raw_hbm.shape[1] // CHUNK
    slots = picks_ref.shape[1]
    pairs = [(taps_hbm, taps_ref), (picks_hbm, picks_ref), (alive_hbm, alive_ref)]
    for j in range(chunks):
        span = slice(CHUNK * j, CHUNK * (j + 1))
        pairs.append((raw_hbm.at[:, span], raw_ref.at[rows * j : rows * (j + 1), :]))
    copies = start_copies(pairs, sems)
    copies[0].wait()
    taps = jnp.broadcast_to(taps_ref[...], (SUBLANES, TAPS))
    eight = jnp.concatenate([taps, jnp.zeros((SUBLANES, CHUNK - TAPS), jnp.float32)], axis=1)
    for _ in range(2):
        eight = pltpu.roll(eight, 0, 1, stride=DEC // 2, stride_axis=0)
    wrapped = jnp.concatenate(
        [eight]
        + [pltpu.roll(eight, DEC * at, 1) for at in range(SUBLANES, CHUNK_OUT, SUBLANES)],
        axis=0,
    )
    lane = lax.broadcasted_iota(jnp.int32, (CHUNK_OUT, CHUNK), 1)
    row = lax.broadcasted_iota(jnp.int32, (CHUNK_OUT, CHUNK), 0)
    main = jnp.where(lane >= DEC * row, wrapped, 0.0)
    rim = wrapped - main
    gap = jnp.zeros((LANES - 2 * CHUNK_OUT, CHUNK), jnp.float32)
    weights_hi, weights_lo = split(jnp.concatenate([main, gap, rim], axis=0).T)
    weights = jnp.concatenate([weights_hi, weights_lo], axis=1)

    def filtered(stacked):
        count = stacked.shape[0] // chunks
        high, low = split(stacked)
        both = dot(high, weights)
        result = both[:, :LANES] + both[:, LANES:] + dot(low, weights_hi)
        part = [result[count * j : count * (j + 1)] for j in range(chunks)]
        per_tile = LANES // CHUNK_OUT
        is_main = lax.broadcasted_iota(jnp.int32, (count, LANES), 1) < LANES // 2
        tiles = []
        for first in range(0, chunks, per_tile):
            total = jnp.where(is_main, part[first], 0.0)
            for step in range(1, min(per_tile, chunks - first)):
                total = total + pltpu.roll(part[first + step], CHUNK_OUT * step, 1)
            if first + per_tile < chunks:
                total = total + jnp.where(is_main, 0.0, part[first + per_tile])
            tiles.append(total)
        return tiles + [jnp.where(is_main, 0.0, part[0])]

    for copy in copies[1:]:
        copy.wait()
    source_ref[...] = jnp.zeros_like(source_ref)
    for slot in range(slots):
        pick = picks_ref[0, slot]
        alive = alive_ref[0, pick].astype(jnp.float32)
        for j in range(chunks):
            at = SUBLANES * j + slot
            source_ref[at : at + 1, :] = raw_ref[pl.ds(rows * j + pick, 1), :] * alive
    sources = filtered(source_ref[...])
    rims = jnp.zeros((1, LANES), jnp.float32)
    for slot in range(slots):
        late = sources[-1][slot : slot + 1]
        rims = rims + pltpu.roll(late, LANES - EDGE * slot if slot else 0, 1)
    piece = [tile[slot : slot + 1] for slot in range(slots) for tile in sources[:-1]] + [rims]
    for device in range(pieces_ref.shape[0]):
        for at, value in enumerate(piece):
            pieces_ref[device, :, LANES * at : LANES * (at + 1)] = value
    sending = pltpu.make_async_copy(pieces_ref, pieces_hbm, sems.at[0])
    sending.start()
    for at, value in enumerate(filtered(raw_ref[...])):
        out_ref[:, LANES * at : LANES * (at + 1)] = value
    sending.wait()


def pack(shard):
    tiles = [shard[:, at : at + LANES] for at in range(0, shard.shape[1] - LANES, LANES)]
    rim = shard[:, shard.shape[1] - LANES :]
    packed = rim[:SUBLANES]
    for at in range(SUBLANES, rim.shape[0], SUBLANES):
        packed = packed + pltpu.roll(rim[at : at + SUBLANES], LANES - EDGE * (at // SUBLANES), 1)
    return jnp.concatenate(tiles + [packed], axis=0)


def unpack(packed, rows):
    tiles = [packed[at : at + rows] for at in range(0, packed.shape[0] - SUBLANES, rows)]
    rims = packed[packed.shape[0] - SUBLANES :]
    rim = jnp.concatenate(
        [rims]
        + [pltpu.roll(rims, EDGE * at, 1) for at in range(1, rows // SUBLANES)],
        axis=0,
    )
    lane = lax.broadcasted_iota(jnp.int32, rim.shape, 1)
    return tiles + [jnp.where(lane >= LANES - EDGE, rim, 0.0)]


def transform(early, late, table_hi, table_lo):
    rows = early.shape[0]
    high, low = split(jnp.concatenate([early, late], axis=0))
    first = dot(jnp.concatenate([high, low], axis=0), table_hi)
    both = first[: 2 * rows] + first[2 * rows :] + dot(high, table_lo)
    quarter = lax.broadcasted_iota(jnp.int32, (1, BINS), 1) & 3
    cosine = jnp.where(quarter == 0, 1.0, 0.0) - jnp.where(quarter == 2, 1.0, 0.0)
    sine = jnp.where(quarter == 1, 1.0, 0.0) - jnp.where(quarter == 3, 1.0, 0.0)
    early_re, early_im = both[:rows, :BINS], both[:rows, BINS:]
    late_re, late_im = both[rows:, :BINS], both[rows:, BINS:]
    return (
        early_re + cosine * late_re + sine * late_im,
        early_im + cosine * late_im - sine * late_re,
    )


def whitening(real_part, imag_part, band):
    rows = real_part.shape[0]
    tiles = BINS // LANES
    stacked = []
    for part in split(real_part * real_part + imag_part * imag_part):
        zero = jnp.zeros((rows, LANES), part.dtype)
        wide = jnp.concatenate([zero, part, zero], axis=1)
        stacked += [wide[:, LANES * tile : LANES * (tile + 3)] for tile in range(tiles)]
    banded = dot(jnp.concatenate(stacked, axis=0), band)
    step = rows * tiles
    summed = banded[:step] + banded[step:]
    total = jnp.concatenate(
        [summed[rows * tile : rows * (tile + 1)] for tile in range(tiles)], axis=1
    )
    bins = lax.broadcasted_iota(jnp.int32, (1, BINS), 1)
    count = jnp.minimum(bins + HALF, BINS - 1) - jnp.maximum(bins - HALF, 0) + 1
    return lax.rsqrt(total * (1.0 / count.astype(jnp.float32)) + 1e-06)


def prepare_kernel(
    series_ref, alive_hbm, picks_hbm, fwd_hi_hbm, fwd_lo_hbm, band_hbm, lag_hbm,
    hi_ref, lo_ref, band_ref, lag_ref, alive_out, picks_out, *refs,
):
    alive_ref, picks_ref, sems = refs[-3:]
    copies = start_copies(
        [
            (alive_hbm, alive_ref),
            (picks_hbm, picks_ref),
            (fwd_hi_hbm, hi_ref),
            (fwd_lo_hbm, lo_ref),
            (band_hbm, band_ref),
            (lag_hbm, lag_ref),
        ],
        sems,
    )
    if len(refs) > 3:
        refs[0][...] = pack(series_ref[...])
    for copy in copies[:2]:
        copy.wait()
    rows = alive_out.shape[0]
    alive_out[...] = jnp.broadcast_to(
        column(alive_ref[...].astype(jnp.float32)), (rows, LANES)
    )
    channel = lax.broadcasted_iota(jnp.int32, (rows, LANES), 0)
    for slot in range(picks_ref.shape[1]):
        pick = jnp.broadcast_to(picks_ref[:, slot : slot + 1], (rows, LANES))
        picks_out[slot] = jnp.where(channel == pick, 1.0, 0.0)
    for copy in copies[2:]:
        copy.wait()


def spectra_kernel(series_ref, hi_ref, lo_ref, band_ref, alive_ref, *refs):
    spectra_ref = refs[-1]
    rows = series_ref.shape[0]
    half = S // 2
    if len(refs) > 1:
        other = unpack(refs[0][...], rows)
        mine = [series_ref[:, at : at + LANES] for at in range(0, half + LANES, LANES)]
        first = lax.axis_index("src") == 0
        early = [jnp.where(first, a, b) for a, b in zip(mine, other)]
        late = [jnp.where(first, b, a) for a, b in zip(mine, other)]
        early[-2] = early[-2] + late[-1]
        early, late = [jnp.concatenate(tiles[:-1], axis=1) for tiles in (early, late)]
    else:
        early, late = series_ref[:, :half], series_ref[:, half:]
    real_part, imag_part = transform(early, late, hi_ref[...], lo_ref[...])
    factor = alive_ref[:, :1] * whitening(real_part, imag_part, band_ref[...])
    spectra_ref[:, :BINS] = real_part * factor
    spectra_ref[:, BINS:] = imag_part * factor


def correlate_kernel(
    slots, spectra_ref, pieces_ref, picks_ref, hi_ref, lo_ref, band_ref, lag_ref, out_hbm,
    series_ref, rims_ref, source_ref, cross_ref, out_ref, sems,
):
    rows = spectra_ref.shape[0]
    group = out_ref.shape[0] // slots
    half = BINS // LANES
    own = lax.axis_index("blk")
    base = lax.axis_index("src") * group
    tiles = S // 2 // LANES

    for slot in range(slots):
        for block in range(group):
            row = slice(slot * group + block, slot * group + block + 1)
            at = 2 * (base + block)
            for tile in range(tiles):
                span = slice(LANES * (slot * tiles + tile), LANES * (slot * tiles + tile + 1))
                early = slice(LANES * tile, LANES * (tile + 1))
                late = slice(S // 2 + LANES * tile, S // 2 + LANES * (tile + 1))
                series_ref[row, early] = pieces_ref[at, :, span]
                series_ref[row, late] = pieces_ref[at + 1, :, span]
            rims_ref[row, :] = pieces_ref[at + 1, :, LANES * slots * tiles :]
    rims = jnp.concatenate(
        [
            pltpu.roll(rims_ref[slot * group : (slot + 1) * group, :], EDGE * slot, 1)
            for slot in range(slots)
        ],
        axis=0,
    )
    lane = lax.broadcasted_iota(jnp.int32, rims.shape, 1)
    seam = slice(S // 2 - LANES, S // 2)
    series_ref[:, seam] = series_ref[:, seam] + jnp.where(lane >= LANES - EDGE, rims, 0.0)
    early, late = series_ref[:, : S // 2], series_ref[:, S // 2 :]
    real_part, imag_part = transform(early, late, hi_ref[...], lo_ref[...])
    factor = whitening(real_part, imag_part, band_ref[...])
    source_ref[:, :BINS] = real_part * factor
    source_ref[:, BINS:] = imag_part * factor
    per_part = max(1, (group * slots) // PARTS)
    copies = []
    for part in range(group * slots // per_part):
        first = part * per_part
        for tile in range(half):
            re = slice(LANES * tile, LANES * (tile + 1))
            im = slice(BINS + LANES * tile, BINS + LANES * (tile + 1))
            rec_re, rec_im = spectra_ref[:, re], spectra_ref[:, im]
            for source in range(first, first + per_part):
                block, slot = divmod(source, slots)
                at = slot * group + block
                src_re, src_im = source_ref[at : at + 1, re], source_ref[at : at + 1, im]
                where = slice(rows * source, rows * (source + 1))
                cross_ref[where, re] = (src_re * rec_re + src_im * rec_im).astype(jnp.bfloat16)
                cross_ref[where, im] = (src_re * rec_im - src_im * rec_re).astype(jnp.bfloat16)
        lagged = dot(cross_ref[rows * first : rows * (first + per_part), :], lag_ref[...])
        for source in range(first, first + per_part):
            block, slot = divmod(source, slots)
            keep = 1.0 - jnp.where(own == base + block, 1.0, 0.0) * picks_ref[slot]
            at = source - first
            kept = lagged[rows * at : rows * (at + 1)] * jnp.concatenate(
                [keep] * (LAGS // LANES), axis=1
            )
            out_ref[source] = kept.astype(jnp.bfloat16)
        span = pl.ds(first, per_part)
        copies.append(pltpu.make_async_copy(out_ref.at[span], out_hbm.at[span], sems.at[part]))
        copies[-1].start()
    for copy in copies:
        copy.wait()


HBM = pl.BlockSpec(memory_space=pltpu.HBM)
VMEM = pl.BlockSpec(memory_space=pltpu.VMEM)
PARAMS = pltpu.CompilerParams(vmem_limit_bytes=VMEM_LIMIT)


def in_hbm(*arrays):
    return [pltpu.with_memory_space_constraint(array, pltpu.HBM) for array in arrays]


def shaped(*shape, dtype=jnp.float32):
    return jax.ShapeDtypeStruct(shape, dtype)


def local(raw_records, fir_taps, alive_mask, source_index):
    src_count = lax.axis_size("src")
    blk_count = lax.axis_size("blk")
    rows, raw_count = raw_records.shape
    slots = source_index.shape[1]
    group = blk_count // src_count
    out_count = raw_count // DEC
    width = -(-out_count // LANES) * LANES + LANES
    chunks = raw_count // CHUNK
    paired = src_count == 2 and 2 * out_count == S
    bf16 = jnp.bfloat16
    forward_hi, forward_lo = split_table(forward_table())
    alive_row = alive_mask.reshape(1, rows)

    with jax.named_scope("decimate"):
        device_count = blk_count * src_count
        main = slots * (width - LANES)
        decimated, pieces = pl.pallas_call(
            decimate_kernel,
            out_shape=(shaped(rows, width), shaped(device_count, 1, main + LANES)),
            in_specs=[HBM] * 4,
            out_specs=(VMEM, HBM),
            scratch_shapes=[
                pltpu.VMEM((rows * chunks, CHUNK), jnp.float32),
                pltpu.VMEM((1, TAPS), jnp.float32),
                pltpu.SMEM((1, rows), jnp.int32),
                pltpu.SMEM((1, slots), jnp.int32),
                pltpu.VMEM((SUBLANES * chunks, CHUNK), jnp.float32),
                pltpu.VMEM((device_count, 1, main + LANES), jnp.float32),
                pltpu.SemaphoreType.DMA((chunks + 3,)),
            ],
            compiler_params=PARAMS,
        )(*in_hbm(raw_records, fir_taps.reshape(1, TAPS), alive_row, source_index))

    def whole(shards):
        rims = jnp.pad(shards[1:, :, width - EDGE :], ((0, 1), (0, 0), (out_count - EDGE, 0)))
        series = shards[:, :, :out_count] + rims
        return series.transpose(1, 0, 2).reshape(shards.shape[1], S)

    with jax.named_scope("gather_sources"):
        gathered = lax.all_to_all(pieces, ("blk", "src"), split_axis=0, concat_axis=0, tiled=True)
        if not paired:
            shards = gathered.reshape(blk_count, src_count, main + LANES)
            shards = shards.transpose(1, 0, 2)
            rims = [shards[:, :, main + LANES - EDGE * (slot + 1) :] for slot in range(slots)]
            rims = jnp.stack([rim[:, :, :EDGE] for rim in rims], axis=2)
            rims = jnp.pad(rims, ((0, 0), (0, 0), (0, 0), (LANES - EDGE, 0)))
            series = shards[:, :, :main].reshape(src_count, blk_count, slots, width - LANES)
            series = jnp.concatenate([series, rims], axis=3)
            series = whole(series.reshape(src_count, blk_count * slots, width))
            series = series.reshape(blk_count, slots, 2, S // 2).transpose(0, 2, 1, 3)
            series = series.reshape(blk_count * 2, 1, slots * S // 2)
            gathered = jnp.pad(series, ((0, 0), (0, 0), (0, LANES)))

    with jax.named_scope("prepare"):
        out_shape = (
            shaped(S // 2, NFFT, dtype=bf16),
            shaped(S // 2, NFFT, dtype=bf16),
            shaped(3 * LANES, LANES, dtype=bf16),
            shaped(NFFT, LAGS, dtype=bf16),
            shaped(rows, LANES),
            shaped(slots, rows, LANES),
        )
        if paired:
            out_shape += (shaped(rows * (S // 2 // LANES) + SUBLANES, LANES),)
        table_hi, table_lo, band, lag, alive, picks, *packed = pl.pallas_call(
            prepare_kernel,
            out_shape=out_shape,
            in_specs=[VMEM] + [HBM] * 6,
            out_specs=(VMEM,) * len(out_shape),
            scratch_shapes=[
                pltpu.VMEM((1, rows), jnp.int32),
                pltpu.VMEM((1, slots), jnp.int32),
                pltpu.SemaphoreType.DMA((6,)),
            ],
            compiler_params=PARAMS,
            cost_estimate=pl.CostEstimate(
                flops=0, bytes_accessed=4 * S * NFFT, transcendentals=0
            ),
        )(
            decimated,
            *in_hbm(
                alive_row,
                source_index,
                jnp.asarray(forward_hi),
                jnp.asarray(forward_lo),
                jnp.asarray(band_table()),
                jnp.asarray(lag_table()),
            ),
        )

    with jax.named_scope("regroup"):
        if paired:
            series = [decimated]
            other = [lax.ppermute(packed[0], "src", [(0, 1), (1, 0)])]
        else:
            series = [whole(lax.all_gather(decimated, "src", axis=0))]
            other = []

    with jax.named_scope("spectra"):
        operands = series + [table_hi, table_lo, band, alive] + other
        spectra = pl.pallas_call(
            spectra_kernel,
            out_shape=shaped(rows, NFFT),
            in_specs=[VMEM] * len(operands),
            out_specs=VMEM,
            compiler_params=PARAMS,
        )(*operands)

    with jax.named_scope("correlate"):
        total = group * slots
        return pl.pallas_call(
            lambda *refs: correlate_kernel(slots, *refs),
            out_shape=shaped(total, rows, LAGS, dtype=bf16),
            in_specs=[VMEM] * 7,
            out_specs=HBM,
            scratch_shapes=[
                pltpu.VMEM((total, S), jnp.float32),
                pltpu.VMEM((total, LANES), jnp.float32),
                pltpu.VMEM((total, NFFT), jnp.float32),
                pltpu.VMEM((total * rows, NFFT), bf16),
                pltpu.VMEM((total, rows, LAGS), bf16),
                pltpu.SemaphoreType.DMA((PARTS,)),
            ],
            compiler_params=PARAMS,
        )(spectra, gathered, picks, table_hi, table_lo, band, lag)


def solution(mesh):
    in_specs = (P("blk", "src"), P(), P("blk"), P("blk", None))
    out_specs = P("src", "blk", None)
    return jax.shard_map(local, mesh=mesh, in_specs=in_specs, out_specs=out_specs, check_vma=False)
```

```python
import math

import jax
import jax.numpy as jnp
import numpy as np
from jax import lax
from jax.experimental import pallas as pl
from jax.experimental.pallas import tpu as pltpu
from jax.sharding import PartitionSpec as P

S = 512
NFFT = 1024
BINS = NFFT // 2
LAGS = 512
TAPS = 64
DEC = 20
HALF = 64
LANES = 128
SUBLANES = 8
PARTS = 2
EDGE = (TAPS - 1) // DEC
CHUNK = 640
CHUNK_OUT = CHUNK // DEC
VMEM_LIMIT = 48 * 1024 * 1024


def forward_table():
    phases = 2.0 * math.pi / NFFT * (np.outer(np.arange(S // 2), np.arange(BINS)) % NFFT)
    return np.concatenate([np.cos(phases), -np.sin(phases)], axis=1).astype(np.float32)


def split_table(table):
    high = table.astype(jnp.bfloat16)
    low = (table - high.astype(np.float32)).astype(jnp.bfloat16)
    return high, low


def band_table():
    bins = np.arange(3 * LANES)[:, None] - LANES
    return (np.abs(bins - np.arange(LANES)[None, :]) <= HALF).astype(jnp.bfloat16)


def lag_table():
    bins = np.arange(BINS)[:, None]
    shift = np.arange(LAGS)[None, :] - LAGS // 2
    phases = 2.0 * math.pi / NFFT * (bins * shift % NFFT)
    weight = np.where(bins == 0, 0.5, 1.0) / math.sqrt(BINS)
    table = np.concatenate([weight * np.cos(phases), -weight * np.sin(phases)], axis=0)
    return table.astype(np.float32).astype(jnp.bfloat16)


def split(value):
    high = value.astype(jnp.bfloat16)
    return high, (value - high.astype(jnp.float32)).astype(jnp.bfloat16)


def dot(a, b):
    return jnp.dot(a, b, preferred_element_type=jnp.float32)


def column(row):
    count = row.shape[1]
    at = [lax.broadcasted_iota(jnp.int32, (count, count), axis) for axis in range(2)]
    rows = jnp.broadcast_to(row, (count, count))
    return jnp.sum(jnp.where(at[0] == at[1], rows, 0.0), axis=1, keepdims=True)


def start_copies(pairs, sems):
    copies = [
        pltpu.make_async_copy(source, target, sems.at[at])
        for at, (source, target) in enumerate(pairs)
    ]
    for copy in copies:
        copy.start()
    return copies


def decimate_kernel(
    raw_hbm, taps_hbm, alive_hbm, picks_hbm, out_ref, pieces_hbm,
    raw_ref, taps_ref, alive_ref, picks_ref, source_ref, pieces_ref, sems,
):
    rows = raw_hbm.shape[0]
    chunks = raw_hbm.shape[1] // CHUNK
    slots = picks_ref.shape[1]
    pairs = [(taps_hbm, taps_ref), (picks_hbm, picks_ref), (alive_hbm, alive_ref)]
    for j in range(chunks):
        span = slice(CHUNK * j, CHUNK * (j + 1))
        pairs.append((raw_hbm.at[:, span], raw_ref.at[rows * j : rows * (j + 1), :]))
    copies = start_copies(pairs, sems)
    copies[0].wait()
    taps = jnp.broadcast_to(taps_ref[...], (SUBLANES, TAPS))
    eight = jnp.concatenate([taps, jnp.zeros((SUBLANES, CHUNK - TAPS), jnp.float32)], axis=1)
    for _ in range(2):
        eight = pltpu.roll(eight, 0, 1, stride=DEC // 2, stride_axis=0)
    wrapped = jnp.concatenate(
        [eight]
        + [pltpu.roll(eight, DEC * at, 1) for at in range(SUBLANES, CHUNK_OUT, SUBLANES)],
        axis=0,
    )
    lane = lax.broadcasted_iota(jnp.int32, (CHUNK_OUT, CHUNK), 1)
    row = lax.broadcasted_iota(jnp.int32, (CHUNK_OUT, CHUNK), 0)
    main = jnp.where(lane >= DEC * row, wrapped, 0.0)
    rim = wrapped - main
    gap = jnp.zeros((LANES - 2 * CHUNK_OUT, CHUNK), jnp.float32)
    weights_hi, weights_lo = split(jnp.concatenate([main, gap, rim], axis=0).T)
    weights = jnp.concatenate([weights_hi, weights_lo], axis=1)

    def filtered(stacked):
        count = stacked.shape[0] // chunks
        high, low = split(stacked)
        both = dot(high, weights)
        result = both[:, :LANES] + both[:, LANES:] + dot(low, weights_hi)
        part = [result[count * j : count * (j + 1)] for j in range(chunks)]
        per_tile = LANES // CHUNK_OUT
        is_main = lax.broadcasted_iota(jnp.int32, (count, LANES), 1) < LANES // 2
        tiles = []
        for first in range(0, chunks, per_tile):
            total = jnp.where(is_main, part[first], 0.0)
            for step in range(1, min(per_tile, chunks - first)):
                total = total + pltpu.roll(part[first + step], CHUNK_OUT * step, 1)
            if first + per_tile < chunks:
                total = total + jnp.where(is_main, 0.0, part[first + per_tile])
            tiles.append(total)
        return tiles + [jnp.where(is_main, 0.0, part[0])]

    for copy in copies[1:]:
        copy.wait()
    source_ref[...] = jnp.zeros_like(source_ref)
    for slot in range(slots):
        pick = picks_ref[0, slot]
        alive = alive_ref[0, pick].astype(jnp.float32)
        for j in range(chunks):
            at = SUBLANES * j + slot
            source_ref[at : at + 1, :] = raw_ref[pl.ds(rows * j + pick, 1), :] * alive
    sources = filtered(source_ref[...])
    rims = jnp.zeros((1, LANES), jnp.float32)
    for slot in range(slots):
        late = sources[-1][slot : slot + 1]
        rims = rims + pltpu.roll(late, LANES - EDGE * slot if slot else 0, 1)
    piece = [tile[slot : slot + 1] for slot in range(slots) for tile in sources[:-1]] + [rims]
    for device in range(pieces_ref.shape[0]):
        for at, value in enumerate(piece):
            pieces_ref[device, :, LANES * at : LANES * (at + 1)] = value
    sending = pltpu.make_async_copy(pieces_ref, pieces_hbm, sems.at[0])
    sending.start()
    for at, value in enumerate(filtered(raw_ref[...])):
        out_ref[:, LANES * at : LANES * (at + 1)] = value
    sending.wait()


def pack(shard):
    tiles = [shard[:, at : at + LANES] for at in range(0, shard.shape[1] - LANES, LANES)]
    rim = shard[:, shard.shape[1] - LANES :]
    packed = rim[:SUBLANES]
    for at in range(SUBLANES, rim.shape[0], SUBLANES):
        packed = packed + pltpu.roll(rim[at : at + SUBLANES], LANES - EDGE * (at // SUBLANES), 1)
    return jnp.concatenate(tiles + [packed], axis=0)


def unpack(packed, rows):
    tiles = [packed[at : at + rows] for at in range(0, packed.shape[0] - SUBLANES, rows)]
    rims = packed[packed.shape[0] - SUBLANES :]
    rim = jnp.concatenate(
        [rims]
        + [pltpu.roll(rims, EDGE * at, 1) for at in range(1, rows // SUBLANES)],
        axis=0,
    )
    lane = lax.broadcasted_iota(jnp.int32, rim.shape, 1)
    return tiles + [jnp.where(lane >= LANES - EDGE, rim, 0.0)]


def transform(early, late, table_hi, table_lo):
    rows = early.shape[0]
    high, low = split(jnp.concatenate([early, late], axis=0))
    first = dot(jnp.concatenate([high, low], axis=0), table_hi)
    both = first[: 2 * rows] + first[2 * rows :] + dot(high, table_lo)
    quarter = lax.broadcasted_iota(jnp.int32, (1, BINS), 1) & 3
    cosine = jnp.where(quarter == 0, 1.0, 0.0) - jnp.where(quarter == 2, 1.0, 0.0)
    sine = jnp.where(quarter == 1, 1.0, 0.0) - jnp.where(quarter == 3, 1.0, 0.0)
    early_re, early_im = both[:rows, :BINS], both[:rows, BINS:]
    late_re, late_im = both[rows:, :BINS], both[rows:, BINS:]
    return (
        early_re + cosine * late_re + sine * late_im,
        early_im + cosine * late_im - sine * late_re,
    )


def whitening(real_part, imag_part, band):
    rows = real_part.shape[0]
    tiles = BINS // LANES
    stacked = []
    for part in split(real_part * real_part + imag_part * imag_part):
        zero = jnp.zeros((rows, LANES), part.dtype)
        wide = jnp.concatenate([zero, part, zero], axis=1)
        stacked += [wide[:, LANES * tile : LANES * (tile + 3)] for tile in range(tiles)]
    banded = dot(jnp.concatenate(stacked, axis=0), band)
    step = rows * tiles
    summed = banded[:step] + banded[step:]
    total = jnp.concatenate(
        [summed[rows * tile : rows * (tile + 1)] for tile in range(tiles)], axis=1
    )
    bins = lax.broadcasted_iota(jnp.int32, (1, BINS), 1)
    count = jnp.minimum(bins + HALF, BINS - 1) - jnp.maximum(bins - HALF, 0) + 1
    return lax.rsqrt(total * (1.0 / count.astype(jnp.float32)) + 1e-06)


def prepare_kernel(
    series_ref, alive_hbm, picks_hbm, fwd_hi_hbm, fwd_lo_hbm, band_hbm, lag_hbm,
    hi_ref, lo_ref, band_ref, lag_ref, alive_out, picks_out, *refs,
):
    alive_ref, picks_ref, sems = refs[-3:]
    copies = start_copies(
        [
            (alive_hbm, alive_ref),
            (picks_hbm, picks_ref),
            (fwd_hi_hbm, hi_ref),
            (fwd_lo_hbm, lo_ref),
            (band_hbm, band_ref),
            (lag_hbm, lag_ref),
        ],
        sems,
    )
    if len(refs) > 3:
        refs[0][...] = pack(series_ref[...])
    for copy in copies[:2]:
        copy.wait()
    rows = alive_out.shape[0]
    alive_out[...] = jnp.broadcast_to(
        column(alive_ref[...].astype(jnp.float32)), (rows, LANES)
    )
    channel = lax.broadcasted_iota(jnp.int32, (rows, LANES), 0)
    for slot in range(picks_ref.shape[1]):
        pick = jnp.broadcast_to(picks_ref[:, slot : slot + 1], (rows, LANES))
        picks_out[slot] = jnp.where(channel == pick, 1.0, 0.0)
    for copy in copies[2:]:
        copy.wait()


def spectra_kernel(series_ref, hi_ref, lo_ref, band_ref, alive_ref, *refs):
    spectra_ref = refs[-1]
    rows = series_ref.shape[0]
    half = S // 2
    if len(refs) > 1:
        other = unpack(refs[0][...], rows)
        mine = [series_ref[:, at : at + LANES] for at in range(0, half + LANES, LANES)]
        first = lax.axis_index("src") == 0
        early = [jnp.where(first, a, b) for a, b in zip(mine, other)]
        late = [jnp.where(first, b, a) for a, b in zip(mine, other)]
        early[-2] = early[-2] + late[-1]
        early, late = [jnp.concatenate(tiles[:-1], axis=1) for tiles in (early, late)]
    else:
        early, late = series_ref[:, :half], series_ref[:, half:]
    real_part, imag_part = transform(early, late, hi_ref[...], lo_ref[...])
    factor = alive_ref[:, :1] * whitening(real_part, imag_part, band_ref[...])
    spectra_ref[:, :BINS] = real_part * factor
    spectra_ref[:, BINS:] = imag_part * factor


def correlate_kernel(
    slots, spectra_ref, pieces_ref, picks_ref, hi_ref, lo_ref, band_ref, lag_ref, out_hbm,
    series_ref, rims_ref, source_ref, cross_ref, out_ref, sems,
):
    rows = spectra_ref.shape[0]
    group = out_ref.shape[0] // slots
    half = BINS // LANES
    own = lax.axis_index("blk")
    base = lax.axis_index("src") * group
    tiles = S // 2 // LANES

    for slot in range(slots):
        for block in range(group):
            row = slice(slot * group + block, slot * group + block + 1)
            at = pieces_ref.shape[0] - 1 - 2 * (base + block)
            for tile in range(tiles):
                span = slice(LANES * (slot * tiles + tile), LANES * (slot * tiles + tile + 1))
                early = slice(LANES * tile, LANES * (tile + 1))
                late = slice(S // 2 + LANES * tile, S // 2 + LANES * (tile + 1))
                series_ref[row, early] = pieces_ref[at, :, span]
                series_ref[row, late] = pieces_ref[at - 1, :, span]
            rims_ref[row, :] = pieces_ref[at - 1, :, LANES * slots * tiles :]
    rims = jnp.concatenate(
        [
            pltpu.roll(rims_ref[slot * group : (slot + 1) * group, :], EDGE * slot, 1)
            for slot in range(slots)
        ],
        axis=0,
    )
    lane = lax.broadcasted_iota(jnp.int32, rims.shape, 1)
    seam = slice(S // 2 - LANES, S // 2)
    series_ref[:, seam] = series_ref[:, seam] + jnp.where(lane >= LANES - EDGE, rims, 0.0)
    early, late = series_ref[:, : S // 2], series_ref[:, S // 2 :]
    real_part, imag_part = transform(early, late, hi_ref[...], lo_ref[...])
    factor = whitening(real_part, imag_part, band_ref[...])
    source_ref[:, :BINS] = real_part * factor
    source_ref[:, BINS:] = imag_part * factor
    per_part = max(1, (group * slots) // PARTS)
    copies = []
    for part in range(group * slots // per_part):
        first = part * per_part
        for tile in range(half):
            re = slice(LANES * tile, LANES * (tile + 1))
            im = slice(BINS + LANES * tile, BINS + LANES * (tile + 1))
            rec_re, rec_im = spectra_ref[:, re], spectra_ref[:, im]
            for source in range(first, first + per_part):
                block, slot = divmod(source, slots)
                at = slot * group + block
                src_re, src_im = source_ref[at : at + 1, re], source_ref[at : at + 1, im]
                where = slice(rows * source, rows * (source + 1))
                cross_ref[where, re] = (src_re * rec_re + src_im * rec_im).astype(jnp.bfloat16)
                cross_ref[where, im] = (src_re * rec_im - src_im * rec_re).astype(jnp.bfloat16)
        lagged = dot(cross_ref[rows * first : rows * (first + per_part), :], lag_ref[...])
        for source in range(first, first + per_part):
            block, slot = divmod(source, slots)
            keep = 1.0 - jnp.where(own == base + block, 1.0, 0.0) * picks_ref[slot]
            at = source - first
            kept = lagged[rows * at : rows * (at + 1)] * jnp.concatenate(
                [keep] * (LAGS // LANES), axis=1
            )
            out_ref[source] = kept.astype(jnp.bfloat16)
        span = pl.ds(first, per_part)
        copies.append(pltpu.make_async_copy(out_ref.at[span], out_hbm.at[span], sems.at[part]))
        copies[-1].start()
    for copy in copies:
        copy.wait()


HBM = pl.BlockSpec(memory_space=pltpu.HBM)
VMEM = pl.BlockSpec(memory_space=pltpu.VMEM)
PARAMS = pltpu.CompilerParams(vmem_limit_bytes=VMEM_LIMIT)


def in_hbm(*arrays):
    return [pltpu.with_memory_space_constraint(array, pltpu.HBM) for array in arrays]


def shaped(*shape, dtype=jnp.float32):
    return jax.ShapeDtypeStruct(shape, dtype)


def local(raw_records, fir_taps, alive_mask, source_index):
    src_count = lax.axis_size("src")
    blk_count = lax.axis_size("blk")
    rows, raw_count = raw_records.shape
    slots = source_index.shape[1]
    group = blk_count // src_count
    out_count = raw_count // DEC
    width = -(-out_count // LANES) * LANES + LANES
    chunks = raw_count // CHUNK
    paired = src_count == 2 and 2 * out_count == S
    bf16 = jnp.bfloat16
    forward_hi, forward_lo = split_table(forward_table())
    alive_row = alive_mask.reshape(1, rows)

    with jax.named_scope("decimate"):
        device_count = blk_count * src_count
        main = slots * (width - LANES)
        decimated, pieces = pl.pallas_call(
            decimate_kernel,
            out_shape=(shaped(rows, width), shaped(device_count, 1, main + LANES)),
            in_specs=[HBM] * 4,
            out_specs=(VMEM, HBM),
            scratch_shapes=[
                pltpu.VMEM((rows * chunks, CHUNK), jnp.float32),
                pltpu.VMEM((1, TAPS), jnp.float32),
                pltpu.SMEM((1, rows), jnp.int32),
                pltpu.SMEM((1, slots), jnp.int32),
                pltpu.VMEM((SUBLANES * chunks, CHUNK), jnp.float32),
                pltpu.VMEM((device_count, 1, main + LANES), jnp.float32),
                pltpu.SemaphoreType.DMA((chunks + 3,)),
            ],
            compiler_params=PARAMS,
        )(*in_hbm(raw_records, fir_taps.reshape(1, TAPS), alive_row, source_index))

    def whole(shards):
        rims = jnp.pad(shards[1:, :, width - EDGE :], ((0, 1), (0, 0), (out_count - EDGE, 0)))
        series = shards[:, :, :out_count] + rims
        return series.transpose(1, 0, 2).reshape(shards.shape[1], S)

    with jax.named_scope("gather_sources"):
        gathered = lax.all_to_all(
            pieces,
            ("blk", "src"),
            split_axis=0,
            concat_axis=0,
            tiled=True,
            axis_index_groups=[list(reversed(range(device_count)))],
        )
        if not paired:
            gathered = gathered[::-1]
            shards = gathered.reshape(blk_count, src_count, main + LANES)
            shards = shards.transpose(1, 0, 2)
            rims = [shards[:, :, main + LANES - EDGE * (slot + 1) :] for slot in range(slots)]
            rims = jnp.stack([rim[:, :, :EDGE] for rim in rims], axis=2)
            rims = jnp.pad(rims, ((0, 0), (0, 0), (0, 0), (LANES - EDGE, 0)))
            series = shards[:, :, :main].reshape(src_count, blk_count, slots, width - LANES)
            series = jnp.concatenate([series, rims], axis=3)
            series = whole(series.reshape(src_count, blk_count * slots, width))
            series = series.reshape(blk_count, slots, 2, S // 2).transpose(0, 2, 1, 3)
            series = series.reshape(blk_count * 2, 1, slots * S // 2)
            gathered = jnp.pad(series, ((0, 0), (0, 0), (0, LANES)))[::-1]

    with jax.named_scope("prepare"):
        out_shape = (
            shaped(S // 2, NFFT, dtype=bf16),
            shaped(S // 2, NFFT, dtype=bf16),
            shaped(3 * LANES, LANES, dtype=bf16),
            shaped(NFFT, LAGS, dtype=bf16),
            shaped(rows, LANES),
            shaped(slots, rows, LANES),
        )
        if paired:
            out_shape += (shaped(rows * (S // 2 // LANES) + SUBLANES, LANES),)
        table_hi, table_lo, band, lag, alive, picks, *packed = pl.pallas_call(
            prepare_kernel,
            out_shape=out_shape,
            in_specs=[VMEM] + [HBM] * 6,
            out_specs=(VMEM,) * len(out_shape),
            scratch_shapes=[
                pltpu.VMEM((1, rows), jnp.int32),
                pltpu.VMEM((1, slots), jnp.int32),
                pltpu.SemaphoreType.DMA((6,)),
            ],
            compiler_params=PARAMS,
            cost_estimate=pl.CostEstimate(
                flops=0, bytes_accessed=4 * S * NFFT, transcendentals=0
            ),
        )(
            decimated,
            *in_hbm(
                alive_row,
                source_index,
                jnp.asarray(forward_hi),
                jnp.asarray(forward_lo),
                jnp.asarray(band_table()),
                jnp.asarray(lag_table()),
            ),
        )

    with jax.named_scope("regroup"):
        if paired:
            series = [decimated]
            other = [lax.ppermute(packed[0], "src", [(0, 1), (1, 0)])]
        else:
            series = [whole(lax.all_gather(decimated, "src", axis=0))]
            other = []

    with jax.named_scope("spectra"):
        operands = series + [table_hi, table_lo, band, alive] + other
        spectra = pl.pallas_call(
            spectra_kernel,
            out_shape=shaped(rows, NFFT),
            in_specs=[VMEM] * len(operands),
            out_specs=VMEM,
            compiler_params=PARAMS,
        )(*operands)

    with jax.named_scope("correlate"):
        total = group * slots
        return pl.pallas_call(
            lambda *refs: correlate_kernel(slots, *refs),
            out_shape=shaped(total, rows, LAGS, dtype=bf16),
            in_specs=[VMEM] * 7,
            out_specs=HBM,
            scratch_shapes=[
                pltpu.VMEM((total, S), jnp.float32),
                pltpu.VMEM((total, LANES), jnp.float32),
                pltpu.VMEM((total, NFFT), jnp.float32),
                pltpu.VMEM((total * rows, NFFT), bf16),
                pltpu.VMEM((total, rows, LAGS), bf16),
                pltpu.SemaphoreType.DMA((PARTS,)),
            ],
            compiler_params=PARAMS,
        )(spectra, gathered, picks, table_hi, table_lo, band, lag)


def solution(mesh):
    in_specs = (P("blk", "src"), P(), P("blk"), P("blk", None))
    out_specs = P("src", "blk", None)
    return jax.shard_map(local, mesh=mesh, in_specs=in_specs, out_specs=out_specs, check_vma=False)
```

```python
import math

import jax
import jax.numpy as jnp
import numpy as np
from jax import lax
from jax.experimental import pallas as pl
from jax.experimental.pallas import tpu as pltpu
from jax.sharding import PartitionSpec as P

S = 512
NFFT = 1024
BINS = NFFT // 2
LAGS = 512
TAPS = 64
DEC = 20
HALF = 64
LANES = 128
SUBLANES = 8
PARTS = 2
EDGE = (TAPS - 1) // DEC
CHUNK = 640
CHUNK_OUT = CHUNK // DEC
VMEM_LIMIT = 48 * 1024 * 1024


def forward_table():
    phases = 2.0 * math.pi / NFFT * (np.outer(np.arange(S // 2), np.arange(BINS)) % NFFT)
    return np.concatenate([np.cos(phases), -np.sin(phases)], axis=1).astype(np.float32)


def split_table(table):
    high = table.astype(jnp.bfloat16)
    low = (table - high.astype(np.float32)).astype(jnp.bfloat16)
    return high, low


def band_table():
    bins = np.arange(3 * LANES)[:, None] - LANES
    return (np.abs(bins - np.arange(LANES)[None, :]) <= HALF).astype(jnp.bfloat16)


def lag_table():
    bins = np.arange(BINS)[:, None]
    shift = np.arange(LAGS)[None, :] - LAGS // 2
    phases = 2.0 * math.pi / NFFT * (bins * shift % NFFT)
    weight = np.where(bins == 0, 0.5, 1.0) / math.sqrt(BINS)
    table = np.concatenate([weight * np.cos(phases), -weight * np.sin(phases)], axis=0)
    return table.astype(np.float32).astype(jnp.bfloat16)


def split(value):
    high = value.astype(jnp.bfloat16)
    return high, (value - high.astype(jnp.float32)).astype(jnp.bfloat16)


def dot(a, b):
    return jnp.dot(a, b, preferred_element_type=jnp.float32)


def column(row):
    count = row.shape[1]
    at = [lax.broadcasted_iota(jnp.int32, (count, count), axis) for axis in range(2)]
    rows = jnp.broadcast_to(row, (count, count))
    return jnp.sum(jnp.where(at[0] == at[1], rows, 0.0), axis=1, keepdims=True)


def start_copies(pairs, sems):
    copies = [
        pltpu.make_async_copy(source, target, sems.at[at])
        for at, (source, target) in enumerate(pairs)
    ]
    for copy in copies:
        copy.start()
    return copies


def decimate_kernel(
    paired, raw_hbm, taps_hbm, alive_hbm, picks_hbm, out_ref, pieces_hbm,
    raw_ref, taps_ref, alive_ref, picks_ref, source_ref, pieces_ref, sems,
):
    rows = raw_hbm.shape[0]
    chunks = raw_hbm.shape[1] // CHUNK
    slots = picks_ref.shape[1]
    per_tile = LANES // CHUNK_OUT
    tiles = -(-chunks // per_tile)
    pairs = [(taps_hbm, taps_ref), (picks_hbm, picks_ref), (alive_hbm, alive_ref)]
    for j in range(chunks):
        span = slice(CHUNK * j, CHUNK * (j + 1))
        pairs.append((raw_hbm.at[:, span], raw_ref.at[rows * j : rows * (j + 1), :]))
    copies = start_copies(pairs, sems)
    source_ref[...] = jnp.zeros_like(source_ref)
    copies[0].wait()
    taps = jnp.broadcast_to(taps_ref[...], (SUBLANES, TAPS))
    eight = jnp.concatenate([taps, jnp.zeros((SUBLANES, CHUNK - TAPS), jnp.float32)], axis=1)
    for _ in range(2):
        eight = pltpu.roll(eight, 0, 1, stride=DEC // 2, stride_axis=0)
    wrapped = jnp.concatenate(
        [eight]
        + [pltpu.roll(eight, DEC * at, 1) for at in range(SUBLANES, CHUNK_OUT, SUBLANES)],
        axis=0,
    )
    lane = lax.broadcasted_iota(jnp.int32, (CHUNK_OUT, CHUNK), 1)
    row = lax.broadcasted_iota(jnp.int32, (CHUNK_OUT, CHUNK), 0)
    main = jnp.where(lane >= DEC * row, wrapped, 0.0)
    rim = wrapped - main
    gap = jnp.zeros((LANES - 2 * CHUNK_OUT, CHUNK), jnp.float32)
    weights_hi, weights_lo = split(jnp.concatenate([main, gap, rim], axis=0).T)
    weights = jnp.concatenate([weights_hi, weights_lo], axis=1)

    def filtered(stacked):
        high, low = split(stacked)
        both = dot(high, weights)
        return both[:, :LANES] + both[:, LANES:] + dot(low, weights_hi)

    for copy in copies[1:]:
        copy.wait()
    for slot in range(slots):
        pick = picks_ref[0, slot]
        alive = alive_ref[0, pick].astype(jnp.float32)
        for j in range(chunks):
            at = SUBLANES * slot + j
            source_ref[at : at + 1, :] = raw_ref[pl.ds(rows * j + pick, 1), :] * alive
    high, low = split(source_ref[...])
    count = slots * SUBLANES
    both = dot(jnp.concatenate([high, low], axis=0), weights)
    sources = both[:count, :LANES] + both[:count, LANES:] + both[count:, :LANES]
    lane = lax.broadcasted_iota(jnp.int32, (SUBLANES, LANES), 1)
    row = lax.broadcasted_iota(jnp.int32, (SUBLANES, LANES), 0)
    piece = []
    rims = jnp.zeros((1, LANES), jnp.float32)
    for slot in range(slots):
        source = sources[SUBLANES * slot : SUBLANES * (slot + 1)]
        main = jnp.where(lane < LANES // 2, source, 0.0)
        rim = source - main
        late = rim[:1]
        for _ in range(2):
            main = pltpu.roll(main, 0, 1, stride=CHUNK_OUT // 2, stride_axis=0)
            rim = pltpu.roll(rim, 0, 1, stride=CHUNK_OUT // 2, stride_axis=0)
        for tile in range(tiles):
            first = per_tile * tile
            inside = (row >= first) & (row < first + per_tile)
            before = (row > first) & (row <= first + per_tile)
            piece.append(
                jnp.sum(
                    jnp.where(inside, main, 0.0) + jnp.where(before, rim, 0.0),
                    axis=0,
                    keepdims=True,
                )
            )
        rims = rims + pltpu.roll(late, LANES - EDGE * slot if slot else 0, 1)
    piece.append(rims)
    for device in range(pieces_ref.shape[0]):
        for at, value in enumerate(piece):
            pieces_ref[device, :, LANES * at : LANES * (at + 1)] = value
    sending = pltpu.make_async_copy(pieces_ref, pieces_hbm, sems.at[0])
    sending.start()

    result = filtered(raw_ref[...])
    part = [result[rows * j : rows * (j + 1)] for j in range(chunks)]
    is_main = lax.broadcasted_iota(jnp.int32, (rows, LANES), 1) < LANES // 2
    values = []
    for first in range(0, chunks, per_tile):
        total = jnp.where(is_main, part[first], 0.0)
        for step in range(1, min(per_tile, chunks - first)):
            total = total + pltpu.roll(part[first + step], CHUNK_OUT * step, 1)
        if first + per_tile < chunks:
            total = total + jnp.where(is_main, 0.0, part[first + per_tile])
        values.append(total)
    rim = jnp.where(is_main, 0.0, part[0])
    if paired:
        packed = rim[:SUBLANES]
        for at in range(1, rows // SUBLANES):
            group = rim[SUBLANES * at : SUBLANES * (at + 1)]
            packed = packed + pltpu.roll(group, LANES - EDGE * at, 1)
        for at, value in enumerate(values):
            out_ref[rows * at : rows * (at + 1), :] = value
        out_ref[rows * tiles :, :] = packed
    else:
        for at, value in enumerate(values + [rim]):
            out_ref[:, LANES * at : LANES * (at + 1)] = value
    sending.wait()


def unpack(packed, rows):
    tiles = [packed[at : at + rows] for at in range(0, packed.shape[0] - SUBLANES, rows)]
    rims = packed[packed.shape[0] - SUBLANES :]
    rim = jnp.concatenate(
        [rims]
        + [pltpu.roll(rims, EDGE * at, 1) for at in range(1, rows // SUBLANES)],
        axis=0,
    )
    lane = lax.broadcasted_iota(jnp.int32, rim.shape, 1)
    return tiles + [jnp.where(lane >= LANES - EDGE, rim, 0.0)]


def transform(early, late, table_hi, table_lo):
    rows = early.shape[0]
    high, low = split(jnp.concatenate([early, late], axis=0))
    first = dot(jnp.concatenate([high, low], axis=0), table_hi)
    both = first[: 2 * rows] + first[2 * rows :] + dot(high, table_lo)
    quarter = lax.broadcasted_iota(jnp.int32, (1, BINS), 1) & 3
    cosine = jnp.where(quarter == 0, 1.0, 0.0) - jnp.where(quarter == 2, 1.0, 0.0)
    sine = jnp.where(quarter == 1, 1.0, 0.0) - jnp.where(quarter == 3, 1.0, 0.0)
    early_re, early_im = both[:rows, :BINS], both[:rows, BINS:]
    late_re, late_im = both[rows:, :BINS], both[rows:, BINS:]
    return (
        early_re + cosine * late_re + sine * late_im,
        early_im + cosine * late_im - sine * late_re,
    )


def whitening(real_part, imag_part, band):
    rows = real_part.shape[0]
    tiles = BINS // LANES
    stacked = []
    for part in split(real_part * real_part + imag_part * imag_part):
        zero = jnp.zeros((rows, LANES), part.dtype)
        wide = jnp.concatenate([zero, part, zero], axis=1)
        stacked += [wide[:, LANES * tile : LANES * (tile + 3)] for tile in range(tiles)]
    banded = dot(jnp.concatenate(stacked, axis=0), band)
    step = rows * tiles
    summed = banded[:step] + banded[step:]
    total = jnp.concatenate(
        [summed[rows * tile : rows * (tile + 1)] for tile in range(tiles)], axis=1
    )
    bins = lax.broadcasted_iota(jnp.int32, (1, BINS), 1)
    count = jnp.minimum(bins + HALF, BINS - 1) - jnp.maximum(bins - HALF, 0) + 1
    return lax.rsqrt(total * (1.0 / count.astype(jnp.float32)) + 1e-06)


def prepare_kernel(
    _, alive_hbm, picks_hbm, fwd_hi_hbm, fwd_lo_hbm, band_hbm, lag_hbm,
    hi_ref, lo_ref, band_ref, lag_ref, alive_out, picks_out, alive_ref, picks_ref, sems,
):
    copies = start_copies(
        [
            (alive_hbm, alive_ref),
            (picks_hbm, picks_ref),
            (fwd_hi_hbm, hi_ref),
            (fwd_lo_hbm, lo_ref),
            (band_hbm, band_ref),
            (lag_hbm, lag_ref),
        ],
        sems,
    )
    for copy in copies[:2]:
        copy.wait()
    rows = alive_out.shape[0]
    alive_out[...] = jnp.broadcast_to(
        column(alive_ref[...].astype(jnp.float32)), (rows, LANES)
    )
    channel = lax.broadcasted_iota(jnp.int32, (rows, LANES), 0)
    for slot in range(picks_ref.shape[1]):
        pick = jnp.broadcast_to(picks_ref[:, slot : slot + 1], (rows, LANES))
        picks_out[slot] = jnp.where(channel == pick, 1.0, 0.0)
    for copy in copies[2:]:
        copy.wait()


def spectra_kernel(series_ref, hi_ref, lo_ref, band_ref, alive_ref, *refs):
    spectra_ref = refs[-1]
    rows = alive_ref.shape[0]
    half = S // 2
    if len(refs) > 1:
        mine, other = [unpack(ref[...], rows) for ref in (series_ref, refs[0])]
        first = lax.axis_index("src") == 0
        early = [jnp.where(first, a, b) for a, b in zip(mine, other)]
        late = [jnp.where(first, b, a) for a, b in zip(mine, other)]
        early[-2] = early[-2] + late[-1]
        early, late = [jnp.concatenate(tiles[:-1], axis=1) for tiles in (early, late)]
    else:
        early, late = series_ref[:, :half], series_ref[:, half:]
    real_part, imag_part = transform(early, late, hi_ref[...], lo_ref[...])
    factor = alive_ref[:, :1] * whitening(real_part, imag_part, band_ref[...])
    spectra_ref[:, :BINS] = real_part * factor
    spectra_ref[:, BINS:] = imag_part * factor


def correlate_kernel(
    slots, spectra_ref, pieces_ref, picks_ref, hi_ref, lo_ref, band_ref, lag_ref, out_hbm,
    series_ref, rims_ref, source_ref, cross_ref, out_ref, sems,
):
    rows = spectra_ref.shape[0]
    group = out_ref.shape[0] // slots
    half = BINS // LANES
    own = lax.axis_index("blk")
    base = lax.axis_index("src") * group
    tiles = S // 2 // LANES

    for slot in range(slots):
        for block in range(group):
            row = slice(slot * group + block, slot * group + block + 1)
            at = pieces_ref.shape[0] - 1 - 2 * (base + block)
            for tile in range(tiles):
                span = slice(LANES * (slot * tiles + tile), LANES * (slot * tiles + tile + 1))
                early = slice(LANES * tile, LANES * (tile + 1))
                late = slice(S // 2 + LANES * tile, S // 2 + LANES * (tile + 1))
                series_ref[row, early] = pieces_ref[at, :, span]
                series_ref[row, late] = pieces_ref[at - 1, :, span]
            rims_ref[row, :] = pieces_ref[at - 1, :, LANES * slots * tiles :]
    rims = jnp.concatenate(
        [
            pltpu.roll(rims_ref[slot * group : (slot + 1) * group, :], EDGE * slot, 1)
            for slot in range(slots)
        ],
        axis=0,
    )
    lane = lax.broadcasted_iota(jnp.int32, rims.shape, 1)
    seam = slice(S // 2 - LANES, S // 2)
    series_ref[:, seam] = series_ref[:, seam] + jnp.where(lane >= LANES - EDGE, rims, 0.0)
    early, late = series_ref[:, : S // 2], series_ref[:, S // 2 :]
    real_part, imag_part = transform(early, late, hi_ref[...], lo_ref[...])
    factor = whitening(real_part, imag_part, band_ref[...])
    source_ref[:, :BINS] = real_part * factor
    source_ref[:, BINS:] = imag_part * factor
    per_part = max(1, (group * slots) // PARTS)
    copies = []
    for part in range(group * slots // per_part):
        first = part * per_part
        for tile in range(half):
            re = slice(LANES * tile, LANES * (tile + 1))
            im = slice(BINS + LANES * tile, BINS + LANES * (tile + 1))
            rec_re, rec_im = spectra_ref[:, re], spectra_ref[:, im]
            for source in range(first, first + per_part):
                block, slot = divmod(source, slots)
                at = slot * group + block
                src_re, src_im = source_ref[at : at + 1, re], source_ref[at : at + 1, im]
                where = slice(rows * source, rows * (source + 1))
                cross_ref[where, re] = (src_re * rec_re + src_im * rec_im).astype(jnp.bfloat16)
                cross_ref[where, im] = (src_re * rec_im - src_im * rec_re).astype(jnp.bfloat16)
        lagged = dot(cross_ref[rows * first : rows * (first + per_part), :], lag_ref[...])
        for source in range(first, first + per_part):
            block, slot = divmod(source, slots)
            keep = 1.0 - jnp.where(own == base + block, 1.0, 0.0) * picks_ref[slot]
            at = source - first
            kept = lagged[rows * at : rows * (at + 1)] * jnp.concatenate(
                [keep] * (LAGS // LANES), axis=1
            )
            out_ref[source] = kept.astype(jnp.bfloat16)
        span = pl.ds(first, per_part)
        copies.append(pltpu.make_async_copy(out_ref.at[span], out_hbm.at[span], sems.at[part]))
        copies[-1].start()
    for copy in copies:
        copy.wait()


HBM = pl.BlockSpec(memory_space=pltpu.HBM)
VMEM = pl.BlockSpec(memory_space=pltpu.VMEM)
PARAMS = pltpu.CompilerParams(vmem_limit_bytes=VMEM_LIMIT)


def in_hbm(*arrays):
    return [pltpu.with_memory_space_constraint(array, pltpu.HBM) for array in arrays]


def shaped(*shape, dtype=jnp.float32):
    return jax.ShapeDtypeStruct(shape, dtype)


def local(raw_records, fir_taps, alive_mask, source_index):
    src_count = lax.axis_size("src")
    blk_count = lax.axis_size("blk")
    rows, raw_count = raw_records.shape
    slots = source_index.shape[1]
    group = blk_count // src_count
    out_count = raw_count // DEC
    width = -(-out_count // LANES) * LANES + LANES
    chunks = raw_count // CHUNK
    paired = src_count == 2 and 2 * out_count == S
    bf16 = jnp.bfloat16
    forward_hi, forward_lo = split_table(forward_table())
    alive_row = alive_mask.reshape(1, rows)

    with jax.named_scope("decimate"):
        device_count = blk_count * src_count
        main = slots * (width - LANES)
        decimated, pieces = pl.pallas_call(
            lambda *refs: decimate_kernel(paired, *refs),
            out_shape=(
                shaped(rows * (S // 2 // LANES) + SUBLANES, LANES)
                if paired
                else shaped(rows, width),
                shaped(device_count, 1, main + LANES),
            ),
            in_specs=[HBM] * 4,
            out_specs=(VMEM, HBM),
            scratch_shapes=[
                pltpu.VMEM((rows * chunks, CHUNK), jnp.float32),
                pltpu.VMEM((1, TAPS), jnp.float32),
                pltpu.SMEM((1, rows), jnp.int32),
                pltpu.SMEM((1, slots), jnp.int32),
                pltpu.VMEM((SUBLANES * slots, CHUNK), jnp.float32),
                pltpu.VMEM((device_count, 1, main + LANES), jnp.float32),
                pltpu.SemaphoreType.DMA((chunks + 3,)),
            ],
            compiler_params=PARAMS,
        )(*in_hbm(raw_records, fir_taps.reshape(1, TAPS), alive_row, source_index))

    def whole(shards):
        rims = jnp.pad(shards[1:, :, width - EDGE :], ((0, 1), (0, 0), (out_count - EDGE, 0)))
        series = shards[:, :, :out_count] + rims
        return series.transpose(1, 0, 2).reshape(shards.shape[1], S)

    with jax.named_scope("gather_sources"):
        gathered = lax.all_to_all(
            pieces,
            ("blk", "src"),
            split_axis=0,
            concat_axis=0,
            tiled=True,
            axis_index_groups=[list(reversed(range(device_count)))],
        )
        if not paired:
            gathered = gathered[::-1]
            shards = gathered.reshape(blk_count, src_count, main + LANES)
            shards = shards.transpose(1, 0, 2)
            rims = [shards[:, :, main + LANES - EDGE * (slot + 1) :] for slot in range(slots)]
            rims = jnp.stack([rim[:, :, :EDGE] for rim in rims], axis=2)
            rims = jnp.pad(rims, ((0, 0), (0, 0), (0, 0), (LANES - EDGE, 0)))
            series = shards[:, :, :main].reshape(src_count, blk_count, slots, width - LANES)
            series = jnp.concatenate([series, rims], axis=3)
            series = whole(series.reshape(src_count, blk_count * slots, width))
            series = series.reshape(blk_count, slots, 2, S // 2).transpose(0, 2, 1, 3)
            series = series.reshape(blk_count * 2, 1, slots * S // 2)
            gathered = jnp.pad(series, ((0, 0), (0, 0), (0, LANES)))[::-1]

    with jax.named_scope("prepare"):
        out_shape = (
            shaped(S // 2, NFFT, dtype=bf16),
            shaped(S // 2, NFFT, dtype=bf16),
            shaped(3 * LANES, LANES, dtype=bf16),
            shaped(NFFT, LAGS, dtype=bf16),
            shaped(rows, LANES),
            shaped(slots, rows, LANES),
        )
        table_hi, table_lo, band, lag, alive, picks = pl.pallas_call(
            prepare_kernel,
            out_shape=out_shape,
            in_specs=[VMEM] + [HBM] * 6,
            out_specs=(VMEM,) * len(out_shape),
            scratch_shapes=[
                pltpu.VMEM((1, rows), jnp.int32),
                pltpu.VMEM((1, slots), jnp.int32),
                pltpu.SemaphoreType.DMA((6,)),
            ],
            compiler_params=PARAMS,
            cost_estimate=pl.CostEstimate(
                flops=0, bytes_accessed=4 * S * NFFT, transcendentals=0
            ),
        )(
            decimated,
            *in_hbm(
                alive_row,
                source_index,
                jnp.asarray(forward_hi),
                jnp.asarray(forward_lo),
                jnp.asarray(band_table()),
                jnp.asarray(lag_table()),
            ),
        )

    with jax.named_scope("regroup"):
        if paired:
            series = [decimated]
            other = [lax.ppermute(decimated, "src", [(0, 1), (1, 0)])]
        else:
            series = [whole(lax.all_gather(decimated, "src", axis=0))]
            other = []

    with jax.named_scope("spectra"):
        operands = series + [table_hi, table_lo, band, alive] + other
        spectra = pl.pallas_call(
            spectra_kernel,
            out_shape=shaped(rows, NFFT),
            in_specs=[VMEM] * len(operands),
            out_specs=VMEM,
            compiler_params=PARAMS,
        )(*operands)

    with jax.named_scope("correlate"):
        total = group * slots
        return pl.pallas_call(
            lambda *refs: correlate_kernel(slots, *refs),
            out_shape=shaped(total, rows, LAGS, dtype=bf16),
            in_specs=[VMEM] * 7,
            out_specs=HBM,
            scratch_shapes=[
                pltpu.VMEM((total, S), jnp.float32),
                pltpu.VMEM((total, LANES), jnp.float32),
                pltpu.VMEM((total, NFFT), jnp.float32),
                pltpu.VMEM((total * rows, NFFT), bf16),
                pltpu.VMEM((total, rows, LAGS), bf16),
                pltpu.SemaphoreType.DMA((PARTS,)),
            ],
            compiler_params=PARAMS,
        )(spectra, gathered, picks, table_hi, table_lo, band, lag)


def solution(mesh):
    in_specs = (P("blk", "src"), P(), P("blk"), P("blk", None))
    out_specs = P("src", "blk", None)
    return jax.shard_map(local, mesh=mesh, in_specs=in_specs, out_specs=out_specs, check_vma=False)
```

```python
import math

import jax
import jax.numpy as jnp
import numpy as np
from jax import lax
from jax.experimental import pallas as pl
from jax.experimental.pallas import tpu as pltpu
from jax.sharding import PartitionSpec as P

S = 512
NFFT = 1024
BINS = NFFT // 2
LAGS = 512
TAPS = 64
DEC = 20
HALF = 64
LANES = 128
SUBLANES = 8
PARTS = 2
EDGE = (TAPS - 1) // DEC
CHUNK = 640
CHUNK_OUT = CHUNK // DEC
VMEM_LIMIT = 48 * 1024 * 1024


def forward_table():
    phases = 2.0 * math.pi / NFFT * (np.outer(np.arange(S // 2), np.arange(BINS)) % NFFT)
    return np.concatenate([np.cos(phases), -np.sin(phases)], axis=1).astype(np.float32)


def split_table(table):
    high = table.astype(jnp.bfloat16)
    low = (table - high.astype(np.float32)).astype(jnp.bfloat16)
    return high, low


def band_table():
    bins = np.arange(3 * LANES)[:, None] - LANES
    return (np.abs(bins - np.arange(LANES)[None, :]) <= HALF).astype(jnp.bfloat16)


def lag_table():
    bins = np.arange(BINS)[:, None]
    shift = np.arange(LAGS)[None, :] - LAGS // 2
    phases = 2.0 * math.pi / NFFT * (bins * shift % NFFT)
    weight = np.where(bins == 0, 0.5, 1.0) / math.sqrt(BINS)
    table = np.concatenate([weight * np.cos(phases), -weight * np.sin(phases)], axis=0)
    return table.astype(np.float32).astype(jnp.bfloat16)


def split(value):
    high = value.astype(jnp.bfloat16)
    return high, (value - high.astype(jnp.float32)).astype(jnp.bfloat16)


def dot(a, b):
    return jnp.dot(a, b, preferred_element_type=jnp.float32)


def column(row):
    count = row.shape[1]
    at = [lax.broadcasted_iota(jnp.int32, (count, count), axis) for axis in range(2)]
    rows = jnp.broadcast_to(row, (count, count))
    return jnp.sum(jnp.where(at[0] == at[1], rows, 0.0), axis=1, keepdims=True)


def start_copies(pairs, sems):
    copies = [
        pltpu.make_async_copy(source, target, sems.at[at])
        for at, (source, target) in enumerate(pairs)
    ]
    for copy in copies:
        copy.start()
    return copies


def decimate_kernel(
    paired, raw_hbm, taps_hbm, alive_hbm, picks_hbm, out_ref, pieces_ref,
    raw_ref, taps_ref, alive_ref, picks_ref, source_ref, sems,
):
    rows = raw_hbm.shape[0]
    chunks = raw_hbm.shape[1] // CHUNK
    slots = picks_ref.shape[1]
    per_tile = LANES // CHUNK_OUT
    tiles = -(-chunks // per_tile)
    pairs = [(taps_hbm, taps_ref), (picks_hbm, picks_ref), (alive_hbm, alive_ref)]
    for at in range(0, rows, SUBLANES):
        span = slice(at, at + SUBLANES)
        pairs.append((raw_hbm.at[span], raw_ref.at[span]))
    copies = start_copies(pairs, sems)
    source_ref[...] = jnp.zeros_like(source_ref)
    copies[0].wait()
    taps = jnp.broadcast_to(taps_ref[...], (SUBLANES, TAPS))
    eight = jnp.concatenate([taps, jnp.zeros((SUBLANES, CHUNK - TAPS), jnp.float32)], axis=1)
    for _ in range(2):
        eight = pltpu.roll(eight, 0, 1, stride=DEC // 2, stride_axis=0)
    wrapped = jnp.concatenate(
        [eight]
        + [pltpu.roll(eight, DEC * at, 1) for at in range(SUBLANES, CHUNK_OUT, SUBLANES)],
        axis=0,
    )
    lane = lax.broadcasted_iota(jnp.int32, (CHUNK_OUT, CHUNK), 1)
    row = lax.broadcasted_iota(jnp.int32, (CHUNK_OUT, CHUNK), 0)
    main = jnp.where(lane >= DEC * row, wrapped, 0.0)
    rim = wrapped - main
    gap = jnp.zeros((LANES - 2 * CHUNK_OUT, CHUNK), jnp.float32)
    weights_hi, weights_lo = split(jnp.concatenate([main, gap, rim], axis=0).T)
    weights = jnp.concatenate([weights_hi, weights_lo], axis=1)

    def filtered(stacked):
        high, low = split(stacked)
        both = dot(high, weights)
        return both[:, :LANES] + both[:, LANES:] + dot(low, weights_hi)

    for copy in copies[1:]:
        copy.wait()
    for slot in range(slots):
        pick = picks_ref[0, slot]
        alive = alive_ref[0, pick].astype(jnp.float32)
        for j in range(chunks):
            at = SUBLANES * slot + j
            span = slice(CHUNK * j, CHUNK * (j + 1))
            source_ref[at : at + 1, :] = raw_ref[pl.ds(pick, 1), span] * alive
    high, low = split(source_ref[...])
    count = slots * SUBLANES
    both = dot(jnp.concatenate([high, low], axis=0), weights)
    sources = both[:count, :LANES] + both[:count, LANES:] + both[count:, :LANES]
    lane = lax.broadcasted_iota(jnp.int32, (SUBLANES, LANES), 1)
    row = lax.broadcasted_iota(jnp.int32, (SUBLANES, LANES), 0)
    piece = []
    rims = jnp.zeros((1, LANES), jnp.float32)
    for slot in range(slots):
        source = sources[SUBLANES * slot : SUBLANES * (slot + 1)]
        main = jnp.where(lane < LANES // 2, source, 0.0)
        rim = source - main
        late = rim[:1]
        for _ in range(2):
            main = pltpu.roll(main, 0, 1, stride=CHUNK_OUT // 2, stride_axis=0)
            rim = pltpu.roll(rim, 0, 1, stride=CHUNK_OUT // 2, stride_axis=0)
        for tile in range(tiles):
            first = per_tile * tile
            inside = (row >= first) & (row < first + per_tile)
            before = (row > first) & (row <= first + per_tile)
            piece.append(
                jnp.sum(
                    jnp.where(inside, main, 0.0) + jnp.where(before, rim, 0.0),
                    axis=0,
                    keepdims=True,
                )
            )
        rims = rims + pltpu.roll(late, LANES - EDGE * slot if slot else 0, 1)
    piece.append(rims)
    for device in range(pieces_ref.shape[0]):
        for at, value in enumerate(piece):
            pieces_ref[device, :, LANES * at : LANES * (at + 1)] = value
    result = filtered(
        jnp.concatenate(
            [raw_ref[:, CHUNK * j : CHUNK * (j + 1)] for j in range(chunks)], axis=0
        )
    )
    part = [result[rows * j : rows * (j + 1)] for j in range(chunks)]
    is_main = lax.broadcasted_iota(jnp.int32, (rows, LANES), 1) < LANES // 2
    values = []
    for first in range(0, chunks, per_tile):
        total = jnp.where(is_main, part[first], 0.0)
        for step in range(1, min(per_tile, chunks - first)):
            total = total + pltpu.roll(part[first + step], CHUNK_OUT * step, 1)
        if first + per_tile < chunks:
            total = total + jnp.where(is_main, 0.0, part[first + per_tile])
        values.append(total)
    rim = jnp.where(is_main, 0.0, part[0])
    if paired:
        packed = rim[:SUBLANES]
        for at in range(1, rows // SUBLANES):
            group = rim[SUBLANES * at : SUBLANES * (at + 1)]
            packed = packed + pltpu.roll(group, LANES - EDGE * at, 1)
        for at, value in enumerate(values):
            out_ref[rows * at : rows * (at + 1), :] = value
        out_ref[rows * tiles :, :] = packed
    else:
        for at, value in enumerate(values + [rim]):
            out_ref[:, LANES * at : LANES * (at + 1)] = value


def unpack(packed, rows):
    tiles = [packed[at : at + rows] for at in range(0, packed.shape[0] - SUBLANES, rows)]
    rims = packed[packed.shape[0] - SUBLANES :]
    rim = jnp.concatenate(
        [rims]
        + [pltpu.roll(rims, EDGE * at, 1) for at in range(1, rows // SUBLANES)],
        axis=0,
    )
    lane = lax.broadcasted_iota(jnp.int32, rim.shape, 1)
    return tiles + [jnp.where(lane >= LANES - EDGE, rim, 0.0)]


def transform(early, late, table_hi, table_lo):
    rows = early.shape[0]
    high, low = split(jnp.concatenate([early, late], axis=0))
    first = dot(jnp.concatenate([high, low], axis=0), table_hi)
    both = first[: 2 * rows] + first[2 * rows :] + dot(high, table_lo)
    quarter = lax.broadcasted_iota(jnp.int32, (1, BINS), 1) & 3
    cosine = jnp.where(quarter == 0, 1.0, 0.0) - jnp.where(quarter == 2, 1.0, 0.0)
    sine = jnp.where(quarter == 1, 1.0, 0.0) - jnp.where(quarter == 3, 1.0, 0.0)
    early_re, early_im = both[:rows, :BINS], both[:rows, BINS:]
    late_re, late_im = both[rows:, :BINS], both[rows:, BINS:]
    return (
        early_re + cosine * late_re + sine * late_im,
        early_im + cosine * late_im - sine * late_re,
    )


def whitening(real_part, imag_part, band):
    rows = real_part.shape[0]
    tiles = BINS // LANES
    stacked = []
    for part in split(real_part * real_part + imag_part * imag_part):
        zero = jnp.zeros((rows, LANES), part.dtype)
        wide = jnp.concatenate([zero, part, zero], axis=1)
        stacked += [wide[:, LANES * tile : LANES * (tile + 3)] for tile in range(tiles)]
    banded = dot(jnp.concatenate(stacked, axis=0), band)
    step = rows * tiles
    summed = banded[:step] + banded[step:]
    total = jnp.concatenate(
        [summed[rows * tile : rows * (tile + 1)] for tile in range(tiles)], axis=1
    )
    bins = lax.broadcasted_iota(jnp.int32, (1, BINS), 1)
    count = jnp.minimum(bins + HALF, BINS - 1) - jnp.maximum(bins - HALF, 0) + 1
    return lax.rsqrt(total * (1.0 / count.astype(jnp.float32)) + 1e-06)


def prepare_kernel(
    _, alive_hbm, picks_hbm, fwd_hi_hbm, fwd_lo_hbm, band_hbm, lag_hbm,
    hi_ref, lo_ref, band_ref, lag_ref, alive_out, picks_out, alive_ref, picks_ref, sems,
):
    copies = start_copies(
        [
            (alive_hbm, alive_ref),
            (picks_hbm, picks_ref),
            (fwd_hi_hbm, hi_ref),
            (fwd_lo_hbm, lo_ref),
            (band_hbm, band_ref),
            (lag_hbm, lag_ref),
        ],
        sems,
    )
    for copy in copies[:2]:
        copy.wait()
    rows = alive_out.shape[0]
    alive_out[...] = jnp.broadcast_to(
        column(alive_ref[...].astype(jnp.float32)), (rows, LANES)
    )
    channel = lax.broadcasted_iota(jnp.int32, (rows, LANES), 0)
    for slot in range(picks_ref.shape[1]):
        pick = jnp.broadcast_to(picks_ref[:, slot : slot + 1], (rows, LANES))
        picks_out[slot] = jnp.where(channel == pick, 1.0, 0.0)
    for copy in copies[2:]:
        copy.wait()


def spectra_kernel(series_ref, hi_ref, lo_ref, band_ref, alive_ref, *refs):
    spectra_ref = refs[-1]
    rows = alive_ref.shape[0]
    half = S // 2
    if len(refs) > 1:
        mine, other = [unpack(ref[...], rows) for ref in (series_ref, refs[0])]
        first = lax.axis_index("src") == 0
        early = [jnp.where(first, a, b) for a, b in zip(mine, other)]
        late = [jnp.where(first, b, a) for a, b in zip(mine, other)]
        early[-2] = early[-2] + late[-1]
        early, late = [jnp.concatenate(tiles[:-1], axis=1) for tiles in (early, late)]
    else:
        early, late = series_ref[:, :half], series_ref[:, half:]
    real_part, imag_part = transform(early, late, hi_ref[...], lo_ref[...])
    factor = alive_ref[:, :1] * whitening(real_part, imag_part, band_ref[...])
    spectra_ref[:, :BINS] = real_part * factor
    spectra_ref[:, BINS:] = imag_part * factor


def correlate_kernel(
    slots, spectra_ref, pieces_ref, picks_ref, hi_ref, lo_ref, band_ref, lag_ref, out_hbm,
    series_ref, rims_ref, source_ref, cross_ref, out_ref, sems,
):
    rows = spectra_ref.shape[0]
    group = out_ref.shape[0] // slots
    half = BINS // LANES
    own = lax.axis_index("blk")
    base = lax.axis_index("src") * group
    tiles = S // 2 // LANES

    for slot in range(slots):
        for block in range(group):
            row = slice(slot * group + block, slot * group + block + 1)
            at = pieces_ref.shape[0] - 1 - 2 * (base + block)
            for tile in range(tiles):
                span = slice(LANES * (slot * tiles + tile), LANES * (slot * tiles + tile + 1))
                early = slice(LANES * tile, LANES * (tile + 1))
                late = slice(S // 2 + LANES * tile, S // 2 + LANES * (tile + 1))
                series_ref[row, early] = pieces_ref[at, :, span]
                series_ref[row, late] = pieces_ref[at - 1, :, span]
            rims_ref[row, :] = pieces_ref[at - 1, :, LANES * slots * tiles :]
    rims = jnp.concatenate(
        [
            pltpu.roll(rims_ref[slot * group : (slot + 1) * group, :], EDGE * slot, 1)
            for slot in range(slots)
        ],
        axis=0,
    )
    lane = lax.broadcasted_iota(jnp.int32, rims.shape, 1)
    seam = slice(S // 2 - LANES, S // 2)
    series_ref[:, seam] = series_ref[:, seam] + jnp.where(lane >= LANES - EDGE, rims, 0.0)
    early, late = series_ref[:, : S // 2], series_ref[:, S // 2 :]
    real_part, imag_part = transform(early, late, hi_ref[...], lo_ref[...])
    factor = whitening(real_part, imag_part, band_ref[...])
    source_ref[:, :BINS] = real_part * factor
    source_ref[:, BINS:] = imag_part * factor
    per_part = max(1, (group * slots) // PARTS)
    copies = []
    for part in range(group * slots // per_part):
        first = part * per_part
        for tile in range(half):
            re = slice(LANES * tile, LANES * (tile + 1))
            im = slice(BINS + LANES * tile, BINS + LANES * (tile + 1))
            rec_re, rec_im = spectra_ref[:, re], spectra_ref[:, im]
            for source in range(first, first + per_part):
                block, slot = divmod(source, slots)
                at = slot * group + block
                src_re, src_im = source_ref[at : at + 1, re], source_ref[at : at + 1, im]
                where = slice(rows * source, rows * (source + 1))
                cross_ref[where, re] = (src_re * rec_re + src_im * rec_im).astype(jnp.bfloat16)
                cross_ref[where, im] = (src_re * rec_im - src_im * rec_re).astype(jnp.bfloat16)
        lagged = dot(cross_ref[rows * first : rows * (first + per_part), :], lag_ref[...])
        for source in range(first, first + per_part):
            block, slot = divmod(source, slots)
            keep = 1.0 - jnp.where(own == base + block, 1.0, 0.0) * picks_ref[slot]
            at = source - first
            kept = lagged[rows * at : rows * (at + 1)] * jnp.concatenate(
                [keep] * (LAGS // LANES), axis=1
            )
            out_ref[source] = kept.astype(jnp.bfloat16)
        span = pl.ds(first, per_part)
        copies.append(pltpu.make_async_copy(out_ref.at[span], out_hbm.at[span], sems.at[part]))
        copies[-1].start()
    for copy in copies:
        copy.wait()


HBM = pl.BlockSpec(memory_space=pltpu.HBM)
VMEM = pl.BlockSpec(memory_space=pltpu.VMEM)
PARAMS = pltpu.CompilerParams(vmem_limit_bytes=VMEM_LIMIT)


def in_hbm(*arrays):
    return [pltpu.with_memory_space_constraint(array, pltpu.HBM) for array in arrays]


def shaped(*shape, dtype=jnp.float32):
    return jax.ShapeDtypeStruct(shape, dtype)


def local(raw_records, fir_taps, alive_mask, source_index):
    src_count = lax.axis_size("src")
    blk_count = lax.axis_size("blk")
    rows, raw_count = raw_records.shape
    slots = source_index.shape[1]
    group = blk_count // src_count
    out_count = raw_count // DEC
    width = -(-out_count // LANES) * LANES + LANES
    chunks = raw_count // CHUNK
    paired = src_count == 2 and 2 * out_count == S
    bf16 = jnp.bfloat16
    forward_hi, forward_lo = split_table(forward_table())
    alive_row = alive_mask.reshape(1, rows)

    with jax.named_scope("decimate"):
        device_count = blk_count * src_count
        main = slots * (width - LANES)
        decimated, pieces = pl.pallas_call(
            lambda *refs: decimate_kernel(paired, *refs),
            out_shape=(
                shaped(rows * (S // 2 // LANES) + SUBLANES, LANES)
                if paired
                else shaped(rows, width),
                pltpu.VMEM((device_count, 1, main + LANES), jnp.float32),
            ),
            in_specs=[HBM] * 4,
            out_specs=(VMEM, VMEM),
            scratch_shapes=[
                pltpu.VMEM((rows, raw_count), jnp.float32),
                pltpu.VMEM((1, TAPS), jnp.float32),
                pltpu.SMEM((1, rows), jnp.int32),
                pltpu.SMEM((1, slots), jnp.int32),
                pltpu.VMEM((SUBLANES * slots, CHUNK), jnp.float32),
                pltpu.SemaphoreType.DMA((rows // SUBLANES + 3,)),
            ],
            compiler_params=PARAMS,
        )(*in_hbm(raw_records, fir_taps.reshape(1, TAPS), alive_row, source_index))

    def whole(shards):
        rims = jnp.pad(shards[1:, :, width - EDGE :], ((0, 1), (0, 0), (out_count - EDGE, 0)))
        series = shards[:, :, :out_count] + rims
        return series.transpose(1, 0, 2).reshape(shards.shape[1], S)

    with jax.named_scope("gather_sources"):
        gathered = lax.all_to_all(
            pieces,
            ("blk", "src"),
            split_axis=0,
            concat_axis=0,
            tiled=True,
            axis_index_groups=[list(reversed(range(device_count)))],
        )
        if not paired:
            gathered = gathered[::-1]
            shards = gathered.reshape(blk_count, src_count, main + LANES)
            shards = shards.transpose(1, 0, 2)
            rims = [shards[:, :, main + LANES - EDGE * (slot + 1) :] for slot in range(slots)]
            rims = jnp.stack([rim[:, :, :EDGE] for rim in rims], axis=2)
            rims = jnp.pad(rims, ((0, 0), (0, 0), (0, 0), (LANES - EDGE, 0)))
            series = shards[:, :, :main].reshape(src_count, blk_count, slots, width - LANES)
            series = jnp.concatenate([series, rims], axis=3)
            series = whole(series.reshape(src_count, blk_count * slots, width))
            series = series.reshape(blk_count, slots, 2, S // 2).transpose(0, 2, 1, 3)
            series = series.reshape(blk_count * 2, 1, slots * S // 2)
            gathered = jnp.pad(series, ((0, 0), (0, 0), (0, LANES)))[::-1]

    with jax.named_scope("prepare"):
        out_shape = (
            shaped(S // 2, NFFT, dtype=bf16),
            shaped(S // 2, NFFT, dtype=bf16),
            shaped(3 * LANES, LANES, dtype=bf16),
            shaped(NFFT, LAGS, dtype=bf16),
            shaped(rows, LANES),
            shaped(slots, rows, LANES),
        )
        table_hi, table_lo, band, lag, alive, picks = pl.pallas_call(
            prepare_kernel,
            out_shape=out_shape,
            in_specs=[VMEM] + [HBM] * 6,
            out_specs=(VMEM,) * len(out_shape),
            scratch_shapes=[
                pltpu.VMEM((1, rows), jnp.int32),
                pltpu.VMEM((1, slots), jnp.int32),
                pltpu.SemaphoreType.DMA((6,)),
            ],
            compiler_params=PARAMS,
            cost_estimate=pl.CostEstimate(
                flops=0, bytes_accessed=4 * S * NFFT, transcendentals=0
            ),
        )(
            decimated,
            *in_hbm(
                alive_row,
                source_index,
                jnp.asarray(forward_hi),
                jnp.asarray(forward_lo),
                jnp.asarray(band_table()),
                jnp.asarray(lag_table()),
            ),
        )

    with jax.named_scope("regroup"):
        if paired:
            series = [decimated]
            other = [lax.ppermute(decimated, "src", [(0, 1), (1, 0)])]
        else:
            series = [whole(lax.all_gather(decimated, "src", axis=0))]
            other = []

    with jax.named_scope("spectra"):
        operands = series + [table_hi, table_lo, band, alive] + other
        spectra = pl.pallas_call(
            spectra_kernel,
            out_shape=shaped(rows, NFFT),
            in_specs=[VMEM] * len(operands),
            out_specs=VMEM,
            compiler_params=PARAMS,
        )(*operands)

    with jax.named_scope("correlate"):
        total = group * slots
        return pl.pallas_call(
            lambda *refs: correlate_kernel(slots, *refs),
            out_shape=shaped(total, rows, LAGS, dtype=bf16),
            in_specs=[VMEM] * 7,
            out_specs=HBM,
            scratch_shapes=[
                pltpu.VMEM((total, S), jnp.float32),
                pltpu.VMEM((total, LANES), jnp.float32),
                pltpu.VMEM((total, NFFT), jnp.float32),
                pltpu.VMEM((total * rows, NFFT), bf16),
                pltpu.VMEM((total, rows, LAGS), bf16),
                pltpu.SemaphoreType.DMA((PARTS,)),
            ],
            compiler_params=PARAMS,
        )(spectra, gathered, picks, table_hi, table_lo, band, lag)


def solution(mesh):
    in_specs = (P("blk", "src"), P(), P("blk"), P("blk", None))
    out_specs = P("src", "blk", None)
    return jax.shard_map(local, mesh=mesh, in_specs=in_specs, out_specs=out_specs, check_vma=False)
```

```python
import math

import jax
import jax.numpy as jnp
import numpy as np
from jax import lax
from jax.experimental import pallas as pl
from jax.experimental.pallas import tpu as pltpu
from jax.sharding import PartitionSpec as P

S = 512
NFFT = 1024
BINS = NFFT // 2
LAGS = 512
TAPS = 64
DEC = 20
HALF = 64
LANES = 128
SUBLANES = 8
PARTS = 2
EDGE = (TAPS - 1) // DEC
CHUNK = 640
CHUNK_OUT = CHUNK // DEC
VMEM_LIMIT = 48 * 1024 * 1024


def forward_table():
    phases = 2.0 * math.pi / NFFT * (np.outer(np.arange(S // 2), np.arange(BINS)) % NFFT)
    return np.concatenate([np.cos(phases), -np.sin(phases)], axis=1).astype(np.float32)


def split_table(table):
    high = table.astype(jnp.bfloat16)
    low = (table - high.astype(np.float32)).astype(jnp.bfloat16)
    return high, low


def band_table():
    bins = np.arange(3 * LANES)[:, None] - LANES
    return (np.abs(bins - np.arange(LANES)[None, :]) <= HALF).astype(jnp.bfloat16)


def lag_table():
    bins = np.arange(BINS)[:, None]
    shift = np.arange(LAGS)[None, :] - LAGS // 2
    phases = 2.0 * math.pi / NFFT * (bins * shift % NFFT)
    weight = np.where(bins == 0, 0.5, 1.0) / math.sqrt(BINS)
    table = np.concatenate([weight * np.cos(phases), -weight * np.sin(phases)], axis=0)
    return table.astype(np.float32).astype(jnp.bfloat16)


def split(value):
    high = value.astype(jnp.bfloat16)
    return high, (value - high.astype(jnp.float32)).astype(jnp.bfloat16)


def dot(a, b):
    return jnp.dot(a, b, preferred_element_type=jnp.float32)


def column(row):
    count = row.shape[1]
    at = [lax.broadcasted_iota(jnp.int32, (count, count), axis) for axis in range(2)]
    rows = jnp.broadcast_to(row, (count, count))
    return jnp.sum(jnp.where(at[0] == at[1], rows, 0.0), axis=1, keepdims=True)


def start_copies(pairs, sems):
    copies = [
        pltpu.make_async_copy(source, target, sems.at[at])
        for at, (source, target) in enumerate(pairs)
    ]
    for copy in copies:
        copy.start()
    return copies


def decimate_kernel(
    paired, raw_hbm, taps_hbm, alive_hbm, picks_hbm, out_ref, pieces_hbm,
    raw_ref, taps_ref, alive_ref, picks_ref, source_ref, pieces_ref, sems,
):
    rows = raw_hbm.shape[0]
    chunks = raw_hbm.shape[1] // CHUNK
    slots = picks_ref.shape[1]
    per_tile = LANES // CHUNK_OUT
    tiles = -(-chunks // per_tile)
    pairs = [(taps_hbm, taps_ref), (picks_hbm, picks_ref), (alive_hbm, alive_ref)]
    for at in range(0, rows, SUBLANES):
        span = slice(at, at + SUBLANES)
        pairs.append((raw_hbm.at[span], raw_ref.at[span]))
    copies = start_copies(pairs, sems)
    source_ref[...] = jnp.zeros_like(source_ref)
    copies[0].wait()
    taps = jnp.broadcast_to(taps_ref[...], (SUBLANES, TAPS))
    eight = jnp.concatenate([taps, jnp.zeros((SUBLANES, CHUNK - TAPS), jnp.float32)], axis=1)
    for _ in range(2):
        eight = pltpu.roll(eight, 0, 1, stride=DEC // 2, stride_axis=0)
    wrapped = jnp.concatenate(
        [eight]
        + [pltpu.roll(eight, DEC * at, 1) for at in range(SUBLANES, CHUNK_OUT, SUBLANES)],
        axis=0,
    )
    lane = lax.broadcasted_iota(jnp.int32, (CHUNK_OUT, CHUNK), 1)
    row = lax.broadcasted_iota(jnp.int32, (CHUNK_OUT, CHUNK), 0)
    main = jnp.where(lane >= DEC * row, wrapped, 0.0)
    rim = wrapped - main
    gap = jnp.zeros((LANES - 2 * CHUNK_OUT, CHUNK), jnp.float32)
    weights_hi, weights_lo = split(jnp.concatenate([main, gap, rim], axis=0).T)
    weights = jnp.concatenate([weights_hi, weights_lo], axis=1)

    def filtered(stacked):
        high, low = split(stacked)
        both = dot(high, weights)
        return both[:, :LANES] + both[:, LANES:] + dot(low, weights_hi)

    for copy in copies[1:]:
        copy.wait()
    for slot in range(slots):
        pick = picks_ref[0, slot]
        alive = alive_ref[0, pick].astype(jnp.float32)
        for j in range(chunks):
            at = SUBLANES * slot + j
            span = slice(CHUNK * j, CHUNK * (j + 1))
            source_ref[at : at + 1, :] = raw_ref[pl.ds(pick, 1), span] * alive
    high, low = split(source_ref[...])
    count = slots * SUBLANES
    both = dot(jnp.concatenate([high, low], axis=0), weights)
    sources = both[:count, :LANES] + both[:count, LANES:] + both[count:, :LANES]
    lane = lax.broadcasted_iota(jnp.int32, (SUBLANES, LANES), 1)
    row = lax.broadcasted_iota(jnp.int32, (SUBLANES, LANES), 0)
    piece = []
    rims = jnp.zeros((1, LANES), jnp.float32)
    for slot in range(slots):
        source = sources[SUBLANES * slot : SUBLANES * (slot + 1)]
        main = jnp.where(lane < LANES // 2, source, 0.0)
        rim = source - main
        late = rim[:1]
        for _ in range(2):
            main = pltpu.roll(main, 0, 1, stride=CHUNK_OUT // 2, stride_axis=0)
            rim = pltpu.roll(rim, 0, 1, stride=CHUNK_OUT // 2, stride_axis=0)
        for tile in range(tiles):
            first = per_tile * tile
            inside = (row >= first) & (row < first + per_tile)
            before = (row > first) & (row <= first + per_tile)
            piece.append(
                jnp.sum(
                    jnp.where(inside, main, 0.0) + jnp.where(before, rim, 0.0),
                    axis=0,
                    keepdims=True,
                )
            )
        rims = rims + pltpu.roll(late, LANES - EDGE * slot if slot else 0, 1)
    piece.append(rims)
    for device in range(pieces_ref.shape[0]):
        for at, value in enumerate(piece):
            pieces_ref[device, :, LANES * at : LANES * (at + 1)] = value
    sending = pltpu.make_async_copy(pieces_ref, pieces_hbm, sems.at[0])
    sending.start()

    result = filtered(
        jnp.concatenate(
            [raw_ref[:, CHUNK * j : CHUNK * (j + 1)] for j in range(chunks)], axis=0
        )
    )
    part = [result[rows * j : rows * (j + 1)] for j in range(chunks)]
    is_main = lax.broadcasted_iota(jnp.int32, (rows, LANES), 1) < LANES // 2
    values = []
    for first in range(0, chunks, per_tile):
        total = jnp.where(is_main, part[first], 0.0)
        for step in range(1, min(per_tile, chunks - first)):
            total = total + pltpu.roll(part[first + step], CHUNK_OUT * step, 1)
        if first + per_tile < chunks:
            total = total + jnp.where(is_main, 0.0, part[first + per_tile])
        values.append(total)
    rim = jnp.where(is_main, 0.0, part[0])
    if paired:
        packed = rim[:SUBLANES]
        for at in range(1, rows // SUBLANES):
            group = rim[SUBLANES * at : SUBLANES * (at + 1)]
            packed = packed + pltpu.roll(group, LANES - EDGE * at, 1)
        for at, value in enumerate(values):
            out_ref[rows * at : rows * (at + 1), :] = value
        out_ref[rows * tiles :, :] = packed
    else:
        for at, value in enumerate(values + [rim]):
            out_ref[:, LANES * at : LANES * (at + 1)] = value
    sending.wait()


def unpack(packed, rows):
    tiles = [packed[at : at + rows] for at in range(0, packed.shape[0] - SUBLANES, rows)]
    rims = packed[packed.shape[0] - SUBLANES :]
    rim = jnp.concatenate(
        [rims]
        + [pltpu.roll(rims, EDGE * at, 1) for at in range(1, rows // SUBLANES)],
        axis=0,
    )
    lane = lax.broadcasted_iota(jnp.int32, rim.shape, 1)
    return tiles + [jnp.where(lane >= LANES - EDGE, rim, 0.0)]


def transform(early, late, table_hi, table_lo):
    rows = early.shape[0]
    high, low = split(jnp.concatenate([early, late], axis=0))
    first = dot(jnp.concatenate([high, low], axis=0), table_hi)
    both = first[: 2 * rows] + first[2 * rows :] + dot(high, table_lo)
    quarter = lax.broadcasted_iota(jnp.int32, (1, BINS), 1) & 3
    cosine = jnp.where(quarter == 0, 1.0, 0.0) - jnp.where(quarter == 2, 1.0, 0.0)
    sine = jnp.where(quarter == 1, 1.0, 0.0) - jnp.where(quarter == 3, 1.0, 0.0)
    early_re, early_im = both[:rows, :BINS], both[:rows, BINS:]
    late_re, late_im = both[rows:, :BINS], both[rows:, BINS:]
    return (
        early_re + cosine * late_re + sine * late_im,
        early_im + cosine * late_im - sine * late_re,
    )


def whitening(real_part, imag_part, band):
    rows = real_part.shape[0]
    tiles = BINS // LANES
    stacked = []
    for part in split(real_part * real_part + imag_part * imag_part):
        zero = jnp.zeros((rows, LANES), part.dtype)
        wide = jnp.concatenate([zero, part, zero], axis=1)
        stacked += [wide[:, LANES * tile : LANES * (tile + 3)] for tile in range(tiles)]
    banded = dot(jnp.concatenate(stacked, axis=0), band)
    step = rows * tiles
    summed = banded[:step] + banded[step:]
    total = jnp.concatenate(
        [summed[rows * tile : rows * (tile + 1)] for tile in range(tiles)], axis=1
    )
    bins = lax.broadcasted_iota(jnp.int32, (1, BINS), 1)
    count = jnp.minimum(bins + HALF, BINS - 1) - jnp.maximum(bins - HALF, 0) + 1
    return lax.rsqrt(total * (1.0 / count.astype(jnp.float32)) + 1e-06)


def prepare_kernel(
    _, alive_hbm, picks_hbm, fwd_hi_hbm, fwd_lo_hbm, band_hbm, lag_hbm,
    hi_ref, lo_ref, band_ref, lag_ref, alive_out, picks_out, alive_ref, picks_ref, sems,
):
    copies = start_copies(
        [
            (alive_hbm, alive_ref),
            (picks_hbm, picks_ref),
            (fwd_hi_hbm, hi_ref),
            (fwd_lo_hbm, lo_ref),
            (band_hbm, band_ref),
            (lag_hbm, lag_ref),
        ],
        sems,
    )
    for copy in copies[:2]:
        copy.wait()
    rows = alive_out.shape[0]
    alive_out[...] = jnp.broadcast_to(
        column(alive_ref[...].astype(jnp.float32)), (rows, LANES)
    )
    channel = lax.broadcasted_iota(jnp.int32, (rows, LANES), 0)
    for slot in range(picks_ref.shape[1]):
        pick = jnp.broadcast_to(picks_ref[:, slot : slot + 1], (rows, LANES))
        picks_out[slot] = jnp.where(channel == pick, 1.0, 0.0)
    for copy in copies[2:]:
        copy.wait()


def spectra_kernel(series_ref, hi_ref, lo_ref, band_ref, alive_ref, *refs):
    spectra_ref = refs[-1]
    rows = alive_ref.shape[0]
    half = S // 2
    if len(refs) > 1:
        mine, other = [unpack(ref[...], rows) for ref in (series_ref, refs[0])]
        first = lax.axis_index("src") == 0
        early = [jnp.where(first, a, b) for a, b in zip(mine, other)]
        late = [jnp.where(first, b, a) for a, b in zip(mine, other)]
        early[-2] = early[-2] + late[-1]
        early, late = [jnp.concatenate(tiles[:-1], axis=1) for tiles in (early, late)]
    else:
        early, late = series_ref[:, :half], series_ref[:, half:]
    real_part, imag_part = transform(early, late, hi_ref[...], lo_ref[...])
    factor = alive_ref[:, :1] * whitening(real_part, imag_part, band_ref[...])
    spectra_ref[:, :BINS] = real_part * factor
    spectra_ref[:, BINS:] = imag_part * factor


def correlate_kernel(
    slots, spectra_ref, pieces_ref, picks_ref, hi_ref, lo_ref, band_ref, lag_ref, out_hbm,
    source_ref, cross_ref, out_ref, sems,
):
    rows = spectra_ref.shape[0]
    group = out_ref.shape[0] // slots
    half = BINS // LANES
    own = lax.axis_index("blk")
    base = lax.axis_index("src") * group
    tiles = S // 2 // LANES
    stride = slots * tiles + 1

    def entry(half_at, row):
        last = pieces_ref.shape[0] // stride - 1 - 2 * (base + group - 1) - half_at
        return pieces_ref[pl.ds(last * stride + row, group, stride=2 * stride), :]

    def halves(half_at):
        return [
            jnp.concatenate([entry(half_at, slot * tiles + tile) for slot in range(slots)], axis=0)
            for tile in range(tiles)
        ]

    early, late = halves(0), halves(1)
    rims = entry(1, slots * tiles)
    rims = jnp.concatenate(
        [rims] + [pltpu.roll(rims, EDGE * slot, 1) for slot in range(1, slots)], axis=0
    )
    lane = lax.broadcasted_iota(jnp.int32, rims.shape, 1)
    early[-1] = early[-1] + jnp.where(lane >= LANES - EDGE, rims, 0.0)
    early, late = [jnp.concatenate(columns, axis=1) for columns in (early, late)]
    real_part, imag_part = transform(early, late, hi_ref[...], lo_ref[...])
    factor = whitening(real_part, imag_part, band_ref[...])
    source_ref[:, :BINS] = real_part * factor
    source_ref[:, BINS:] = imag_part * factor
    per_part = max(1, (group * slots) // PARTS)
    copies = []
    for part in range(group * slots // per_part):
        first = part * per_part
        for tile in range(half):
            re = slice(LANES * tile, LANES * (tile + 1))
            im = slice(BINS + LANES * tile, BINS + LANES * (tile + 1))
            rec_re, rec_im = spectra_ref[:, re], spectra_ref[:, im]
            for source in range(first, first + per_part):
                block, slot = divmod(source, slots)
                at = slot * group + group - 1 - block
                src_re, src_im = source_ref[at : at + 1, re], source_ref[at : at + 1, im]
                where = slice(rows * source, rows * (source + 1))
                cross_ref[where, re] = (src_re * rec_re + src_im * rec_im).astype(jnp.bfloat16)
                cross_ref[where, im] = (src_re * rec_im - src_im * rec_re).astype(jnp.bfloat16)
        lagged = dot(cross_ref[rows * first : rows * (first + per_part), :], lag_ref[...])
        for source in range(first, first + per_part):
            block, slot = divmod(source, slots)
            keep = 1.0 - jnp.where(own == base + block, 1.0, 0.0) * picks_ref[slot]
            at = source - first
            kept = lagged[rows * at : rows * (at + 1)] * jnp.concatenate(
                [keep] * (LAGS // LANES), axis=1
            )
            out_ref[source] = kept.astype(jnp.bfloat16)
        span = pl.ds(first, per_part)
        copies.append(pltpu.make_async_copy(out_ref.at[span], out_hbm.at[span], sems.at[part]))
        copies[-1].start()
    for copy in copies:
        copy.wait()


HBM = pl.BlockSpec(memory_space=pltpu.HBM)
VMEM = pl.BlockSpec(memory_space=pltpu.VMEM)
PARAMS = pltpu.CompilerParams(vmem_limit_bytes=VMEM_LIMIT)


def in_hbm(*arrays):
    return [pltpu.with_memory_space_constraint(array, pltpu.HBM) for array in arrays]


def shaped(*shape, dtype=jnp.float32):
    return jax.ShapeDtypeStruct(shape, dtype)


def local(raw_records, fir_taps, alive_mask, source_index):
    src_count = lax.axis_size("src")
    blk_count = lax.axis_size("blk")
    rows, raw_count = raw_records.shape
    slots = source_index.shape[1]
    group = blk_count // src_count
    out_count = raw_count // DEC
    width = -(-out_count // LANES) * LANES + LANES
    chunks = raw_count // CHUNK
    paired = src_count == 2 and 2 * out_count == S
    bf16 = jnp.bfloat16
    forward_hi, forward_lo = split_table(forward_table())
    alive_row = alive_mask.reshape(1, rows)

    with jax.named_scope("decimate"):
        device_count = blk_count * src_count
        main = slots * (width - LANES)
        decimated, pieces = pl.pallas_call(
            lambda *refs: decimate_kernel(paired, *refs),
            out_shape=(
                shaped(rows * (S // 2 // LANES) + SUBLANES, LANES)
                if paired
                else shaped(rows, width),
                shaped(device_count, 1, main + LANES),
            ),
            in_specs=[HBM] * 4,
            out_specs=(VMEM, HBM),
            scratch_shapes=[
                pltpu.VMEM((rows, raw_count), jnp.float32),
                pltpu.VMEM((1, TAPS), jnp.float32),
                pltpu.SMEM((1, rows), jnp.int32),
                pltpu.SMEM((1, slots), jnp.int32),
                pltpu.VMEM((SUBLANES * slots, CHUNK), jnp.float32),
                pltpu.VMEM((device_count, 1, main + LANES), jnp.float32),
                pltpu.SemaphoreType.DMA((rows // SUBLANES + 3,)),
            ],
            compiler_params=PARAMS,
        )(*in_hbm(raw_records, fir_taps.reshape(1, TAPS), alive_row, source_index))

    def whole(shards):
        rims = jnp.pad(shards[1:, :, width - EDGE :], ((0, 1), (0, 0), (out_count - EDGE, 0)))
        series = shards[:, :, :out_count] + rims
        return series.transpose(1, 0, 2).reshape(shards.shape[1], S)

    with jax.named_scope("gather_sources"):
        gathered = lax.all_to_all(
            pieces,
            ("blk", "src"),
            split_axis=0,
            concat_axis=0,
            tiled=True,
            axis_index_groups=[list(reversed(range(device_count)))],
        )
        if not paired:
            gathered = gathered[::-1]
            shards = gathered.reshape(blk_count, src_count, main + LANES)
            shards = shards.transpose(1, 0, 2)
            rims = [shards[:, :, main + LANES - EDGE * (slot + 1) :] for slot in range(slots)]
            rims = jnp.stack([rim[:, :, :EDGE] for rim in rims], axis=2)
            rims = jnp.pad(rims, ((0, 0), (0, 0), (0, 0), (LANES - EDGE, 0)))
            series = shards[:, :, :main].reshape(src_count, blk_count, slots, width - LANES)
            series = jnp.concatenate([series, rims], axis=3)
            series = whole(series.reshape(src_count, blk_count * slots, width))
            series = series.reshape(blk_count, slots, 2, S // 2).transpose(0, 2, 1, 3)
            series = series.reshape(blk_count * 2, 1, slots * S // 2)
            gathered = jnp.pad(series, ((0, 0), (0, 0), (0, LANES)))[::-1]

    with jax.named_scope("prepare"):
        out_shape = (
            shaped(S // 2, NFFT, dtype=bf16),
            shaped(S // 2, NFFT, dtype=bf16),
            shaped(3 * LANES, LANES, dtype=bf16),
            shaped(NFFT, LAGS, dtype=bf16),
            shaped(rows, LANES),
            shaped(slots, rows, LANES),
        )
        table_hi, table_lo, band, lag, alive, picks = pl.pallas_call(
            prepare_kernel,
            out_shape=out_shape,
            in_specs=[VMEM] + [HBM] * 6,
            out_specs=(VMEM,) * len(out_shape),
            scratch_shapes=[
                pltpu.VMEM((1, rows), jnp.int32),
                pltpu.VMEM((1, slots), jnp.int32),
                pltpu.SemaphoreType.DMA((6,)),
            ],
            compiler_params=PARAMS,
            cost_estimate=pl.CostEstimate(
                flops=0, bytes_accessed=4 * S * NFFT, transcendentals=0
            ),
        )(
            decimated,
            *in_hbm(
                alive_row,
                source_index,
                jnp.asarray(forward_hi),
                jnp.asarray(forward_lo),
                jnp.asarray(band_table()),
                jnp.asarray(lag_table()),
            ),
        )

    with jax.named_scope("regroup"):
        if paired:
            series = [decimated]
            other = [lax.ppermute(decimated, "src", [(0, 1), (1, 0)])]
        else:
            series = [whole(lax.all_gather(decimated, "src", axis=0))]
            other = []

    with jax.named_scope("spectra"):
        operands = series + [table_hi, table_lo, band, alive] + other
        spectra = pl.pallas_call(
            spectra_kernel,
            out_shape=shaped(rows, NFFT),
            in_specs=[VMEM] * len(operands),
            out_specs=VMEM,
            compiler_params=PARAMS,
        )(*operands)

    with jax.named_scope("correlate"):
        total = group * slots
        return pl.pallas_call(
            lambda *refs: correlate_kernel(slots, *refs),
            out_shape=shaped(total, rows, LAGS, dtype=bf16),
            in_specs=[VMEM] * 7,
            out_specs=HBM,
            scratch_shapes=[
                pltpu.VMEM((total, NFFT), jnp.float32),
                pltpu.VMEM((total * rows, NFFT), bf16),
                pltpu.VMEM((total, rows, LAGS), bf16),
                pltpu.SemaphoreType.DMA((PARTS,)),
            ],
            compiler_params=PARAMS,
        )(spectra, gathered.reshape(-1, LANES), picks, table_hi, table_lo, band, lag)


def solution(mesh):
    in_specs = (P("blk", "src"), P(), P("blk"), P("blk", None))
    out_specs = P("src", "blk", None)
    return jax.shard_map(local, mesh=mesh, in_specs=in_specs, out_specs=out_specs, check_vma=False)
```

```python
import math

import jax
import jax.numpy as jnp
import numpy as np
from jax import lax
from jax.experimental import pallas as pl
from jax.experimental.pallas import tpu as pltpu
from jax.sharding import PartitionSpec as P

S = 512
NFFT = 1024
BINS = NFFT // 2
LAGS = 512
TAPS = 64
DEC = 20
HALF = 64
LANES = 128
SUBLANES = 8
PARTS = 2
EDGE = (TAPS - 1) // DEC
CHUNK = 640
CHUNK_OUT = CHUNK // DEC
VMEM_LIMIT = 48 * 1024 * 1024


def forward_table():
    phases = 2.0 * math.pi / NFFT * (np.outer(np.arange(S // 2), np.arange(BINS)) % NFFT)
    return np.concatenate([np.cos(phases), -np.sin(phases)], axis=1).astype(np.float32)


def split_table(table):
    high = table.astype(jnp.bfloat16)
    low = (table - high.astype(np.float32)).astype(jnp.bfloat16)
    return high, low


def band_table():
    bins = np.arange(3 * LANES)[:, None] - LANES
    return (np.abs(bins - np.arange(LANES)[None, :]) <= HALF).astype(jnp.bfloat16)


def lag_table():
    bins = np.arange(BINS)[:, None]
    shift = np.arange(LAGS)[None, :] - LAGS // 2
    phases = 2.0 * math.pi / NFFT * (bins * shift % NFFT)
    weight = np.where(bins == 0, 0.5, 1.0) / math.sqrt(BINS)
    table = np.concatenate([weight * np.cos(phases), -weight * np.sin(phases)], axis=0)
    return table.astype(np.float32).astype(jnp.bfloat16)


def split(value):
    high = value.astype(jnp.bfloat16)
    return high, (value - high.astype(jnp.float32)).astype(jnp.bfloat16)


def dot(a, b):
    return jnp.dot(a, b, preferred_element_type=jnp.float32)


def column(row):
    count = row.shape[1]
    at = [lax.broadcasted_iota(jnp.int32, (count, count), axis) for axis in range(2)]
    rows = jnp.broadcast_to(row, (count, count))
    return jnp.sum(jnp.where(at[0] == at[1], rows, 0.0), axis=1, keepdims=True)


def start_copies(pairs, sems):
    copies = [
        pltpu.make_async_copy(source, target, sems.at[at])
        for at, (source, target) in enumerate(pairs)
    ]
    for copy in copies:
        copy.start()
    return copies


def decimate_kernel(
    paired, raw_hbm, taps_hbm, alive_hbm, picks_hbm, out_ref, pieces_hbm,
    raw_ref, taps_ref, alive_ref, picks_ref, source_ref, pieces_ref, sems,
):
    rows = raw_hbm.shape[0]
    chunks = raw_hbm.shape[1] // CHUNK
    slots = picks_ref.shape[1]
    per_tile = LANES // CHUNK_OUT
    tiles = -(-chunks // per_tile)
    pairs = [(taps_hbm, taps_ref), (picks_hbm, picks_ref), (alive_hbm, alive_ref)]
    for at in range(0, rows, SUBLANES):
        span = slice(at, at + SUBLANES)
        pairs.append((raw_hbm.at[span], raw_ref.at[span]))
    copies = start_copies(pairs, sems)
    source_ref[...] = jnp.zeros_like(source_ref)
    copies[0].wait()
    taps = jnp.broadcast_to(taps_ref[...], (SUBLANES, TAPS))
    eight = jnp.concatenate([taps, jnp.zeros((SUBLANES, CHUNK - TAPS), jnp.float32)], axis=1)
    for _ in range(2):
        eight = pltpu.roll(eight, 0, 1, stride=DEC // 2, stride_axis=0)
    wrapped = jnp.concatenate(
        [eight]
        + [pltpu.roll(eight, DEC * at, 1) for at in range(SUBLANES, CHUNK_OUT, SUBLANES)],
        axis=0,
    )
    lane = lax.broadcasted_iota(jnp.int32, (CHUNK_OUT, CHUNK), 1)
    row = lax.broadcasted_iota(jnp.int32, (CHUNK_OUT, CHUNK), 0)
    main = jnp.where(lane >= DEC * row, wrapped, 0.0)
    rim = wrapped - main
    gap = jnp.zeros((LANES - 2 * CHUNK_OUT, CHUNK), jnp.float32)
    weights_hi, weights_lo = split(jnp.concatenate([main, gap, rim], axis=0).T)
    weights = jnp.concatenate([weights_hi, weights_lo], axis=1)

    def filtered(stacked):
        high, low = split(stacked)
        both = dot(high, weights)
        return both[:, :LANES] + both[:, LANES:] + dot(low, weights_hi)

    for copy in copies[1:]:
        copy.wait()
    for slot in range(slots):
        pick = picks_ref[0, slot]
        alive = alive_ref[0, pick].astype(jnp.float32)
        for j in range(chunks):
            at = SUBLANES * slot + j
            span = slice(CHUNK * j, CHUNK * (j + 1))
            source_ref[at : at + 1, :] = raw_ref[pl.ds(pick, 1), span] * alive
    high, low = split(source_ref[...])
    count = slots * SUBLANES
    both = dot(jnp.concatenate([high, low], axis=0), weights)
    sources = both[:count, :LANES] + both[:count, LANES:] + both[count:, :LANES]
    lane = lax.broadcasted_iota(jnp.int32, (SUBLANES, LANES), 1)
    row = lax.broadcasted_iota(jnp.int32, (SUBLANES, LANES), 0)
    piece = []
    rims = jnp.zeros((1, LANES), jnp.float32)
    for slot in range(slots):
        source = sources[SUBLANES * slot : SUBLANES * (slot + 1)]
        main = jnp.where(lane < LANES // 2, source, 0.0)
        rim = source - main
        late = rim[:1]
        for _ in range(2):
            main = pltpu.roll(main, 0, 1, stride=CHUNK_OUT // 2, stride_axis=0)
            rim = pltpu.roll(rim, 0, 1, stride=CHUNK_OUT // 2, stride_axis=0)
        for tile in range(tiles):
            first = per_tile * tile
            inside = (row >= first) & (row < first + per_tile)
            before = (row > first) & (row <= first + per_tile)
            piece.append(
                jnp.sum(
                    jnp.where(inside, main, 0.0) + jnp.where(before, rim, 0.0),
                    axis=0,
                    keepdims=True,
                )
            )
        rims = rims + pltpu.roll(late, LANES - EDGE * slot if slot else 0, 1)
    piece.append(rims)
    size = len(piece)
    spread = [jnp.broadcast_to(value, (SUBLANES, LANES)) for value in piece]
    eight = []
    for group in range(size):
        place = (row + SUBLANES * group) % size
        total = spread[0]
        for at in range(1, size):
            total = jnp.where(place == at, spread[at], total)
        eight.append(total)
    eight = jnp.concatenate(eight, axis=0)
    for at in range(0, pieces_ref.shape[0], SUBLANES * size):
        pieces_ref[at : at + SUBLANES * size, :] = eight
    sending = pltpu.make_async_copy(pieces_ref, pieces_hbm, sems.at[0])
    sending.start()

    result = filtered(
        jnp.concatenate(
            [raw_ref[:, CHUNK * j : CHUNK * (j + 1)] for j in range(chunks)], axis=0
        )
    )
    part = [result[rows * j : rows * (j + 1)] for j in range(chunks)]
    is_main = lax.broadcasted_iota(jnp.int32, (rows, LANES), 1) < LANES // 2
    values = []
    for first in range(0, chunks, per_tile):
        total = jnp.where(is_main, part[first], 0.0)
        for step in range(1, min(per_tile, chunks - first)):
            total = total + pltpu.roll(part[first + step], CHUNK_OUT * step, 1)
        if first + per_tile < chunks:
            total = total + jnp.where(is_main, 0.0, part[first + per_tile])
        values.append(total)
    rim = jnp.where(is_main, 0.0, part[0])
    if paired:
        packed = rim[:SUBLANES]
        for at in range(1, rows // SUBLANES):
            group = rim[SUBLANES * at : SUBLANES * (at + 1)]
            packed = packed + pltpu.roll(group, LANES - EDGE * at, 1)
        for at, value in enumerate(values):
            out_ref[rows * at : rows * (at + 1), :] = value
        out_ref[rows * tiles :, :] = packed
    else:
        for at, value in enumerate(values + [rim]):
            out_ref[:, LANES * at : LANES * (at + 1)] = value
    sending.wait()


def unpack(packed, rows):
    tiles = [packed[at : at + rows] for at in range(0, packed.shape[0] - SUBLANES, rows)]
    rims = packed[packed.shape[0] - SUBLANES :]
    rim = jnp.concatenate(
        [rims]
        + [pltpu.roll(rims, EDGE * at, 1) for at in range(1, rows // SUBLANES)],
        axis=0,
    )
    lane = lax.broadcasted_iota(jnp.int32, rim.shape, 1)
    return tiles + [jnp.where(lane >= LANES - EDGE, rim, 0.0)]


def transform(early, late, table_hi, table_lo):
    rows = early.shape[0]
    high, low = split(jnp.concatenate([early, late], axis=0))
    first = dot(jnp.concatenate([high, low], axis=0), table_hi)
    both = first[: 2 * rows] + first[2 * rows :] + dot(high, table_lo)
    quarter = lax.broadcasted_iota(jnp.int32, (1, BINS), 1) & 3
    cosine = jnp.where(quarter == 0, 1.0, 0.0) - jnp.where(quarter == 2, 1.0, 0.0)
    sine = jnp.where(quarter == 1, 1.0, 0.0) - jnp.where(quarter == 3, 1.0, 0.0)
    early_re, early_im = both[:rows, :BINS], both[:rows, BINS:]
    late_re, late_im = both[rows:, :BINS], both[rows:, BINS:]
    return (
        early_re + cosine * late_re + sine * late_im,
        early_im + cosine * late_im - sine * late_re,
    )


def whitening(real_part, imag_part, band):
    rows = real_part.shape[0]
    tiles = BINS // LANES
    stacked = []
    for part in split(real_part * real_part + imag_part * imag_part):
        zero = jnp.zeros((rows, LANES), part.dtype)
        wide = jnp.concatenate([zero, part, zero], axis=1)
        stacked += [wide[:, LANES * tile : LANES * (tile + 3)] for tile in range(tiles)]
    banded = dot(jnp.concatenate(stacked, axis=0), band)
    step = rows * tiles
    summed = banded[:step] + banded[step:]
    total = jnp.concatenate(
        [summed[rows * tile : rows * (tile + 1)] for tile in range(tiles)], axis=1
    )
    bins = lax.broadcasted_iota(jnp.int32, (1, BINS), 1)
    count = jnp.minimum(bins + HALF, BINS - 1) - jnp.maximum(bins - HALF, 0) + 1
    return lax.rsqrt(total * (1.0 / count.astype(jnp.float32)) + 1e-06)


def prepare_kernel(
    _, alive_hbm, picks_hbm, fwd_hi_hbm, fwd_lo_hbm, band_hbm, lag_hbm,
    hi_ref, lo_ref, band_ref, lag_ref, alive_out, picks_out, alive_ref, picks_ref, sems,
):
    copies = start_copies(
        [
            (alive_hbm, alive_ref),
            (picks_hbm, picks_ref),
            (fwd_hi_hbm, hi_ref),
            (fwd_lo_hbm, lo_ref),
            (band_hbm, band_ref),
            (lag_hbm, lag_ref),
        ],
        sems,
    )
    for copy in copies[:2]:
        copy.wait()
    rows = alive_out.shape[0]
    alive_out[...] = jnp.broadcast_to(
        column(alive_ref[...].astype(jnp.float32)), (rows, LANES)
    )
    channel = lax.broadcasted_iota(jnp.int32, (rows, LANES), 0)
    for slot in range(picks_ref.shape[1]):
        pick = jnp.broadcast_to(picks_ref[:, slot : slot + 1], (rows, LANES))
        picks_out[slot] = jnp.where(channel == pick, 1.0, 0.0)
    for copy in copies[2:]:
        copy.wait()


def spectra_kernel(series_ref, hi_ref, lo_ref, band_ref, alive_ref, *refs):
    spectra_ref = refs[-1]
    rows = alive_ref.shape[0]
    half = S // 2
    if len(refs) > 1:
        mine, other = [unpack(ref[...], rows) for ref in (series_ref, refs[0])]
        first = lax.axis_index("src") == 0
        early = [jnp.where(first, a, b) for a, b in zip(mine, other)]
        late = [jnp.where(first, b, a) for a, b in zip(mine, other)]
        early[-2] = early[-2] + late[-1]
        early, late = [jnp.concatenate(tiles[:-1], axis=1) for tiles in (early, late)]
    else:
        early, late = series_ref[:, :half], series_ref[:, half:]
    real_part, imag_part = transform(early, late, hi_ref[...], lo_ref[...])
    factor = alive_ref[:, :1] * whitening(real_part, imag_part, band_ref[...])
    spectra_ref[:, :BINS] = real_part * factor
    spectra_ref[:, BINS:] = imag_part * factor


def correlate_kernel(
    slots, spectra_ref, pieces_ref, picks_ref, hi_ref, lo_ref, band_ref, lag_ref, out_hbm,
    source_ref, cross_ref, out_ref, sems,
):
    rows = spectra_ref.shape[0]
    group = out_ref.shape[0] // slots
    half = BINS // LANES
    own = lax.axis_index("blk")
    base = lax.axis_index("src") * group
    tiles = S // 2 // LANES
    stride = slots * tiles + 1

    def entry(half_at, row):
        last = pieces_ref.shape[0] // stride - 1 - 2 * (base + group - 1) - half_at
        return pieces_ref[pl.ds(last * stride + row, group, stride=2 * stride), :]

    def halves(half_at):
        return [
            jnp.concatenate([entry(half_at, slot * tiles + tile) for slot in range(slots)], axis=0)
            for tile in range(tiles)
        ]

    early, late = halves(0), halves(1)
    rims = entry(1, slots * tiles)
    rims = jnp.concatenate(
        [rims] + [pltpu.roll(rims, EDGE * slot, 1) for slot in range(1, slots)], axis=0
    )
    lane = lax.broadcasted_iota(jnp.int32, rims.shape, 1)
    early[-1] = early[-1] + jnp.where(lane >= LANES - EDGE, rims, 0.0)
    early, late = [jnp.concatenate(columns, axis=1) for columns in (early, late)]
    real_part, imag_part = transform(early, late, hi_ref[...], lo_ref[...])
    factor = whitening(real_part, imag_part, band_ref[...])
    source_ref[:, :BINS] = real_part * factor
    source_ref[:, BINS:] = imag_part * factor
    per_part = max(1, (group * slots) // PARTS)
    copies = []
    for part in range(group * slots // per_part):
        first = part * per_part
        for tile in range(half):
            re = slice(LANES * tile, LANES * (tile + 1))
            im = slice(BINS + LANES * tile, BINS + LANES * (tile + 1))
            rec_re, rec_im = spectra_ref[:, re], spectra_ref[:, im]
            for source in range(first, first + per_part):
                block, slot = divmod(source, slots)
                at = slot * group + group - 1 - block
                src_re, src_im = source_ref[at : at + 1, re], source_ref[at : at + 1, im]
                where = slice(rows * source, rows * (source + 1))
                cross_ref[where, re] = (src_re * rec_re + src_im * rec_im).astype(jnp.bfloat16)
                cross_ref[where, im] = (src_re * rec_im - src_im * rec_re).astype(jnp.bfloat16)
        lagged = dot(cross_ref[rows * first : rows * (first + per_part), :], lag_ref[...])
        for source in range(first, first + per_part):
            block, slot = divmod(source, slots)
            keep = 1.0 - jnp.where(own == base + block, 1.0, 0.0) * picks_ref[slot]
            at = source - first
            kept = lagged[rows * at : rows * (at + 1)] * jnp.concatenate(
                [keep] * (LAGS // LANES), axis=1
            )
            out_ref[source] = kept.astype(jnp.bfloat16)
        span = pl.ds(first, per_part)
        copies.append(pltpu.make_async_copy(out_ref.at[span], out_hbm.at[span], sems.at[part]))
        copies[-1].start()
    for copy in copies:
        copy.wait()


HBM = pl.BlockSpec(memory_space=pltpu.HBM)
VMEM = pl.BlockSpec(memory_space=pltpu.VMEM)
PARAMS = pltpu.CompilerParams(vmem_limit_bytes=VMEM_LIMIT)


def in_hbm(*arrays):
    return [pltpu.with_memory_space_constraint(array, pltpu.HBM) for array in arrays]


def shaped(*shape, dtype=jnp.float32):
    return jax.ShapeDtypeStruct(shape, dtype)


def local(raw_records, fir_taps, alive_mask, source_index):
    src_count = lax.axis_size("src")
    blk_count = lax.axis_size("blk")
    rows, raw_count = raw_records.shape
    slots = source_index.shape[1]
    group = blk_count // src_count
    out_count = raw_count // DEC
    width = -(-out_count // LANES) * LANES + LANES
    chunks = raw_count // CHUNK
    paired = src_count == 2 and 2 * out_count == S
    bf16 = jnp.bfloat16
    forward_hi, forward_lo = split_table(forward_table())
    alive_row = alive_mask.reshape(1, rows)

    with jax.named_scope("decimate"):
        device_count = blk_count * src_count
        main = slots * (width - LANES)
        decimated, pieces = pl.pallas_call(
            lambda *refs: decimate_kernel(paired, *refs),
            out_shape=(
                shaped(rows * (S // 2 // LANES) + SUBLANES, LANES)
                if paired
                else shaped(rows, width),
                shaped(device_count * (main // LANES + 1), LANES),
            ),
            in_specs=[HBM] * 4,
            out_specs=(VMEM, HBM),
            scratch_shapes=[
                pltpu.VMEM((rows, raw_count), jnp.float32),
                pltpu.VMEM((1, TAPS), jnp.float32),
                pltpu.SMEM((1, rows), jnp.int32),
                pltpu.SMEM((1, slots), jnp.int32),
                pltpu.VMEM((SUBLANES * slots, CHUNK), jnp.float32),
                pltpu.VMEM((device_count * (main // LANES + 1), LANES), jnp.float32),
                pltpu.SemaphoreType.DMA((rows // SUBLANES + 3,)),
            ],
            compiler_params=PARAMS,
        )(*in_hbm(raw_records, fir_taps.reshape(1, TAPS), alive_row, source_index))

    def whole(shards):
        rims = jnp.pad(shards[1:, :, width - EDGE :], ((0, 1), (0, 0), (out_count - EDGE, 0)))
        series = shards[:, :, :out_count] + rims
        return series.transpose(1, 0, 2).reshape(shards.shape[1], S)

    with jax.named_scope("gather_sources"):
        gathered = lax.all_to_all(
            pieces.reshape(device_count, 1, main + LANES),
            ("blk", "src"),
            split_axis=0,
            concat_axis=0,
            tiled=True,
            axis_index_groups=[list(reversed(range(device_count)))],
        )
        if not paired:
            gathered = gathered[::-1]
            shards = gathered.reshape(blk_count, src_count, main + LANES)
            shards = shards.transpose(1, 0, 2)
            rims = [shards[:, :, main + LANES - EDGE * (slot + 1) :] for slot in range(slots)]
            rims = jnp.stack([rim[:, :, :EDGE] for rim in rims], axis=2)
            rims = jnp.pad(rims, ((0, 0), (0, 0), (0, 0), (LANES - EDGE, 0)))
            series = shards[:, :, :main].reshape(src_count, blk_count, slots, width - LANES)
            series = jnp.concatenate([series, rims], axis=3)
            series = whole(series.reshape(src_count, blk_count * slots, width))
            series = series.reshape(blk_count, slots, 2, S // 2).transpose(0, 2, 1, 3)
            series = series.reshape(blk_count * 2, 1, slots * S // 2)
            gathered = jnp.pad(series, ((0, 0), (0, 0), (0, LANES)))[::-1]

    with jax.named_scope("prepare"):
        out_shape = (
            shaped(S // 2, NFFT, dtype=bf16),
            shaped(S // 2, NFFT, dtype=bf16),
            shaped(3 * LANES, LANES, dtype=bf16),
            shaped(NFFT, LAGS, dtype=bf16),
            shaped(rows, LANES),
            shaped(slots, rows, LANES),
        )
        table_hi, table_lo, band, lag, alive, picks = pl.pallas_call(
            prepare_kernel,
            out_shape=out_shape,
            in_specs=[VMEM] + [HBM] * 6,
            out_specs=(VMEM,) * len(out_shape),
            scratch_shapes=[
                pltpu.VMEM((1, rows), jnp.int32),
                pltpu.VMEM((1, slots), jnp.int32),
                pltpu.SemaphoreType.DMA((6,)),
            ],
            compiler_params=PARAMS,
            cost_estimate=pl.CostEstimate(
                flops=0, bytes_accessed=4 * S * NFFT, transcendentals=0
            ),
        )(
            decimated,
            *in_hbm(
                alive_row,
                source_index,
                jnp.asarray(forward_hi),
                jnp.asarray(forward_lo),
                jnp.asarray(band_table()),
                jnp.asarray(lag_table()),
            ),
        )

    with jax.named_scope("regroup"):
        if paired:
            series = [decimated]
            other = [lax.ppermute(decimated, "src", [(0, 1), (1, 0)])]
        else:
            series = [whole(lax.all_gather(decimated, "src", axis=0))]
            other = []

    with jax.named_scope("spectra"):
        operands = series + [table_hi, table_lo, band, alive] + other
        spectra = pl.pallas_call(
            spectra_kernel,
            out_shape=shaped(rows, NFFT),
            in_specs=[VMEM] * len(operands),
            out_specs=VMEM,
            compiler_params=PARAMS,
        )(*operands)

    with jax.named_scope("correlate"):
        total = group * slots
        return pl.pallas_call(
            lambda *refs: correlate_kernel(slots, *refs),
            out_shape=shaped(total, rows, LAGS, dtype=bf16),
            in_specs=[VMEM] * 7,
            out_specs=HBM,
            scratch_shapes=[
                pltpu.VMEM((total, NFFT), jnp.float32),
                pltpu.VMEM((total * rows, NFFT), bf16),
                pltpu.VMEM((total, rows, LAGS), bf16),
                pltpu.SemaphoreType.DMA((PARTS,)),
            ],
            compiler_params=PARAMS,
        )(spectra, gathered.reshape(-1, LANES), picks, table_hi, table_lo, band, lag)


def solution(mesh):
    in_specs = (P("blk", "src"), P(), P("blk"), P("blk", None))
    out_specs = P("src", "blk", None)
    return jax.shard_map(local, mesh=mesh, in_specs=in_specs, out_specs=out_specs, check_vma=False)
```

```python
import math

import jax
import jax.numpy as jnp
import numpy as np
from jax import lax
from jax.experimental import pallas as pl
from jax.experimental.pallas import tpu as pltpu
from jax.sharding import PartitionSpec as P

S = 512
NFFT = 1024
BINS = NFFT // 2
LAGS = 512
TAPS = 64
DEC = 20
HALF = 64
LANES = 128
SUBLANES = 8
PARTS = 4
EDGE = (TAPS - 1) // DEC
CHUNK = 640
CHUNK_OUT = CHUNK // DEC
RECORD_WIDTH = 2 * CHUNK
VMEM_LIMIT = 48 * 1024 * 1024


def forward_table():
    phases = 2.0 * math.pi / NFFT * (np.outer(np.arange(S // 2), np.arange(BINS)) % NFFT)
    return np.concatenate([np.cos(phases), -np.sin(phases)], axis=1).astype(np.float32)


def split_table(table):
    high = table.astype(jnp.bfloat16)
    low = (table - high.astype(np.float32)).astype(jnp.bfloat16)
    return high, low


def band_table():
    bins = np.arange(3 * LANES)[:, None] - LANES
    return (np.abs(bins - np.arange(LANES)[None, :]) <= HALF).astype(jnp.bfloat16)


def lag_table():
    bins = np.arange(BINS)[:, None]
    shift = np.arange(LAGS)[None, :] - LAGS // 2
    phases = 2.0 * math.pi / NFFT * (bins * shift % NFFT)
    weight = np.where(bins == 0, 0.5, 1.0) / math.sqrt(BINS)
    table = np.concatenate([weight * np.cos(phases), -weight * np.sin(phases)], axis=0)
    return table.astype(np.float32).astype(jnp.bfloat16)


def split(value):
    high = value.astype(jnp.bfloat16)
    return high, (value - high.astype(jnp.float32)).astype(jnp.bfloat16)


def dot(a, b):
    return jnp.dot(a, b, preferred_element_type=jnp.float32)


def column(row):
    count = row.shape[1]
    at = [lax.broadcasted_iota(jnp.int32, (count, count), axis) for axis in range(2)]
    rows = jnp.broadcast_to(row, (count, count))
    return jnp.sum(jnp.where(at[0] == at[1], rows, 0.0), axis=1, keepdims=True)


def start_copies(pairs, sems):
    copies = [
        pltpu.make_async_copy(source, target, sems.at[at])
        for at, (source, target) in enumerate(pairs)
    ]
    for copy in copies:
        copy.start()
    return copies


def decimate_kernel(
    paired, raw_hbm, taps_hbm, alive_hbm, picks_hbm, out_ref, pieces_hbm,
    raw_ref, taps_ref, alive_ref, picks_ref, source_ref, pieces_ref, sems,
):
    rows = raw_hbm.shape[0]
    chunks = raw_hbm.shape[1] // CHUNK
    slots = picks_ref.shape[1]
    per_tile = LANES // CHUNK_OUT
    tiles = -(-chunks // per_tile)
    pairs = [(taps_hbm, taps_ref), (picks_hbm, picks_ref), (alive_hbm, alive_ref)]
    for at in range(0, rows, SUBLANES):
        for start in range(0, raw_hbm.shape[1], RECORD_WIDTH):
            place = (slice(at, at + SUBLANES), slice(start, start + RECORD_WIDTH))
            pairs.append((raw_hbm.at[place], raw_ref.at[place]))
    copies = start_copies(pairs, sems)
    source_ref[...] = jnp.zeros_like(source_ref)
    copies[0].wait()
    taps = jnp.broadcast_to(taps_ref[...], (SUBLANES, TAPS))
    eight = jnp.concatenate([taps, jnp.zeros((SUBLANES, CHUNK - TAPS), jnp.float32)], axis=1)
    for _ in range(2):
        eight = pltpu.roll(eight, 0, 1, stride=DEC // 2, stride_axis=0)
    wrapped = jnp.concatenate(
        [eight]
        + [pltpu.roll(eight, DEC * at, 1) for at in range(SUBLANES, CHUNK_OUT, SUBLANES)],
        axis=0,
    )
    lane = lax.broadcasted_iota(jnp.int32, (CHUNK_OUT, CHUNK), 1)
    row = lax.broadcasted_iota(jnp.int32, (CHUNK_OUT, CHUNK), 0)
    main = jnp.where(lane >= DEC * row, wrapped, 0.0)
    rim = wrapped - main
    gap = jnp.zeros((LANES - 2 * CHUNK_OUT, CHUNK), jnp.float32)
    weights_hi, weights_lo = split(jnp.concatenate([main, gap, rim], axis=0).T)
    weights = jnp.concatenate([weights_hi, weights_lo], axis=1)

    def filtered(stacked):
        high, low = split(stacked)
        both = dot(high, weights)
        return both[:, :LANES] + both[:, LANES:] + dot(low, weights_hi)

    for copy in copies[1:]:
        copy.wait()
    for slot in range(slots):
        pick = picks_ref[0, slot]
        alive = alive_ref[0, pick].astype(jnp.float32)
        for j in range(chunks):
            at = SUBLANES * slot + j
            span = slice(CHUNK * j, CHUNK * (j + 1))
            source_ref[at : at + 1, :] = raw_ref[pl.ds(pick, 1), span] * alive
    high, low = split(source_ref[...])
    count = slots * SUBLANES
    both = dot(jnp.concatenate([high, low], axis=0), weights)
    sources = both[:count, :LANES] + both[:count, LANES:] + both[count:, :LANES]
    lane = lax.broadcasted_iota(jnp.int32, (SUBLANES, LANES), 1)
    row = lax.broadcasted_iota(jnp.int32, (SUBLANES, LANES), 0)
    piece = []
    rims = jnp.zeros((1, LANES), jnp.float32)
    for slot in range(slots):
        source = sources[SUBLANES * slot : SUBLANES * (slot + 1)]
        main = jnp.where(lane < LANES // 2, source, 0.0)
        rim = source - main
        late = rim[:1]
        for _ in range(2):
            main = pltpu.roll(main, 0, 1, stride=CHUNK_OUT // 2, stride_axis=0)
            rim = pltpu.roll(rim, 0, 1, stride=CHUNK_OUT // 2, stride_axis=0)
        for tile in range(tiles):
            first = per_tile * tile
            inside = (row >= first) & (row < first + per_tile)
            before = (row > first) & (row <= first + per_tile)
            piece.append(
                jnp.sum(
                    jnp.where(inside, main, 0.0) + jnp.where(before, rim, 0.0),
                    axis=0,
                    keepdims=True,
                )
            )
        rims = rims + pltpu.roll(late, LANES - EDGE * slot if slot else 0, 1)
    piece.append(rims)
    size = len(piece)
    spread = [jnp.broadcast_to(value, (SUBLANES, LANES)) for value in piece]
    eight = []
    for group in range(size):
        place = (row + SUBLANES * group) % size
        total = spread[0]
        for at in range(1, size):
            total = jnp.where(place == at, spread[at], total)
        eight.append(total)
    eight = jnp.concatenate(eight, axis=0)
    for at in range(0, pieces_ref.shape[0], SUBLANES * size):
        pieces_ref[at : at + SUBLANES * size, :] = eight
    sending = pltpu.make_async_copy(pieces_ref, pieces_hbm, sems.at[0])
    sending.start()

    result = filtered(
        jnp.concatenate(
            [raw_ref[:, CHUNK * j : CHUNK * (j + 1)] for j in range(chunks)], axis=0
        )
    )
    part = [result[rows * j : rows * (j + 1)] for j in range(chunks)]
    is_main = lax.broadcasted_iota(jnp.int32, (rows, LANES), 1) < LANES // 2
    values = []
    for first in range(0, chunks, per_tile):
        total = jnp.where(is_main, part[first], 0.0)
        for step in range(1, min(per_tile, chunks - first)):
            total = total + pltpu.roll(part[first + step], CHUNK_OUT * step, 1)
        if first + per_tile < chunks:
            total = total + jnp.where(is_main, 0.0, part[first + per_tile])
        values.append(total)
    rim = jnp.where(is_main, 0.0, part[0])
    if paired:
        packed = rim[:SUBLANES]
        for at in range(1, rows // SUBLANES):
            group = rim[SUBLANES * at : SUBLANES * (at + 1)]
            packed = packed + pltpu.roll(group, LANES - EDGE * at, 1)
        for at, value in enumerate(values):
            out_ref[rows * at : rows * (at + 1), :] = value
        out_ref[rows * tiles :, :] = packed
    else:
        for at, value in enumerate(values + [rim]):
            out_ref[:, LANES * at : LANES * (at + 1)] = value
    sending.wait()


def unpack(packed, rows):
    tiles = [packed[at : at + rows] for at in range(0, packed.shape[0] - SUBLANES, rows)]
    rims = packed[packed.shape[0] - SUBLANES :]
    rim = jnp.concatenate(
        [rims]
        + [pltpu.roll(rims, EDGE * at, 1) for at in range(1, rows // SUBLANES)],
        axis=0,
    )
    lane = lax.broadcasted_iota(jnp.int32, rim.shape, 1)
    return tiles + [jnp.where(lane >= LANES - EDGE, rim, 0.0)]


def transform(early, late, table_hi, table_lo):
    rows = early.shape[0]
    high, low = split(jnp.concatenate([early, late], axis=0))
    first = dot(jnp.concatenate([high, low], axis=0), table_hi)
    both = first[: 2 * rows] + first[2 * rows :] + dot(high, table_lo)
    quarter = lax.broadcasted_iota(jnp.int32, (1, BINS), 1) & 3
    cosine = jnp.where(quarter == 0, 1.0, 0.0) - jnp.where(quarter == 2, 1.0, 0.0)
    sine = jnp.where(quarter == 1, 1.0, 0.0) - jnp.where(quarter == 3, 1.0, 0.0)
    early_re, early_im = both[:rows, :BINS], both[:rows, BINS:]
    late_re, late_im = both[rows:, :BINS], both[rows:, BINS:]
    return (
        early_re + cosine * late_re + sine * late_im,
        early_im + cosine * late_im - sine * late_re,
    )


def whitening(real_part, imag_part, band):
    rows = real_part.shape[0]
    tiles = BINS // LANES
    stacked = []
    for part in split(real_part * real_part + imag_part * imag_part):
        zero = jnp.zeros((rows, LANES), part.dtype)
        wide = jnp.concatenate([zero, part, zero], axis=1)
        stacked += [wide[:, LANES * tile : LANES * (tile + 3)] for tile in range(tiles)]
    banded = dot(jnp.concatenate(stacked, axis=0), band)
    step = rows * tiles
    summed = banded[:step] + banded[step:]
    total = jnp.concatenate(
        [summed[rows * tile : rows * (tile + 1)] for tile in range(tiles)], axis=1
    )
    bins = lax.broadcasted_iota(jnp.int32, (1, BINS), 1)
    count = jnp.minimum(bins + HALF, BINS - 1) - jnp.maximum(bins - HALF, 0) + 1
    return lax.rsqrt(total * (1.0 / count.astype(jnp.float32)) + 1e-06)


def prepare_kernel(
    _, alive_hbm, picks_hbm, fwd_hi_hbm, fwd_lo_hbm, band_hbm, lag_hbm,
    hi_ref, lo_ref, band_ref, lag_ref, alive_out, picks_out, alive_ref, picks_ref, sems,
):
    copies = start_copies(
        [
            (alive_hbm, alive_ref),
            (picks_hbm, picks_ref),
            (fwd_hi_hbm, hi_ref),
            (fwd_lo_hbm, lo_ref),
            (band_hbm, band_ref),
            (lag_hbm, lag_ref),
        ],
        sems,
    )
    for copy in copies[:2]:
        copy.wait()
    rows = alive_out.shape[0]
    alive_out[...] = jnp.broadcast_to(
        column(alive_ref[...].astype(jnp.float32)), (rows, LANES)
    )
    channel = lax.broadcasted_iota(jnp.int32, (rows, LANES), 0)
    for slot in range(picks_ref.shape[1]):
        pick = jnp.broadcast_to(picks_ref[:, slot : slot + 1], (rows, LANES))
        picks_out[slot] = jnp.where(channel == pick, 1.0, 0.0)
    for copy in copies[2:]:
        copy.wait()


def spectra_kernel(series_ref, hi_ref, lo_ref, band_ref, alive_ref, *refs):
    spectra_ref = refs[-1]
    rows = alive_ref.shape[0]
    half = S // 2
    if len(refs) > 1:
        mine, other = [unpack(ref[...], rows) for ref in (series_ref, refs[0])]
        first = lax.axis_index("src") == 0
        early = [jnp.where(first, a, b) for a, b in zip(mine, other)]
        late = [jnp.where(first, b, a) for a, b in zip(mine, other)]
        early[-2] = early[-2] + late[-1]
        early, late = [jnp.concatenate(tiles[:-1], axis=1) for tiles in (early, late)]
    else:
        early, late = series_ref[:, :half], series_ref[:, half:]
    real_part, imag_part = transform(early, late, hi_ref[...], lo_ref[...])
    factor = alive_ref[:, :1] * whitening(real_part, imag_part, band_ref[...])
    spectra_ref[:, :BINS] = real_part * factor
    spectra_ref[:, BINS:] = imag_part * factor


def correlate_kernel(
    slots, spectra_ref, pieces_ref, picks_ref, hi_ref, lo_ref, band_ref, lag_ref, out_hbm,
    source_ref, cross_ref, out_ref, sems,
):
    rows = spectra_ref.shape[0]
    group = out_ref.shape[0] // slots
    half = BINS // LANES
    own = lax.axis_index("blk")
    base = lax.axis_index("src") * group
    tiles = S // 2 // LANES
    stride = slots * tiles + 1

    def entry(half_at, row):
        last = pieces_ref.shape[0] // stride - 1 - 2 * (base + group - 1) - half_at
        return pieces_ref[pl.ds(last * stride + row, group, stride=2 * stride), :]

    def halves(half_at):
        return [
            jnp.concatenate([entry(half_at, slot * tiles + tile) for slot in range(slots)], axis=0)
            for tile in range(tiles)
        ]

    early, late = halves(0), halves(1)
    rims = entry(1, slots * tiles)
    rims = jnp.concatenate(
        [rims] + [pltpu.roll(rims, EDGE * slot, 1) for slot in range(1, slots)], axis=0
    )
    lane = lax.broadcasted_iota(jnp.int32, rims.shape, 1)
    early[-1] = early[-1] + jnp.where(lane >= LANES - EDGE, rims, 0.0)
    early, late = [jnp.concatenate(columns, axis=1) for columns in (early, late)]
    real_part, imag_part = transform(early, late, hi_ref[...], lo_ref[...])
    factor = whitening(real_part, imag_part, band_ref[...])
    source_ref[:, :BINS] = real_part * factor
    source_ref[:, BINS:] = imag_part * factor
    per_part = max(1, (group * slots) // PARTS)
    copies = []
    for part in range(group * slots // per_part):
        first = part * per_part
        for tile in range(half):
            re = slice(LANES * tile, LANES * (tile + 1))
            im = slice(BINS + LANES * tile, BINS + LANES * (tile + 1))
            rec_re, rec_im = spectra_ref[:, re], spectra_ref[:, im]
            for source in range(first, first + per_part):
                block, slot = divmod(source, slots)
                at = slot * group + group - 1 - block
                src_re, src_im = source_ref[at : at + 1, re], source_ref[at : at + 1, im]
                where = slice(rows * source, rows * (source + 1))
                cross_ref[where, re] = (src_re * rec_re + src_im * rec_im).astype(jnp.bfloat16)
                cross_ref[where, im] = (src_re * rec_im - src_im * rec_re).astype(jnp.bfloat16)
        lagged = dot(cross_ref[rows * first : rows * (first + per_part), :], lag_ref[...])
        for source in range(first, first + per_part):
            block, slot = divmod(source, slots)
            keep = 1.0 - jnp.where(own == base + block, 1.0, 0.0) * picks_ref[slot]
            at = source - first
            kept = lagged[rows * at : rows * (at + 1)] * jnp.concatenate(
                [keep] * (LAGS // LANES), axis=1
            )
            out_ref[source] = kept.astype(jnp.bfloat16)
            copies.append(
                pltpu.make_async_copy(out_ref.at[source], out_hbm.at[source], sems.at[source])
            )
            copies[-1].start()
    for copy in copies:
        copy.wait()


HBM = pl.BlockSpec(memory_space=pltpu.HBM)
VMEM = pl.BlockSpec(memory_space=pltpu.VMEM)
PARAMS = pltpu.CompilerParams(vmem_limit_bytes=VMEM_LIMIT)


def in_hbm(*arrays):
    return [pltpu.with_memory_space_constraint(array, pltpu.HBM) for array in arrays]


def shaped(*shape, dtype=jnp.float32):
    return jax.ShapeDtypeStruct(shape, dtype)


def local(raw_records, fir_taps, alive_mask, source_index):
    src_count = lax.axis_size("src")
    blk_count = lax.axis_size("blk")
    rows, raw_count = raw_records.shape
    slots = source_index.shape[1]
    group = blk_count // src_count
    out_count = raw_count // DEC
    width = -(-out_count // LANES) * LANES + LANES
    chunks = raw_count // CHUNK
    paired = src_count == 2 and 2 * out_count == S
    bf16 = jnp.bfloat16
    forward_hi, forward_lo = split_table(forward_table())
    alive_row = alive_mask.reshape(1, rows)

    with jax.named_scope("decimate"):
        device_count = blk_count * src_count
        main = slots * (width - LANES)
        decimated, pieces = pl.pallas_call(
            lambda *refs: decimate_kernel(paired, *refs),
            out_shape=(
                shaped(rows * (S // 2 // LANES) + SUBLANES, LANES)
                if paired
                else shaped(rows, width),
                shaped(device_count * (main // LANES + 1), LANES),
            ),
            in_specs=[HBM] * 4,
            out_specs=(VMEM, HBM),
            scratch_shapes=[
                pltpu.VMEM((rows, raw_count), jnp.float32),
                pltpu.VMEM((1, TAPS), jnp.float32),
                pltpu.SMEM((1, rows), jnp.int32),
                pltpu.SMEM((1, slots), jnp.int32),
                pltpu.VMEM((SUBLANES * slots, CHUNK), jnp.float32),
                pltpu.VMEM((device_count * (main // LANES + 1), LANES), jnp.float32),
                pltpu.SemaphoreType.DMA((rows // SUBLANES * (raw_count // RECORD_WIDTH) + 3,)),
            ],
            compiler_params=PARAMS,
        )(*in_hbm(raw_records, fir_taps.reshape(1, TAPS), alive_row, source_index))

    def whole(shards):
        rims = jnp.pad(shards[1:, :, width - EDGE :], ((0, 1), (0, 0), (out_count - EDGE, 0)))
        series = shards[:, :, :out_count] + rims
        return series.transpose(1, 0, 2).reshape(shards.shape[1], S)

    with jax.named_scope("gather_sources"):
        gathered = lax.all_to_all(
            pieces.reshape(device_count, 1, main + LANES),
            ("blk", "src"),
            split_axis=0,
            concat_axis=0,
            tiled=True,
            axis_index_groups=[list(reversed(range(device_count)))],
        )
        if not paired:
            gathered = gathered[::-1]
            shards = gathered.reshape(blk_count, src_count, main + LANES)
            shards = shards.transpose(1, 0, 2)
            rims = [shards[:, :, main + LANES - EDGE * (slot + 1) :] for slot in range(slots)]
            rims = jnp.stack([rim[:, :, :EDGE] for rim in rims], axis=2)
            rims = jnp.pad(rims, ((0, 0), (0, 0), (0, 0), (LANES - EDGE, 0)))
            series = shards[:, :, :main].reshape(src_count, blk_count, slots, width - LANES)
            series = jnp.concatenate([series, rims], axis=3)
            series = whole(series.reshape(src_count, blk_count * slots, width))
            series = series.reshape(blk_count, slots, 2, S // 2).transpose(0, 2, 1, 3)
            series = series.reshape(blk_count * 2, 1, slots * S // 2)
            gathered = jnp.pad(series, ((0, 0), (0, 0), (0, LANES)))[::-1]

    with jax.named_scope("prepare"):
        out_shape = (
            shaped(S // 2, NFFT, dtype=bf16),
            shaped(S // 2, NFFT, dtype=bf16),
            shaped(3 * LANES, LANES, dtype=bf16),
            shaped(NFFT, LAGS, dtype=bf16),
            shaped(rows, LANES),
            shaped(slots, rows, LANES),
        )
        table_hi, table_lo, band, lag, alive, picks = pl.pallas_call(
            prepare_kernel,
            out_shape=out_shape,
            in_specs=[VMEM] + [HBM] * 6,
            out_specs=(VMEM,) * len(out_shape),
            scratch_shapes=[
                pltpu.VMEM((1, rows), jnp.int32),
                pltpu.VMEM((1, slots), jnp.int32),
                pltpu.SemaphoreType.DMA((6,)),
            ],
            compiler_params=PARAMS,
            cost_estimate=pl.CostEstimate(
                flops=0, bytes_accessed=4 * S * NFFT, transcendentals=0
            ),
        )(
            decimated,
            *in_hbm(
                alive_row,
                source_index,
                jnp.asarray(forward_hi),
                jnp.asarray(forward_lo),
                jnp.asarray(band_table()),
                jnp.asarray(lag_table()),
            ),
        )

    with jax.named_scope("regroup"):
        if paired:
            series = [decimated]
            other = [lax.ppermute(decimated, "src", [(0, 1), (1, 0)])]
        else:
            series = [whole(lax.all_gather(decimated, "src", axis=0))]
            other = []

    with jax.named_scope("spectra"):
        operands = series + [table_hi, table_lo, band, alive] + other
        spectra = pl.pallas_call(
            spectra_kernel,
            out_shape=shaped(rows, NFFT),
            in_specs=[VMEM] * len(operands),
            out_specs=VMEM,
            compiler_params=PARAMS,
        )(*operands)

    with jax.named_scope("correlate"):
        total = group * slots
        return pl.pallas_call(
            lambda *refs: correlate_kernel(slots, *refs),
            out_shape=shaped(total, rows, LAGS, dtype=bf16),
            in_specs=[VMEM] * 7,
            out_specs=HBM,
            scratch_shapes=[
                pltpu.VMEM((total, NFFT), jnp.float32),
                pltpu.VMEM((total * rows, NFFT), bf16),
                pltpu.VMEM((total, rows, LAGS), bf16),
                pltpu.SemaphoreType.DMA((total,)),
            ],
            compiler_params=PARAMS,
        )(spectra, gathered.reshape(-1, LANES), picks, table_hi, table_lo, band, lag)


def solution(mesh):
    in_specs = (P("blk", "src"), P(), P("blk"), P("blk", None))
    out_specs = P("src", "blk", None)
    return jax.shard_map(local, mesh=mesh, in_specs=in_specs, out_specs=out_specs, check_vma=False)
```

```python
import math

import jax
import jax.numpy as jnp
import numpy as np
from jax import lax
from jax.experimental import pallas as pl
from jax.experimental.pallas import tpu as pltpu
from jax.sharding import PartitionSpec as P

S = 512
NFFT = 1024
BINS = NFFT // 2
LAGS = 512
TAPS = 64
DEC = 20
HALF = 64
LANES = 128
SUBLANES = 8
PARTS = 2
EDGE = (TAPS - 1) // DEC
CHUNK = 640
CHUNK_OUT = CHUNK // DEC
VMEM_LIMIT = 20 * 1024 * 1024


def forward_table():
    phases = 2.0 * math.pi / NFFT * (np.outer(np.arange(S // 2), np.arange(BINS)) % NFFT)
    return np.concatenate([np.cos(phases), -np.sin(phases)], axis=1).astype(np.float32)


def split_table(table):
    high = table.astype(jnp.bfloat16)
    low = (table - high.astype(np.float32)).astype(jnp.bfloat16)
    return high, low


def band_table():
    bins = np.arange(3 * LANES)[:, None] - LANES
    return (np.abs(bins - np.arange(LANES)[None, :]) <= HALF).astype(jnp.bfloat16)


def lag_table():
    bins = np.arange(BINS)[:, None]
    shift = np.arange(LAGS)[None, :] - LAGS // 2
    phases = 2.0 * math.pi / NFFT * (bins * shift % NFFT)
    weight = np.where(bins == 0, 0.5, 1.0) / math.sqrt(BINS)
    table = np.concatenate([weight * np.cos(phases), -weight * np.sin(phases)], axis=0)
    return table.astype(np.float32).astype(jnp.bfloat16)


def split(value):
    high = value.astype(jnp.bfloat16)
    return high, (value - high.astype(jnp.float32)).astype(jnp.bfloat16)


def dot(a, b):
    return jnp.dot(a, b, preferred_element_type=jnp.float32)


def column(row):
    count = row.shape[1]
    at = [lax.broadcasted_iota(jnp.int32, (count, count), axis) for axis in range(2)]
    rows = jnp.broadcast_to(row, (count, count))
    return jnp.sum(jnp.where(at[0] == at[1], rows, 0.0), axis=1, keepdims=True)


def start_copies(pairs, sems):
    copies = [
        pltpu.make_async_copy(source, target, sems.at[at])
        for at, (source, target) in enumerate(pairs)
    ]
    for copy in copies:
        copy.start()
    return copies


def decimate_kernel(
    paired, raw_hbm, taps_hbm, alive_hbm, picks_hbm, out_ref, piece_ref,
    raw_ref, taps_ref, alive_ref, picks_ref, tiles_ref, sems,
):
    rows = raw_hbm.shape[0]
    chunks = raw_hbm.shape[1] // CHUNK
    slots = picks_ref.shape[1]
    per_tile = LANES // CHUNK_OUT
    tiles = -(-chunks // per_tile)
    pairs = [(taps_hbm, taps_ref), (alive_hbm, alive_ref), (picks_hbm, picks_ref)]
    for at in range(0, rows, SUBLANES):
        span = slice(at, at + SUBLANES)
        pairs.append((raw_hbm.at[span], raw_ref.at[span]))
    copies = start_copies(pairs, sems)
    copies[0].wait()
    taps = jnp.broadcast_to(taps_ref[...], (SUBLANES, TAPS))
    eight = jnp.concatenate([taps, jnp.zeros((SUBLANES, CHUNK - TAPS), jnp.float32)], axis=1)
    for _ in range(2):
        eight = pltpu.roll(eight, 0, 1, stride=DEC // 2, stride_axis=0)
    wrapped = jnp.concatenate(
        [eight]
        + [pltpu.roll(eight, DEC * at, 1) for at in range(SUBLANES, CHUNK_OUT, SUBLANES)],
        axis=0,
    )
    lane = lax.broadcasted_iota(jnp.int32, (CHUNK_OUT, CHUNK), 1)
    row = lax.broadcasted_iota(jnp.int32, (CHUNK_OUT, CHUNK), 0)
    main = jnp.where(lane >= DEC * row, wrapped, 0.0)
    rim = wrapped - main
    gap = jnp.zeros((LANES - 2 * CHUNK_OUT, CHUNK), jnp.float32)
    weights_hi, weights_lo = split(jnp.concatenate([main, gap, rim], axis=0).T)
    weights = jnp.concatenate([weights_hi, weights_lo], axis=1)

    def filtered(stacked):
        high, low = split(stacked)
        both = dot(high, weights)
        return both[:, :LANES] + both[:, LANES:] + dot(low, weights_hi)

    copies[1].wait()
    alive = jnp.broadcast_to(column(alive_ref[...].astype(jnp.float32)), (rows, LANES))
    for copy in copies[2:]:
        copy.wait()
    result = filtered(
        jnp.concatenate(
            [raw_ref[:, CHUNK * j : CHUNK * (j + 1)] for j in range(chunks)], axis=0
        )
    )
    part = [result[rows * j : rows * (j + 1)] * alive for j in range(chunks)]
    is_main = lax.broadcasted_iota(jnp.int32, (rows, LANES), 1) < LANES // 2
    values = []
    for first in range(0, chunks, per_tile):
        total = jnp.where(is_main, part[first], 0.0)
        for step in range(1, min(per_tile, chunks - first)):
            total = total + pltpu.roll(part[first + step], CHUNK_OUT * step, 1)
        if first + per_tile < chunks:
            total = total + jnp.where(is_main, 0.0, part[first + per_tile])
        values.append(total)
    rim = jnp.where(is_main, 0.0, part[0])
    for at, value in enumerate(values + [rim]):
        tiles_ref[rows * at : rows * (at + 1), :] = value
    if paired:
        packed = rim[:SUBLANES]
        for at in range(1, rows // SUBLANES):
            group = rim[SUBLANES * at : SUBLANES * (at + 1)]
            packed = packed + pltpu.roll(group, LANES - EDGE * at, 1)
        for at, value in enumerate(values):
            out_ref[rows * at : rows * (at + 1), :] = value
        out_ref[rows * tiles :, :] = packed
    else:
        for at, value in enumerate(values + [rim]):
            out_ref[:, LANES * at : LANES * (at + 1)] = value
    piece_ref[...] = jnp.zeros_like(piece_ref)
    rims = jnp.zeros((1, LANES), jnp.float32)
    for slot in range(slots):
        pick = picks_ref[0, slot]
        for tile in range(tiles):
            at = slot * tiles + tile
            piece_ref[at : at + 1, :] = tiles_ref[pl.ds(rows * tile + pick, 1), :]
        late = tiles_ref[pl.ds(rows * tiles + pick, 1), :]
        rims = rims + pltpu.roll(late, LANES - EDGE * slot if slot else 0, 1)
    piece_ref[slots * tiles : slots * tiles + 1, :] = rims


def spread_kernel(size, piece_ref, pieces_ref):
    row = lax.broadcasted_iota(jnp.int32, (SUBLANES, LANES), 0)
    rows = [
        jnp.broadcast_to(piece_ref[at : at + 1, :], (SUBLANES, LANES)) for at in range(size)
    ]
    eight = []
    for group in range(size):
        place = (row + SUBLANES * group) % size
        total = rows[0]
        for at in range(1, size):
            total = jnp.where(place == at, rows[at], total)
        eight.append(total)
    eight = jnp.concatenate(eight, axis=0)
    for at in range(0, pieces_ref.shape[0], SUBLANES * size):
        pieces_ref[at : at + SUBLANES * size, :] = eight


def unpack(packed, rows):
    tiles = [packed[at : at + rows] for at in range(0, packed.shape[0] - SUBLANES, rows)]
    rims = packed[packed.shape[0] - SUBLANES :]
    rim = jnp.concatenate(
        [rims]
        + [pltpu.roll(rims, EDGE * at, 1) for at in range(1, rows // SUBLANES)],
        axis=0,
    )
    lane = lax.broadcasted_iota(jnp.int32, rim.shape, 1)
    return tiles + [jnp.where(lane >= LANES - EDGE, rim, 0.0)]


def transform(early, late, table_hi, table_lo):
    rows = early.shape[0]
    high, low = split(jnp.concatenate([early, late], axis=0))
    first = dot(jnp.concatenate([high, low], axis=0), table_hi)
    both = first[: 2 * rows] + first[2 * rows :] + dot(high, table_lo)
    quarter = lax.broadcasted_iota(jnp.int32, (1, BINS), 1) & 3
    cosine = jnp.where(quarter == 0, 1.0, 0.0) - jnp.where(quarter == 2, 1.0, 0.0)
    sine = jnp.where(quarter == 1, 1.0, 0.0) - jnp.where(quarter == 3, 1.0, 0.0)
    early_re, early_im = both[:rows, :BINS], both[:rows, BINS:]
    late_re, late_im = both[rows:, :BINS], both[rows:, BINS:]
    return (
        early_re + cosine * late_re + sine * late_im,
        early_im + cosine * late_im - sine * late_re,
    )


def whitening(real_part, imag_part, band):
    rows = real_part.shape[0]
    tiles = BINS // LANES
    stacked = []
    for part in split(real_part * real_part + imag_part * imag_part):
        zero = jnp.zeros((rows, LANES), part.dtype)
        wide = jnp.concatenate([zero, part, zero], axis=1)
        stacked += [wide[:, LANES * tile : LANES * (tile + 3)] for tile in range(tiles)]
    banded = dot(jnp.concatenate(stacked, axis=0), band)
    step = rows * tiles
    summed = banded[:step] + banded[step:]
    total = jnp.concatenate(
        [summed[rows * tile : rows * (tile + 1)] for tile in range(tiles)], axis=1
    )
    bins = lax.broadcasted_iota(jnp.int32, (1, BINS), 1)
    count = jnp.minimum(bins + HALF, BINS - 1) - jnp.maximum(bins - HALF, 0) + 1
    return lax.rsqrt(total * (1.0 / count.astype(jnp.float32)) + 1e-06)


def correlate_kernel(
    paired, slots, pieces_ref, picks_ref, hi_ref, lo_ref, band_ref, lag_ref, *refs
):
    out_hbm, spectra_ref, cross_ref, out_ref, sems = refs[-5:]
    group = out_ref.shape[0] // slots
    rows = out_ref.shape[1]
    half = BINS // LANES
    own = lax.axis_index("blk")
    base = lax.axis_index("src") * group
    channel = lax.broadcasted_iota(jnp.int32, (rows, LANES), 0)
    picks = [
        channel == jnp.broadcast_to(picks_ref[:, slot : slot + 1], (rows, LANES))
        for slot in range(slots)
    ]
    tiles = S // 2 // LANES
    stride = slots * tiles + 1

    def entry(half_at, row):
        last = pieces_ref.shape[0] // stride - 1 - 2 * (base + group - 1) - half_at
        return pieces_ref[pl.ds(last * stride + row, group, stride=2 * stride), :]

    def halves(half_at):
        return [
            jnp.concatenate([entry(half_at, slot * tiles + tile) for slot in range(slots)], axis=0)
            for tile in range(tiles)
        ]

    early, late = halves(0), halves(1)
    rims = entry(1, slots * tiles)
    rims = jnp.concatenate(
        [rims] + [pltpu.roll(rims, EDGE * slot, 1) for slot in range(1, slots)], axis=0
    )
    lane = lax.broadcasted_iota(jnp.int32, rims.shape, 1)
    early[-1] = early[-1] + jnp.where(lane >= LANES - EDGE, rims, 0.0)
    early, late = [jnp.concatenate(columns, axis=1) for columns in (early, late)]
    if paired:
        mine, other = [unpack(ref[...], rows) for ref in refs[:2]]
        first = lax.axis_index("src") == 0
        before = [jnp.where(first, a, b) for a, b in zip(mine, other)]
        after = [jnp.where(first, b, a) for a, b in zip(mine, other)]
        before[-2] = before[-2] + after[-1]
        before, after = [jnp.concatenate(columns[:-1], axis=1) for columns in (before, after)]
    else:
        before, after = refs[0][:, : S // 2], refs[0][:, S // 2 :]
    real_part, imag_part = transform(
        jnp.concatenate([before, early], axis=0),
        jnp.concatenate([after, late], axis=0),
        hi_ref[...],
        lo_ref[...],
    )
    factor = whitening(real_part, imag_part, band_ref[...])
    spectra_ref[:, :BINS] = real_part * factor
    spectra_ref[:, BINS:] = imag_part * factor
    per_part = max(1, (group * slots) // PARTS)
    copies = []
    for part in range(group * slots // per_part):
        first = part * per_part
        for tile in range(half):
            re = slice(LANES * tile, LANES * (tile + 1))
            im = slice(BINS + LANES * tile, BINS + LANES * (tile + 1))
            rec_re, rec_im = spectra_ref[:rows, re], spectra_ref[:rows, im]
            for source in range(first, first + per_part):
                block, slot = divmod(source, slots)
                at = rows + slot * group + group - 1 - block
                src_re, src_im = spectra_ref[at : at + 1, re], spectra_ref[at : at + 1, im]
                where = slice(rows * source, rows * (source + 1))
                cross_ref[where, re] = (src_re * rec_re + src_im * rec_im).astype(jnp.bfloat16)
                cross_ref[where, im] = (src_re * rec_im - src_im * rec_re).astype(jnp.bfloat16)
        lagged = dot(cross_ref[rows * first : rows * (first + per_part), :], lag_ref[...])
        for source in range(first, first + per_part):
            block, slot = divmod(source, slots)
            keep = jnp.where(picks[slot] & (own == base + block), 0.0, 1.0)
            at = source - first
            kept = lagged[rows * at : rows * (at + 1)] * jnp.concatenate(
                [keep] * (LAGS // LANES), axis=1
            )
            out_ref[source] = kept.astype(jnp.bfloat16)
        span = pl.ds(first, per_part)
        copies.append(pltpu.make_async_copy(out_ref.at[span], out_hbm.at[span], sems.at[part]))
        copies[-1].start()
    for copy in copies:
        copy.wait()


HBM = pl.BlockSpec(memory_space=pltpu.HBM)
VMEM = pl.BlockSpec(memory_space=pltpu.VMEM)
PARAMS = pltpu.CompilerParams(vmem_limit_bytes=VMEM_LIMIT)


def in_hbm(*arrays):
    return [pltpu.with_memory_space_constraint(array, pltpu.HBM) for array in arrays]


def shaped(*shape, dtype=jnp.float32):
    return jax.ShapeDtypeStruct(shape, dtype)


def local(raw_records, fir_taps, alive_mask, source_index):
    src_count = lax.axis_size("src")
    blk_count = lax.axis_size("blk")
    rows, raw_count = raw_records.shape
    slots = source_index.shape[1]
    group = blk_count // src_count
    out_count = raw_count // DEC
    width = -(-out_count // LANES) * LANES + LANES
    chunks = raw_count // CHUNK
    paired = src_count == 2 and 2 * out_count == S
    bf16 = jnp.bfloat16
    forward_hi, forward_lo = split_table(forward_table())
    alive_row = alive_mask.reshape(1, rows)

    with jax.named_scope("decimate"):
        device_count = blk_count * src_count
        main = slots * (width - LANES)
        decimated, piece = pl.pallas_call(
            lambda *refs: decimate_kernel(paired, *refs),
            out_shape=(
                shaped(rows * (S // 2 // LANES) + SUBLANES, LANES)
                if paired
                else shaped(rows, width),
                shaped(SUBLANES, LANES),
            ),
            in_specs=[HBM] * 4,
            out_specs=(VMEM, VMEM),
            scratch_shapes=[
                pltpu.VMEM((rows, raw_count), jnp.float32),
                pltpu.VMEM((1, TAPS), jnp.float32),
                pltpu.VMEM((1, rows), jnp.int32),
                pltpu.SMEM((1, slots), jnp.int32),
                pltpu.VMEM((rows * (width // LANES), LANES), jnp.float32),
                pltpu.SemaphoreType.DMA((rows // SUBLANES + 3,)),
            ],
            compiler_params=PARAMS,
        )(*in_hbm(raw_records, fir_taps.reshape(1, TAPS), alive_row, source_index))

    def whole(shards):
        rims = jnp.pad(shards[1:, :, width - EDGE :], ((0, 1), (0, 0), (out_count - EDGE, 0)))
        series = shards[:, :, :out_count] + rims
        return series.transpose(1, 0, 2).reshape(shards.shape[1], S)

    with jax.named_scope("regroup"):
        if paired:
            own = [decimated, lax.ppermute(decimated, "src", [(0, 1), (1, 0)])]
        else:
            own = [whole(lax.all_gather(decimated, "src", axis=0))]

    with jax.named_scope("gather_sources"):
        size = main // LANES + 1
        pieces = pl.pallas_call(
            lambda *refs: spread_kernel(size, *refs),
            out_shape=shaped(device_count * size, LANES),
            in_specs=[VMEM],
            out_specs=VMEM,
            compiler_params=PARAMS,
        )(piece)
        gathered = lax.all_to_all(
            pieces.reshape(device_count, 1, main + LANES),
            ("blk", "src"),
            split_axis=0,
            concat_axis=0,
            tiled=True,
            axis_index_groups=[list(reversed(range(device_count)))],
        )
        if not paired:
            gathered = gathered[::-1]
            shards = gathered.reshape(blk_count, src_count, main + LANES)
            shards = shards.transpose(1, 0, 2)
            rims = [shards[:, :, main + LANES - EDGE * (slot + 1) :] for slot in range(slots)]
            rims = jnp.stack([rim[:, :, :EDGE] for rim in rims], axis=2)
            rims = jnp.pad(rims, ((0, 0), (0, 0), (0, 0), (LANES - EDGE, 0)))
            series = shards[:, :, :main].reshape(src_count, blk_count, slots, width - LANES)
            series = jnp.concatenate([series, rims], axis=3)
            series = whole(series.reshape(src_count, blk_count * slots, width))
            series = series.reshape(blk_count, slots, 2, S // 2).transpose(0, 2, 1, 3)
            series = series.reshape(blk_count * 2, 1, slots * S // 2)
            gathered = jnp.pad(series, ((0, 0), (0, 0), (0, LANES)))[::-1]

    with jax.named_scope("correlate"):
        total = group * slots
        return pl.pallas_call(
            lambda *refs: correlate_kernel(paired, slots, *refs),
            out_shape=shaped(total, rows, LAGS, dtype=bf16),
            in_specs=[VMEM] * (6 + len(own)),
            out_specs=HBM,
            scratch_shapes=[
                pltpu.VMEM((rows + total, NFFT), jnp.float32),
                pltpu.VMEM((total * rows, NFFT), bf16),
                pltpu.VMEM((total, rows, LAGS), bf16),
                pltpu.SemaphoreType.DMA((PARTS,)),
            ],
            compiler_params=PARAMS,
        )(
            gathered.reshape(-1, LANES),
            source_index,
            jnp.asarray(forward_hi),
            jnp.asarray(forward_lo),
            jnp.asarray(band_table()),
            jnp.asarray(lag_table()),
            *own,
        )


def solution(mesh):
    in_specs = (P("blk", "src"), P(), P("blk"), P("blk", None))
    out_specs = P("src", "blk", None)
    return jax.shard_map(local, mesh=mesh, in_specs=in_specs, out_specs=out_specs, check_vma=False)
```

```python
import math

import jax
import jax.numpy as jnp
import numpy as np
from jax import lax
from jax.experimental import pallas as pl
from jax.experimental.pallas import tpu as pltpu
from jax.sharding import PartitionSpec as P

S = 512
NFFT = 1024
BINS = NFFT // 2
LAGS = 512
TAPS = 64
DEC = 20
HALF = 64
LANES = 128
SUBLANES = 8
PARTS = 3
EDGE = (TAPS - 1) // DEC
CHUNK = 640
CHUNK_OUT = CHUNK // DEC
VMEM_LIMIT = 48 * 1024 * 1024


def forward_table():
    phases = 2.0 * math.pi / NFFT * (np.outer(np.arange(S // 2), np.arange(BINS)) % NFFT)
    return np.concatenate([np.cos(phases), -np.sin(phases)], axis=1).astype(np.float32)


def split_table(table):
    high = table.astype(jnp.bfloat16)
    low = (table - high.astype(np.float32)).astype(jnp.bfloat16)
    return high, low


def band_table():
    bins = np.arange(3 * LANES)[:, None] - LANES
    return (np.abs(bins - np.arange(LANES)[None, :]) <= HALF).astype(jnp.bfloat16)


def lag_table():
    bins = np.arange(BINS)[:, None]
    shift = np.arange(LAGS)[None, :] - LAGS // 2
    phases = 2.0 * math.pi / NFFT * (bins * shift % NFFT)
    weight = np.where(bins == 0, 0.5, 1.0) / math.sqrt(BINS)
    table = np.concatenate([weight * np.cos(phases), -weight * np.sin(phases)], axis=0)
    return table.astype(np.float32).astype(jnp.bfloat16)


def split(value):
    high = value.astype(jnp.bfloat16)
    return high, (value - high.astype(jnp.float32)).astype(jnp.bfloat16)


def dot(a, b):
    return jnp.dot(a, b, preferred_element_type=jnp.float32)


def column(row):
    count = row.shape[1]
    at = [lax.broadcasted_iota(jnp.int32, (count, count), axis) for axis in range(2)]
    rows = jnp.broadcast_to(row, (count, count))
    return jnp.sum(jnp.where(at[0] == at[1], rows, 0.0), axis=1, keepdims=True)


def start_copies(pairs, sems):
    copies = [
        pltpu.make_async_copy(source, target, sems.at[at])
        for at, (source, target) in enumerate(pairs)
    ]
    for copy in copies:
        copy.start()
    return copies


def decimate_kernel(
    paired, raw_hbm, taps_hbm, alive_hbm, picks_hbm, out_ref, pieces_hbm,
    raw_ref, taps_ref, alive_ref, picks_ref, source_ref, pieces_ref, sems,
):
    rows = raw_hbm.shape[0]
    chunks = raw_hbm.shape[1] // CHUNK
    slots = picks_ref.shape[1]
    per_tile = LANES // CHUNK_OUT
    tiles = -(-chunks // per_tile)
    pairs = [(taps_hbm, taps_ref), (picks_hbm, picks_ref), (alive_hbm, alive_ref)]
    for at in range(0, rows, SUBLANES):
        span = slice(at, at + SUBLANES)
        pairs.append((raw_hbm.at[span], raw_ref.at[span]))
    copies = start_copies(pairs, sems)
    source_ref[...] = jnp.zeros_like(source_ref)
    copies[0].wait()
    taps = jnp.broadcast_to(taps_ref[...], (SUBLANES, TAPS))
    eight = jnp.concatenate([taps, jnp.zeros((SUBLANES, CHUNK - TAPS), jnp.float32)], axis=1)
    for _ in range(2):
        eight = pltpu.roll(eight, 0, 1, stride=DEC // 2, stride_axis=0)
    wrapped = jnp.concatenate(
        [eight]
        + [pltpu.roll(eight, DEC * at, 1) for at in range(SUBLANES, CHUNK_OUT, SUBLANES)],
        axis=0,
    )
    lane = lax.broadcasted_iota(jnp.int32, (CHUNK_OUT, CHUNK), 1)
    row = lax.broadcasted_iota(jnp.int32, (CHUNK_OUT, CHUNK), 0)
    main = jnp.where(lane >= DEC * row, wrapped, 0.0)
    rim = wrapped - main
    gap = jnp.zeros((LANES - 2 * CHUNK_OUT, CHUNK), jnp.float32)
    weights_hi, weights_lo = split(jnp.concatenate([main, gap, rim], axis=0).T)
    weights = jnp.concatenate([weights_hi, weights_lo], axis=1)

    def filtered(stacked):
        high, low = split(stacked)
        both = dot(high, weights)
        return both[:, :LANES] + both[:, LANES:] + dot(low, weights_hi)

    for copy in copies[1:]:
        copy.wait()
    for slot in range(slots):
        pick = picks_ref[0, slot]
        alive = alive_ref[0, pick].astype(jnp.float32)
        for j in range(chunks):
            at = SUBLANES * slot + j
            span = slice(CHUNK * j, CHUNK * (j + 1))
            source_ref[at : at + 1, :] = raw_ref[pl.ds(pick, 1), span] * alive
    high, low = split(source_ref[...])
    count = slots * SUBLANES
    both = dot(jnp.concatenate([high, low], axis=0), weights)
    sources = both[:count, :LANES] + both[:count, LANES:] + both[count:, :LANES]
    lane = lax.broadcasted_iota(jnp.int32, (SUBLANES, LANES), 1)
    row = lax.broadcasted_iota(jnp.int32, (SUBLANES, LANES), 0)
    leads = row % per_tile == 0
    wraps = lane >= LANES - EDGE
    piece = []
    rims = jnp.zeros((1, LANES), jnp.float32)
    for slot in range(slots):
        source = sources[SUBLANES * slot : SUBLANES * (slot + 1)]
        placed = source
        for step in range(1, per_tile):
            rolled = pltpu.roll(source, CHUNK_OUT * step, 1)
            placed = jnp.where(row % per_tile == step, rolled, placed)
        own = jnp.where(leads & wraps, 0.0, placed)
        rim = placed - own
        for tile in range(tiles):
            first = per_tile * tile
            inside = jnp.where((row >= first) & (row < first + per_tile), own, 0.0)
            before = jnp.where(row == first + per_tile, rim, 0.0)
            piece.append(jnp.sum(inside + before, axis=0, keepdims=True))
        rims = rims + pltpu.roll(rim[:1], LANES - EDGE * slot if slot else 0, 1)
    piece.append(rims)
    size = len(piece)
    spread = [jnp.broadcast_to(value, (SUBLANES, LANES)) for value in piece]
    eight = []
    for group in range(size):
        place = (row + SUBLANES * group) % size
        total = spread[0]
        for at in range(1, size):
            total = jnp.where(place == at, spread[at], total)
        eight.append(total)
    eight = jnp.concatenate(eight, axis=0)
    for at in range(0, pieces_ref.shape[0], SUBLANES * size):
        pieces_ref[at : at + SUBLANES * size, :] = eight
    sending = pltpu.make_async_copy(pieces_ref, pieces_hbm, sems.at[0])
    sending.start()

    result = filtered(
        jnp.concatenate(
            [raw_ref[:, CHUNK * j : CHUNK * (j + 1)] for j in range(chunks)], axis=0
        )
    )
    part = [result[rows * j : rows * (j + 1)] for j in range(chunks)]
    is_main = lax.broadcasted_iota(jnp.int32, (rows, LANES), 1) < LANES // 2
    values = []
    for first in range(0, chunks, per_tile):
        total = jnp.where(is_main, part[first], 0.0)
        for step in range(1, min(per_tile, chunks - first)):
            total = total + pltpu.roll(part[first + step], CHUNK_OUT * step, 1)
        if first + per_tile < chunks:
            total = total + jnp.where(is_main, 0.0, part[first + per_tile])
        values.append(total)
    rim = jnp.where(is_main, 0.0, part[0])
    if paired:
        packed = rim[:SUBLANES]
        for at in range(1, rows // SUBLANES):
            group = rim[SUBLANES * at : SUBLANES * (at + 1)]
            packed = packed + pltpu.roll(group, LANES - EDGE * at, 1)
        for at, value in enumerate(values):
            out_ref[rows * at : rows * (at + 1), :] = value
        out_ref[rows * tiles :, :] = packed
    else:
        for at, value in enumerate(values + [rim]):
            out_ref[:, LANES * at : LANES * (at + 1)] = value
    sending.wait()


def unpack(packed, rows):
    tiles = [packed[at : at + rows] for at in range(0, packed.shape[0] - SUBLANES, rows)]
    rims = packed[packed.shape[0] - SUBLANES :]
    rim = jnp.concatenate(
        [rims]
        + [pltpu.roll(rims, EDGE * at, 1) for at in range(1, rows // SUBLANES)],
        axis=0,
    )
    lane = lax.broadcasted_iota(jnp.int32, rim.shape, 1)
    return tiles + [jnp.where(lane >= LANES - EDGE, rim, 0.0)]


def transform(early, late, table_hi, table_lo):
    rows = early.shape[0]
    high, low = split(jnp.concatenate([early, late], axis=0))
    first = dot(jnp.concatenate([high, low], axis=0), table_hi)
    both = first[: 2 * rows] + first[2 * rows :] + dot(high, table_lo)
    quarter = lax.broadcasted_iota(jnp.int32, (1, BINS), 1) & 3
    cosine = jnp.where(quarter == 0, 1.0, 0.0) - jnp.where(quarter == 2, 1.0, 0.0)
    sine = jnp.where(quarter == 1, 1.0, 0.0) - jnp.where(quarter == 3, 1.0, 0.0)
    early_re, early_im = both[:rows, :BINS], both[:rows, BINS:]
    late_re, late_im = both[rows:, :BINS], both[rows:, BINS:]
    return (
        early_re + cosine * late_re + sine * late_im,
        early_im + cosine * late_im - sine * late_re,
    )


def whitening(real_part, imag_part, band):
    rows = real_part.shape[0]
    tiles = BINS // LANES
    stacked = []
    for part in split(real_part * real_part + imag_part * imag_part):
        zero = jnp.zeros((rows, LANES), part.dtype)
        wide = jnp.concatenate([zero, part, zero], axis=1)
        stacked += [wide[:, LANES * tile : LANES * (tile + 3)] for tile in range(tiles)]
    banded = dot(jnp.concatenate(stacked, axis=0), band)
    step = rows * tiles
    summed = banded[:step] + banded[step:]
    total = jnp.concatenate(
        [summed[rows * tile : rows * (tile + 1)] for tile in range(tiles)], axis=1
    )
    bins = lax.broadcasted_iota(jnp.int32, (1, BINS), 1)
    count = jnp.minimum(bins + HALF, BINS - 1) - jnp.maximum(bins - HALF, 0) + 1
    return lax.rsqrt(total * (1.0 / count.astype(jnp.float32)) + 1e-06)


def prepare_kernel(
    _, alive_hbm, picks_hbm, fwd_hi_hbm, fwd_lo_hbm, band_hbm, lag_hbm,
    hi_ref, lo_ref, band_ref, lag_ref, alive_out, picks_out, alive_ref, picks_ref, sems,
):
    copies = start_copies(
        [
            (alive_hbm, alive_ref),
            (picks_hbm, picks_ref),
            (fwd_hi_hbm, hi_ref),
            (fwd_lo_hbm, lo_ref),
            (band_hbm, band_ref),
            (lag_hbm, lag_ref),
        ],
        sems,
    )
    for copy in copies[:2]:
        copy.wait()
    rows = alive_out.shape[0]
    alive_out[...] = jnp.broadcast_to(
        column(alive_ref[...].astype(jnp.float32)), (rows, LANES)
    )
    channel = lax.broadcasted_iota(jnp.int32, (rows, LANES), 0)
    for slot in range(picks_ref.shape[1]):
        pick = jnp.broadcast_to(picks_ref[:, slot : slot + 1], (rows, LANES))
        picks_out[slot] = jnp.where(channel == pick, 1.0, 0.0)
    for copy in copies[2:]:
        copy.wait()


def spectra_kernel(series_ref, hi_ref, lo_ref, band_ref, alive_ref, *refs):
    spectra_ref = refs[-1]
    rows = alive_ref.shape[0]
    half = S // 2
    if len(refs) > 1:
        mine, other = [unpack(ref[...], rows) for ref in (series_ref, refs[0])]
        first = lax.axis_index("src") == 0
        early = [jnp.where(first, a, b) for a, b in zip(mine, other)]
        late = [jnp.where(first, b, a) for a, b in zip(mine, other)]
        early[-2] = early[-2] + late[-1]
        early, late = [jnp.concatenate(tiles[:-1], axis=1) for tiles in (early, late)]
    else:
        early, late = series_ref[:, :half], series_ref[:, half:]
    real_part, imag_part = transform(early, late, hi_ref[...], lo_ref[...])
    factor = alive_ref[:, :1] * whitening(real_part, imag_part, band_ref[...])
    spectra_ref[:, :BINS] = real_part * factor
    spectra_ref[:, BINS:] = imag_part * factor


def part_bounds(total):
    ends = [3 * total // 8, 3 * total // 4, total]
    return [(a, b) for a, b in zip([0] + ends, ends) if b > a]


def correlate_kernel(
    slots, spectra_ref, pieces_ref, picks_ref, hi_ref, lo_ref, band_ref, lag_ref, out_hbm,
    series_ref, rims_ref, source_ref, cross_ref, out_ref, sems,
):
    rows = spectra_ref.shape[0]
    group = out_ref.shape[0] // slots
    half = BINS // LANES
    own = lax.axis_index("blk")
    base = lax.axis_index("src") * group
    tiles = S // 2 // LANES

    for slot in range(slots):
        for block in range(group):
            row = slice(slot * group + block, slot * group + block + 1)
            at = pieces_ref.shape[0] - 1 - 2 * (base + block)
            for tile in range(tiles):
                span = slice(LANES * (slot * tiles + tile), LANES * (slot * tiles + tile + 1))
                early = slice(LANES * tile, LANES * (tile + 1))
                late = slice(S // 2 + LANES * tile, S // 2 + LANES * (tile + 1))
                series_ref[row, early] = pieces_ref[at, :, span]
                series_ref[row, late] = pieces_ref[at - 1, :, span]
            rims_ref[row, :] = pieces_ref[at - 1, :, LANES * slots * tiles :]
    rims = jnp.concatenate(
        [
            pltpu.roll(rims_ref[slot * group : (slot + 1) * group, :], EDGE * slot, 1)
            for slot in range(slots)
        ],
        axis=0,
    )
    lane = lax.broadcasted_iota(jnp.int32, rims.shape, 1)
    seam = slice(S // 2 - LANES, S // 2)
    series_ref[:, seam] = series_ref[:, seam] + jnp.where(lane >= LANES - EDGE, rims, 0.0)
    early, late = series_ref[:, : S // 2], series_ref[:, S // 2 :]
    real_part, imag_part = transform(early, late, hi_ref[...], lo_ref[...])
    factor = whitening(real_part, imag_part, band_ref[...])
    source_ref[:, :BINS] = real_part * factor
    source_ref[:, BINS:] = imag_part * factor
    copies = []
    for part, (first, last) in enumerate(part_bounds(group * slots)):
        per_part = last - first
        for tile in range(half):
            re = slice(LANES * tile, LANES * (tile + 1))
            im = slice(BINS + LANES * tile, BINS + LANES * (tile + 1))
            rec_re, rec_im = spectra_ref[:, re], spectra_ref[:, im]
            for source in range(first, first + per_part):
                block, slot = divmod(source, slots)
                at = slot * group + block
                src_re, src_im = source_ref[at : at + 1, re], source_ref[at : at + 1, im]
                where = slice(rows * source, rows * (source + 1))
                cross_ref[where, re] = (src_re * rec_re + src_im * rec_im).astype(jnp.bfloat16)
                cross_ref[where, im] = (src_re * rec_im - src_im * rec_re).astype(jnp.bfloat16)
        lagged = dot(cross_ref[rows * first : rows * (first + per_part), :], lag_ref[...])
        for source in range(first, first + per_part):
            block, slot = divmod(source, slots)
            keep = 1.0 - jnp.where(own == base + block, 1.0, 0.0) * picks_ref[slot]
            at = source - first
            kept = lagged[rows * at : rows * (at + 1)] * jnp.concatenate(
                [keep] * (LAGS // LANES), axis=1
            )
            out_ref[source] = kept.astype(jnp.bfloat16)
        span = pl.ds(first, per_part)
        copies.append(pltpu.make_async_copy(out_ref.at[span], out_hbm.at[span], sems.at[part]))
        copies[-1].start()
    for copy in copies:
        copy.wait()


HBM = pl.BlockSpec(memory_space=pltpu.HBM)
VMEM = pl.BlockSpec(memory_space=pltpu.VMEM)
PARAMS = pltpu.CompilerParams(vmem_limit_bytes=VMEM_LIMIT)


def in_hbm(*arrays):
    return [pltpu.with_memory_space_constraint(array, pltpu.HBM) for array in arrays]


def shaped(*shape, dtype=jnp.float32):
    return jax.ShapeDtypeStruct(shape, dtype)


def local(raw_records, fir_taps, alive_mask, source_index):
    src_count = lax.axis_size("src")
    blk_count = lax.axis_size("blk")
    rows, raw_count = raw_records.shape
    slots = source_index.shape[1]
    group = blk_count // src_count
    out_count = raw_count // DEC
    width = -(-out_count // LANES) * LANES + LANES
    chunks = raw_count // CHUNK
    paired = src_count == 2 and 2 * out_count == S
    bf16 = jnp.bfloat16
    forward_hi, forward_lo = split_table(forward_table())
    alive_row = alive_mask.reshape(1, rows)

    with jax.named_scope("decimate"):
        device_count = blk_count * src_count
        main = slots * (width - LANES)
        decimated, pieces = pl.pallas_call(
            lambda *refs: decimate_kernel(paired, *refs),
            out_shape=(
                shaped(rows * (S // 2 // LANES) + SUBLANES, LANES)
                if paired
                else shaped(rows, width),
                shaped(device_count * (main // LANES + 1), LANES),
            ),
            in_specs=[HBM] * 4,
            out_specs=(VMEM, HBM),
            scratch_shapes=[
                pltpu.VMEM((rows, raw_count), jnp.float32),
                pltpu.VMEM((1, TAPS), jnp.float32),
                pltpu.SMEM((1, rows), jnp.int32),
                pltpu.SMEM((1, slots), jnp.int32),
                pltpu.VMEM((SUBLANES * slots, CHUNK), jnp.float32),
                pltpu.VMEM((device_count * (main // LANES + 1), LANES), jnp.float32),
                pltpu.SemaphoreType.DMA((rows // SUBLANES + 3,)),
            ],
            compiler_params=PARAMS,
        )(*in_hbm(raw_records, fir_taps.reshape(1, TAPS), alive_row, source_index))

    def whole(shards):
        rims = jnp.pad(shards[1:, :, width - EDGE :], ((0, 1), (0, 0), (out_count - EDGE, 0)))
        series = shards[:, :, :out_count] + rims
        return series.transpose(1, 0, 2).reshape(shards.shape[1], S)

    with jax.named_scope("gather_sources"):
        gathered = lax.all_to_all(
            pieces.reshape(device_count, 1, main + LANES),
            ("blk", "src"),
            split_axis=0,
            concat_axis=0,
            tiled=True,
            axis_index_groups=[list(reversed(range(device_count)))],
        )
        if not paired:
            gathered = gathered[::-1]
            shards = gathered.reshape(blk_count, src_count, main + LANES)
            shards = shards.transpose(1, 0, 2)
            rims = [shards[:, :, main + LANES - EDGE * (slot + 1) :] for slot in range(slots)]
            rims = jnp.stack([rim[:, :, :EDGE] for rim in rims], axis=2)
            rims = jnp.pad(rims, ((0, 0), (0, 0), (0, 0), (LANES - EDGE, 0)))
            series = shards[:, :, :main].reshape(src_count, blk_count, slots, width - LANES)
            series = jnp.concatenate([series, rims], axis=3)
            series = whole(series.reshape(src_count, blk_count * slots, width))
            series = series.reshape(blk_count, slots, 2, S // 2).transpose(0, 2, 1, 3)
            series = series.reshape(blk_count * 2, 1, slots * S // 2)
            gathered = jnp.pad(series, ((0, 0), (0, 0), (0, LANES)))[::-1]

    with jax.named_scope("prepare"):
        out_shape = (
            shaped(S // 2, NFFT, dtype=bf16),
            shaped(S // 2, NFFT, dtype=bf16),
            shaped(3 * LANES, LANES, dtype=bf16),
            shaped(NFFT, LAGS, dtype=bf16),
            shaped(rows, LANES),
            shaped(slots, rows, LANES),
        )
        table_hi, table_lo, band, lag, alive, picks = pl.pallas_call(
            prepare_kernel,
            out_shape=out_shape,
            in_specs=[VMEM] + [HBM] * 6,
            out_specs=(VMEM,) * len(out_shape),
            scratch_shapes=[
                pltpu.VMEM((1, rows), jnp.int32),
                pltpu.VMEM((1, slots), jnp.int32),
                pltpu.SemaphoreType.DMA((6,)),
            ],
            compiler_params=PARAMS,
            cost_estimate=pl.CostEstimate(
                flops=0, bytes_accessed=4 * S * NFFT, transcendentals=0
            ),
        )(
            decimated,
            *in_hbm(
                alive_row,
                source_index,
                jnp.asarray(forward_hi),
                jnp.asarray(forward_lo),
                jnp.asarray(band_table()),
                jnp.asarray(lag_table()),
            ),
        )

    with jax.named_scope("regroup"):
        if paired:
            series = [decimated]
            other = [lax.ppermute(decimated, "src", [(0, 1), (1, 0)])]
        else:
            series = [whole(lax.all_gather(decimated, "src", axis=0))]
            other = []

    with jax.named_scope("spectra"):
        operands = series + [table_hi, table_lo, band, alive] + other
        spectra = pl.pallas_call(
            spectra_kernel,
            out_shape=shaped(rows, NFFT),
            in_specs=[VMEM] * len(operands),
            out_specs=VMEM,
            compiler_params=PARAMS,
        )(*operands)

    with jax.named_scope("correlate"):
        total = group * slots
        return pl.pallas_call(
            lambda *refs: correlate_kernel(slots, *refs),
            out_shape=shaped(total, rows, LAGS, dtype=bf16),
            in_specs=[VMEM] * 7,
            out_specs=HBM,
            scratch_shapes=[
                pltpu.VMEM((total, S), jnp.float32),
                pltpu.VMEM((total, LANES), jnp.float32),
                pltpu.VMEM((total, NFFT), jnp.float32),
                pltpu.VMEM((total * rows, NFFT), bf16),
                pltpu.VMEM((total, rows, LAGS), bf16),
                pltpu.SemaphoreType.DMA((PARTS,)),
            ],
            compiler_params=PARAMS,
        )(spectra, gathered, picks, table_hi, table_lo, band, lag)


def solution(mesh):
    in_specs = (P("blk", "src"), P(), P("blk"), P("blk", None))
    out_specs = P("src", "blk", None)
    return jax.shard_map(local, mesh=mesh, in_specs=in_specs, out_specs=out_specs, check_vma=False)
```

```python
import math

import jax
import jax.numpy as jnp
import numpy as np
from jax import lax
from jax.experimental import pallas as pl
from jax.experimental.pallas import tpu as pltpu
from jax.sharding import PartitionSpec as P

S = 512
NFFT = 1024
BINS = NFFT // 2
LAGS = 512
TAPS = 64
DEC = 20
HALF = 64
LANES = 128
SUBLANES = 8
PARTS = 4
EDGE = (TAPS - 1) // DEC
CHUNK = 640
CHUNK_OUT = CHUNK // DEC
VMEM_LIMIT = 48 * 1024 * 1024


def forward_table():
    phases = 2.0 * math.pi / NFFT * (np.outer(np.arange(S // 2), np.arange(BINS)) % NFFT)
    return np.concatenate([np.cos(phases), -np.sin(phases)], axis=1).astype(np.float32)


def split_table(table):
    high = table.astype(jnp.bfloat16)
    low = (table - high.astype(np.float32)).astype(jnp.bfloat16)
    return high, low


def band_table():
    bins = np.arange(3 * LANES)[:, None] - LANES
    return (np.abs(bins - np.arange(LANES)[None, :]) <= HALF).astype(jnp.bfloat16)


def lag_table():
    bins = np.arange(BINS)[:, None]
    shift = np.arange(LAGS)[None, :] - LAGS // 2
    phases = 2.0 * math.pi / NFFT * (bins * shift % NFFT)
    weight = np.where(bins == 0, 0.5, 1.0) / math.sqrt(BINS)
    table = np.concatenate([weight * np.cos(phases), -weight * np.sin(phases)], axis=0)
    return table.astype(np.float32).astype(jnp.bfloat16)


def split(value):
    high = value.astype(jnp.bfloat16)
    return high, (value - high.astype(jnp.float32)).astype(jnp.bfloat16)


def dot(a, b):
    return jnp.dot(a, b, preferred_element_type=jnp.float32)


def column(row):
    count = row.shape[1]
    at = [lax.broadcasted_iota(jnp.int32, (count, count), axis) for axis in range(2)]
    rows = jnp.broadcast_to(row, (count, count))
    return jnp.sum(jnp.where(at[0] == at[1], rows, 0.0), axis=1, keepdims=True)


def start_copies(pairs, sems):
    copies = [
        pltpu.make_async_copy(source, target, sems.at[at])
        for at, (source, target) in enumerate(pairs)
    ]
    for copy in copies:
        copy.start()
    return copies


def decimate_kernel(
    paired, raw_hbm, taps_hbm, alive_hbm, picks_hbm, out_ref, pieces_hbm,
    raw_ref, taps_ref, alive_ref, picks_ref, source_ref, pieces_ref, sems,
):
    rows = raw_hbm.shape[0]
    chunks = raw_hbm.shape[1] // CHUNK
    slots = picks_ref.shape[1]
    per_tile = LANES // CHUNK_OUT
    tiles = -(-chunks // per_tile)
    pairs = [(taps_hbm, taps_ref), (picks_hbm, picks_ref), (alive_hbm, alive_ref)]
    for at in range(0, rows, SUBLANES):
        span = slice(at, at + SUBLANES)
        pairs.append((raw_hbm.at[span], raw_ref.at[span]))
    copies = start_copies(pairs, sems)
    source_ref[...] = jnp.zeros_like(source_ref)
    copies[0].wait()
    taps = jnp.broadcast_to(taps_ref[...], (SUBLANES, TAPS))
    eight = jnp.concatenate([taps, jnp.zeros((SUBLANES, CHUNK - TAPS), jnp.float32)], axis=1)
    for _ in range(2):
        eight = pltpu.roll(eight, 0, 1, stride=DEC // 2, stride_axis=0)
    wrapped = jnp.concatenate(
        [eight]
        + [pltpu.roll(eight, DEC * at, 1) for at in range(SUBLANES, CHUNK_OUT, SUBLANES)],
        axis=0,
    )
    lane = lax.broadcasted_iota(jnp.int32, (CHUNK_OUT, CHUNK), 1)
    row = lax.broadcasted_iota(jnp.int32, (CHUNK_OUT, CHUNK), 0)
    main = jnp.where(lane >= DEC * row, wrapped, 0.0)
    rim = wrapped - main
    gap = jnp.zeros((LANES - 2 * CHUNK_OUT, CHUNK), jnp.float32)
    weights_hi, weights_lo = split(jnp.concatenate([main, gap, rim], axis=0).T)
    weights = jnp.concatenate([weights_hi, weights_lo], axis=1)

    def filtered(stacked):
        high, low = split(stacked)
        both = dot(high, weights)
        return both[:, :LANES] + both[:, LANES:] + dot(low, weights_hi)

    for copy in copies[1:]:
        copy.wait()
    for slot in range(slots):
        pick = picks_ref[0, slot]
        alive = alive_ref[0, pick].astype(jnp.float32)
        for j in range(chunks):
            at = SUBLANES * slot + j
            span = slice(CHUNK * j, CHUNK * (j + 1))
            source_ref[at : at + 1, :] = raw_ref[pl.ds(pick, 1), span] * alive
    high, low = split(source_ref[...])
    count = slots * SUBLANES
    both = dot(jnp.concatenate([high, low], axis=0), weights)
    sources = both[:count, :LANES] + both[:count, LANES:] + both[count:, :LANES]
    lane = lax.broadcasted_iota(jnp.int32, (SUBLANES, LANES), 1)
    row = lax.broadcasted_iota(jnp.int32, (SUBLANES, LANES), 0)
    leads = row % per_tile == 0
    wraps = lane >= LANES - EDGE
    piece = []
    rims = jnp.zeros((1, LANES), jnp.float32)
    for slot in range(slots):
        source = sources[SUBLANES * slot : SUBLANES * (slot + 1)]
        placed = source
        for step in range(1, per_tile):
            rolled = pltpu.roll(source, CHUNK_OUT * step, 1)
            placed = jnp.where(row % per_tile == step, rolled, placed)
        own = jnp.where(leads & wraps, 0.0, placed)
        rim = placed - own
        for tile in range(tiles):
            first = per_tile * tile
            inside = jnp.where((row >= first) & (row < first + per_tile), own, 0.0)
            before = jnp.where(row == first + per_tile, rim, 0.0)
            piece.append(jnp.sum(inside + before, axis=0, keepdims=True))
        rims = rims + pltpu.roll(rim[:1], LANES - EDGE * slot if slot else 0, 1)
    piece.append(rims)
    size = len(piece)
    spread = [jnp.broadcast_to(value, (SUBLANES, LANES)) for value in piece]
    eight = []
    for group in range(size):
        place = (row + SUBLANES * group) % size
        total = spread[0]
        for at in range(1, size):
            total = jnp.where(place == at, spread[at], total)
        eight.append(total)
    eight = jnp.concatenate(eight, axis=0)
    for at in range(0, pieces_ref.shape[0], SUBLANES * size):
        pieces_ref[at : at + SUBLANES * size, :] = eight
    sending = pltpu.make_async_copy(pieces_ref, pieces_hbm, sems.at[0])
    sending.start()

    result = filtered(
        jnp.concatenate(
            [raw_ref[:, CHUNK * j : CHUNK * (j + 1)] for j in range(chunks)], axis=0
        )
    )
    part = [result[rows * j : rows * (j + 1)] for j in range(chunks)]
    is_main = lax.broadcasted_iota(jnp.int32, (rows, LANES), 1) < LANES // 2
    values = []
    for first in range(0, chunks, per_tile):
        total = jnp.where(is_main, part[first], 0.0)
        for step in range(1, min(per_tile, chunks - first)):
            total = total + pltpu.roll(part[first + step], CHUNK_OUT * step, 1)
        if first + per_tile < chunks:
            total = total + jnp.where(is_main, 0.0, part[first + per_tile])
        values.append(total)
    rim = jnp.where(is_main, 0.0, part[0])
    if paired:
        packed = rim[:SUBLANES]
        for at in range(1, rows // SUBLANES):
            group = rim[SUBLANES * at : SUBLANES * (at + 1)]
            packed = packed + pltpu.roll(group, LANES - EDGE * at, 1)
        for at, value in enumerate(values):
            out_ref[rows * at : rows * (at + 1), :] = value
        out_ref[rows * tiles :, :] = packed
    else:
        for at, value in enumerate(values + [rim]):
            out_ref[:, LANES * at : LANES * (at + 1)] = value
    sending.wait()


def unpack(packed, rows):
    tiles = [packed[at : at + rows] for at in range(0, packed.shape[0] - SUBLANES, rows)]
    rims = packed[packed.shape[0] - SUBLANES :]
    rim = jnp.concatenate(
        [rims]
        + [pltpu.roll(rims, EDGE * at, 1) for at in range(1, rows // SUBLANES)],
        axis=0,
    )
    lane = lax.broadcasted_iota(jnp.int32, rim.shape, 1)
    return tiles + [jnp.where(lane >= LANES - EDGE, rim, 0.0)]


def transform(early, late, table_hi, table_lo):
    rows = early.shape[0]
    high, low = split(jnp.concatenate([early, late], axis=0))
    first = dot(jnp.concatenate([high, low], axis=0), table_hi)
    both = first[: 2 * rows] + first[2 * rows :] + dot(high, table_lo)
    quarter = lax.broadcasted_iota(jnp.int32, (1, BINS), 1) & 3
    cosine = jnp.where(quarter == 0, 1.0, 0.0) - jnp.where(quarter == 2, 1.0, 0.0)
    sine = jnp.where(quarter == 1, 1.0, 0.0) - jnp.where(quarter == 3, 1.0, 0.0)
    early_re, early_im = both[:rows, :BINS], both[:rows, BINS:]
    late_re, late_im = both[rows:, :BINS], both[rows:, BINS:]
    return (
        early_re + cosine * late_re + sine * late_im,
        early_im + cosine * late_im - sine * late_re,
    )


def whitening(real_part, imag_part, band):
    rows = real_part.shape[0]
    tiles = BINS // LANES
    stacked = []
    for part in split(real_part * real_part + imag_part * imag_part):
        zero = jnp.zeros((rows, LANES), part.dtype)
        wide = jnp.concatenate([zero, part, zero], axis=1)
        stacked += [wide[:, LANES * tile : LANES * (tile + 3)] for tile in range(tiles)]
    banded = dot(jnp.concatenate(stacked, axis=0), band)
    step = rows * tiles
    summed = banded[:step] + banded[step:]
    total = jnp.concatenate(
        [summed[rows * tile : rows * (tile + 1)] for tile in range(tiles)], axis=1
    )
    bins = lax.broadcasted_iota(jnp.int32, (1, BINS), 1)
    count = jnp.minimum(bins + HALF, BINS - 1) - jnp.maximum(bins - HALF, 0) + 1
    return lax.rsqrt(total * (1.0 / count.astype(jnp.float32)) + 1e-06)


def prepare_kernel(
    _, alive_hbm, picks_hbm, fwd_hi_hbm, fwd_lo_hbm, band_hbm, lag_hbm,
    hi_ref, lo_ref, band_ref, lag_ref, alive_out, picks_out, alive_ref, picks_ref, sems,
):
    copies = start_copies(
        [
            (alive_hbm, alive_ref),
            (picks_hbm, picks_ref),
            (fwd_hi_hbm, hi_ref),
            (fwd_lo_hbm, lo_ref),
            (band_hbm, band_ref),
            (lag_hbm, lag_ref),
        ],
        sems,
    )
    for copy in copies[:2]:
        copy.wait()
    rows = alive_out.shape[0]
    alive_out[...] = jnp.broadcast_to(
        column(alive_ref[...].astype(jnp.float32)), (rows, LANES)
    )
    channel = lax.broadcasted_iota(jnp.int32, (rows, LANES), 0)
    for slot in range(picks_ref.shape[1]):
        pick = jnp.broadcast_to(picks_ref[:, slot : slot + 1], (rows, LANES))
        picks_out[slot] = jnp.where(channel == pick, 1.0, 0.0)
    for copy in copies[2:]:
        copy.wait()


def spectra_kernel(series_ref, hi_ref, lo_ref, band_ref, alive_ref, *refs):
    spectra_ref = refs[-1]
    rows = alive_ref.shape[0]
    half = S // 2
    if len(refs) > 1:
        mine, other = [unpack(ref[...], rows) for ref in (series_ref, refs[0])]
        first = lax.axis_index("src") == 0
        early = [jnp.where(first, a, b) for a, b in zip(mine, other)]
        late = [jnp.where(first, b, a) for a, b in zip(mine, other)]
        early[-2] = early[-2] + late[-1]
        early, late = [jnp.concatenate(tiles[:-1], axis=1) for tiles in (early, late)]
    else:
        early, late = series_ref[:, :half], series_ref[:, half:]
    real_part, imag_part = transform(early, late, hi_ref[...], lo_ref[...])
    factor = alive_ref[:, :1] * whitening(real_part, imag_part, band_ref[...])
    spectra_ref[:, :BINS] = real_part * factor
    spectra_ref[:, BINS:] = imag_part * factor


def correlate_kernel(
    slots, spectra_ref, pieces_ref, picks_ref, hi_ref, lo_ref, band_ref, lag_ref, out_hbm,
    series_ref, rims_ref, source_ref, cross_ref, out_ref, sems,
):
    rows = spectra_ref.shape[0]
    group = out_ref.shape[0] // slots
    half = BINS // LANES
    own = lax.axis_index("blk")
    base = lax.axis_index("src") * group
    tiles = S // 2 // LANES

    for slot in range(slots):
        for block in range(group):
            row = slice(slot * group + block, slot * group + block + 1)
            at = pieces_ref.shape[0] - 1 - 2 * (base + block)
            for tile in range(tiles):
                span = slice(LANES * (slot * tiles + tile), LANES * (slot * tiles + tile + 1))
                early = slice(LANES * tile, LANES * (tile + 1))
                late = slice(S // 2 + LANES * tile, S // 2 + LANES * (tile + 1))
                series_ref[row, early] = pieces_ref[at, :, span]
                series_ref[row, late] = pieces_ref[at - 1, :, span]
            rims_ref[row, :] = pieces_ref[at - 1, :, LANES * slots * tiles :]
    rims = jnp.concatenate(
        [
            pltpu.roll(rims_ref[slot * group : (slot + 1) * group, :], EDGE * slot, 1)
            for slot in range(slots)
        ],
        axis=0,
    )
    lane = lax.broadcasted_iota(jnp.int32, rims.shape, 1)
    seam = slice(S // 2 - LANES, S // 2)
    series_ref[:, seam] = series_ref[:, seam] + jnp.where(lane >= LANES - EDGE, rims, 0.0)
    early, late = series_ref[:, : S // 2], series_ref[:, S // 2 :]
    real_part, imag_part = transform(early, late, hi_ref[...], lo_ref[...])
    factor = whitening(real_part, imag_part, band_ref[...])
    source_ref[:, :BINS] = real_part * factor
    source_ref[:, BINS:] = imag_part * factor
    total = group * slots
    for tile in range(half):
        re = slice(LANES * tile, LANES * (tile + 1))
        im = slice(BINS + LANES * tile, BINS + LANES * (tile + 1))
        rec_re, rec_im = spectra_ref[:, re], spectra_ref[:, im]
        for source in range(total):
            block, slot = divmod(source, slots)
            at = slot * group + block
            src_re, src_im = source_ref[at : at + 1, re], source_ref[at : at + 1, im]
            where = slice(rows * source, rows * (source + 1))
            cross_ref[where, re] = (src_re * rec_re + src_im * rec_im).astype(jnp.bfloat16)
            cross_ref[where, im] = (src_re * rec_im - src_im * rec_re).astype(jnp.bfloat16)
    lagged = dot(cross_ref[...], lag_ref[...])
    copies = []
    per_part = max(1, total // PARTS)
    for part in range(total // per_part):
        first = part * per_part
        for source in range(first, first + per_part):
            block, slot = divmod(source, slots)
            keep = 1.0 - jnp.where(own == base + block, 1.0, 0.0) * picks_ref[slot]
            kept = lagged[rows * source : rows * (source + 1)] * jnp.concatenate(
                [keep] * (LAGS // LANES), axis=1
            )
            out_ref[source] = kept.astype(jnp.bfloat16)
        span = pl.ds(first, per_part)
        copies.append(pltpu.make_async_copy(out_ref.at[span], out_hbm.at[span], sems.at[part]))
        copies[-1].start()
    for copy in copies:
        copy.wait()


HBM = pl.BlockSpec(memory_space=pltpu.HBM)
VMEM = pl.BlockSpec(memory_space=pltpu.VMEM)
PARAMS = pltpu.CompilerParams(vmem_limit_bytes=VMEM_LIMIT)


def in_hbm(*arrays):
    return [pltpu.with_memory_space_constraint(array, pltpu.HBM) for array in arrays]


def shaped(*shape, dtype=jnp.float32):
    return jax.ShapeDtypeStruct(shape, dtype)


def local(raw_records, fir_taps, alive_mask, source_index):
    src_count = lax.axis_size("src")
    blk_count = lax.axis_size("blk")
    rows, raw_count = raw_records.shape
    slots = source_index.shape[1]
    group = blk_count // src_count
    out_count = raw_count // DEC
    width = -(-out_count // LANES) * LANES + LANES
    chunks = raw_count // CHUNK
    paired = src_count == 2 and 2 * out_count == S
    bf16 = jnp.bfloat16
    forward_hi, forward_lo = split_table(forward_table())
    alive_row = alive_mask.reshape(1, rows)

    with jax.named_scope("decimate"):
        device_count = blk_count * src_count
        main = slots * (width - LANES)
        decimated, pieces = pl.pallas_call(
            lambda *refs: decimate_kernel(paired, *refs),
            out_shape=(
                shaped(rows * (S // 2 // LANES) + SUBLANES, LANES)
                if paired
                else shaped(rows, width),
                shaped(device_count * (main // LANES + 1), LANES),
            ),
            in_specs=[HBM] * 4,
            out_specs=(VMEM, HBM),
            scratch_shapes=[
                pltpu.VMEM((rows, raw_count), jnp.float32),
                pltpu.VMEM((1, TAPS), jnp.float32),
                pltpu.SMEM((1, rows), jnp.int32),
                pltpu.SMEM((1, slots), jnp.int32),
                pltpu.VMEM((SUBLANES * slots, CHUNK), jnp.float32),
                pltpu.VMEM((device_count * (main // LANES + 1), LANES), jnp.float32),
                pltpu.SemaphoreType.DMA((rows // SUBLANES + 3,)),
            ],
            compiler_params=PARAMS,
        )(*in_hbm(raw_records, fir_taps.reshape(1, TAPS), alive_row, source_index))

    def whole(shards):
        rims = jnp.pad(shards[1:, :, width - EDGE :], ((0, 1), (0, 0), (out_count - EDGE, 0)))
        series = shards[:, :, :out_count] + rims
        return series.transpose(1, 0, 2).reshape(shards.shape[1], S)

    with jax.named_scope("gather_sources"):
        gathered = lax.all_to_all(
            pieces.reshape(device_count, 1, main + LANES),
            ("blk", "src"),
            split_axis=0,
            concat_axis=0,
            tiled=True,
            axis_index_groups=[list(reversed(range(device_count)))],
        )
        if not paired:
            gathered = gathered[::-1]
            shards = gathered.reshape(blk_count, src_count, main + LANES)
            shards = shards.transpose(1, 0, 2)
            rims = [shards[:, :, main + LANES - EDGE * (slot + 1) :] for slot in range(slots)]
            rims = jnp.stack([rim[:, :, :EDGE] for rim in rims], axis=2)
            rims = jnp.pad(rims, ((0, 0), (0, 0), (0, 0), (LANES - EDGE, 0)))
            series = shards[:, :, :main].reshape(src_count, blk_count, slots, width - LANES)
            series = jnp.concatenate([series, rims], axis=3)
            series = whole(series.reshape(src_count, blk_count * slots, width))
            series = series.reshape(blk_count, slots, 2, S // 2).transpose(0, 2, 1, 3)
            series = series.reshape(blk_count * 2, 1, slots * S // 2)
            gathered = jnp.pad(series, ((0, 0), (0, 0), (0, LANES)))[::-1]

    with jax.named_scope("prepare"):
        out_shape = (
            shaped(S // 2, NFFT, dtype=bf16),
            shaped(S // 2, NFFT, dtype=bf16),
            shaped(3 * LANES, LANES, dtype=bf16),
            shaped(NFFT, LAGS, dtype=bf16),
            shaped(rows, LANES),
            shaped(slots, rows, LANES),
        )
        table_hi, table_lo, band, lag, alive, picks = pl.pallas_call(
            prepare_kernel,
            out_shape=out_shape,
            in_specs=[VMEM] + [HBM] * 6,
            out_specs=(VMEM,) * len(out_shape),
            scratch_shapes=[
                pltpu.VMEM((1, rows), jnp.int32),
                pltpu.VMEM((1, slots), jnp.int32),
                pltpu.SemaphoreType.DMA((6,)),
            ],
            compiler_params=PARAMS,
            cost_estimate=pl.CostEstimate(
                flops=0, bytes_accessed=4 * S * NFFT, transcendentals=0
            ),
        )(
            decimated,
            *in_hbm(
                alive_row,
                source_index,
                jnp.asarray(forward_hi),
                jnp.asarray(forward_lo),
                jnp.asarray(band_table()),
                jnp.asarray(lag_table()),
            ),
        )

    with jax.named_scope("regroup"):
        if paired:
            series = [decimated]
            other = [lax.ppermute(decimated, "src", [(0, 1), (1, 0)])]
        else:
            series = [whole(lax.all_gather(decimated, "src", axis=0))]
            other = []

    with jax.named_scope("spectra"):
        operands = series + [table_hi, table_lo, band, alive] + other
        spectra = pl.pallas_call(
            spectra_kernel,
            out_shape=shaped(rows, NFFT),
            in_specs=[VMEM] * len(operands),
            out_specs=VMEM,
            compiler_params=PARAMS,
        )(*operands)

    with jax.named_scope("correlate"):
        total = group * slots
        return pl.pallas_call(
            lambda *refs: correlate_kernel(slots, *refs),
            out_shape=shaped(total, rows, LAGS, dtype=bf16),
            in_specs=[VMEM] * 7,
            out_specs=HBM,
            scratch_shapes=[
                pltpu.VMEM((total, S), jnp.float32),
                pltpu.VMEM((total, LANES), jnp.float32),
                pltpu.VMEM((total, NFFT), jnp.float32),
                pltpu.VMEM((total * rows, NFFT), bf16),
                pltpu.VMEM((total, rows, LAGS), bf16),
                pltpu.SemaphoreType.DMA((PARTS,)),
            ],
            compiler_params=PARAMS,
        )(spectra, gathered, picks, table_hi, table_lo, band, lag)


def solution(mesh):
    in_specs = (P("blk", "src"), P(), P("blk"), P("blk", None))
    out_specs = P("src", "blk", None)
    return jax.shard_map(local, mesh=mesh, in_specs=in_specs, out_specs=out_specs, check_vma=False)
```

```python
import math

import jax
import jax.numpy as jnp
import numpy as np
from jax import lax
from jax.experimental import pallas as pl
from jax.experimental.pallas import tpu as pltpu
from jax.sharding import PartitionSpec as P

S = 512
NFFT = 1024
BINS = NFFT // 2
LAGS = 512
TAPS = 64
DEC = 20
HALF = 64
LANES = 128
SUBLANES = 8
PARTS = 4
EDGE = (TAPS - 1) // DEC
CHUNK = 640
CHUNK_OUT = CHUNK // DEC
VMEM_LIMIT = 48 * 1024 * 1024


def forward_table():
    phases = 2.0 * math.pi / NFFT * (np.outer(np.arange(S // 2), np.arange(BINS)) % NFFT)
    return np.concatenate([np.cos(phases), -np.sin(phases)], axis=1).astype(np.float32)


def split_table(table):
    high = table.astype(jnp.bfloat16)
    low = (table - high.astype(np.float32)).astype(jnp.bfloat16)
    return high, low


def band_table():
    bins = np.arange(3 * LANES)[:, None] - LANES
    return (np.abs(bins - np.arange(LANES)[None, :]) <= HALF).astype(jnp.bfloat16)


def lag_table():
    bins = np.arange(BINS)[:, None]
    shift = np.arange(LAGS)[None, :] - LAGS // 2
    phases = 2.0 * math.pi / NFFT * (bins * shift % NFFT)
    weight = np.where(bins == 0, 0.5, 1.0) / math.sqrt(BINS)
    table = np.concatenate([weight * np.cos(phases), -weight * np.sin(phases)], axis=0)
    return table.astype(np.float32).astype(jnp.bfloat16)


def split(value):
    high = value.astype(jnp.bfloat16)
    return high, (value - high.astype(jnp.float32)).astype(jnp.bfloat16)


def dot(a, b):
    return jnp.dot(a, b, preferred_element_type=jnp.float32)


def column(row):
    count = row.shape[1]
    at = [lax.broadcasted_iota(jnp.int32, (count, count), axis) for axis in range(2)]
    rows = jnp.broadcast_to(row, (count, count))
    return jnp.sum(jnp.where(at[0] == at[1], rows, 0.0), axis=1, keepdims=True)


def start_copies(pairs, sems):
    copies = [
        pltpu.make_async_copy(source, target, sems.at[at])
        for at, (source, target) in enumerate(pairs)
    ]
    for copy in copies:
        copy.start()
    return copies


def decimate_kernel(
    paired, raw_hbm, taps_hbm, alive_hbm, picks_hbm, out_ref, pieces_hbm,
    raw_ref, taps_ref, alive_ref, picks_ref, source_ref, pieces_ref, sems,
):
    rows = raw_hbm.shape[0]
    chunks = raw_hbm.shape[1] // CHUNK
    slots = picks_ref.shape[1]
    per_tile = LANES // CHUNK_OUT
    tiles = -(-chunks // per_tile)
    pairs = [(taps_hbm, taps_ref), (picks_hbm, picks_ref), (alive_hbm, alive_ref)]
    for at in range(0, rows, SUBLANES):
        span = slice(at, at + SUBLANES)
        pairs.append((raw_hbm.at[span], raw_ref.at[span]))
    copies = start_copies(pairs, sems)
    source_ref[...] = jnp.zeros_like(source_ref)
    copies[0].wait()
    taps = jnp.broadcast_to(taps_ref[...], (SUBLANES, TAPS))
    eight = jnp.concatenate([taps, jnp.zeros((SUBLANES, CHUNK - TAPS), jnp.float32)], axis=1)
    for _ in range(2):
        eight = pltpu.roll(eight, 0, 1, stride=DEC // 2, stride_axis=0)
    wrapped = jnp.concatenate(
        [eight]
        + [pltpu.roll(eight, DEC * at, 1) for at in range(SUBLANES, CHUNK_OUT, SUBLANES)],
        axis=0,
    )
    lane = lax.broadcasted_iota(jnp.int32, (CHUNK_OUT, CHUNK), 1)
    row = lax.broadcasted_iota(jnp.int32, (CHUNK_OUT, CHUNK), 0)
    main = jnp.where(lane >= DEC * row, wrapped, 0.0)
    rim = wrapped - main
    gap = jnp.zeros((LANES - 2 * CHUNK_OUT, CHUNK), jnp.float32)
    weights_hi, weights_lo = split(jnp.concatenate([main, gap, rim], axis=0).T)
    weights = jnp.concatenate([weights_hi, weights_lo], axis=1)

    def filtered(stacked):
        high, low = split(stacked)
        both = dot(high, weights)
        return both[:, :LANES] + both[:, LANES:] + dot(low, weights_hi)

    for copy in copies[1:]:
        copy.wait()
    for slot in range(slots):
        pick = picks_ref[0, slot]
        alive = alive_ref[0, pick].astype(jnp.float32)
        for j in range(chunks):
            at = SUBLANES * slot + j
            span = slice(CHUNK * j, CHUNK * (j + 1))
            source_ref[at : at + 1, :] = raw_ref[pl.ds(pick, 1), span] * alive
    high, low = split(source_ref[...])
    count = slots * SUBLANES
    both = dot(jnp.concatenate([high, low], axis=0), weights)
    sources = both[:count, :LANES] + both[:count, LANES:] + both[count:, :LANES]
    lane = lax.broadcasted_iota(jnp.int32, (SUBLANES, LANES), 1)
    row = lax.broadcasted_iota(jnp.int32, (SUBLANES, LANES), 0)
    leads = row % per_tile == 0
    wraps = lane >= LANES - EDGE
    piece = []
    rims = jnp.zeros((1, LANES), jnp.float32)
    for slot in range(slots):
        source = sources[SUBLANES * slot : SUBLANES * (slot + 1)]
        placed = source
        for step in range(1, per_tile):
            rolled = pltpu.roll(source, CHUNK_OUT * step, 1)
            placed = jnp.where(row % per_tile == step, rolled, placed)
        own = jnp.where(leads & wraps, 0.0, placed)
        rim = placed - own
        for tile in range(tiles):
            first = per_tile * tile
            inside = jnp.where((row >= first) & (row < first + per_tile), own, 0.0)
            before = jnp.where(row == first + per_tile, rim, 0.0)
            piece.append(jnp.sum(inside + before, axis=0, keepdims=True))
        rims = rims + pltpu.roll(rim[:1], LANES - EDGE * slot if slot else 0, 1)
    piece.append(rims)
    size = len(piece)
    spread = [jnp.broadcast_to(value, (SUBLANES, LANES)) for value in piece]
    eight = []
    for group in range(size):
        place = (row + SUBLANES * group) % size
        total = spread[0]
        for at in range(1, size):
            total = jnp.where(place == at, spread[at], total)
        eight.append(total)
    eight = jnp.concatenate(eight, axis=0)
    for at in range(0, pieces_ref.shape[0], SUBLANES * size):
        pieces_ref[at : at + SUBLANES * size, :] = eight
    sending = pltpu.make_async_copy(pieces_ref, pieces_hbm, sems.at[0])
    sending.start()

    result = filtered(
        jnp.concatenate(
            [raw_ref[:, CHUNK * j : CHUNK * (j + 1)] for j in range(chunks)], axis=0
        )
    )
    part = [result[rows * j : rows * (j + 1)] for j in range(chunks)]
    is_main = lax.broadcasted_iota(jnp.int32, (rows, LANES), 1) < LANES // 2
    values = []
    for first in range(0, chunks, per_tile):
        total = jnp.where(is_main, part[first], 0.0)
        for step in range(1, min(per_tile, chunks - first)):
            total = total + pltpu.roll(part[first + step], CHUNK_OUT * step, 1)
        if first + per_tile < chunks:
            total = total + jnp.where(is_main, 0.0, part[first + per_tile])
        values.append(total)
    rim = jnp.where(is_main, 0.0, part[0])
    if paired:
        packed = rim[:SUBLANES]
        for at in range(1, rows // SUBLANES):
            group = rim[SUBLANES * at : SUBLANES * (at + 1)]
            packed = packed + pltpu.roll(group, LANES - EDGE * at, 1)
        for at, value in enumerate(values):
            out_ref[rows * at : rows * (at + 1), :] = value
        out_ref[rows * tiles :, :] = packed
    else:
        for at, value in enumerate(values + [rim]):
            out_ref[:, LANES * at : LANES * (at + 1)] = value
    sending.wait()


def unpack(packed, rows):
    tiles = [packed[at : at + rows] for at in range(0, packed.shape[0] - SUBLANES, rows)]
    rims = packed[packed.shape[0] - SUBLANES :]
    rim = jnp.concatenate(
        [rims]
        + [pltpu.roll(rims, EDGE * at, 1) for at in range(1, rows // SUBLANES)],
        axis=0,
    )
    lane = lax.broadcasted_iota(jnp.int32, rim.shape, 1)
    return tiles + [jnp.where(lane >= LANES - EDGE, rim, 0.0)]


def transform(early, late, table_hi, table_lo):
    rows = early.shape[0]
    high, low = split(jnp.concatenate([early, late], axis=0))
    first = dot(jnp.concatenate([high, low], axis=0), table_hi)
    both = first[: 2 * rows] + first[2 * rows :] + dot(high, table_lo)
    quarter = lax.broadcasted_iota(jnp.int32, (1, BINS), 1) & 3
    cosine = jnp.where(quarter == 0, 1.0, 0.0) - jnp.where(quarter == 2, 1.0, 0.0)
    sine = jnp.where(quarter == 1, 1.0, 0.0) - jnp.where(quarter == 3, 1.0, 0.0)
    early_re, early_im = both[:rows, :BINS], both[:rows, BINS:]
    late_re, late_im = both[rows:, :BINS], both[rows:, BINS:]
    return (
        early_re + cosine * late_re + sine * late_im,
        early_im + cosine * late_im - sine * late_re,
    )


def whitening(real_part, imag_part, band):
    rows = real_part.shape[0]
    tiles = BINS // LANES
    stacked = []
    for part in split(real_part * real_part + imag_part * imag_part):
        zero = jnp.zeros((rows, LANES), part.dtype)
        wide = jnp.concatenate([zero, part, zero], axis=1)
        stacked += [wide[:, LANES * tile : LANES * (tile + 3)] for tile in range(tiles)]
    banded = dot(jnp.concatenate(stacked, axis=0), band)
    step = rows * tiles
    summed = banded[:step] + banded[step:]
    total = jnp.concatenate(
        [summed[rows * tile : rows * (tile + 1)] for tile in range(tiles)], axis=1
    )
    bins = lax.broadcasted_iota(jnp.int32, (1, BINS), 1)
    count = jnp.minimum(bins + HALF, BINS - 1) - jnp.maximum(bins - HALF, 0) + 1
    return lax.rsqrt(total * (1.0 / count.astype(jnp.float32)) + 1e-06)


def prepare_kernel(
    _, alive_hbm, picks_hbm, fwd_hi_hbm, fwd_lo_hbm, band_hbm, lag_hbm,
    hi_ref, lo_ref, band_ref, lag_ref, alive_out, picks_out, alive_ref, picks_ref, sems,
):
    copies = start_copies(
        [
            (alive_hbm, alive_ref),
            (picks_hbm, picks_ref),
            (fwd_hi_hbm, hi_ref),
            (fwd_lo_hbm, lo_ref),
            (band_hbm, band_ref),
            (lag_hbm, lag_ref),
        ],
        sems,
    )
    for copy in copies[:2]:
        copy.wait()
    rows = alive_out.shape[0]
    alive_out[...] = jnp.broadcast_to(
        column(alive_ref[...].astype(jnp.float32)), (rows, LANES)
    )
    channel = lax.broadcasted_iota(jnp.int32, (rows, LANES), 0)
    for slot in range(picks_ref.shape[1]):
        pick = jnp.broadcast_to(picks_ref[:, slot : slot + 1], (rows, LANES))
        picks_out[slot] = jnp.where(channel == pick, 1.0, 0.0)
    for copy in copies[2:]:
        copy.wait()


def spectra_kernel(series_ref, hi_ref, lo_ref, band_ref, alive_ref, *refs):
    spectra_ref = refs[-1]
    rows = alive_ref.shape[0]
    half = S // 2
    if len(refs) > 1:
        mine, other = [unpack(ref[...], rows) for ref in (series_ref, refs[0])]
        first = lax.axis_index("src") == 0
        early = [jnp.where(first, a, b) for a, b in zip(mine, other)]
        late = [jnp.where(first, b, a) for a, b in zip(mine, other)]
        early[-2] = early[-2] + late[-1]
        early, late = [jnp.concatenate(tiles[:-1], axis=1) for tiles in (early, late)]
    else:
        early, late = series_ref[:, :half], series_ref[:, half:]
    real_part, imag_part = transform(early, late, hi_ref[...], lo_ref[...])
    factor = alive_ref[:, :1] * whitening(real_part, imag_part, band_ref[...])
    spectra_ref[:, :BINS] = real_part * factor
    spectra_ref[:, BINS:] = imag_part * factor


def correlate_kernel(
    slots, spectra_ref, pieces_ref, picks_ref, hi_ref, lo_ref, band_ref, lag_ref, out_hbm,
    series_ref, rims_ref, source_ref, out_ref, sems, *cross_refs,
):
    rows = spectra_ref.shape[0]
    group = out_ref.shape[0] // slots
    half = BINS // LANES
    own = lax.axis_index("blk")
    base = lax.axis_index("src") * group
    tiles = S // 2 // LANES

    for slot in range(slots):
        for block in range(group):
            row = slice(slot * group + block, slot * group + block + 1)
            at = pieces_ref.shape[0] - 1 - 2 * (base + block)
            for tile in range(tiles):
                span = slice(LANES * (slot * tiles + tile), LANES * (slot * tiles + tile + 1))
                early = slice(LANES * tile, LANES * (tile + 1))
                late = slice(S // 2 + LANES * tile, S // 2 + LANES * (tile + 1))
                series_ref[row, early] = pieces_ref[at, :, span]
                series_ref[row, late] = pieces_ref[at - 1, :, span]
            rims_ref[row, :] = pieces_ref[at - 1, :, LANES * slots * tiles :]
    rims = jnp.concatenate(
        [
            pltpu.roll(rims_ref[slot * group : (slot + 1) * group, :], EDGE * slot, 1)
            for slot in range(slots)
        ],
        axis=0,
    )
    lane = lax.broadcasted_iota(jnp.int32, rims.shape, 1)
    seam = slice(S // 2 - LANES, S // 2)
    series_ref[:, seam] = series_ref[:, seam] + jnp.where(lane >= LANES - EDGE, rims, 0.0)
    early, late = series_ref[:, : S // 2], series_ref[:, S // 2 :]
    real_part, imag_part = transform(early, late, hi_ref[...], lo_ref[...])
    factor = whitening(real_part, imag_part, band_ref[...])
    source_ref[:, :BINS] = real_part * factor
    source_ref[:, BINS:] = imag_part * factor
    def make_cross(part):
        cross_ref = cross_refs[part]
        for tile in range(half):
            re = slice(LANES * tile, LANES * (tile + 1))
            im = slice(BINS + LANES * tile, BINS + LANES * (tile + 1))
            rec_re, rec_im = spectra_ref[:, re], spectra_ref[:, im]
            for at in range(per_part):
                block, slot = divmod(part * per_part + at, slots)
                row = slot * group + block
                src_re, src_im = source_ref[row : row + 1, re], source_ref[row : row + 1, im]
                where = slice(rows * at, rows * (at + 1))
                cross_ref[where, re] = (src_re * rec_re + src_im * rec_im).astype(jnp.bfloat16)
                cross_ref[where, im] = (src_re * rec_im - src_im * rec_re).astype(jnp.bfloat16)

    per_part = group * slots // PARTS
    copies = []
    make_cross(0)
    for part in range(PARTS):
        if part + 1 < PARTS:
            make_cross(part + 1)
        lagged = dot(cross_refs[part][...], lag_ref[...])
        first = part * per_part
        for source in range(first, first + per_part):
            block, slot = divmod(source, slots)
            keep = 1.0 - jnp.where(own == base + block, 1.0, 0.0) * picks_ref[slot]
            at = source - first
            kept = lagged[rows * at : rows * (at + 1)] * jnp.concatenate(
                [keep] * (LAGS // LANES), axis=1
            )
            out_ref[source] = kept.astype(jnp.bfloat16)
        span = pl.ds(first, per_part)
        copies.append(pltpu.make_async_copy(out_ref.at[span], out_hbm.at[span], sems.at[part]))
        copies[-1].start()
    for copy in copies:
        copy.wait()


HBM = pl.BlockSpec(memory_space=pltpu.HBM)
VMEM = pl.BlockSpec(memory_space=pltpu.VMEM)
PARAMS = pltpu.CompilerParams(vmem_limit_bytes=VMEM_LIMIT)


def in_hbm(*arrays):
    return [pltpu.with_memory_space_constraint(array, pltpu.HBM) for array in arrays]


def shaped(*shape, dtype=jnp.float32):
    return jax.ShapeDtypeStruct(shape, dtype)


def local(raw_records, fir_taps, alive_mask, source_index):
    src_count = lax.axis_size("src")
    blk_count = lax.axis_size("blk")
    rows, raw_count = raw_records.shape
    slots = source_index.shape[1]
    group = blk_count // src_count
    out_count = raw_count // DEC
    width = -(-out_count // LANES) * LANES + LANES
    chunks = raw_count // CHUNK
    paired = src_count == 2 and 2 * out_count == S
    bf16 = jnp.bfloat16
    forward_hi, forward_lo = split_table(forward_table())
    alive_row = alive_mask.reshape(1, rows)

    with jax.named_scope("decimate"):
        device_count = blk_count * src_count
        main = slots * (width - LANES)
        decimated, pieces = pl.pallas_call(
            lambda *refs: decimate_kernel(paired, *refs),
            out_shape=(
                shaped(rows * (S // 2 // LANES) + SUBLANES, LANES)
                if paired
                else shaped(rows, width),
                shaped(device_count * (main // LANES + 1), LANES),
            ),
            in_specs=[HBM] * 4,
            out_specs=(VMEM, HBM),
            scratch_shapes=[
                pltpu.VMEM((rows, raw_count), jnp.float32),
                pltpu.VMEM((1, TAPS), jnp.float32),
                pltpu.SMEM((1, rows), jnp.int32),
                pltpu.SMEM((1, slots), jnp.int32),
                pltpu.VMEM((SUBLANES * slots, CHUNK), jnp.float32),
                pltpu.VMEM((device_count * (main // LANES + 1), LANES), jnp.float32),
                pltpu.SemaphoreType.DMA((rows // SUBLANES + 3,)),
            ],
            compiler_params=PARAMS,
        )(*in_hbm(raw_records, fir_taps.reshape(1, TAPS), alive_row, source_index))

    def whole(shards):
        rims = jnp.pad(shards[1:, :, width - EDGE :], ((0, 1), (0, 0), (out_count - EDGE, 0)))
        series = shards[:, :, :out_count] + rims
        return series.transpose(1, 0, 2).reshape(shards.shape[1], S)

    with jax.named_scope("gather_sources"):
        gathered = lax.all_to_all(
            pieces.reshape(device_count, 1, main + LANES),
            ("blk", "src"),
            split_axis=0,
            concat_axis=0,
            tiled=True,
            axis_index_groups=[list(reversed(range(device_count)))],
        )
        if not paired:
            gathered = gathered[::-1]
            shards = gathered.reshape(blk_count, src_count, main + LANES)
            shards = shards.transpose(1, 0, 2)
            rims = [shards[:, :, main + LANES - EDGE * (slot + 1) :] for slot in range(slots)]
            rims = jnp.stack([rim[:, :, :EDGE] for rim in rims], axis=2)
            rims = jnp.pad(rims, ((0, 0), (0, 0), (0, 0), (LANES - EDGE, 0)))
            series = shards[:, :, :main].reshape(src_count, blk_count, slots, width - LANES)
            series = jnp.concatenate([series, rims], axis=3)
            series = whole(series.reshape(src_count, blk_count * slots, width))
            series = series.reshape(blk_count, slots, 2, S // 2).transpose(0, 2, 1, 3)
            series = series.reshape(blk_count * 2, 1, slots * S // 2)
            gathered = jnp.pad(series, ((0, 0), (0, 0), (0, LANES)))[::-1]

    with jax.named_scope("prepare"):
        out_shape = (
            shaped(S // 2, NFFT, dtype=bf16),
            shaped(S // 2, NFFT, dtype=bf16),
            shaped(3 * LANES, LANES, dtype=bf16),
            shaped(NFFT, LAGS, dtype=bf16),
            shaped(rows, LANES),
            shaped(slots, rows, LANES),
        )
        table_hi, table_lo, band, lag, alive, picks = pl.pallas_call(
            prepare_kernel,
            out_shape=out_shape,
            in_specs=[VMEM] + [HBM] * 6,
            out_specs=(VMEM,) * len(out_shape),
            scratch_shapes=[
                pltpu.VMEM((1, rows), jnp.int32),
                pltpu.VMEM((1, slots), jnp.int32),
                pltpu.SemaphoreType.DMA((6,)),
            ],
            compiler_params=PARAMS,
            cost_estimate=pl.CostEstimate(
                flops=0, bytes_accessed=4 * S * NFFT, transcendentals=0
            ),
        )(
            decimated,
            *in_hbm(
                alive_row,
                source_index,
                jnp.asarray(forward_hi),
                jnp.asarray(forward_lo),
                jnp.asarray(band_table()),
                jnp.asarray(lag_table()),
            ),
        )

    with jax.named_scope("regroup"):
        if paired:
            series = [decimated]
            other = [lax.ppermute(decimated, "src", [(0, 1), (1, 0)])]
        else:
            series = [whole(lax.all_gather(decimated, "src", axis=0))]
            other = []

    with jax.named_scope("spectra"):
        operands = series + [table_hi, table_lo, band, alive] + other
        spectra = pl.pallas_call(
            spectra_kernel,
            out_shape=shaped(rows, NFFT),
            in_specs=[VMEM] * len(operands),
            out_specs=VMEM,
            compiler_params=PARAMS,
        )(*operands)

    with jax.named_scope("correlate"):
        total = group * slots
        return pl.pallas_call(
            lambda *refs: correlate_kernel(slots, *refs),
            out_shape=shaped(total, rows, LAGS, dtype=bf16),
            in_specs=[VMEM] * 7,
            out_specs=HBM,
            scratch_shapes=[
                pltpu.VMEM((total, S), jnp.float32),
                pltpu.VMEM((total, LANES), jnp.float32),
                pltpu.VMEM((total, NFFT), jnp.float32),
                pltpu.VMEM((total, rows, LAGS), bf16),
                pltpu.SemaphoreType.DMA((PARTS,)),
            ]
            + [pltpu.VMEM((total // PARTS * rows, NFFT), bf16)] * PARTS,
            compiler_params=PARAMS,
        )(spectra, gathered, picks, table_hi, table_lo, band, lag)


def solution(mesh):
    in_specs = (P("blk", "src"), P(), P("blk"), P("blk", None))
    out_specs = P("src", "blk", None)
    return jax.shard_map(local, mesh=mesh, in_specs=in_specs, out_specs=out_specs, check_vma=False)
```

```python
import math

import jax
import jax.numpy as jnp
import numpy as np
from jax import lax
from jax.experimental import pallas as pl
from jax.experimental.pallas import tpu as pltpu
from jax.sharding import PartitionSpec as P

S = 512
NFFT = 1024
BINS = NFFT // 2
LAGS = 512
TAPS = 64
DEC = 20
HALF = 64
LANES = 128
SUBLANES = 8
PARTS = 3
EDGE = (TAPS - 1) // DEC
CHUNK = 640
CHUNK_OUT = CHUNK // DEC
VMEM_LIMIT = 48 * 1024 * 1024


def forward_table():
    phases = 2.0 * math.pi / NFFT * (np.outer(np.arange(S // 2), np.arange(BINS)) % NFFT)
    return np.concatenate([np.cos(phases), -np.sin(phases)], axis=1).astype(np.float32)


def split_table(table):
    high = table.astype(jnp.bfloat16)
    low = (table - high.astype(np.float32)).astype(jnp.bfloat16)
    return high, low


def band_table():
    bins = np.arange(3 * LANES)[:, None] - LANES
    return (np.abs(bins - np.arange(LANES)[None, :]) <= HALF).astype(jnp.bfloat16)


def lag_table():
    bins = np.arange(BINS)[:, None]
    shift = np.arange(LAGS)[None, :] - LAGS // 2
    phases = 2.0 * math.pi / NFFT * (bins * shift % NFFT)
    weight = np.where(bins == 0, 0.5, 1.0) / math.sqrt(BINS)
    table = np.concatenate([weight * np.cos(phases), -weight * np.sin(phases)], axis=0)
    return table.astype(np.float32).astype(jnp.bfloat16)


def split(value):
    high = value.astype(jnp.bfloat16)
    return high, (value - high.astype(jnp.float32)).astype(jnp.bfloat16)


def dot(a, b):
    return jnp.dot(a, b, preferred_element_type=jnp.float32)


def column(row):
    count = row.shape[1]
    at = [lax.broadcasted_iota(jnp.int32, (count, count), axis) for axis in range(2)]
    rows = jnp.broadcast_to(row, (count, count))
    return jnp.sum(jnp.where(at[0] == at[1], rows, 0.0), axis=1, keepdims=True)


def start_copies(pairs, sems):
    copies = [
        pltpu.make_async_copy(source, target, sems.at[at])
        for at, (source, target) in enumerate(pairs)
    ]
    for copy in copies:
        copy.start()
    return copies


def decimate_kernel(
    paired, raw_hbm, taps_hbm, alive_hbm, picks_hbm, out_ref, pieces_hbm,
    raw_ref, taps_ref, alive_ref, picks_ref, source_ref, pieces_ref, sems,
):
    rows = raw_hbm.shape[0]
    chunks = raw_hbm.shape[1] // CHUNK
    slots = picks_ref.shape[1]
    per_tile = LANES // CHUNK_OUT
    tiles = -(-chunks // per_tile)
    pairs = [(taps_hbm, taps_ref), (picks_hbm, picks_ref), (alive_hbm, alive_ref)]
    for at in range(0, rows, SUBLANES):
        span = slice(at, at + SUBLANES)
        pairs.append((raw_hbm.at[span], raw_ref.at[span]))
    copies = start_copies(pairs, sems)
    source_ref[...] = jnp.zeros_like(source_ref)
    copies[0].wait()
    taps = jnp.broadcast_to(taps_ref[...], (SUBLANES, TAPS))
    eight = jnp.concatenate([taps, jnp.zeros((SUBLANES, CHUNK - TAPS), jnp.float32)], axis=1)
    for _ in range(2):
        eight = pltpu.roll(eight, 0, 1, stride=DEC // 2, stride_axis=0)
    wrapped = jnp.concatenate(
        [eight]
        + [pltpu.roll(eight, DEC * at, 1) for at in range(SUBLANES, CHUNK_OUT, SUBLANES)],
        axis=0,
    )
    lane = lax.broadcasted_iota(jnp.int32, (CHUNK_OUT, CHUNK), 1)
    row = lax.broadcasted_iota(jnp.int32, (CHUNK_OUT, CHUNK), 0)
    main = jnp.where(lane >= DEC * row, wrapped, 0.0)
    rim = wrapped - main
    gap = jnp.zeros((LANES - 2 * CHUNK_OUT, CHUNK), jnp.float32)
    weights_hi, weights_lo = split(jnp.concatenate([main, gap, rim], axis=0).T)
    weights = jnp.concatenate([weights_hi, weights_lo], axis=1)

    def filtered(stacked):
        high, low = split(stacked)
        both = dot(high, weights)
        return both[:, :LANES] + both[:, LANES:] + dot(low, weights_hi)

    for copy in copies[1:]:
        copy.wait()
    for slot in range(slots):
        pick = picks_ref[0, slot]
        alive = alive_ref[0, pick].astype(jnp.float32)
        for j in range(chunks):
            at = SUBLANES * slot + j
            span = slice(CHUNK * j, CHUNK * (j + 1))
            source_ref[at : at + 1, :] = raw_ref[pl.ds(pick, 1), span] * alive
    high, low = split(source_ref[...])
    count = slots * SUBLANES
    both = dot(jnp.concatenate([high, low], axis=0), weights)
    sources = both[:count, :LANES] + both[:count, LANES:] + both[count:, :LANES]
    lane = lax.broadcasted_iota(jnp.int32, (SUBLANES, LANES), 1)
    row = lax.broadcasted_iota(jnp.int32, (SUBLANES, LANES), 0)
    leads = row % per_tile == 0
    wraps = lane >= LANES - EDGE
    piece = []
    rims = jnp.zeros((1, LANES), jnp.float32)
    for slot in range(slots):
        source = sources[SUBLANES * slot : SUBLANES * (slot + 1)]
        placed = source
        for step in range(1, per_tile):
            rolled = pltpu.roll(source, CHUNK_OUT * step, 1)
            placed = jnp.where(row % per_tile == step, rolled, placed)
        own = jnp.where(leads & wraps, 0.0, placed)
        rim = placed - own
        for tile in range(tiles):
            first = per_tile * tile
            inside = jnp.where((row >= first) & (row < first + per_tile), own, 0.0)
            before = jnp.where(row == first + per_tile, rim, 0.0)
            piece.append(jnp.sum(inside + before, axis=0, keepdims=True))
        rims = rims + pltpu.roll(rim[:1], LANES - EDGE * slot if slot else 0, 1)
    piece.append(rims)
    size = len(piece)
    spread = [jnp.broadcast_to(value, (SUBLANES, LANES)) for value in piece]
    eight = []
    for group in range(size):
        place = (row + SUBLANES * group) % size
        total = spread[0]
        for at in range(1, size):
            total = jnp.where(place == at, spread[at], total)
        eight.append(total)
    eight = jnp.concatenate(eight, axis=0)
    for at in range(0, pieces_ref.shape[0], SUBLANES * size):
        pieces_ref[at : at + SUBLANES * size, :] = eight
    sending = pltpu.make_async_copy(pieces_ref, pieces_hbm, sems.at[0])
    sending.start()

    result = filtered(
        jnp.concatenate(
            [raw_ref[:, CHUNK * j : CHUNK * (j + 1)] for j in range(chunks)], axis=0
        )
    )
    part = [result[rows * j : rows * (j + 1)] for j in range(chunks)]
    is_main = lax.broadcasted_iota(jnp.int32, (rows, LANES), 1) < LANES // 2
    values = []
    for first in range(0, chunks, per_tile):
        total = jnp.where(is_main, part[first], 0.0)
        for step in range(1, min(per_tile, chunks - first)):
            total = total + pltpu.roll(part[first + step], CHUNK_OUT * step, 1)
        if first + per_tile < chunks:
            total = total + jnp.where(is_main, 0.0, part[first + per_tile])
        values.append(total)
    rim = jnp.where(is_main, 0.0, part[0])
    if paired:
        packed = rim[:SUBLANES]
        for at in range(1, rows // SUBLANES):
            group = rim[SUBLANES * at : SUBLANES * (at + 1)]
            packed = packed + pltpu.roll(group, LANES - EDGE * at, 1)
        for at, value in enumerate(values):
            out_ref[rows * at : rows * (at + 1), :] = value
        out_ref[rows * tiles :, :] = packed
    else:
        for at, value in enumerate(values + [rim]):
            out_ref[:, LANES * at : LANES * (at + 1)] = value
    sending.wait()


def unpack(packed, rows):
    tiles = [packed[at : at + rows] for at in range(0, packed.shape[0] - SUBLANES, rows)]
    rims = packed[packed.shape[0] - SUBLANES :]
    rim = jnp.concatenate(
        [rims]
        + [pltpu.roll(rims, EDGE * at, 1) for at in range(1, rows // SUBLANES)],
        axis=0,
    )
    lane = lax.broadcasted_iota(jnp.int32, rim.shape, 1)
    return tiles + [jnp.where(lane >= LANES - EDGE, rim, 0.0)]


def transform(early, late, table_hi, table_lo):
    rows = early.shape[0]
    high, low = split(jnp.concatenate([early, late], axis=0))
    first = dot(jnp.concatenate([high, low], axis=0), table_hi)
    both = first[: 2 * rows] + first[2 * rows :] + dot(high, table_lo)
    quarter = lax.broadcasted_iota(jnp.int32, (1, BINS), 1) & 3
    cosine = jnp.where(quarter == 0, 1.0, 0.0) - jnp.where(quarter == 2, 1.0, 0.0)
    sine = jnp.where(quarter == 1, 1.0, 0.0) - jnp.where(quarter == 3, 1.0, 0.0)
    early_re, early_im = both[:rows, :BINS], both[:rows, BINS:]
    late_re, late_im = both[rows:, :BINS], both[rows:, BINS:]
    return (
        early_re + cosine * late_re + sine * late_im,
        early_im + cosine * late_im - sine * late_re,
    )


def whitening(real_part, imag_part, band):
    rows = real_part.shape[0]
    tiles = BINS // LANES
    stacked = []
    for part in split(real_part * real_part + imag_part * imag_part):
        zero = jnp.zeros((rows, LANES), part.dtype)
        wide = jnp.concatenate([zero, part, zero], axis=1)
        stacked += [wide[:, LANES * tile : LANES * (tile + 3)] for tile in range(tiles)]
    banded = dot(jnp.concatenate(stacked, axis=0), band)
    step = rows * tiles
    summed = banded[:step] + banded[step:]
    total = jnp.concatenate(
        [summed[rows * tile : rows * (tile + 1)] for tile in range(tiles)], axis=1
    )
    bins = lax.broadcasted_iota(jnp.int32, (1, BINS), 1)
    count = jnp.minimum(bins + HALF, BINS - 1) - jnp.maximum(bins - HALF, 0) + 1
    return lax.rsqrt(total * (1.0 / count.astype(jnp.float32)) + 1e-06)


def prepare_kernel(
    _, alive_hbm, picks_hbm, fwd_hi_hbm, fwd_lo_hbm, band_hbm, lag_hbm,
    hi_ref, lo_ref, band_ref, lag_ref, alive_out, picks_out, alive_ref, picks_ref, sems,
):
    copies = start_copies(
        [
            (alive_hbm, alive_ref),
            (picks_hbm, picks_ref),
            (fwd_hi_hbm, hi_ref),
            (fwd_lo_hbm, lo_ref),
            (band_hbm, band_ref),
            (lag_hbm, lag_ref),
        ],
        sems,
    )
    for copy in copies[:2]:
        copy.wait()
    rows = alive_out.shape[0]
    alive_out[...] = jnp.broadcast_to(
        column(alive_ref[...].astype(jnp.float32)), (rows, LANES)
    )
    channel = lax.broadcasted_iota(jnp.int32, (rows, LANES), 0)
    for slot in range(picks_ref.shape[1]):
        pick = jnp.broadcast_to(picks_ref[:, slot : slot + 1], (rows, LANES))
        picks_out[slot] = jnp.where(channel == pick, 1.0, 0.0)
    for copy in copies[2:]:
        copy.wait()


def spectra_kernel(series_ref, hi_ref, lo_ref, band_ref, alive_ref, *refs):
    spectra_ref = refs[-1]
    rows = alive_ref.shape[0]
    half = S // 2
    if len(refs) > 1:
        mine, other = [unpack(ref[...], rows) for ref in (series_ref, refs[0])]
        first = lax.axis_index("src") == 0
        early = [jnp.where(first, a, b) for a, b in zip(mine, other)]
        late = [jnp.where(first, b, a) for a, b in zip(mine, other)]
        early[-2] = early[-2] + late[-1]
        early, late = [jnp.concatenate(tiles[:-1], axis=1) for tiles in (early, late)]
    else:
        early, late = series_ref[:, :half], series_ref[:, half:]
    real_part, imag_part = transform(early, late, hi_ref[...], lo_ref[...])
    factor = alive_ref[:, :1] * whitening(real_part, imag_part, band_ref[...])
    spectra_ref[:, :BINS] = real_part * factor
    spectra_ref[:, BINS:] = imag_part * factor


def part_bounds(total):
    ends = [3 * total // 8, 3 * total // 4, total]
    return [(a, b) for a, b in zip([0] + ends, ends) if b > a]


def correlate_kernel(
    slots, spectra_ref, pieces_ref, picks_ref, hi_ref, lo_ref, band_ref, lag_ref, out_hbm,
    series_ref, rims_ref, source_ref, cross_ref, out_ref, sems,
):
    rows = spectra_ref.shape[0]
    group = out_ref.shape[0] // slots
    half = BINS // LANES
    own = lax.axis_index("blk")
    base = lax.axis_index("src") * group
    tiles = S // 2 // LANES
    quarter = pieces_ref.shape[0] // 4

    def entry(device):
        place = (device & (quarter - 1)) * 4 + (device >> (quarter.bit_length() - 1))
        return pieces_ref.shape[0] - 1 - place

    for slot in range(slots):
        for block in range(group):
            row = slice(slot * group + block, slot * group + block + 1)
            at, after = [entry(2 * (base + block) + half_at) for half_at in range(2)]
            for tile in range(tiles):
                span = slice(LANES * (slot * tiles + tile), LANES * (slot * tiles + tile + 1))
                early = slice(LANES * tile, LANES * (tile + 1))
                late = slice(S // 2 + LANES * tile, S // 2 + LANES * (tile + 1))
                series_ref[row, early] = pieces_ref[at, :, span]
                series_ref[row, late] = pieces_ref[after, :, span]
            rims_ref[row, :] = pieces_ref[after, :, LANES * slots * tiles :]
    rims = jnp.concatenate(
        [
            pltpu.roll(rims_ref[slot * group : (slot + 1) * group, :], EDGE * slot, 1)
            for slot in range(slots)
        ],
        axis=0,
    )
    lane = lax.broadcasted_iota(jnp.int32, rims.shape, 1)
    seam = slice(S // 2 - LANES, S // 2)
    series_ref[:, seam] = series_ref[:, seam] + jnp.where(lane >= LANES - EDGE, rims, 0.0)
    early, late = series_ref[:, : S // 2], series_ref[:, S // 2 :]
    real_part, imag_part = transform(early, late, hi_ref[...], lo_ref[...])
    factor = whitening(real_part, imag_part, band_ref[...])
    source_ref[:, :BINS] = real_part * factor
    source_ref[:, BINS:] = imag_part * factor
    copies = []
    for part, (first, last) in enumerate(part_bounds(group * slots)):
        per_part = last - first
        for tile in range(half):
            re = slice(LANES * tile, LANES * (tile + 1))
            im = slice(BINS + LANES * tile, BINS + LANES * (tile + 1))
            rec_re, rec_im = spectra_ref[:, re], spectra_ref[:, im]
            for source in range(first, first + per_part):
                block, slot = divmod(source, slots)
                at = slot * group + block
                src_re, src_im = source_ref[at : at + 1, re], source_ref[at : at + 1, im]
                where = slice(rows * source, rows * (source + 1))
                cross_ref[where, re] = (src_re * rec_re + src_im * rec_im).astype(jnp.bfloat16)
                cross_ref[where, im] = (src_re * rec_im - src_im * rec_re).astype(jnp.bfloat16)
        lagged = dot(cross_ref[rows * first : rows * (first + per_part), :], lag_ref[...])
        for source in range(first, first + per_part):
            block, slot = divmod(source, slots)
            keep = 1.0 - jnp.where(own == base + block, 1.0, 0.0) * picks_ref[slot]
            at = source - first
            kept = lagged[rows * at : rows * (at + 1)] * jnp.concatenate(
                [keep] * (LAGS // LANES), axis=1
            )
            out_ref[source] = kept.astype(jnp.bfloat16)
        span = pl.ds(first, per_part)
        copies.append(pltpu.make_async_copy(out_ref.at[span], out_hbm.at[span], sems.at[part]))
        copies[-1].start()
    for copy in copies:
        copy.wait()


HBM = pl.BlockSpec(memory_space=pltpu.HBM)
VMEM = pl.BlockSpec(memory_space=pltpu.VMEM)
PARAMS = pltpu.CompilerParams(vmem_limit_bytes=VMEM_LIMIT)


def in_hbm(*arrays):
    return [pltpu.with_memory_space_constraint(array, pltpu.HBM) for array in arrays]


def shaped(*shape, dtype=jnp.float32):
    return jax.ShapeDtypeStruct(shape, dtype)


def exchange_order(count):
    quarter = count // 4
    return [a + b for a in range(quarter) for b in range(0, count, quarter)][::-1]


def local(raw_records, fir_taps, alive_mask, source_index):
    src_count = lax.axis_size("src")
    blk_count = lax.axis_size("blk")
    rows, raw_count = raw_records.shape
    slots = source_index.shape[1]
    group = blk_count // src_count
    out_count = raw_count // DEC
    width = -(-out_count // LANES) * LANES + LANES
    chunks = raw_count // CHUNK
    paired = src_count == 2 and 2 * out_count == S
    bf16 = jnp.bfloat16
    forward_hi, forward_lo = split_table(forward_table())
    alive_row = alive_mask.reshape(1, rows)

    with jax.named_scope("decimate"):
        device_count = blk_count * src_count
        main = slots * (width - LANES)
        decimated, pieces = pl.pallas_call(
            lambda *refs: decimate_kernel(paired, *refs),
            out_shape=(
                shaped(rows * (S // 2 // LANES) + SUBLANES, LANES)
                if paired
                else shaped(rows, width),
                shaped(device_count * (main // LANES + 1), LANES),
            ),
            in_specs=[HBM] * 4,
            out_specs=(VMEM, HBM),
            scratch_shapes=[
                pltpu.VMEM((rows, raw_count), jnp.float32),
                pltpu.VMEM((1, TAPS), jnp.float32),
                pltpu.SMEM((1, rows), jnp.int32),
                pltpu.SMEM((1, slots), jnp.int32),
                pltpu.VMEM((SUBLANES * slots, CHUNK), jnp.float32),
                pltpu.VMEM((device_count * (main // LANES + 1), LANES), jnp.float32),
                pltpu.SemaphoreType.DMA((rows // SUBLANES + 3,)),
            ],
            compiler_params=PARAMS,
        )(*in_hbm(raw_records, fir_taps.reshape(1, TAPS), alive_row, source_index))

    def whole(shards):
        rims = jnp.pad(shards[1:, :, width - EDGE :], ((0, 1), (0, 0), (out_count - EDGE, 0)))
        series = shards[:, :, :out_count] + rims
        return series.transpose(1, 0, 2).reshape(shards.shape[1], S)

    with jax.named_scope("gather_sources"):
        gathered = lax.all_to_all(
            pieces.reshape(device_count, 1, main + LANES),
            ("blk", "src"),
            split_axis=0,
            concat_axis=0,
            tiled=True,
            axis_index_groups=[exchange_order(device_count)] if paired else None,
        )
        if not paired:
            shards = gathered.reshape(blk_count, src_count, main + LANES)
            shards = shards.transpose(1, 0, 2)
            rims = [shards[:, :, main + LANES - EDGE * (slot + 1) :] for slot in range(slots)]
            rims = jnp.stack([rim[:, :, :EDGE] for rim in rims], axis=2)
            rims = jnp.pad(rims, ((0, 0), (0, 0), (0, 0), (LANES - EDGE, 0)))
            series = shards[:, :, :main].reshape(src_count, blk_count, slots, width - LANES)
            series = jnp.concatenate([series, rims], axis=3)
            series = whole(series.reshape(src_count, blk_count * slots, width))
            series = series.reshape(blk_count, slots, 2, S // 2).transpose(0, 2, 1, 3)
            series = series.reshape(blk_count * 2, 1, slots * S // 2)
            gathered = jnp.pad(series, ((0, 0), (0, 0), (0, LANES)))
            gathered = gathered[np.array(exchange_order(blk_count * 2))]

    with jax.named_scope("prepare"):
        out_shape = (
            shaped(S // 2, NFFT, dtype=bf16),
            shaped(S // 2, NFFT, dtype=bf16),
            shaped(3 * LANES, LANES, dtype=bf16),
            shaped(NFFT, LAGS, dtype=bf16),
            shaped(rows, LANES),
            shaped(slots, rows, LANES),
        )
        table_hi, table_lo, band, lag, alive, picks = pl.pallas_call(
            prepare_kernel,
            out_shape=out_shape,
            in_specs=[VMEM] + [HBM] * 6,
            out_specs=(VMEM,) * len(out_shape),
            scratch_shapes=[
                pltpu.VMEM((1, rows), jnp.int32),
                pltpu.VMEM((1, slots), jnp.int32),
                pltpu.SemaphoreType.DMA((6,)),
            ],
            compiler_params=PARAMS,
            cost_estimate=pl.CostEstimate(
                flops=0, bytes_accessed=4 * S * NFFT, transcendentals=0
            ),
        )(
            decimated,
            *in_hbm(
                alive_row,
                source_index,
                jnp.asarray(forward_hi),
                jnp.asarray(forward_lo),
                jnp.asarray(band_table()),
                jnp.asarray(lag_table()),
            ),
        )

    with jax.named_scope("regroup"):
        if paired:
            series = [decimated]
            other = [lax.ppermute(decimated, "src", [(0, 1), (1, 0)])]
        else:
            series = [whole(lax.all_gather(decimated, "src", axis=0))]
            other = []

    with jax.named_scope("spectra"):
        operands = series + [table_hi, table_lo, band, alive] + other
        spectra = pl.pallas_call(
            spectra_kernel,
            out_shape=shaped(rows, NFFT),
            in_specs=[VMEM] * len(operands),
            out_specs=VMEM,
            compiler_params=PARAMS,
        )(*operands)

    with jax.named_scope("correlate"):
        total = group * slots
        return pl.pallas_call(
            lambda *refs: correlate_kernel(slots, *refs),
            out_shape=shaped(total, rows, LAGS, dtype=bf16),
            in_specs=[VMEM] * 7,
            out_specs=HBM,
            scratch_shapes=[
                pltpu.VMEM((total, S), jnp.float32),
                pltpu.VMEM((total, LANES), jnp.float32),
                pltpu.VMEM((total, NFFT), jnp.float32),
                pltpu.VMEM((total * rows, NFFT), bf16),
                pltpu.VMEM((total, rows, LAGS), bf16),
                pltpu.SemaphoreType.DMA((PARTS,)),
            ],
            compiler_params=PARAMS,
        )(spectra, gathered, picks, table_hi, table_lo, band, lag)


def solution(mesh):
    in_specs = (P("blk", "src"), P(), P("blk"), P("blk", None))
    out_specs = P("src", "blk", None)
    return jax.shard_map(local, mesh=mesh, in_specs=in_specs, out_specs=out_specs, check_vma=False)
```

```python
import math

import jax
import jax.numpy as jnp
import numpy as np
from jax import lax
from jax.experimental import pallas as pl
from jax.experimental.pallas import tpu as pltpu
from jax.sharding import PartitionSpec as P

S = 512
NFFT = 1024
BINS = NFFT // 2
LAGS = 512
TAPS = 64
DEC = 20
HALF = 64
LANES = 128
SUBLANES = 8
PARTS = 2
EDGE = (TAPS - 1) // DEC
CHUNK = 640
CHUNK_OUT = CHUNK // DEC
VMEM_LIMIT = 48 * 1024 * 1024


def forward_table():
    phases = 2.0 * math.pi / NFFT * (np.outer(np.arange(S // 2), np.arange(BINS)) % NFFT)
    return np.concatenate([np.cos(phases), -np.sin(phases)], axis=1).astype(np.float32)


def split_table(table):
    high = table.astype(jnp.bfloat16)
    low = (table - high.astype(np.float32)).astype(jnp.bfloat16)
    return high, low


def band_table():
    bins = np.arange(3 * LANES)[:, None] - LANES
    return (np.abs(bins - np.arange(LANES)[None, :]) <= HALF).astype(jnp.bfloat16)


def lag_table():
    bins = np.arange(BINS)[:, None]
    shift = np.arange(LAGS)[None, :] - LAGS // 2
    phases = 2.0 * math.pi / NFFT * (bins * shift % NFFT)
    weight = np.where(bins == 0, 0.5, 1.0) / math.sqrt(BINS)
    table = np.concatenate([weight * np.cos(phases), -weight * np.sin(phases)], axis=0)
    return table.astype(np.float32).astype(jnp.bfloat16)


def folded_lag_tables():
    table = lag_table()
    half = LAGS // 2
    columns = table[:, half:].copy()
    columns[BINS:, 0] = table[BINS:, 0]
    lags = np.arange(half)
    order = (lags[:, None] == (half - lags[None, :]) % half).astype(jnp.bfloat16)
    return columns, table[:BINS, 0].astype(np.float32).reshape(1, BINS), order


def split(value):
    high = value.astype(jnp.bfloat16)
    return high, (value - high.astype(jnp.float32)).astype(jnp.bfloat16)


def dot(a, b):
    return jnp.dot(a, b, preferred_element_type=jnp.float32)


def column(row):
    count = row.shape[1]
    at = [lax.broadcasted_iota(jnp.int32, (count, count), axis) for axis in range(2)]
    rows = jnp.broadcast_to(row, (count, count))
    return jnp.sum(jnp.where(at[0] == at[1], rows, 0.0), axis=1, keepdims=True)


def start_copies(pairs, sems):
    copies = [
        pltpu.make_async_copy(source, target, sems.at[at])
        for at, (source, target) in enumerate(pairs)
    ]
    for copy in copies:
        copy.start()
    return copies


def decimate_kernel(
    paired, raw_hbm, taps_hbm, alive_hbm, picks_hbm, out_ref, pieces_hbm,
    raw_ref, taps_ref, alive_ref, picks_ref, source_ref, pieces_ref, sems,
):
    rows = raw_hbm.shape[0]
    chunks = raw_hbm.shape[1] // CHUNK
    slots = picks_ref.shape[1]
    per_tile = LANES // CHUNK_OUT
    tiles = -(-chunks // per_tile)
    pairs = [(taps_hbm, taps_ref), (picks_hbm, picks_ref), (alive_hbm, alive_ref)]
    for at in range(0, rows, SUBLANES):
        span = slice(at, at + SUBLANES)
        pairs.append((raw_hbm.at[span], raw_ref.at[span]))
    copies = start_copies(pairs, sems)
    source_ref[...] = jnp.zeros_like(source_ref)
    copies[0].wait()
    taps = jnp.broadcast_to(taps_ref[...], (SUBLANES, TAPS))
    eight = jnp.concatenate([taps, jnp.zeros((SUBLANES, CHUNK - TAPS), jnp.float32)], axis=1)
    for _ in range(2):
        eight = pltpu.roll(eight, 0, 1, stride=DEC // 2, stride_axis=0)
    wrapped = jnp.concatenate(
        [eight]
        + [pltpu.roll(eight, DEC * at, 1) for at in range(SUBLANES, CHUNK_OUT, SUBLANES)],
        axis=0,
    )
    lane = lax.broadcasted_iota(jnp.int32, (CHUNK_OUT, CHUNK), 1)
    row = lax.broadcasted_iota(jnp.int32, (CHUNK_OUT, CHUNK), 0)
    main = jnp.where(lane >= DEC * row, wrapped, 0.0)
    rim = wrapped - main
    gap = jnp.zeros((LANES - 2 * CHUNK_OUT, CHUNK), jnp.float32)
    weights_hi, weights_lo = split(jnp.concatenate([main, gap, rim], axis=0).T)
    weights = jnp.concatenate([weights_hi, weights_lo], axis=1)

    def filtered(stacked):
        high, low = split(stacked)
        both = dot(high, weights)
        return both[:, :LANES] + both[:, LANES:] + dot(low, weights_hi)

    for copy in copies[1:]:
        copy.wait()
    for slot in range(slots):
        pick = picks_ref[0, slot]
        alive = alive_ref[0, pick].astype(jnp.float32)
        for j in range(chunks):
            at = SUBLANES * slot + j
            span = slice(CHUNK * j, CHUNK * (j + 1))
            source_ref[at : at + 1, :] = raw_ref[pl.ds(pick, 1), span] * alive
    high, low = split(source_ref[...])
    count = slots * SUBLANES
    both = dot(jnp.concatenate([high, low], axis=0), weights)
    sources = both[:count, :LANES] + both[:count, LANES:] + both[count:, :LANES]
    lane = lax.broadcasted_iota(jnp.int32, (SUBLANES, LANES), 1)
    row = lax.broadcasted_iota(jnp.int32, (SUBLANES, LANES), 0)
    leads = row % per_tile == 0
    wraps = lane >= LANES - EDGE
    piece = []
    rims = jnp.zeros((1, LANES), jnp.float32)
    for slot in range(slots):
        source = sources[SUBLANES * slot : SUBLANES * (slot + 1)]
        placed = source
        for step in range(1, per_tile):
            rolled = pltpu.roll(source, CHUNK_OUT * step, 1)
            placed = jnp.where(row % per_tile == step, rolled, placed)
        own = jnp.where(leads & wraps, 0.0, placed)
        rim = placed - own
        for tile in range(tiles):
            first = per_tile * tile
            inside = jnp.where((row >= first) & (row < first + per_tile), own, 0.0)
            before = jnp.where(row == first + per_tile, rim, 0.0)
            piece.append(jnp.sum(inside + before, axis=0, keepdims=True))
        rims = rims + pltpu.roll(rim[:1], LANES - EDGE * slot if slot else 0, 1)
    piece.append(rims)
    size = len(piece)
    spread = [jnp.broadcast_to(value, (SUBLANES, LANES)) for value in piece]
    eight = []
    for group in range(size):
        place = (row + SUBLANES * group) % size
        total = spread[0]
        for at in range(1, size):
            total = jnp.where(place == at, spread[at], total)
        eight.append(total)
    eight = jnp.concatenate(eight, axis=0)
    for at in range(0, pieces_ref.shape[0], SUBLANES * size):
        pieces_ref[at : at + SUBLANES * size, :] = eight
    sending = pltpu.make_async_copy(pieces_ref, pieces_hbm, sems.at[0])
    sending.start()

    result = filtered(
        jnp.concatenate(
            [raw_ref[:, CHUNK * j : CHUNK * (j + 1)] for j in range(chunks)], axis=0
        )
    )
    part = [result[rows * j : rows * (j + 1)] for j in range(chunks)]
    is_main = lax.broadcasted_iota(jnp.int32, (rows, LANES), 1) < LANES // 2
    values = []
    for first in range(0, chunks, per_tile):
        total = jnp.where(is_main, part[first], 0.0)
        for step in range(1, min(per_tile, chunks - first)):
            total = total + pltpu.roll(part[first + step], CHUNK_OUT * step, 1)
        if first + per_tile < chunks:
            total = total + jnp.where(is_main, 0.0, part[first + per_tile])
        values.append(total)
    rim = jnp.where(is_main, 0.0, part[0])
    if paired:
        packed = rim[:SUBLANES]
        for at in range(1, rows // SUBLANES):
            group = rim[SUBLANES * at : SUBLANES * (at + 1)]
            packed = packed + pltpu.roll(group, LANES - EDGE * at, 1)
        for at, value in enumerate(values):
            out_ref[rows * at : rows * (at + 1), :] = value
        out_ref[rows * tiles :, :] = packed
    else:
        for at, value in enumerate(values + [rim]):
            out_ref[:, LANES * at : LANES * (at + 1)] = value
    sending.wait()


def unpack(packed, rows):
    tiles = [packed[at : at + rows] for at in range(0, packed.shape[0] - SUBLANES, rows)]
    rims = packed[packed.shape[0] - SUBLANES :]
    rim = jnp.concatenate(
        [rims]
        + [pltpu.roll(rims, EDGE * at, 1) for at in range(1, rows // SUBLANES)],
        axis=0,
    )
    lane = lax.broadcasted_iota(jnp.int32, rim.shape, 1)
    return tiles + [jnp.where(lane >= LANES - EDGE, rim, 0.0)]


def transform(early, late, table_hi, table_lo):
    rows = early.shape[0]
    high, low = split(jnp.concatenate([early, late], axis=0))
    first = dot(jnp.concatenate([high, low], axis=0), table_hi)
    both = first[: 2 * rows] + first[2 * rows :] + dot(high, table_lo)
    quarter = lax.broadcasted_iota(jnp.int32, (1, BINS), 1) & 3
    cosine = jnp.where(quarter == 0, 1.0, 0.0) - jnp.where(quarter == 2, 1.0, 0.0)
    sine = jnp.where(quarter == 1, 1.0, 0.0) - jnp.where(quarter == 3, 1.0, 0.0)
    early_re, early_im = both[:rows, :BINS], both[:rows, BINS:]
    late_re, late_im = both[rows:, :BINS], both[rows:, BINS:]
    return (
        early_re + cosine * late_re + sine * late_im,
        early_im + cosine * late_im - sine * late_re,
    )


def whitening(real_part, imag_part, band):
    rows = real_part.shape[0]
    tiles = BINS // LANES
    stacked = []
    for part in split(real_part * real_part + imag_part * imag_part):
        zero = jnp.zeros((rows, LANES), part.dtype)
        wide = jnp.concatenate([zero, part, zero], axis=1)
        stacked += [wide[:, LANES * tile : LANES * (tile + 3)] for tile in range(tiles)]
    banded = dot(jnp.concatenate(stacked, axis=0), band)
    step = rows * tiles
    summed = banded[:step] + banded[step:]
    total = jnp.concatenate(
        [summed[rows * tile : rows * (tile + 1)] for tile in range(tiles)], axis=1
    )
    bins = lax.broadcasted_iota(jnp.int32, (1, BINS), 1)
    count = jnp.minimum(bins + HALF, BINS - 1) - jnp.maximum(bins - HALF, 0) + 1
    return lax.rsqrt(total * (1.0 / count.astype(jnp.float32)) + 1e-06)


def prepare_kernel(
    _, alive_hbm, picks_hbm, fwd_hi_hbm, fwd_lo_hbm, band_hbm, lag_hbm, edge_hbm, order_hbm,
    hi_ref, lo_ref, band_ref, lag_ref, edge_ref, order_ref, alive_out, picks_out,
    alive_ref, picks_ref, sems,
):
    copies = start_copies(
        [
            (alive_hbm, alive_ref),
            (picks_hbm, picks_ref),
            (fwd_hi_hbm, hi_ref),
            (fwd_lo_hbm, lo_ref),
            (band_hbm, band_ref),
            (lag_hbm, lag_ref),
            (edge_hbm, edge_ref),
            (order_hbm, order_ref),
        ],
        sems,
    )
    for copy in copies[:2]:
        copy.wait()
    rows = alive_out.shape[0]
    alive_out[...] = jnp.broadcast_to(
        column(alive_ref[...].astype(jnp.float32)), (rows, LANES)
    )
    channel = lax.broadcasted_iota(jnp.int32, (rows, LANES), 0)
    for slot in range(picks_ref.shape[1]):
        pick = jnp.broadcast_to(picks_ref[:, slot : slot + 1], (rows, LANES))
        picks_out[slot] = jnp.where(channel == pick, 1.0, 0.0)
    for copy in copies[2:]:
        copy.wait()


def spectra_kernel(series_ref, hi_ref, lo_ref, band_ref, alive_ref, *refs):
    spectra_ref = refs[-1]
    rows = alive_ref.shape[0]
    half = S // 2
    if len(refs) > 1:
        mine, other = [unpack(ref[...], rows) for ref in (series_ref, refs[0])]
        first = lax.axis_index("src") == 0
        early = [jnp.where(first, a, b) for a, b in zip(mine, other)]
        late = [jnp.where(first, b, a) for a, b in zip(mine, other)]
        early[-2] = early[-2] + late[-1]
        early, late = [jnp.concatenate(tiles[:-1], axis=1) for tiles in (early, late)]
    else:
        early, late = series_ref[:, :half], series_ref[:, half:]
    real_part, imag_part = transform(early, late, hi_ref[...], lo_ref[...])
    factor = alive_ref[:, :1] * whitening(real_part, imag_part, band_ref[...])
    spectra_ref[:, :BINS] = real_part * factor
    spectra_ref[:, BINS:] = imag_part * factor


def part_bounds(total):
    ends = [total // 2, total]
    return [(a, b) for a, b in zip([0] + ends, ends) if b > a]


def correlate_kernel(
    slots, spectra_ref, pieces_ref, picks_ref, hi_ref, lo_ref, band_ref, lag_ref,
    edge_ref, order_ref, out_hbm, series_ref, rims_ref, source_ref, cross_ref, out_ref, sems,
):
    rows = spectra_ref.shape[0]
    group = out_ref.shape[0] // slots
    half = BINS // LANES
    own = lax.axis_index("blk")
    base = lax.axis_index("src") * group
    tiles = S // 2 // LANES

    for slot in range(slots):
        for block in range(group):
            row = slice(slot * group + block, slot * group + block + 1)
            at = pieces_ref.shape[0] - 1 - 2 * (base + block)
            for tile in range(tiles):
                span = slice(LANES * (slot * tiles + tile), LANES * (slot * tiles + tile + 1))
                early = slice(LANES * tile, LANES * (tile + 1))
                late = slice(S // 2 + LANES * tile, S // 2 + LANES * (tile + 1))
                series_ref[row, early] = pieces_ref[at, :, span]
                series_ref[row, late] = pieces_ref[at - 1, :, span]
            rims_ref[row, :] = pieces_ref[at - 1, :, LANES * slots * tiles :]
    rims = jnp.concatenate(
        [
            pltpu.roll(rims_ref[slot * group : (slot + 1) * group, :], EDGE * slot, 1)
            for slot in range(slots)
        ],
        axis=0,
    )
    lane = lax.broadcasted_iota(jnp.int32, rims.shape, 1)
    seam = slice(S // 2 - LANES, S // 2)
    series_ref[:, seam] = series_ref[:, seam] + jnp.where(lane >= LANES - EDGE, rims, 0.0)
    early, late = series_ref[:, : S // 2], series_ref[:, S // 2 :]
    real_part, imag_part = transform(early, late, hi_ref[...], lo_ref[...])
    factor = whitening(real_part, imag_part, band_ref[...])
    source_ref[:, :BINS] = real_part * factor
    source_ref[:, BINS:] = imag_part * factor
    copies = []
    for part, (first, last) in enumerate(part_bounds(group * slots)):
        per_part = last - first
        edges = [0.0] * per_part
        for tile in range(half):
            re = slice(LANES * tile, LANES * (tile + 1))
            im = slice(BINS + LANES * tile, BINS + LANES * (tile + 1))
            rec_re, rec_im = spectra_ref[:, re], spectra_ref[:, im]
            for source in range(first, last):
                block, slot = divmod(source, slots)
                at = slot * group + block
                src_re, src_im = source_ref[at : at + 1, re], source_ref[at : at + 1, im]
                where = slice(rows * source, rows * (source + 1))
                cross_re = (src_re * rec_re + src_im * rec_im).astype(jnp.bfloat16)
                edges[source - first] += cross_re.astype(jnp.float32) * edge_ref[:, re]
                cross_ref[where, re] = cross_re
                cross_ref[where, im] = (src_re * rec_im - src_im * rec_re).astype(jnp.bfloat16)
        where = slice(rows * first, rows * last)
        even = dot(cross_ref[where, :BINS], lag_ref[:BINS, :])
        odd = dot(cross_ref[where, BINS:], lag_ref[BINS:, :])
        edge = jnp.sum(jnp.concatenate(edges, axis=0), axis=1, keepdims=True)
        at_zero = lax.broadcasted_iota(jnp.int32, even.shape, 1) == 0
        keep = []
        for source in range(first, last):
            block, slot = divmod(source, slots)
            mask = 1.0 - jnp.where(own == base + block, 1.0, 0.0) * picks_ref[slot]
            keep.append(jnp.concatenate([mask] * (LAGS // 2 // LANES), axis=1))
        keep = jnp.concatenate(keep, axis=0)
        later = (jnp.where(at_zero, even, even + odd) * keep).astype(jnp.bfloat16)
        earlier = (jnp.where(at_zero, edge + odd, even - odd) * keep).astype(jnp.bfloat16)
        earlier = dot(earlier, order_ref[...]).astype(jnp.bfloat16)
        for source in range(first, last):
            at = slice(rows * (source - first), rows * (source - first + 1))
            out_ref[source, :, : LAGS // 2] = earlier[at]
            out_ref[source, :, LAGS // 2 :] = later[at]
        span = pl.ds(first, per_part)
        copies.append(pltpu.make_async_copy(out_ref.at[span], out_hbm.at[span], sems.at[part]))
        copies[-1].start()
    for copy in copies:
        copy.wait()


HBM = pl.BlockSpec(memory_space=pltpu.HBM)
VMEM = pl.BlockSpec(memory_space=pltpu.VMEM)
PARAMS = pltpu.CompilerParams(vmem_limit_bytes=VMEM_LIMIT)


def in_hbm(*arrays):
    return [pltpu.with_memory_space_constraint(array, pltpu.HBM) for array in arrays]


def shaped(*shape, dtype=jnp.float32):
    return jax.ShapeDtypeStruct(shape, dtype)


def local(raw_records, fir_taps, alive_mask, source_index):
    src_count = lax.axis_size("src")
    blk_count = lax.axis_size("blk")
    rows, raw_count = raw_records.shape
    slots = source_index.shape[1]
    group = blk_count // src_count
    out_count = raw_count // DEC
    width = -(-out_count // LANES) * LANES + LANES
    chunks = raw_count // CHUNK
    paired = src_count == 2 and 2 * out_count == S
    bf16 = jnp.bfloat16
    forward_hi, forward_lo = split_table(forward_table())
    alive_row = alive_mask.reshape(1, rows)

    with jax.named_scope("decimate"):
        device_count = blk_count * src_count
        main = slots * (width - LANES)
        decimated, pieces = pl.pallas_call(
            lambda *refs: decimate_kernel(paired, *refs),
            out_shape=(
                shaped(rows * (S // 2 // LANES) + SUBLANES, LANES)
                if paired
                else shaped(rows, width),
                shaped(device_count * (main // LANES + 1), LANES),
            ),
            in_specs=[HBM] * 4,
            out_specs=(VMEM, HBM),
            scratch_shapes=[
                pltpu.VMEM((rows, raw_count), jnp.float32),
                pltpu.VMEM((1, TAPS), jnp.float32),
                pltpu.SMEM((1, rows), jnp.int32),
                pltpu.SMEM((1, slots), jnp.int32),
                pltpu.VMEM((SUBLANES * slots, CHUNK), jnp.float32),
                pltpu.VMEM((device_count * (main // LANES + 1), LANES), jnp.float32),
                pltpu.SemaphoreType.DMA((rows // SUBLANES + 3,)),
            ],
            compiler_params=PARAMS,
        )(*in_hbm(raw_records, fir_taps.reshape(1, TAPS), alive_row, source_index))

    def whole(shards):
        rims = jnp.pad(shards[1:, :, width - EDGE :], ((0, 1), (0, 0), (out_count - EDGE, 0)))
        series = shards[:, :, :out_count] + rims
        return series.transpose(1, 0, 2).reshape(shards.shape[1], S)

    with jax.named_scope("gather_sources"):
        gathered = lax.all_to_all(
            pieces.reshape(device_count, 1, main + LANES),
            ("blk", "src"),
            split_axis=0,
            concat_axis=0,
            tiled=True,
            axis_index_groups=[list(reversed(range(device_count)))],
        )
        if not paired:
            gathered = gathered[::-1]
            shards = gathered.reshape(blk_count, src_count, main + LANES)
            shards = shards.transpose(1, 0, 2)
            rims = [shards[:, :, main + LANES - EDGE * (slot + 1) :] for slot in range(slots)]
            rims = jnp.stack([rim[:, :, :EDGE] for rim in rims], axis=2)
            rims = jnp.pad(rims, ((0, 0), (0, 0), (0, 0), (LANES - EDGE, 0)))
            series = shards[:, :, :main].reshape(src_count, blk_count, slots, width - LANES)
            series = jnp.concatenate([series, rims], axis=3)
            series = whole(series.reshape(src_count, blk_count * slots, width))
            series = series.reshape(blk_count, slots, 2, S // 2).transpose(0, 2, 1, 3)
            series = series.reshape(blk_count * 2, 1, slots * S // 2)
            gathered = jnp.pad(series, ((0, 0), (0, 0), (0, LANES)))[::-1]

    with jax.named_scope("prepare"):
        out_shape = (
            shaped(S // 2, NFFT, dtype=bf16),
            shaped(S // 2, NFFT, dtype=bf16),
            shaped(3 * LANES, LANES, dtype=bf16),
            shaped(NFFT, LAGS // 2, dtype=bf16),
            shaped(1, BINS),
            shaped(LAGS // 2, LAGS // 2, dtype=bf16),
            shaped(rows, LANES),
            shaped(slots, rows, LANES),
        )
        table_hi, table_lo, band, lag, edge, order, alive, picks = pl.pallas_call(
            prepare_kernel,
            out_shape=out_shape,
            in_specs=[VMEM] + [HBM] * 8,
            out_specs=(VMEM,) * len(out_shape),
            scratch_shapes=[
                pltpu.VMEM((1, rows), jnp.int32),
                pltpu.VMEM((1, slots), jnp.int32),
                pltpu.SemaphoreType.DMA((8,)),
            ],
            compiler_params=PARAMS,
            cost_estimate=pl.CostEstimate(
                flops=0, bytes_accessed=4 * S * NFFT, transcendentals=0
            ),
        )(
            decimated,
            *in_hbm(
                alive_row,
                source_index,
                jnp.asarray(forward_hi),
                jnp.asarray(forward_lo),
                jnp.asarray(band_table()),
                *map(jnp.asarray, folded_lag_tables()),
            ),
        )

    with jax.named_scope("regroup"):
        if paired:
            series = [decimated]
            other = [lax.ppermute(decimated, "src", [(0, 1), (1, 0)])]
        else:
            series = [whole(lax.all_gather(decimated, "src", axis=0))]
            other = []

    with jax.named_scope("spectra"):
        operands = series + [table_hi, table_lo, band, alive] + other
        spectra = pl.pallas_call(
            spectra_kernel,
            out_shape=shaped(rows, NFFT),
            in_specs=[VMEM] * len(operands),
            out_specs=VMEM,
            compiler_params=PARAMS,
        )(*operands)

    with jax.named_scope("correlate"):
        total = group * slots
        return pl.pallas_call(
            lambda *refs: correlate_kernel(slots, *refs),
            out_shape=shaped(total, rows, LAGS, dtype=bf16),
            in_specs=[VMEM] * 9,
            out_specs=HBM,
            scratch_shapes=[
                pltpu.VMEM((total, S), jnp.float32),
                pltpu.VMEM((total, LANES), jnp.float32),
                pltpu.VMEM((total, NFFT), jnp.float32),
                pltpu.VMEM((total * rows, NFFT), bf16),
                pltpu.VMEM((total, rows, LAGS), bf16),
                pltpu.SemaphoreType.DMA((PARTS,)),
            ],
            compiler_params=PARAMS,
        )(spectra, gathered, picks, table_hi, table_lo, band, lag, edge, order)


def solution(mesh):
    in_specs = (P("blk", "src"), P(), P("blk"), P("blk", None))
    out_specs = P("src", "blk", None)
    return jax.shard_map(local, mesh=mesh, in_specs=in_specs, out_specs=out_specs, check_vma=False)
```

```python
import math

import jax
import jax.numpy as jnp
import numpy as np
from jax import lax
from jax.experimental import pallas as pl
from jax.experimental.pallas import tpu as pltpu
from jax.sharding import PartitionSpec as P

S = 512
NFFT = 1024
BINS = NFFT // 2
LAGS = 512
TAPS = 64
DEC = 20
HALF = 64
LANES = 128
SUBLANES = 8
PARTS = 3
EDGE = (TAPS - 1) // DEC
CHUNK = 640
CHUNK_OUT = CHUNK // DEC
VMEM_LIMIT = 48 * 1024 * 1024


def forward_table():
    phases = 2.0 * math.pi / NFFT * (np.outer(np.arange(S // 2), np.arange(BINS)) % NFFT)
    return np.concatenate([np.cos(phases), -np.sin(phases)], axis=1).astype(np.float32)


def split_table(table):
    high = table.astype(jnp.bfloat16)
    low = (table - high.astype(np.float32)).astype(jnp.bfloat16)
    return high, low


def band_table():
    bins = np.arange(3 * LANES)[:, None] - LANES
    return (np.abs(bins - np.arange(LANES)[None, :]) <= HALF).astype(jnp.bfloat16)


def lag_table():
    bins = np.arange(BINS)[:, None]
    shift = np.arange(LAGS)[None, :] - LAGS // 2
    phases = 2.0 * math.pi / NFFT * (bins * shift % NFFT)
    weight = np.where(bins == 0, 0.5, 1.0) / math.sqrt(BINS)
    table = np.concatenate([weight * np.cos(phases), -weight * np.sin(phases)], axis=0)
    return table.astype(np.float32).astype(jnp.bfloat16)


def split(value):
    high = value.astype(jnp.bfloat16)
    return high, (value - high.astype(jnp.float32)).astype(jnp.bfloat16)


def dot(a, b):
    return jnp.dot(a, b, preferred_element_type=jnp.float32)


def column(row):
    count = row.shape[1]
    at = [lax.broadcasted_iota(jnp.int32, (count, count), axis) for axis in range(2)]
    rows = jnp.broadcast_to(row, (count, count))
    return jnp.sum(jnp.where(at[0] == at[1], rows, 0.0), axis=1, keepdims=True)


def start_copies(pairs, sems):
    copies = [
        pltpu.make_async_copy(source, target, sems.at[at])
        for at, (source, target) in enumerate(pairs)
    ]
    for copy in copies:
        copy.start()
    return copies


def decimate_kernel(
    paired, raw_hbm, taps_hbm, alive_hbm, picks_hbm, out_ref, pieces_hbm,
    raw_ref, taps_ref, alive_ref, picks_ref, source_ref, pieces_ref, sems,
):
    rows = raw_hbm.shape[0]
    chunks = raw_hbm.shape[1] // CHUNK
    slots = picks_ref.shape[1]
    per_tile = LANES // CHUNK_OUT
    tiles = -(-chunks // per_tile)
    pairs = [(taps_hbm, taps_ref)]
    for at in range(0, rows, SUBLANES):
        span = slice(at, at + SUBLANES)
        pairs.append((raw_hbm.at[span], raw_ref.at[span]))
    pairs += [(picks_hbm, picks_ref), (alive_hbm, alive_ref)]
    copies = start_copies(pairs, sems)
    source_ref[...] = jnp.zeros_like(source_ref)
    copies[0].wait()
    taps = jnp.broadcast_to(taps_ref[...], (SUBLANES, TAPS))
    eight = jnp.concatenate([taps, jnp.zeros((SUBLANES, CHUNK - TAPS), jnp.float32)], axis=1)
    for _ in range(2):
        eight = pltpu.roll(eight, 0, 1, stride=DEC // 2, stride_axis=0)
    wrapped = jnp.concatenate(
        [eight]
        + [pltpu.roll(eight, DEC * at, 1) for at in range(SUBLANES, CHUNK_OUT, SUBLANES)],
        axis=0,
    )
    lane = lax.broadcasted_iota(jnp.int32, (CHUNK_OUT, CHUNK), 1)
    row = lax.broadcasted_iota(jnp.int32, (CHUNK_OUT, CHUNK), 0)
    main = jnp.where(lane >= DEC * row, wrapped, 0.0)
    rim = wrapped - main
    gap = jnp.zeros((LANES - 2 * CHUNK_OUT, CHUNK), jnp.float32)
    weights_hi, weights_lo = split(jnp.concatenate([main, gap, rim], axis=0).T)
    weights = jnp.concatenate([weights_hi, weights_lo], axis=1)

    def filtered(stacked):
        high, low = split(stacked)
        both = dot(high, weights)
        return both[:, :LANES] + both[:, LANES:] + dot(low, weights_hi)

    for copy in copies[1:]:
        copy.wait()
    for slot in range(slots):
        pick = picks_ref[0, slot]
        alive = alive_ref[0, pick].astype(jnp.float32)
        for j in range(chunks):
            at = SUBLANES * slot + j
            span = slice(CHUNK * j, CHUNK * (j + 1))
            source_ref[at : at + 1, :] = raw_ref[pl.ds(pick, 1), span] * alive
    high, low = split(source_ref[...])
    count = slots * SUBLANES
    both = dot(jnp.concatenate([high, low], axis=0), weights)
    sources = both[:count, :LANES] + both[:count, LANES:] + both[count:, :LANES]
    lane = lax.broadcasted_iota(jnp.int32, (SUBLANES, LANES), 1)
    row = lax.broadcasted_iota(jnp.int32, (SUBLANES, LANES), 0)
    leads = row % per_tile == 0
    wraps = lane >= LANES - EDGE
    piece = []
    rims = jnp.zeros((1, LANES), jnp.float32)
    for slot in range(slots):
        source = sources[SUBLANES * slot : SUBLANES * (slot + 1)]
        placed = source
        for step in range(1, per_tile):
            rolled = pltpu.roll(source, CHUNK_OUT * step, 1)
            placed = jnp.where(row % per_tile == step, rolled, placed)
        own = jnp.where(leads & wraps, 0.0, placed)
        rim = placed - own
        for tile in range(tiles):
            first = per_tile * tile
            inside = jnp.where((row >= first) & (row < first + per_tile), own, 0.0)
            before = jnp.where(row == first + per_tile, rim, 0.0)
            piece.append(jnp.sum(inside + before, axis=0, keepdims=True))
        rims = rims + pltpu.roll(rim[:1], LANES - EDGE * slot if slot else 0, 1)
    piece.append(rims)
    size = len(piece)
    spread = [jnp.broadcast_to(value, (SUBLANES, LANES)) for value in piece]
    eight = []
    for group in range(size):
        place = (row + SUBLANES * group) % size
        total = spread[0]
        for at in range(1, size):
            total = jnp.where(place == at, spread[at], total)
        eight.append(total)
    eight = jnp.concatenate(eight, axis=0)
    for at in range(0, pieces_ref.shape[0], SUBLANES * size):
        pieces_ref[at : at + SUBLANES * size, :] = eight
    sending = pltpu.make_async_copy(pieces_ref, pieces_hbm, sems.at[0])
    sending.start()

    result = filtered(
        jnp.concatenate(
            [raw_ref[:, CHUNK * j : CHUNK * (j + 1)] for j in range(chunks)], axis=0
        )
    )
    part = [result[rows * j : rows * (j + 1)] for j in range(chunks)]
    is_main = lax.broadcasted_iota(jnp.int32, (rows, LANES), 1) < LANES // 2
    values = []
    for first in range(0, chunks, per_tile):
        total = jnp.where(is_main, part[first], 0.0)
        for step in range(1, min(per_tile, chunks - first)):
            total = total + pltpu.roll(part[first + step], CHUNK_OUT * step, 1)
        if first + per_tile < chunks:
            total = total + jnp.where(is_main, 0.0, part[first + per_tile])
        values.append(total)
    rim = jnp.where(is_main, 0.0, part[0])
    if paired:
        packed = rim[:SUBLANES]
        for at in range(1, rows // SUBLANES):
            group = rim[SUBLANES * at : SUBLANES * (at + 1)]
            packed = packed + pltpu.roll(group, LANES - EDGE * at, 1)
        for at, value in enumerate(values):
            out_ref[rows * at : rows * (at + 1), :] = value
        out_ref[rows * tiles :, :] = packed
    else:
        for at, value in enumerate(values + [rim]):
            out_ref[:, LANES * at : LANES * (at + 1)] = value
    sending.wait()


def unpack(packed, rows):
    tiles = [packed[at : at + rows] for at in range(0, packed.shape[0] - SUBLANES, rows)]
    rims = packed[packed.shape[0] - SUBLANES :]
    rim = jnp.concatenate(
        [rims]
        + [pltpu.roll(rims, EDGE * at, 1) for at in range(1, rows // SUBLANES)],
        axis=0,
    )
    lane = lax.broadcasted_iota(jnp.int32, rim.shape, 1)
    return tiles + [jnp.where(lane >= LANES - EDGE, rim, 0.0)]


def transform(early, late, table_hi, table_lo):
    rows = early.shape[0]
    high, low = split(jnp.concatenate([early, late], axis=0))
    first = dot(jnp.concatenate([high, low], axis=0), table_hi)
    both = first[: 2 * rows] + first[2 * rows :] + dot(high, table_lo)
    quarter = lax.broadcasted_iota(jnp.int32, (1, BINS), 1) & 3
    cosine = jnp.where(quarter == 0, 1.0, 0.0) - jnp.where(quarter == 2, 1.0, 0.0)
    sine = jnp.where(quarter == 1, 1.0, 0.0) - jnp.where(quarter == 3, 1.0, 0.0)
    early_re, early_im = both[:rows, :BINS], both[:rows, BINS:]
    late_re, late_im = both[rows:, :BINS], both[rows:, BINS:]
    return (
        early_re + cosine * late_re + sine * late_im,
        early_im + cosine * late_im - sine * late_re,
    )


def whitening(real_part, imag_part, band):
    rows = real_part.shape[0]
    tiles = BINS // LANES
    stacked = []
    for part in split(real_part * real_part + imag_part * imag_part):
        zero = jnp.zeros((rows, LANES), part.dtype)
        wide = jnp.concatenate([zero, part, zero], axis=1)
        stacked += [wide[:, LANES * tile : LANES * (tile + 3)] for tile in range(tiles)]
    banded = dot(jnp.concatenate(stacked, axis=0), band)
    step = rows * tiles
    summed = banded[:step] + banded[step:]
    total = jnp.concatenate(
        [summed[rows * tile : rows * (tile + 1)] for tile in range(tiles)], axis=1
    )
    bins = lax.broadcasted_iota(jnp.int32, (1, BINS), 1)
    count = jnp.minimum(bins + HALF, BINS - 1) - jnp.maximum(bins - HALF, 0) + 1
    return lax.rsqrt(total * (1.0 / count.astype(jnp.float32)) + 1e-06)


def prepare_kernel(
    _, alive_hbm, picks_hbm, fwd_hi_hbm, fwd_lo_hbm, band_hbm, lag_hbm,
    hi_ref, lo_ref, band_ref, lag_ref, alive_out, picks_out, alive_ref, picks_ref, sems,
):
    copies = start_copies(
        [
            (alive_hbm, alive_ref),
            (picks_hbm, picks_ref),
            (fwd_hi_hbm, hi_ref),
            (fwd_lo_hbm, lo_ref),
            (band_hbm, band_ref),
            (lag_hbm, lag_ref),
        ],
        sems,
    )
    for copy in copies[:2]:
        copy.wait()
    rows = alive_out.shape[0]
    alive_out[...] = jnp.broadcast_to(
        column(alive_ref[...].astype(jnp.float32)), (rows, LANES)
    )
    channel = lax.broadcasted_iota(jnp.int32, (rows, LANES), 0)
    for slot in range(picks_ref.shape[1]):
        pick = jnp.broadcast_to(picks_ref[:, slot : slot + 1], (rows, LANES))
        picks_out[slot] = jnp.where(channel == pick, 1.0, 0.0)
    for copy in copies[2:]:
        copy.wait()


def spectra_kernel(series_ref, hi_ref, lo_ref, band_ref, alive_ref, *refs):
    spectra_ref = refs[-1]
    rows = alive_ref.shape[0]
    half = S // 2
    if len(refs) > 1:
        mine, other = [unpack(ref[...], rows) for ref in (series_ref, refs[0])]
        first = lax.axis_index("src") == 0
        early = [jnp.where(first, a, b) for a, b in zip(mine, other)]
        late = [jnp.where(first, b, a) for a, b in zip(mine, other)]
        early[-2] = early[-2] + late[-1]
        early, late = [jnp.concatenate(tiles[:-1], axis=1) for tiles in (early, late)]
    else:
        early, late = series_ref[:, :half], series_ref[:, half:]
    real_part, imag_part = transform(early, late, hi_ref[...], lo_ref[...])
    factor = alive_ref[:, :1] * whitening(real_part, imag_part, band_ref[...])
    spectra_ref[:, :BINS] = real_part * factor
    spectra_ref[:, BINS:] = imag_part * factor


def part_bounds(total):
    ends = [3 * total // 8, 3 * total // 4, total]
    return [(a, b) for a, b in zip([0] + ends, ends) if b > a]


def correlate_kernel(
    slots, spectra_ref, pieces_ref, picks_ref, hi_ref, lo_ref, band_ref, lag_ref, out_hbm,
    series_ref, rims_ref, source_ref, difference_ref, sum_ref, cross_ref, out_ref, sems,
):
    rows = spectra_ref.shape[0]
    group = out_ref.shape[0] // slots
    half = BINS // LANES
    own = lax.axis_index("blk")
    base = lax.axis_index("src") * group
    tiles = S // 2 // LANES

    for slot in range(slots):
        for block in range(group):
            row = slice(slot * group + block, slot * group + block + 1)
            at = pieces_ref.shape[0] - 1 - 2 * (base + block)
            for tile in range(tiles):
                span = slice(LANES * (slot * tiles + tile), LANES * (slot * tiles + tile + 1))
                early = slice(LANES * tile, LANES * (tile + 1))
                late = slice(S // 2 + LANES * tile, S // 2 + LANES * (tile + 1))
                series_ref[row, early] = pieces_ref[at, :, span]
                series_ref[row, late] = pieces_ref[at - 1, :, span]
            rims_ref[row, :] = pieces_ref[at - 1, :, LANES * slots * tiles :]
    rims = jnp.concatenate(
        [
            pltpu.roll(rims_ref[slot * group : (slot + 1) * group, :], EDGE * slot, 1)
            for slot in range(slots)
        ],
        axis=0,
    )
    lane = lax.broadcasted_iota(jnp.int32, rims.shape, 1)
    seam = slice(S // 2 - LANES, S // 2)
    series_ref[:, seam] = series_ref[:, seam] + jnp.where(lane >= LANES - EDGE, rims, 0.0)
    early, late = series_ref[:, : S // 2], series_ref[:, S // 2 :]
    real_part, imag_part = transform(early, late, hi_ref[...], lo_ref[...])
    factor = whitening(real_part, imag_part, band_ref[...])
    real_part, imag_part = real_part * factor, imag_part * factor
    source_ref[...] = real_part
    difference_ref[...] = imag_part - real_part
    sum_ref[...] = imag_part + real_part
    copies = []
    for part, (first, last) in enumerate(part_bounds(group * slots)):
        per_part = last - first
        for tile in range(half):
            re = slice(LANES * tile, LANES * (tile + 1))
            im = slice(BINS + LANES * tile, BINS + LANES * (tile + 1))
            rec_re, rec_im = spectra_ref[:, re], spectra_ref[:, im]
            rec_sum = rec_re + rec_im
            for source in range(first, last):
                block, slot = divmod(source, slots)
                at = slot * group + block
                common = source_ref[at : at + 1, re] * rec_sum
                where = slice(rows * source, rows * (source + 1))
                cross_ref[where, re] = (common + difference_ref[at : at + 1, re] * rec_im).astype(
                    jnp.bfloat16
                )
                cross_ref[where, im] = (common - sum_ref[at : at + 1, re] * rec_re).astype(
                    jnp.bfloat16
                )
        lagged = dot(cross_ref[rows * first : rows * (first + per_part), :], lag_ref[...])
        for source in range(first, last):
            at = source - first
            out_ref[source] = lagged[rows * at : rows * (at + 1)].astype(jnp.bfloat16)
        for slot in range(slots):
            mine = (own - base) * slots + slot
            inside = (mine >= first) & (mine < last)
            at = jnp.where(inside, mine, first)
            keep = 1.0 - jnp.where(inside, 1.0, 0.0) * picks_ref[slot]
            keep = jnp.concatenate([keep] * (LAGS // LANES), axis=1)
            out_ref[at] = (out_ref[at].astype(jnp.float32) * keep).astype(jnp.bfloat16)
        span = pl.ds(first, per_part)
        copies.append(pltpu.make_async_copy(out_ref.at[span], out_hbm.at[span], sems.at[part]))
        copies[-1].start()
    for copy in copies:
        copy.wait()


HBM = pl.BlockSpec(memory_space=pltpu.HBM)
VMEM = pl.BlockSpec(memory_space=pltpu.VMEM)
PARAMS = pltpu.CompilerParams(vmem_limit_bytes=VMEM_LIMIT)


def in_hbm(*arrays):
    return [pltpu.with_memory_space_constraint(array, pltpu.HBM) for array in arrays]


def shaped(*shape, dtype=jnp.float32):
    return jax.ShapeDtypeStruct(shape, dtype)


def local(raw_records, fir_taps, alive_mask, source_index):
    src_count = lax.axis_size("src")
    blk_count = lax.axis_size("blk")
    rows, raw_count = raw_records.shape
    slots = source_index.shape[1]
    group = blk_count // src_count
    out_count = raw_count // DEC
    width = -(-out_count // LANES) * LANES + LANES
    chunks = raw_count // CHUNK
    paired = src_count == 2 and 2 * out_count == S
    bf16 = jnp.bfloat16
    forward_hi, forward_lo = split_table(forward_table())
    alive_row = alive_mask.reshape(1, rows)

    with jax.named_scope("decimate"):
        device_count = blk_count * src_count
        main = slots * (width - LANES)
        decimated, pieces = pl.pallas_call(
            lambda *refs: decimate_kernel(paired, *refs),
            out_shape=(
                shaped(rows * (S // 2 // LANES) + SUBLANES, LANES)
                if paired
                else shaped(rows, width),
                shaped(device_count * (main // LANES + 1), LANES),
            ),
            in_specs=[HBM] * 4,
            out_specs=(VMEM, HBM),
            scratch_shapes=[
                pltpu.VMEM((rows, raw_count), jnp.float32),
                pltpu.VMEM((1, TAPS), jnp.float32),
                pltpu.SMEM((1, rows), jnp.int32),
                pltpu.SMEM((1, slots), jnp.int32),
                pltpu.VMEM((SUBLANES * slots, CHUNK), jnp.float32),
                pltpu.VMEM((device_count * (main // LANES + 1), LANES), jnp.float32),
                pltpu.SemaphoreType.DMA((rows // SUBLANES + 3,)),
            ],
            compiler_params=PARAMS,
        )(*in_hbm(raw_records, fir_taps.reshape(1, TAPS), alive_row, source_index))

    def whole(shards):
        rims = jnp.pad(shards[1:, :, width - EDGE :], ((0, 1), (0, 0), (out_count - EDGE, 0)))
        series = shards[:, :, :out_count] + rims
        return series.transpose(1, 0, 2).reshape(shards.shape[1], S)

    with jax.named_scope("gather_sources"):
        gathered = lax.all_to_all(
            pieces.reshape(device_count, 1, main + LANES),
            ("blk", "src"),
            split_axis=0,
            concat_axis=0,
            tiled=True,
            axis_index_groups=[list(reversed(range(device_count)))],
        )
        if not paired:
            gathered = gathered[::-1]
            shards = gathered.reshape(blk_count, src_count, main + LANES)
            shards = shards.transpose(1, 0, 2)
            rims = [shards[:, :, main + LANES - EDGE * (slot + 1) :] for slot in range(slots)]
            rims = jnp.stack([rim[:, :, :EDGE] for rim in rims], axis=2)
            rims = jnp.pad(rims, ((0, 0), (0, 0), (0, 0), (LANES - EDGE, 0)))
            series = shards[:, :, :main].reshape(src_count, blk_count, slots, width - LANES)
            series = jnp.concatenate([series, rims], axis=3)
            series = whole(series.reshape(src_count, blk_count * slots, width))
            series = series.reshape(blk_count, slots, 2, S // 2).transpose(0, 2, 1, 3)
            series = series.reshape(blk_count * 2, 1, slots * S // 2)
            gathered = jnp.pad(series, ((0, 0), (0, 0), (0, LANES)))[::-1]

    with jax.named_scope("prepare"):
        out_shape = (
            shaped(S // 2, NFFT, dtype=bf16),
            shaped(S // 2, NFFT, dtype=bf16),
            shaped(3 * LANES, LANES, dtype=bf16),
            shaped(NFFT, LAGS, dtype=bf16),
            shaped(rows, LANES),
            shaped(slots, rows, LANES),
        )
        table_hi, table_lo, band, lag, alive, picks = pl.pallas_call(
            prepare_kernel,
            out_shape=out_shape,
            in_specs=[VMEM] + [HBM] * 6,
            out_specs=(VMEM,) * len(out_shape),
            scratch_shapes=[
                pltpu.VMEM((1, rows), jnp.int32),
                pltpu.VMEM((1, slots), jnp.int32),
                pltpu.SemaphoreType.DMA((6,)),
            ],
            compiler_params=PARAMS,
            cost_estimate=pl.CostEstimate(
                flops=0, bytes_accessed=4 * S * NFFT, transcendentals=0
            ),
        )(
            decimated,
            *in_hbm(
                alive_row,
                source_index,
                jnp.asarray(forward_hi),
                jnp.asarray(forward_lo),
                jnp.asarray(band_table()),
                jnp.asarray(lag_table()),
            ),
        )

    with jax.named_scope("regroup"):
        if paired:
            series = [decimated]
            other = [lax.ppermute(decimated, "src", [(0, 1), (1, 0)])]
        else:
            series = [whole(lax.all_gather(decimated, "src", axis=0))]
            other = []

    with jax.named_scope("spectra"):
        operands = series + [table_hi, table_lo, band, alive] + other
        spectra = pl.pallas_call(
            spectra_kernel,
            out_shape=shaped(rows, NFFT),
            in_specs=[VMEM] * len(operands),
            out_specs=VMEM,
            compiler_params=PARAMS,
        )(*operands)

    with jax.named_scope("correlate"):
        total = group * slots
        return pl.pallas_call(
            lambda *refs: correlate_kernel(slots, *refs),
            out_shape=shaped(total, rows, LAGS, dtype=bf16),
            in_specs=[VMEM] * 7,
            out_specs=HBM,
            scratch_shapes=[
                pltpu.VMEM((total, S), jnp.float32),
                pltpu.VMEM((total, LANES), jnp.float32),
                pltpu.VMEM((total, BINS), jnp.float32),
                pltpu.VMEM((total, BINS), jnp.float32),
                pltpu.VMEM((total, BINS), jnp.float32),
                pltpu.VMEM((total * rows, NFFT), bf16),
                pltpu.VMEM((total, rows, LAGS), bf16),
                pltpu.SemaphoreType.DMA((PARTS,)),
            ],
            compiler_params=PARAMS,
        )(spectra, gathered, picks, table_hi, table_lo, band, lag)


def solution(mesh):
    in_specs = (P("blk", "src"), P(), P("blk"), P("blk", None))
    out_specs = P("src", "blk", None)
    return jax.shard_map(local, mesh=mesh, in_specs=in_specs, out_specs=out_specs, check_vma=False)
```

```python
import math

import jax
import jax.numpy as jnp
import numpy as np
from jax import lax
from jax.experimental import pallas as pl
from jax.experimental.pallas import tpu as pltpu
from jax.sharding import PartitionSpec as P

S = 512
NFFT = 1024
BINS = NFFT // 2
LAGS = 512
TAPS = 64
DEC = 20
HALF = 64
LANES = 128
SUBLANES = 8
PARTS = 2
EDGE = (TAPS - 1) // DEC
CHUNK = 640
CHUNK_OUT = CHUNK // DEC
VMEM_LIMIT = 48 * 1024 * 1024


def forward_table():
    phases = 2.0 * math.pi / NFFT * (np.outer(np.arange(S // 2), np.arange(BINS)) % NFFT)
    return np.concatenate([np.cos(phases), -np.sin(phases)], axis=1).astype(np.float32)


def split_table(table):
    high = table.astype(jnp.bfloat16)
    low = (table - high.astype(np.float32)).astype(jnp.bfloat16)
    return high, low


def band_table():
    bins = np.arange(3 * LANES)[:, None] - LANES
    return (np.abs(bins - np.arange(LANES)[None, :]) <= HALF).astype(jnp.bfloat16)


def lag_table():
    bins = np.arange(BINS)[:, None]
    shift = np.arange(LAGS)[None, :] - LAGS // 2
    phases = 2.0 * math.pi / NFFT * (bins * shift % NFFT)
    weight = np.where(bins == 0, 0.5, 1.0) / math.sqrt(BINS)
    table = np.concatenate([weight * np.cos(phases), -weight * np.sin(phases)], axis=0)
    return table.astype(np.float32).astype(jnp.bfloat16)


def split(value):
    high = value.astype(jnp.bfloat16)
    return high, (value - high.astype(jnp.float32)).astype(jnp.bfloat16)


def dot(a, b):
    return jnp.dot(a, b, preferred_element_type=jnp.float32)


def column(row):
    count = row.shape[1]
    at = [lax.broadcasted_iota(jnp.int32, (count, count), axis) for axis in range(2)]
    rows = jnp.broadcast_to(row, (count, count))
    return jnp.sum(jnp.where(at[0] == at[1], rows, 0.0), axis=1, keepdims=True)


def start_copies(pairs, sems):
    copies = [
        pltpu.make_async_copy(source, target, sems.at[at])
        for at, (source, target) in enumerate(pairs)
    ]
    for copy in copies:
        copy.start()
    return copies


def decimate_kernel(
    paired, raw_hbm, taps_hbm, alive_hbm, picks_hbm, out_ref, pieces_hbm,
    raw_ref, taps_ref, alive_ref, picks_ref, source_ref, pieces_ref, sems,
):
    rows = raw_hbm.shape[0]
    chunks = raw_hbm.shape[1] // CHUNK
    slots = picks_ref.shape[1]
    per_tile = LANES // CHUNK_OUT
    tiles = -(-chunks // per_tile)
    pairs = [(taps_hbm, taps_ref), (picks_hbm, picks_ref), (alive_hbm, alive_ref)]
    for at in range(0, rows, SUBLANES):
        span = slice(at, at + SUBLANES)
        pairs.append((raw_hbm.at[span], raw_ref.at[span]))
    copies = start_copies(pairs, sems)
    source_ref[...] = jnp.zeros_like(source_ref)
    copies[0].wait()
    taps = jnp.broadcast_to(taps_ref[...], (SUBLANES, TAPS))
    eight = jnp.concatenate([taps, jnp.zeros((SUBLANES, CHUNK - TAPS), jnp.float32)], axis=1)
    for _ in range(2):
        eight = pltpu.roll(eight, 0, 1, stride=DEC // 2, stride_axis=0)
    wrapped = jnp.concatenate(
        [eight]
        + [pltpu.roll(eight, DEC * at, 1) for at in range(SUBLANES, CHUNK_OUT, SUBLANES)],
        axis=0,
    )
    lane = lax.broadcasted_iota(jnp.int32, (CHUNK_OUT, CHUNK), 1)
    row = lax.broadcasted_iota(jnp.int32, (CHUNK_OUT, CHUNK), 0)
    main = jnp.where(lane >= DEC * row, wrapped, 0.0)
    rim = wrapped - main
    gap = jnp.zeros((LANES - 2 * CHUNK_OUT, CHUNK), jnp.float32)
    weights_hi, weights_lo = split(jnp.concatenate([main, gap, rim], axis=0).T)
    weights = jnp.concatenate([weights_hi, weights_lo], axis=1)

    def filtered(stacked):
        high, low = split(stacked)
        both = dot(high, weights)
        return both[:, :LANES] + both[:, LANES:] + dot(low, weights_hi)

    for copy in copies[1:]:
        copy.wait()
    for slot in range(slots):
        pick = picks_ref[0, slot]
        alive = alive_ref[0, pick].astype(jnp.float32)
        for j in range(chunks):
            at = SUBLANES * slot + j
            span = slice(CHUNK * j, CHUNK * (j + 1))
            source_ref[at : at + 1, :] = raw_ref[pl.ds(pick, 1), span] * alive
    high, low = split(source_ref[...])
    count = slots * SUBLANES
    both = dot(jnp.concatenate([high, low], axis=0), weights)
    sources = both[:count, :LANES] + both[:count, LANES:] + both[count:, :LANES]
    lane = lax.broadcasted_iota(jnp.int32, (SUBLANES, LANES), 1)
    row = lax.broadcasted_iota(jnp.int32, (SUBLANES, LANES), 0)
    leads = row % per_tile == 0
    wraps = lane >= LANES - EDGE
    piece = []
    rims = jnp.zeros((1, LANES), jnp.float32)
    for slot in range(slots):
        source = sources[SUBLANES * slot : SUBLANES * (slot + 1)]
        placed = source
        for step in range(1, per_tile):
            rolled = pltpu.roll(source, CHUNK_OUT * step, 1)
            placed = jnp.where(row % per_tile == step, rolled, placed)
        own = jnp.where(leads & wraps, 0.0, placed)
        rim = placed - own
        for tile in range(tiles):
            first = per_tile * tile
            inside = jnp.where((row >= first) & (row < first + per_tile), own, 0.0)
            before = jnp.where(row == first + per_tile, rim, 0.0)
            piece.append(jnp.sum(inside + before, axis=0, keepdims=True))
        rims = rims + pltpu.roll(rim[:1], LANES - EDGE * slot if slot else 0, 1)
    piece.append(rims)
    size = len(piece)
    spread = [jnp.broadcast_to(value, (SUBLANES, LANES)) for value in piece]
    eight = []
    for group in range(size):
        place = (row + SUBLANES * group) % size
        total = spread[0]
        for at in range(1, size):
            total = jnp.where(place == at, spread[at], total)
        eight.append(total)
    eight = jnp.concatenate(eight, axis=0)
    for at in range(0, pieces_ref.shape[0], SUBLANES * size):
        pieces_ref[at : at + SUBLANES * size, :] = eight
    sending = pltpu.make_async_copy(pieces_ref, pieces_hbm, sems.at[0])
    sending.start()

    result = filtered(
        jnp.concatenate(
            [raw_ref[:, CHUNK * j : CHUNK * (j + 1)] for j in range(chunks)], axis=0
        )
    )
    part = [result[rows * j : rows * (j + 1)] for j in range(chunks)]
    is_main = lax.broadcasted_iota(jnp.int32, (rows, LANES), 1) < LANES // 2
    values = []
    for first in range(0, chunks, per_tile):
        total = jnp.where(is_main, part[first], 0.0)
        for step in range(1, min(per_tile, chunks - first)):
            total = total + pltpu.roll(part[first + step], CHUNK_OUT * step, 1)
        if first + per_tile < chunks:
            total = total + jnp.where(is_main, 0.0, part[first + per_tile])
        values.append(total)
    rim = jnp.where(is_main, 0.0, part[0])
    if paired:
        packed = rim[:SUBLANES]
        for at in range(1, rows // SUBLANES):
            group = rim[SUBLANES * at : SUBLANES * (at + 1)]
            packed = packed + pltpu.roll(group, LANES - EDGE * at, 1)
        for at, value in enumerate(values):
            out_ref[rows * at : rows * (at + 1), :] = value
        out_ref[rows * tiles :, :] = packed
    else:
        for at, value in enumerate(values + [rim]):
            out_ref[:, LANES * at : LANES * (at + 1)] = value
    sending.wait()


def unpack(packed, rows):
    tiles = [packed[at : at + rows] for at in range(0, packed.shape[0] - SUBLANES, rows)]
    rims = packed[packed.shape[0] - SUBLANES :]
    rim = jnp.concatenate(
        [rims]
        + [pltpu.roll(rims, EDGE * at, 1) for at in range(1, rows // SUBLANES)],
        axis=0,
    )
    lane = lax.broadcasted_iota(jnp.int32, rim.shape, 1)
    return tiles + [jnp.where(lane >= LANES - EDGE, rim, 0.0)]


def transform(early, late, table_hi, table_lo):
    rows = early.shape[0]
    high, low = split(jnp.concatenate([early, late], axis=0))
    first = dot(jnp.concatenate([high, low], axis=0), table_hi)
    both = first[: 2 * rows] + first[2 * rows :] + dot(high, table_lo)
    quarter = lax.broadcasted_iota(jnp.int32, (1, BINS), 1) & 3
    cosine = jnp.where(quarter == 0, 1.0, 0.0) - jnp.where(quarter == 2, 1.0, 0.0)
    sine = jnp.where(quarter == 1, 1.0, 0.0) - jnp.where(quarter == 3, 1.0, 0.0)
    early_re, early_im = both[:rows, :BINS], both[:rows, BINS:]
    late_re, late_im = both[rows:, :BINS], both[rows:, BINS:]
    return (
        early_re + cosine * late_re + sine * late_im,
        early_im + cosine * late_im - sine * late_re,
    )


def whitening(real_part, imag_part, band):
    rows = real_part.shape[0]
    tiles = BINS // LANES
    stacked = []
    for part in split(real_part * real_part + imag_part * imag_part):
        zero = jnp.zeros((rows, LANES), part.dtype)
        wide = jnp.concatenate([zero, part, zero], axis=1)
        stacked += [wide[:, LANES * tile : LANES * (tile + 3)] for tile in range(tiles)]
    banded = dot(jnp.concatenate(stacked, axis=0), band)
    step = rows * tiles
    summed = banded[:step] + banded[step:]
    total = jnp.concatenate(
        [summed[rows * tile : rows * (tile + 1)] for tile in range(tiles)], axis=1
    )
    bins = lax.broadcasted_iota(jnp.int32, (1, BINS), 1)
    count = jnp.minimum(bins + HALF, BINS - 1) - jnp.maximum(bins - HALF, 0) + 1
    return lax.rsqrt(total * (1.0 / count.astype(jnp.float32)) + 1e-06)


def prepare_kernel(
    _, alive_hbm, picks_hbm, fwd_hi_hbm, fwd_lo_hbm, band_hbm, lag_hbm,
    hi_ref, lo_ref, band_ref, lag_ref, alive_out, picks_out, alive_ref, picks_ref, sems,
):
    copies = start_copies(
        [
            (alive_hbm, alive_ref),
            (picks_hbm, picks_ref),
            (fwd_hi_hbm, hi_ref),
            (fwd_lo_hbm, lo_ref),
            (band_hbm, band_ref),
            (lag_hbm, lag_ref),
        ],
        sems,
    )
    for copy in copies[:2]:
        copy.wait()
    rows = alive_out.shape[0]
    alive_out[...] = jnp.broadcast_to(
        column(alive_ref[...].astype(jnp.float32)), (rows, LANES)
    )
    channel = lax.broadcasted_iota(jnp.int32, (rows, LANES), 0)
    for slot in range(picks_ref.shape[1]):
        pick = jnp.broadcast_to(picks_ref[:, slot : slot + 1], (rows, LANES))
        picks_out[slot] = jnp.where(channel == pick, 1.0, 0.0)
    for copy in copies[2:]:
        copy.wait()


def spectra_kernel(series_ref, hi_ref, lo_ref, band_ref, alive_ref, *refs):
    spectra_ref = refs[-1]
    rows = alive_ref.shape[0]
    half = S // 2
    if len(refs) > 1:
        mine, other = [unpack(ref[...], rows) for ref in (series_ref, refs[0])]
        first = lax.axis_index("src") == 0
        early = [jnp.where(first, a, b) for a, b in zip(mine, other)]
        late = [jnp.where(first, b, a) for a, b in zip(mine, other)]
        early[-2] = early[-2] + late[-1]
        early, late = [jnp.concatenate(tiles[:-1], axis=1) for tiles in (early, late)]
    else:
        early, late = series_ref[:, :half], series_ref[:, half:]
    real_part, imag_part = transform(early, late, hi_ref[...], lo_ref[...])
    factor = alive_ref[:, :1] * whitening(real_part, imag_part, band_ref[...])
    spectra_ref[:, :BINS] = real_part * factor
    spectra_ref[:, BINS:] = imag_part * factor


def correlate_kernel(
    slots, spectra_ref, pieces_ref, picks_ref, hi_ref, lo_ref, band_ref, lag_ref, out_hbm,
    series_ref, rims_ref, source_ref, cross_ref, out_ref, sems,
):
    rows = spectra_ref.shape[0]
    group = out_ref.shape[0] // slots
    half = BINS // LANES
    own = lax.axis_index("blk")
    base = lax.axis_index("src") * group
    tiles = S // 2 // LANES
    total = group * slots

    for block in range(group):
        at = pieces_ref.shape[0] - 1 - 2 * (base + block)
        for slot in range(slots):
            row = slice(block * slots + slot, block * slots + slot + 1)
            for tile in range(tiles):
                span = slice(LANES * (slot * tiles + tile), LANES * (slot * tiles + tile + 1))
                early = slice(LANES * tile, LANES * (tile + 1))
                late = slice(S // 2 + LANES * tile, S // 2 + LANES * (tile + 1))
                series_ref[row, early] = pieces_ref[at, :, span]
                series_ref[row, late] = pieces_ref[at - 1, :, span]
            rims_ref[row, :] = pieces_ref[at - 1, :, LANES * slots * tiles :]

    rims = rims_ref[...]
    lane = lax.broadcasted_iota(jnp.int32, rims.shape, 1)
    row = lax.broadcasted_iota(jnp.int32, rims.shape, 0)
    seam = slice(S // 2 - LANES, S // 2)
    for slot in range(slots):
        rolled = pltpu.roll(rims, EDGE * slot, 1) if slot else rims
        inside = (lane >= LANES - EDGE) & (row % slots == slot)
        series_ref[:, seam] = series_ref[:, seam] + jnp.where(inside, rolled, 0.0)
    early, late = series_ref[:, : S // 2], series_ref[:, S // 2 :]
    real_part, imag_part = transform(early, late, hi_ref[...], lo_ref[...])
    factor = whitening(real_part, imag_part, band_ref[...])
    source_ref[:, :BINS] = real_part * factor
    source_ref[:, BINS:] = imag_part * factor
    per_part = total // PARTS

    def copy_of(part):
        span = pl.ds(part * per_part, per_part)
        return pltpu.make_async_copy(out_ref.at[span], out_hbm.at[span], sems.at[part])

    @pl.loop(0, PARTS)
    def _(part):
        rows_of = pl.ds(pl.multiple_of(part * per_part, per_part), per_part)
        for tile in range(half):
            re = slice(LANES * tile, LANES * (tile + 1))
            im = slice(BINS + LANES * tile, BINS + LANES * (tile + 1))
            rec_re, rec_im = spectra_ref[:, re], spectra_ref[:, im]
            all_re, all_im = source_ref[rows_of, re], source_ref[rows_of, im]
            for at in range(per_part):
                src_re, src_im = all_re[at : at + 1], all_im[at : at + 1]
                where = slice(rows * at, rows * (at + 1))
                cross_ref[where, re] = (src_re * rec_re + src_im * rec_im).astype(jnp.bfloat16)
                cross_ref[where, im] = (src_re * rec_im - src_im * rec_re).astype(jnp.bfloat16)

        lagged = dot(cross_ref[...], lag_ref[...])
        for at in range(per_part):
            block, slot = part * (per_part // slots) + at // slots, at % slots
            keep = 1.0 - jnp.where(own == base + block, 1.0, 0.0) * picks_ref[slot]
            kept = lagged[rows * at : rows * (at + 1)] * jnp.concatenate(
                [keep] * (LAGS // LANES), axis=1
            )
            out_ref[part * per_part + at] = kept.astype(jnp.bfloat16)
        copy_of(part).start()

    for part in range(PARTS):
        copy_of(part).wait()


HBM = pl.BlockSpec(memory_space=pltpu.HBM)
VMEM = pl.BlockSpec(memory_space=pltpu.VMEM)
PARAMS = pltpu.CompilerParams(vmem_limit_bytes=VMEM_LIMIT)


def in_hbm(*arrays):
    return [pltpu.with_memory_space_constraint(array, pltpu.HBM) for array in arrays]


def shaped(*shape, dtype=jnp.float32):
    return jax.ShapeDtypeStruct(shape, dtype)


def local(raw_records, fir_taps, alive_mask, source_index):
    src_count = lax.axis_size("src")
    blk_count = lax.axis_size("blk")
    rows, raw_count = raw_records.shape
    slots = source_index.shape[1]
    group = blk_count // src_count
    out_count = raw_count // DEC
    width = -(-out_count // LANES) * LANES + LANES
    chunks = raw_count // CHUNK
    paired = src_count == 2 and 2 * out_count == S
    bf16 = jnp.bfloat16
    forward_hi, forward_lo = split_table(forward_table())
    alive_row = alive_mask.reshape(1, rows)

    with jax.named_scope("decimate"):
        device_count = blk_count * src_count
        main = slots * (width - LANES)
        decimated, pieces = pl.pallas_call(
            lambda *refs: decimate_kernel(paired, *refs),
            out_shape=(
                shaped(rows * (S // 2 // LANES) + SUBLANES, LANES)
                if paired
                else shaped(rows, width),
                shaped(device_count * (main // LANES + 1), LANES),
            ),
            in_specs=[HBM] * 4,
            out_specs=(VMEM, HBM),
            scratch_shapes=[
                pltpu.VMEM((rows, raw_count), jnp.float32),
                pltpu.VMEM((1, TAPS), jnp.float32),
                pltpu.SMEM((1, rows), jnp.int32),
                pltpu.SMEM((1, slots), jnp.int32),
                pltpu.VMEM((SUBLANES * slots, CHUNK), jnp.float32),
                pltpu.VMEM((device_count * (main // LANES + 1), LANES), jnp.float32),
                pltpu.SemaphoreType.DMA((rows // SUBLANES + 3,)),
            ],
            compiler_params=PARAMS,
        )(*in_hbm(raw_records, fir_taps.reshape(1, TAPS), alive_row, source_index))

    def whole(shards):
        rims = jnp.pad(shards[1:, :, width - EDGE :], ((0, 1), (0, 0), (out_count - EDGE, 0)))
        series = shards[:, :, :out_count] + rims
        return series.transpose(1, 0, 2).reshape(shards.shape[1], S)

    with jax.named_scope("gather_sources"):
        gathered = lax.all_to_all(
            pieces.reshape(device_count, 1, main + LANES),
            ("blk", "src"),
            split_axis=0,
            concat_axis=0,
            tiled=True,
            axis_index_groups=[list(reversed(range(device_count)))],
        )
        if not paired:
            gathered = gathered[::-1]
            shards = gathered.reshape(blk_count, src_count, main + LANES)
            shards = shards.transpose(1, 0, 2)
            rims = [shards[:, :, main + LANES - EDGE * (slot + 1) :] for slot in range(slots)]
            rims = jnp.stack([rim[:, :, :EDGE] for rim in rims], axis=2)
            rims = jnp.pad(rims, ((0, 0), (0, 0), (0, 0), (LANES - EDGE, 0)))
            series = shards[:, :, :main].reshape(src_count, blk_count, slots, width - LANES)
            series = jnp.concatenate([series, rims], axis=3)
            series = whole(series.reshape(src_count, blk_count * slots, width))
            series = series.reshape(blk_count, slots, 2, S // 2).transpose(0, 2, 1, 3)
            series = series.reshape(blk_count * 2, 1, slots * S // 2)
            gathered = jnp.pad(series, ((0, 0), (0, 0), (0, LANES)))[::-1]

    with jax.named_scope("prepare"):
        out_shape = (
            shaped(S // 2, NFFT, dtype=bf16),
            shaped(S // 2, NFFT, dtype=bf16),
            shaped(3 * LANES, LANES, dtype=bf16),
            shaped(NFFT, LAGS, dtype=bf16),
            shaped(rows, LANES),
            shaped(slots, rows, LANES),
        )
        table_hi, table_lo, band, lag, alive, picks = pl.pallas_call(
            prepare_kernel,
            out_shape=out_shape,
            in_specs=[VMEM] + [HBM] * 6,
            out_specs=(VMEM,) * len(out_shape),
            scratch_shapes=[
                pltpu.VMEM((1, rows), jnp.int32),
                pltpu.VMEM((1, slots), jnp.int32),
                pltpu.SemaphoreType.DMA((6,)),
            ],
            compiler_params=PARAMS,
            cost_estimate=pl.CostEstimate(
                flops=0, bytes_accessed=4 * S * NFFT, transcendentals=0
            ),
        )(
            decimated,
            *in_hbm(
                alive_row,
                source_index,
                jnp.asarray(forward_hi),
                jnp.asarray(forward_lo),
                jnp.asarray(band_table()),
                jnp.asarray(lag_table()),
            ),
        )

    with jax.named_scope("regroup"):
        if paired:
            series = [decimated]
            other = [lax.ppermute(decimated, "src", [(0, 1), (1, 0)])]
        else:
            series = [whole(lax.all_gather(decimated, "src", axis=0))]
            other = []

    with jax.named_scope("spectra"):
        operands = series + [table_hi, table_lo, band, alive] + other
        spectra = pl.pallas_call(
            spectra_kernel,
            out_shape=shaped(rows, NFFT),
            in_specs=[VMEM] * len(operands),
            out_specs=VMEM,
            compiler_params=PARAMS,
        )(*operands)

    with jax.named_scope("correlate"):
        total = group * slots
        return pl.pallas_call(
            lambda *refs: correlate_kernel(slots, *refs),
            out_shape=shaped(total, rows, LAGS, dtype=bf16),
            in_specs=[VMEM] * 7,
            out_specs=HBM,
            scratch_shapes=[
                pltpu.VMEM((total, S), jnp.float32),
                pltpu.VMEM((total, LANES), jnp.float32),
                pltpu.VMEM((total, NFFT), jnp.float32),
                pltpu.VMEM((total // PARTS * rows, NFFT), bf16),
                pltpu.VMEM((total, rows, LAGS), bf16),
                pltpu.SemaphoreType.DMA((PARTS,)),
            ],
            compiler_params=PARAMS,
        )(spectra, gathered, picks, table_hi, table_lo, band, lag)


def solution(mesh):
    in_specs = (P("blk", "src"), P(), P("blk"), P("blk", None))
    out_specs = P("src", "blk", None)
    return jax.shard_map(local, mesh=mesh, in_specs=in_specs, out_specs=out_specs, check_vma=False)
```

```python
import math

import jax
import jax.numpy as jnp
import numpy as np
from jax import lax
from jax.experimental import pallas as pl
from jax.experimental.pallas import tpu as pltpu
from jax.sharding import PartitionSpec as P

S = 512
NFFT = 1024
BINS = NFFT // 2
LAGS = 512
TAPS = 64
DEC = 20
HALF = 64
LANES = 128
SUBLANES = 8
PARTS = 3
EDGE = (TAPS - 1) // DEC
CHUNK = 640
CHUNK_OUT = CHUNK // DEC
VMEM_LIMIT = 48 * 1024 * 1024


def forward_table():
    phases = 2.0 * math.pi / NFFT * (np.outer(np.arange(S // 2), np.arange(BINS)) % NFFT)
    return np.concatenate([np.cos(phases), -np.sin(phases)], axis=1).astype(np.float32)


def split_table(table):
    high = table.astype(jnp.bfloat16)
    low = (table - high.astype(np.float32)).astype(jnp.bfloat16)
    return high, low


def band_table():
    bins = np.arange(3 * LANES)[:, None] - LANES
    return (np.abs(bins - np.arange(LANES)[None, :]) <= HALF).astype(jnp.bfloat16)


def lag_table():
    bins = np.arange(BINS)[:, None]
    shift = np.arange(LAGS)[None, :] - LAGS // 2
    phases = 2.0 * math.pi / NFFT * (bins * shift % NFFT)
    weight = np.where(bins == 0, 0.5, 1.0) / math.sqrt(BINS)
    table = np.concatenate([weight * np.cos(phases), -weight * np.sin(phases)], axis=0)
    return table.astype(np.float32).astype(jnp.bfloat16)


def split(value):
    high = value.astype(jnp.bfloat16)
    return high, (value - high.astype(jnp.float32)).astype(jnp.bfloat16)


def dot(a, b):
    return jnp.dot(a, b, preferred_element_type=jnp.float32)


def column(row):
    count = row.shape[1]
    at = [lax.broadcasted_iota(jnp.int32, (count, count), axis) for axis in range(2)]
    rows = jnp.broadcast_to(row, (count, count))
    return jnp.sum(jnp.where(at[0] == at[1], rows, 0.0), axis=1, keepdims=True)


def start_copies(pairs, sems):
    copies = [
        pltpu.make_async_copy(source, target, sems.at[at])
        for at, (source, target) in enumerate(pairs)
    ]
    for copy in copies:
        copy.start()
    return copies


def decimate_kernel(
    paired, raw_hbm, taps_hbm, alive_hbm, picks_hbm, out_ref, pieces_hbm,
    raw_ref, taps_ref, alive_ref, picks_ref, source_ref, pieces_ref, sems,
):
    rows = raw_hbm.shape[0]
    chunks = raw_hbm.shape[1] // CHUNK
    slots = picks_ref.shape[1]
    per_tile = LANES // CHUNK_OUT
    tiles = -(-chunks // per_tile)
    pairs = [(taps_hbm, taps_ref), (picks_hbm, picks_ref), (alive_hbm, alive_ref)]
    for at in range(0, rows, SUBLANES):
        span = slice(at, at + SUBLANES)
        pairs.append((raw_hbm.at[span], raw_ref.at[span]))
    copies = start_copies(pairs, sems)
    source_ref[...] = jnp.zeros_like(source_ref)
    copies[0].wait()
    taps = jnp.broadcast_to(taps_ref[...], (SUBLANES, TAPS))
    eight = jnp.concatenate([taps, jnp.zeros((SUBLANES, CHUNK - TAPS), jnp.float32)], axis=1)
    for _ in range(2):
        eight = pltpu.roll(eight, 0, 1, stride=DEC // 2, stride_axis=0)
    wrapped = jnp.concatenate(
        [eight]
        + [pltpu.roll(eight, DEC * at, 1) for at in range(SUBLANES, CHUNK_OUT, SUBLANES)],
        axis=0,
    )
    lane = lax.broadcasted_iota(jnp.int32, (CHUNK_OUT, CHUNK), 1)
    row = lax.broadcasted_iota(jnp.int32, (CHUNK_OUT, CHUNK), 0)
    main = jnp.where(lane >= DEC * row, wrapped, 0.0)
    rim = wrapped - main
    gap = jnp.zeros((LANES - 2 * CHUNK_OUT, CHUNK), jnp.float32)
    weights_hi, weights_lo = split(jnp.concatenate([main, gap, rim], axis=0).T)
    weights = jnp.concatenate([weights_hi, weights_lo], axis=1)

    def filtered(stacked):
        high, low = split(stacked)
        both = dot(high, weights)
        return both[:, :LANES] + both[:, LANES:] + dot(low, weights_hi)

    for copy in copies[1:]:
        copy.wait()
    for slot in range(slots):
        pick = picks_ref[0, slot]
        alive = alive_ref[0, pick].astype(jnp.float32)
        for j in range(chunks):
            at = SUBLANES * slot + j
            span = slice(CHUNK * j, CHUNK * (j + 1))
            source_ref[at : at + 1, :] = raw_ref[pl.ds(pick, 1), span] * alive
    high, low = split(source_ref[...])
    count = slots * SUBLANES
    both = dot(jnp.concatenate([high, low], axis=0), weights)
    sources = both[:count, :LANES] + both[:count, LANES:] + both[count:, :LANES]
    lane = lax.broadcasted_iota(jnp.int32, (SUBLANES, LANES), 1)
    row = lax.broadcasted_iota(jnp.int32, (SUBLANES, LANES), 0)
    leads = row % per_tile == 0
    wraps = lane >= LANES - EDGE
    piece = []
    rims = jnp.zeros((1, LANES), jnp.float32)
    for slot in range(slots):
        source = sources[SUBLANES * slot : SUBLANES * (slot + 1)]
        placed = source
        for step in range(1, per_tile):
            rolled = pltpu.roll(source, CHUNK_OUT * step, 1)
            placed = jnp.where(row % per_tile == step, rolled, placed)
        own = jnp.where(leads & wraps, 0.0, placed)
        rim = placed - own
        for tile in range(tiles):
            first = per_tile * tile
            inside = jnp.where((row >= first) & (row < first + per_tile), own, 0.0)
            before = jnp.where(row == first + per_tile, rim, 0.0)
            piece.append(jnp.sum(inside + before, axis=0, keepdims=True))
        rims = rims + pltpu.roll(rim[:1], LANES - EDGE * slot if slot else 0, 1)
    piece.append(rims)
    size = len(piece)
    spread = [jnp.broadcast_to(value, (SUBLANES, LANES)) for value in piece]
    eight = []
    for group in range(size):
        place = (row + SUBLANES * group) % size
        total = spread[0]
        for at in range(1, size):
            total = jnp.where(place == at, spread[at], total)
        eight.append(total)
    eight = jnp.concatenate(eight, axis=0)
    for at in range(0, pieces_ref.shape[0], SUBLANES * size):
        pieces_ref[at : at + SUBLANES * size, :] = eight
    sending = pltpu.make_async_copy(pieces_ref, pieces_hbm, sems.at[0])
    sending.start()

    result = filtered(
        jnp.concatenate(
            [raw_ref[:, CHUNK * j : CHUNK * (j + 1)] for j in range(chunks)], axis=0
        )
    )
    part = [result[rows * j : rows * (j + 1)] for j in range(chunks)]
    is_main = lax.broadcasted_iota(jnp.int32, (rows, LANES), 1) < LANES // 2
    values = []
    for first in range(0, chunks, per_tile):
        total = jnp.where(is_main, part[first], 0.0)
        for step in range(1, min(per_tile, chunks - first)):
            total = total + pltpu.roll(part[first + step], CHUNK_OUT * step, 1)
        if first + per_tile < chunks:
            total = total + jnp.where(is_main, 0.0, part[first + per_tile])
        values.append(total)
    rim = jnp.where(is_main, 0.0, part[0])
    if paired:
        packed = rim[:SUBLANES]
        for at in range(1, rows // SUBLANES):
            group = rim[SUBLANES * at : SUBLANES * (at + 1)]
            packed = packed + pltpu.roll(group, LANES - EDGE * at, 1)
        for at, value in enumerate(values):
            out_ref[rows * at : rows * (at + 1), :] = value
        out_ref[rows * tiles :, :] = packed
    else:
        for at, value in enumerate(values + [rim]):
            out_ref[:, LANES * at : LANES * (at + 1)] = value
    sending.wait()


def unpack(packed, rows):
    tiles = [packed[at : at + rows] for at in range(0, packed.shape[0] - SUBLANES, rows)]
    rims = packed[packed.shape[0] - SUBLANES :]
    rim = jnp.concatenate(
        [rims]
        + [pltpu.roll(rims, EDGE * at, 1) for at in range(1, rows // SUBLANES)],
        axis=0,
    )
    lane = lax.broadcasted_iota(jnp.int32, rim.shape, 1)
    return tiles + [jnp.where(lane >= LANES - EDGE, rim, 0.0)]


def transform(early, late, table_hi, table_lo):
    rows = early.shape[0]
    high, low = split(jnp.concatenate([early, late], axis=0))
    first = dot(jnp.concatenate([high, low], axis=0), table_hi)
    both = first[: 2 * rows] + first[2 * rows :] + dot(high, table_lo)
    quarter = lax.broadcasted_iota(jnp.int32, (1, BINS), 1) & 3
    cosine = jnp.where(quarter == 0, 1.0, 0.0) - jnp.where(quarter == 2, 1.0, 0.0)
    sine = jnp.where(quarter == 1, 1.0, 0.0) - jnp.where(quarter == 3, 1.0, 0.0)
    early_re, early_im = both[:rows, :BINS], both[:rows, BINS:]
    late_re, late_im = both[rows:, :BINS], both[rows:, BINS:]
    return (
        early_re + cosine * late_re + sine * late_im,
        early_im + cosine * late_im - sine * late_re,
    )


def whitening(real_part, imag_part, band):
    rows = real_part.shape[0]
    tiles = BINS // LANES
    stacked = []
    for part in split(real_part * real_part + imag_part * imag_part):
        zero = jnp.zeros((rows, LANES), part.dtype)
        wide = jnp.concatenate([zero, part, zero], axis=1)
        stacked += [wide[:, LANES * tile : LANES * (tile + 3)] for tile in range(tiles)]
    banded = dot(jnp.concatenate(stacked, axis=0), band)
    step = rows * tiles
    summed = banded[:step] + banded[step:]
    total = jnp.concatenate(
        [summed[rows * tile : rows * (tile + 1)] for tile in range(tiles)], axis=1
    )
    bins = lax.broadcasted_iota(jnp.int32, (1, BINS), 1)
    count = jnp.minimum(bins + HALF, BINS - 1) - jnp.maximum(bins - HALF, 0) + 1
    return lax.rsqrt(total * (1.0 / count.astype(jnp.float32)) + 1e-06)


def prepare_kernel(
    _, alive_hbm, picks_hbm, fwd_hi_hbm, fwd_lo_hbm, band_hbm, lag_hbm,
    hi_ref, lo_ref, band_ref, lag_ref, alive_out, picks_out, alive_ref, picks_ref, sems,
):
    copies = start_copies(
        [
            (alive_hbm, alive_ref),
            (picks_hbm, picks_ref),
            (fwd_hi_hbm, hi_ref),
            (fwd_lo_hbm, lo_ref),
            (band_hbm, band_ref),
            (lag_hbm, lag_ref),
        ],
        sems,
    )
    for copy in copies[:2]:
        copy.wait()
    rows = alive_out.shape[0]
    alive_out[...] = jnp.broadcast_to(
        column(alive_ref[...].astype(jnp.float32)), (rows, LANES)
    )
    channel = lax.broadcasted_iota(jnp.int32, (rows, LANES), 0)
    for slot in range(picks_ref.shape[1]):
        pick = jnp.broadcast_to(picks_ref[:, slot : slot + 1], (rows, LANES))
        picks_out[slot] = jnp.where(channel == pick, 1.0, 0.0)
    for copy in copies[2:]:
        copy.wait()


def spectra_kernel(series_ref, hi_ref, lo_ref, band_ref, alive_ref, *refs):
    spectra_ref = refs[-1]
    rows = alive_ref.shape[0]
    half = S // 2
    if len(refs) > 1:
        mine, other = [unpack(ref[...], rows) for ref in (series_ref, refs[0])]
        first = lax.axis_index("src") == 0
        early = [jnp.where(first, a, b) for a, b in zip(mine, other)]
        late = [jnp.where(first, b, a) for a, b in zip(mine, other)]
        early[-2] = early[-2] + late[-1]
        early, late = [jnp.concatenate(tiles[:-1], axis=1) for tiles in (early, late)]
    else:
        early, late = series_ref[:, :half], series_ref[:, half:]
    real_part, imag_part = transform(early, late, hi_ref[...], lo_ref[...])
    factor = alive_ref[:, :1] * whitening(real_part, imag_part, band_ref[...])
    spectra_ref[:, :BINS] = real_part * factor
    spectra_ref[:, BINS:] = imag_part * factor


def part_bounds(total):
    ends = [3 * total // 8, 3 * total // 4, total]
    return [(a, b) for a, b in zip([0] + ends, ends) if b > a]


def correlate_kernel(
    paired, slots, spectra_ref, pieces_ref, picks_ref, hi_ref, lo_ref, band_ref, lag_ref, out_hbm,
    series_ref, rims_ref, source_ref, cross_ref, out_ref, sems,
):
    rows = spectra_ref.shape[0]
    group = out_ref.shape[0] // slots
    half = BINS // LANES
    own = lax.axis_index("blk")
    base = lax.axis_index("src") * group
    tiles = S // 2 // LANES

    def entry(block, half_at):
        if not paired:
            return 2 * (base + block) + half_at
        order = exchange_order(pieces_ref.shape[0])
        places = [order.index(2 * (side * group + block) + half_at) for side in range(2)]
        return jnp.where(base == 0, places[0], places[1])

    for slot in range(slots):
        for block in range(group):
            row = slice(slot * group + block, slot * group + block + 1)
            at, after = entry(block, 0), entry(block, 1)
            for tile in range(tiles):
                span = slice(LANES * (slot * tiles + tile), LANES * (slot * tiles + tile + 1))
                early = slice(LANES * tile, LANES * (tile + 1))
                late = slice(S // 2 + LANES * tile, S // 2 + LANES * (tile + 1))
                series_ref[row, early] = pieces_ref[at, :, span]
                series_ref[row, late] = pieces_ref[after, :, span]
            rims_ref[row, :] = pieces_ref[after, :, LANES * slots * tiles :]
    rims = jnp.concatenate(
        [
            pltpu.roll(rims_ref[slot * group : (slot + 1) * group, :], EDGE * slot, 1)
            for slot in range(slots)
        ],
        axis=0,
    )
    lane = lax.broadcasted_iota(jnp.int32, rims.shape, 1)
    seam = slice(S // 2 - LANES, S // 2)
    series_ref[:, seam] = series_ref[:, seam] + jnp.where(lane >= LANES - EDGE, rims, 0.0)
    early, late = series_ref[:, : S // 2], series_ref[:, S // 2 :]
    real_part, imag_part = transform(early, late, hi_ref[...], lo_ref[...])
    factor = whitening(real_part, imag_part, band_ref[...])
    source_ref[:, :BINS] = real_part * factor
    source_ref[:, BINS:] = imag_part * factor
    copies = []
    for part, (first, last) in enumerate(part_bounds(group * slots)):
        per_part = last - first
        for tile in range(half):
            re = slice(LANES * tile, LANES * (tile + 1))
            im = slice(BINS + LANES * tile, BINS + LANES * (tile + 1))
            rec_re, rec_im = spectra_ref[:, re], spectra_ref[:, im]
            for source in range(first, first + per_part):
                block, slot = divmod(source, slots)
                at = slot * group + block
                src_re, src_im = source_ref[at : at + 1, re], source_ref[at : at + 1, im]
                where = slice(rows * source, rows * (source + 1))
                cross_ref[where, re] = (src_re * rec_re + src_im * rec_im).astype(jnp.bfloat16)
                cross_ref[where, im] = (src_re * rec_im - src_im * rec_re).astype(jnp.bfloat16)
        lagged = dot(cross_ref[rows * first : rows * (first + per_part), :], lag_ref[...])
        for source in range(first, first + per_part):
            block, slot = divmod(source, slots)
            keep = 1.0 - jnp.where(own == base + block, 1.0, 0.0) * picks_ref[slot]
            at = source - first
            kept = lagged[rows * at : rows * (at + 1)] * jnp.concatenate(
                [keep] * (LAGS // LANES), axis=1
            )
            out_ref[source] = kept.astype(jnp.bfloat16)
        span = pl.ds(first, per_part)
        copies.append(pltpu.make_async_copy(out_ref.at[span], out_hbm.at[span], sems.at[part]))
        copies[-1].start()
    for copy in copies:
        copy.wait()


HBM = pl.BlockSpec(memory_space=pltpu.HBM)
VMEM = pl.BlockSpec(memory_space=pltpu.VMEM)
PARAMS = pltpu.CompilerParams(vmem_limit_bytes=VMEM_LIMIT)


def in_hbm(*arrays):
    return [pltpu.with_memory_space_constraint(array, pltpu.HBM) for array in arrays]


def shaped(*shape, dtype=jnp.float32):
    return jax.ShapeDtypeStruct(shape, dtype)


def exchange_order(count):
    quarter = count // 4
    near = sorted(range(quarter), key=lambda place: place & ~2)
    far = sorted(range(quarter), key=lambda place: (-(place & 2), place))
    return (near + [quarter * at + place for at in range(1, 4) for place in far])[::-1]


def local(raw_records, fir_taps, alive_mask, source_index):
    src_count = lax.axis_size("src")
    blk_count = lax.axis_size("blk")
    rows, raw_count = raw_records.shape
    slots = source_index.shape[1]
    group = blk_count // src_count
    out_count = raw_count // DEC
    width = -(-out_count // LANES) * LANES + LANES
    chunks = raw_count // CHUNK
    paired = src_count == 2 and 2 * out_count == S
    bf16 = jnp.bfloat16
    forward_hi, forward_lo = split_table(forward_table())
    alive_row = alive_mask.reshape(1, rows)

    with jax.named_scope("decimate"):
        device_count = blk_count * src_count
        main = slots * (width - LANES)
        decimated, pieces = pl.pallas_call(
            lambda *refs: decimate_kernel(paired, *refs),
            out_shape=(
                shaped(rows * (S // 2 // LANES) + SUBLANES, LANES)
                if paired
                else shaped(rows, width),
                shaped(device_count * (main // LANES + 1), LANES),
            ),
            in_specs=[HBM] * 4,
            out_specs=(VMEM, HBM),
            scratch_shapes=[
                pltpu.VMEM((rows, raw_count), jnp.float32),
                pltpu.VMEM((1, TAPS), jnp.float32),
                pltpu.SMEM((1, rows), jnp.int32),
                pltpu.SMEM((1, slots), jnp.int32),
                pltpu.VMEM((SUBLANES * slots, CHUNK), jnp.float32),
                pltpu.VMEM((device_count * (main // LANES + 1), LANES), jnp.float32),
                pltpu.SemaphoreType.DMA((rows // SUBLANES + 3,)),
            ],
            compiler_params=PARAMS,
        )(*in_hbm(raw_records, fir_taps.reshape(1, TAPS), alive_row, source_index))

    def whole(shards):
        rims = jnp.pad(shards[1:, :, width - EDGE :], ((0, 1), (0, 0), (out_count - EDGE, 0)))
        series = shards[:, :, :out_count] + rims
        return series.transpose(1, 0, 2).reshape(shards.shape[1], S)

    with jax.named_scope("gather_sources"):
        gathered = lax.all_to_all(
            pieces.reshape(device_count, 1, main + LANES),
            ("blk", "src"),
            split_axis=0,
            concat_axis=0,
            tiled=True,
            axis_index_groups=[exchange_order(device_count)] if paired else None,
        )
        if not paired:
            shards = gathered.reshape(blk_count, src_count, main + LANES)
            shards = shards.transpose(1, 0, 2)
            rims = [shards[:, :, main + LANES - EDGE * (slot + 1) :] for slot in range(slots)]
            rims = jnp.stack([rim[:, :, :EDGE] for rim in rims], axis=2)
            rims = jnp.pad(rims, ((0, 0), (0, 0), (0, 0), (LANES - EDGE, 0)))
            series = shards[:, :, :main].reshape(src_count, blk_count, slots, width - LANES)
            series = jnp.concatenate([series, rims], axis=3)
            series = whole(series.reshape(src_count, blk_count * slots, width))
            series = series.reshape(blk_count, slots, 2, S // 2).transpose(0, 2, 1, 3)
            series = series.reshape(blk_count * 2, 1, slots * S // 2)
            gathered = jnp.pad(series, ((0, 0), (0, 0), (0, LANES)))

    with jax.named_scope("prepare"):
        out_shape = (
            shaped(S // 2, NFFT, dtype=bf16),
            shaped(S // 2, NFFT, dtype=bf16),
            shaped(3 * LANES, LANES, dtype=bf16),
            shaped(NFFT, LAGS, dtype=bf16),
            shaped(rows, LANES),
            shaped(slots, rows, LANES),
        )
        table_hi, table_lo, band, lag, alive, picks = pl.pallas_call(
            prepare_kernel,
            out_shape=out_shape,
            in_specs=[VMEM] + [HBM] * 6,
            out_specs=(VMEM,) * len(out_shape),
            scratch_shapes=[
                pltpu.VMEM((1, rows), jnp.int32),
                pltpu.VMEM((1, slots), jnp.int32),
                pltpu.SemaphoreType.DMA((6,)),
            ],
            compiler_params=PARAMS,
            cost_estimate=pl.CostEstimate(
                flops=0, bytes_accessed=4 * S * NFFT, transcendentals=0
            ),
        )(
            decimated,
            *in_hbm(
                alive_row,
                source_index,
                jnp.asarray(forward_hi),
                jnp.asarray(forward_lo),
                jnp.asarray(band_table()),
                jnp.asarray(lag_table()),
            ),
        )

    with jax.named_scope("regroup"):
        if paired:
            series = [decimated]
            other = [lax.ppermute(decimated, "src", [(0, 1), (1, 0)])]
        else:
            series = [whole(lax.all_gather(decimated, "src", axis=0))]
            other = []

    with jax.named_scope("spectra"):
        operands = series + [table_hi, table_lo, band, alive] + other
        spectra = pl.pallas_call(
            spectra_kernel,
            out_shape=shaped(rows, NFFT),
            in_specs=[VMEM] * len(operands),
            out_specs=VMEM,
            compiler_params=PARAMS,
        )(*operands)

    with jax.named_scope("correlate"):
        total = group * slots
        return pl.pallas_call(
            lambda *refs: correlate_kernel(paired, slots, *refs),
            out_shape=shaped(total, rows, LAGS, dtype=bf16),
            in_specs=[VMEM] * 7,
            out_specs=HBM,
            scratch_shapes=[
                pltpu.VMEM((total, S), jnp.float32),
                pltpu.VMEM((total, LANES), jnp.float32),
                pltpu.VMEM((total, NFFT), jnp.float32),
                pltpu.VMEM((total * rows, NFFT), bf16),
                pltpu.VMEM((total, rows, LAGS), bf16),
                pltpu.SemaphoreType.DMA((PARTS,)),
            ],
            compiler_params=PARAMS,
        )(spectra, gathered, picks, table_hi, table_lo, band, lag)


def solution(mesh):
    in_specs = (P("blk", "src"), P(), P("blk"), P("blk", None))
    out_specs = P("src", "blk", None)
    return jax.shard_map(local, mesh=mesh, in_specs=in_specs, out_specs=out_specs, check_vma=False)
```

```python
import math

import jax
import jax.numpy as jnp
import numpy as np
from jax import lax
from jax.experimental import pallas as pl
from jax.experimental.pallas import tpu as pltpu
from jax.sharding import PartitionSpec as P

S = 512
NFFT = 1024
BINS = NFFT // 2
LAGS = 512
TAPS = 64
DEC = 20
HALF = 64
LANES = 128
SUBLANES = 8
PARTS = 3
EDGE = (TAPS - 1) // DEC
CHUNK = 640
CHUNK_OUT = CHUNK // DEC
VMEM_LIMIT = 48 * 1024 * 1024


def forward_table():
    phases = 2.0 * math.pi / NFFT * (np.outer(np.arange(S // 2), np.arange(BINS)) % NFFT)
    return np.concatenate([np.cos(phases), -np.sin(phases)], axis=1).astype(np.float32)


def split_table(table):
    high = table.astype(jnp.bfloat16)
    low = (table - high.astype(np.float32)).astype(jnp.bfloat16)
    return high, low


def band_table():
    bins = np.arange(3 * LANES)[:, None] - LANES
    return (np.abs(bins - np.arange(LANES)[None, :]) <= HALF).astype(jnp.bfloat16)


def lag_table():
    bins = np.arange(BINS)[:, None]
    shift = np.arange(LAGS)[None, :] - LAGS // 2
    phases = 2.0 * math.pi / NFFT * (bins * shift % NFFT)
    weight = np.where(bins == 0, 0.5, 1.0) / math.sqrt(BINS)
    table = np.concatenate([weight * np.cos(phases), -weight * np.sin(phases)], axis=0)
    return table.astype(np.float32).astype(jnp.bfloat16)


def split(value):
    high = value.astype(jnp.bfloat16)
    return high, (value - high.astype(jnp.float32)).astype(jnp.bfloat16)


def dot(a, b):
    return jnp.dot(a, b, preferred_element_type=jnp.float32)


def column(row):
    count = row.shape[1]
    at = [lax.broadcasted_iota(jnp.int32, (count, count), axis) for axis in range(2)]
    rows = jnp.broadcast_to(row, (count, count))
    return jnp.sum(jnp.where(at[0] == at[1], rows, 0.0), axis=1, keepdims=True)


def start_copies(pairs, sems):
    copies = [
        pltpu.make_async_copy(source, target, sems.at[at])
        for at, (source, target) in enumerate(pairs)
    ]
    for copy in copies:
        copy.start()
    return copies


def decimate_kernel(
    paired, raw_hbm, taps_hbm, alive_hbm, picks_hbm, out_ref, pieces_hbm,
    raw_ref, taps_ref, alive_ref, picks_ref, source_ref, pieces_ref, sems,
):
    rows = raw_hbm.shape[0]
    chunks = raw_hbm.shape[1] // CHUNK
    slots = picks_ref.shape[1]
    per_tile = LANES // CHUNK_OUT
    tiles = -(-chunks // per_tile)
    pairs = [(taps_hbm, taps_ref), (picks_hbm, picks_ref), (alive_hbm, alive_ref)]
    for at in range(0, rows, SUBLANES):
        span = slice(at, at + SUBLANES)
        pairs.append((raw_hbm.at[span], raw_ref.at[span]))
    copies = start_copies(pairs, sems)
    source_ref[...] = jnp.zeros_like(source_ref)
    copies[0].wait()
    taps = jnp.broadcast_to(taps_ref[...], (SUBLANES, TAPS))
    eight = jnp.concatenate([taps, jnp.zeros((SUBLANES, CHUNK - TAPS), jnp.float32)], axis=1)
    for _ in range(2):
        eight = pltpu.roll(eight, 0, 1, stride=DEC // 2, stride_axis=0)
    wrapped = jnp.concatenate(
        [eight]
        + [pltpu.roll(eight, DEC * at, 1) for at in range(SUBLANES, CHUNK_OUT, SUBLANES)],
        axis=0,
    )
    lane = lax.broadcasted_iota(jnp.int32, (CHUNK_OUT, CHUNK), 1)
    row = lax.broadcasted_iota(jnp.int32, (CHUNK_OUT, CHUNK), 0)
    main = jnp.where(lane >= DEC * row, wrapped, 0.0)
    rim = wrapped - main
    gap = jnp.zeros((LANES - 2 * CHUNK_OUT, CHUNK), jnp.float32)
    weights_hi, weights_lo = split(jnp.concatenate([main, gap, rim], axis=0).T)
    weights = jnp.concatenate([weights_hi, weights_lo], axis=1)

    def filtered(stacked):
        high, low = split(stacked)
        both = dot(high, weights)
        return both[:, :LANES] + both[:, LANES:] + dot(low, weights_hi)

    for copy in copies[1:]:
        copy.wait()
    for slot in range(slots):
        pick = picks_ref[0, slot]
        alive = alive_ref[0, pick].astype(jnp.float32)
        for j in range(chunks):
            at = SUBLANES * slot + j
            span = slice(CHUNK * j, CHUNK * (j + 1))
            source_ref[at : at + 1, :] = raw_ref[pl.ds(pick, 1), span] * alive
    high, low = split(source_ref[...])
    count = slots * SUBLANES
    both = dot(jnp.concatenate([high, low], axis=0), weights)
    sources = both[:count, :LANES] + both[:count, LANES:] + both[count:, :LANES]
    lane = lax.broadcasted_iota(jnp.int32, (SUBLANES, LANES), 1)
    row = lax.broadcasted_iota(jnp.int32, (SUBLANES, LANES), 0)
    leads = row % per_tile == 0
    wraps = lane >= LANES - EDGE
    piece = []
    rims = jnp.zeros((1, LANES), jnp.float32)
    for slot in range(slots):
        source = sources[SUBLANES * slot : SUBLANES * (slot + 1)]
        placed = source
        for step in range(1, per_tile):
            rolled = pltpu.roll(source, CHUNK_OUT * step, 1)
            placed = jnp.where(row % per_tile == step, rolled, placed)
        own = jnp.where(leads & wraps, 0.0, placed)
        rim = placed - own
        for tile in range(tiles):
            first = per_tile * tile
            inside = jnp.where((row >= first) & (row < first + per_tile), own, 0.0)
            before = jnp.where(row == first + per_tile, rim, 0.0)
            piece.append(jnp.sum(inside + before, axis=0, keepdims=True))
        rims = rims + pltpu.roll(rim[:1], LANES - EDGE * slot if slot else 0, 1)
    piece.append(rims)
    size = len(piece)
    spread = [jnp.broadcast_to(value, (SUBLANES, LANES)) for value in piece]
    eight = []
    for group in range(size):
        place = (row + SUBLANES * group) % size
        total = spread[0]
        for at in range(1, size):
            total = jnp.where(place == at, spread[at], total)
        eight.append(total)
    eight = jnp.concatenate(eight, axis=0)
    for at in range(0, pieces_ref.shape[0], SUBLANES * size):
        pieces_ref[at : at + SUBLANES * size, :] = eight
    sending = pltpu.make_async_copy(pieces_ref, pieces_hbm, sems.at[0])
    sending.start()

    result = filtered(
        jnp.concatenate(
            [raw_ref[:, CHUNK * j : CHUNK * (j + 1)] for j in range(chunks)], axis=0
        )
    )
    part = [result[rows * j : rows * (j + 1)] for j in range(chunks)]
    is_main = lax.broadcasted_iota(jnp.int32, (rows, LANES), 1) < LANES // 2
    values = []
    for first in range(0, chunks, per_tile):
        total = jnp.where(is_main, part[first], 0.0)
        for step in range(1, min(per_tile, chunks - first)):
            total = total + pltpu.roll(part[first + step], CHUNK_OUT * step, 1)
        if first + per_tile < chunks:
            total = total + jnp.where(is_main, 0.0, part[first + per_tile])
        values.append(total)
    rim = jnp.where(is_main, 0.0, part[0])
    if paired:
        packed = rim[:SUBLANES]
        for at in range(1, rows // SUBLANES):
            group = rim[SUBLANES * at : SUBLANES * (at + 1)]
            packed = packed + pltpu.roll(group, LANES - EDGE * at, 1)
        for at, value in enumerate(values):
            out_ref[rows * at : rows * (at + 1), :] = value
        out_ref[rows * tiles :, :] = packed
    else:
        for at, value in enumerate(values + [rim]):
            out_ref[:, LANES * at : LANES * (at + 1)] = value
    sending.wait()


def unpack(packed, rows):
    tiles = [packed[at : at + rows] for at in range(0, packed.shape[0] - SUBLANES, rows)]
    rims = packed[packed.shape[0] - SUBLANES :]
    rim = jnp.concatenate(
        [rims]
        + [pltpu.roll(rims, EDGE * at, 1) for at in range(1, rows // SUBLANES)],
        axis=0,
    )
    lane = lax.broadcasted_iota(jnp.int32, rim.shape, 1)
    return tiles + [jnp.where(lane >= LANES - EDGE, rim, 0.0)]


def transform(early, late, table_hi, table_lo):
    rows = early.shape[0]
    high, low = split(jnp.concatenate([early, late], axis=0))
    first = dot(jnp.concatenate([high, low], axis=0), table_hi)
    both = first[: 2 * rows] + first[2 * rows :] + dot(high, table_lo)
    quarter = lax.broadcasted_iota(jnp.int32, (1, BINS), 1) & 3
    cosine = jnp.where(quarter == 0, 1.0, 0.0) - jnp.where(quarter == 2, 1.0, 0.0)
    sine = jnp.where(quarter == 1, 1.0, 0.0) - jnp.where(quarter == 3, 1.0, 0.0)
    early_re, early_im = both[:rows, :BINS], both[:rows, BINS:]
    late_re, late_im = both[rows:, :BINS], both[rows:, BINS:]
    return (
        early_re + cosine * late_re + sine * late_im,
        early_im + cosine * late_im - sine * late_re,
    )


def whitening(real_part, imag_part, band):
    rows = real_part.shape[0]
    tiles = BINS // LANES
    stacked = []
    for part in split(real_part * real_part + imag_part * imag_part):
        zero = jnp.zeros((rows, LANES), part.dtype)
        wide = jnp.concatenate([zero, part, zero], axis=1)
        stacked += [wide[:, LANES * tile : LANES * (tile + 3)] for tile in range(tiles)]
    banded = dot(jnp.concatenate(stacked, axis=0), band)
    step = rows * tiles
    summed = banded[:step] + banded[step:]
    total = jnp.concatenate(
        [summed[rows * tile : rows * (tile + 1)] for tile in range(tiles)], axis=1
    )
    bins = lax.broadcasted_iota(jnp.int32, (1, BINS), 1)
    count = jnp.minimum(bins + HALF, BINS - 1) - jnp.maximum(bins - HALF, 0) + 1
    return lax.rsqrt(total * (1.0 / count.astype(jnp.float32)) + 1e-06)


def prepare_kernel(
    _, alive_hbm, picks_hbm, fwd_hi_hbm, fwd_lo_hbm, band_hbm, lag_hbm,
    hi_ref, lo_ref, band_ref, lag_ref, alive_out, picks_out, alive_ref, picks_ref, sems,
):
    copies = start_copies(
        [
            (alive_hbm, alive_ref),
            (picks_hbm, picks_ref),
            (fwd_hi_hbm, hi_ref),
            (fwd_lo_hbm, lo_ref),
            (band_hbm, band_ref),
            (lag_hbm, lag_ref),
        ],
        sems,
    )
    for copy in copies[:2]:
        copy.wait()
    rows = alive_out.shape[0]
    alive_out[...] = jnp.broadcast_to(
        column(alive_ref[...].astype(jnp.float32)), (rows, LANES)
    )
    channel = lax.broadcasted_iota(jnp.int32, (rows, LANES), 0)
    for slot in range(picks_ref.shape[1]):
        pick = jnp.broadcast_to(picks_ref[:, slot : slot + 1], (rows, LANES))
        picks_out[slot] = jnp.where(channel == pick, 1.0, 0.0)
    for copy in copies[2:]:
        copy.wait()


def spectra_kernel(series_ref, hi_ref, lo_ref, band_ref, alive_ref, *refs):
    spectra_ref = refs[-1]
    rows = alive_ref.shape[0]
    half = S // 2
    if len(refs) > 1:
        mine, other = [unpack(ref[...], rows) for ref in (series_ref, refs[0])]
        first = lax.axis_index("src") == 0
        early = [jnp.where(first, a, b) for a, b in zip(mine, other)]
        late = [jnp.where(first, b, a) for a, b in zip(mine, other)]
        early[-2] = early[-2] + late[-1]
        early, late = [jnp.concatenate(tiles[:-1], axis=1) for tiles in (early, late)]
    else:
        early, late = series_ref[:, :half], series_ref[:, half:]
    real_part, imag_part = transform(early, late, hi_ref[...], lo_ref[...])
    factor = alive_ref[:, :1] * whitening(real_part, imag_part, band_ref[...])
    spectra_ref[:, :BINS] = real_part * factor
    spectra_ref[:, BINS:] = imag_part * factor


def part_bounds(total):
    ends = [3 * total // 8, 3 * total // 4, total]
    return [(a, b) for a, b in zip([0] + ends, ends) if b > a]


def correlate_kernel(
    paired, slots, spectra_ref, pieces_ref, picks_ref, hi_ref, lo_ref, band_ref, lag_ref, out_hbm,
    series_ref, rims_ref, source_ref, cross_ref, out_ref, sems,
):
    rows = spectra_ref.shape[0]
    group = out_ref.shape[0] // slots
    half = BINS // LANES
    own = lax.axis_index("blk")
    base = lax.axis_index("src") * group
    tiles = S // 2 // LANES

    def entry(block, half_at):
        if not paired:
            return 2 * (base + block) + half_at
        order = exchange_order(pieces_ref.shape[0])
        places = [order.index(2 * (side * group + block) + half_at) for side in range(2)]
        return jnp.where(base == 0, places[0], places[1])

    for slot in range(slots):
        for block in range(group):
            row = slice(slot * group + block, slot * group + block + 1)
            at, after = entry(block, 0), entry(block, 1)
            for tile in range(tiles):
                span = slice(LANES * (slot * tiles + tile), LANES * (slot * tiles + tile + 1))
                early = slice(LANES * tile, LANES * (tile + 1))
                late = slice(S // 2 + LANES * tile, S // 2 + LANES * (tile + 1))
                series_ref[row, early] = pieces_ref[at, :, span]
                series_ref[row, late] = pieces_ref[after, :, span]
            rims_ref[row, :] = pieces_ref[after, :, LANES * slots * tiles :]
    rims = jnp.concatenate(
        [
            pltpu.roll(rims_ref[slot * group : (slot + 1) * group, :], EDGE * slot, 1)
            for slot in range(slots)
        ],
        axis=0,
    )
    lane = lax.broadcasted_iota(jnp.int32, rims.shape, 1)
    seam = slice(S // 2 - LANES, S // 2)
    series_ref[:, seam] = series_ref[:, seam] + jnp.where(lane >= LANES - EDGE, rims, 0.0)
    early, late = series_ref[:, : S // 2], series_ref[:, S // 2 :]
    real_part, imag_part = transform(early, late, hi_ref[...], lo_ref[...])
    factor = whitening(real_part, imag_part, band_ref[...])
    source_ref[:, :BINS] = real_part * factor
    source_ref[:, BINS:] = imag_part * factor
    copies = []
    for part, (first, last) in enumerate(part_bounds(group * slots)):
        per_part = last - first
        for tile in range(half):
            re = slice(LANES * tile, LANES * (tile + 1))
            im = slice(BINS + LANES * tile, BINS + LANES * (tile + 1))
            rec_re, rec_im = spectra_ref[:, re], spectra_ref[:, im]
            for source in range(first, first + per_part):
                block, slot = divmod(source, slots)
                at = slot * group + block
                src_re, src_im = source_ref[at : at + 1, re], source_ref[at : at + 1, im]
                where = slice(rows * source, rows * (source + 1))
                cross_ref[where, re] = (src_re * rec_re + src_im * rec_im).astype(jnp.bfloat16)
                cross_ref[where, im] = (src_re * rec_im - src_im * rec_re).astype(jnp.bfloat16)
        lagged = dot(cross_ref[rows * first : rows * (first + per_part), :], lag_ref[...])
        for source in range(first, first + per_part):
            block, slot = divmod(source, slots)
            keep = 1.0 - jnp.where(own == base + block, 1.0, 0.0) * picks_ref[slot]
            at = source - first
            kept = lagged[rows * at : rows * (at + 1)] * jnp.concatenate(
                [keep] * (LAGS // LANES), axis=1
            )
            out_ref[source] = kept.astype(jnp.bfloat16)
        span = pl.ds(first, per_part)
        copies.append(pltpu.make_async_copy(out_ref.at[span], out_hbm.at[span], sems.at[part]))
        copies[-1].start()
    for copy in copies:
        copy.wait()


HBM = pl.BlockSpec(memory_space=pltpu.HBM)
VMEM = pl.BlockSpec(memory_space=pltpu.VMEM)
PARAMS = pltpu.CompilerParams(vmem_limit_bytes=VMEM_LIMIT)


def in_hbm(*arrays):
    return [pltpu.with_memory_space_constraint(array, pltpu.HBM) for array in arrays]


def shaped(*shape, dtype=jnp.float32):
    return jax.ShapeDtypeStruct(shape, dtype)


def exchange_order(count):
    quarter = count // 4
    return [at + place for at in range(count - quarter, -1, -quarter) for place in range(quarter)]


def local(raw_records, fir_taps, alive_mask, source_index):
    src_count = lax.axis_size("src")
    blk_count = lax.axis_size("blk")
    rows, raw_count = raw_records.shape
    slots = source_index.shape[1]
    group = blk_count // src_count
    out_count = raw_count // DEC
    width = -(-out_count // LANES) * LANES + LANES
    chunks = raw_count // CHUNK
    paired = src_count == 2 and 2 * out_count == S
    bf16 = jnp.bfloat16
    forward_hi, forward_lo = split_table(forward_table())
    alive_row = alive_mask.reshape(1, rows)

    with jax.named_scope("decimate"):
        device_count = blk_count * src_count
        main = slots * (width - LANES)
        decimated, pieces = pl.pallas_call(
            lambda *refs: decimate_kernel(paired, *refs),
            out_shape=(
                shaped(rows * (S // 2 // LANES) + SUBLANES, LANES)
                if paired
                else shaped(rows, width),
                shaped(device_count * (main // LANES + 1), LANES),
            ),
            in_specs=[HBM] * 4,
            out_specs=(VMEM, HBM),
            scratch_shapes=[
                pltpu.VMEM((rows, raw_count), jnp.float32),
                pltpu.VMEM((1, TAPS), jnp.float32),
                pltpu.SMEM((1, rows), jnp.int32),
                pltpu.SMEM((1, slots), jnp.int32),
                pltpu.VMEM((SUBLANES * slots, CHUNK), jnp.float32),
                pltpu.VMEM((device_count * (main // LANES + 1), LANES), jnp.float32),
                pltpu.SemaphoreType.DMA((rows // SUBLANES + 3,)),
            ],
            compiler_params=PARAMS,
        )(*in_hbm(raw_records, fir_taps.reshape(1, TAPS), alive_row, source_index))

    def whole(shards):
        rims = jnp.pad(shards[1:, :, width - EDGE :], ((0, 1), (0, 0), (out_count - EDGE, 0)))
        series = shards[:, :, :out_count] + rims
        return series.transpose(1, 0, 2).reshape(shards.shape[1], S)

    with jax.named_scope("gather_sources"):
        gathered = lax.all_to_all(
            pieces.reshape(device_count, 1, main + LANES),
            ("blk", "src"),
            split_axis=0,
            concat_axis=0,
            tiled=True,
            axis_index_groups=[exchange_order(device_count)] if paired else None,
        )
        if not paired:
            shards = gathered.reshape(blk_count, src_count, main + LANES)
            shards = shards.transpose(1, 0, 2)
            rims = [shards[:, :, main + LANES - EDGE * (slot + 1) :] for slot in range(slots)]
            rims = jnp.stack([rim[:, :, :EDGE] for rim in rims], axis=2)
            rims = jnp.pad(rims, ((0, 0), (0, 0), (0, 0), (LANES - EDGE, 0)))
            series = shards[:, :, :main].reshape(src_count, blk_count, slots, width - LANES)
            series = jnp.concatenate([series, rims], axis=3)
            series = whole(series.reshape(src_count, blk_count * slots, width))
            series = series.reshape(blk_count, slots, 2, S // 2).transpose(0, 2, 1, 3)
            series = series.reshape(blk_count * 2, 1, slots * S // 2)
            gathered = jnp.pad(series, ((0, 0), (0, 0), (0, LANES)))

    with jax.named_scope("prepare"):
        out_shape = (
            shaped(S // 2, NFFT, dtype=bf16),
            shaped(S // 2, NFFT, dtype=bf16),
            shaped(3 * LANES, LANES, dtype=bf16),
            shaped(NFFT, LAGS, dtype=bf16),
            shaped(rows, LANES),
            shaped(slots, rows, LANES),
        )
        table_hi, table_lo, band, lag, alive, picks = pl.pallas_call(
            prepare_kernel,
            out_shape=out_shape,
            in_specs=[VMEM] + [HBM] * 6,
            out_specs=(VMEM,) * len(out_shape),
            scratch_shapes=[
                pltpu.VMEM((1, rows), jnp.int32),
                pltpu.VMEM((1, slots), jnp.int32),
                pltpu.SemaphoreType.DMA((6,)),
            ],
            compiler_params=PARAMS,
            cost_estimate=pl.CostEstimate(
                flops=0, bytes_accessed=4 * S * NFFT, transcendentals=0
            ),
        )(
            decimated,
            *in_hbm(
                alive_row,
                source_index,
                jnp.asarray(forward_hi),
                jnp.asarray(forward_lo),
                jnp.asarray(band_table()),
                jnp.asarray(lag_table()),
            ),
        )

    with jax.named_scope("regroup"):
        if paired:
            series = [decimated]
            other = [lax.ppermute(decimated, "src", [(0, 1), (1, 0)])]
        else:
            series = [whole(lax.all_gather(decimated, "src", axis=0))]
            other = []

    with jax.named_scope("spectra"):
        operands = series + [table_hi, table_lo, band, alive] + other
        spectra = pl.pallas_call(
            spectra_kernel,
            out_shape=shaped(rows, NFFT),
            in_specs=[VMEM] * len(operands),
            out_specs=VMEM,
            compiler_params=PARAMS,
        )(*operands)

    with jax.named_scope("correlate"):
        total = group * slots
        return pl.pallas_call(
            lambda *refs: correlate_kernel(paired, slots, *refs),
            out_shape=shaped(total, rows, LAGS, dtype=bf16),
            in_specs=[VMEM] * 7,
            out_specs=HBM,
            scratch_shapes=[
                pltpu.VMEM((total, S), jnp.float32),
                pltpu.VMEM((total, LANES), jnp.float32),
                pltpu.VMEM((total, NFFT), jnp.float32),
                pltpu.VMEM((total * rows, NFFT), bf16),
                pltpu.VMEM((total, rows, LAGS), bf16),
                pltpu.SemaphoreType.DMA((PARTS,)),
            ],
            compiler_params=PARAMS,
        )(spectra, gathered, picks, table_hi, table_lo, band, lag)


def solution(mesh):
    in_specs = (P("blk", "src"), P(), P("blk"), P("blk", None))
    out_specs = P("src", "blk", None)
    return jax.shard_map(local, mesh=mesh, in_specs=in_specs, out_specs=out_specs, check_vma=False)
```

```python
import math

import jax
import jax.numpy as jnp
import numpy as np
from jax import lax
from jax.experimental import pallas as pl
from jax.experimental.pallas import tpu as pltpu
from jax.sharding import PartitionSpec as P

S = 512
NFFT = 1024
BINS = NFFT // 2
LAGS = 512
TAPS = 64
DEC = 20
HALF = 64
LANES = 128
SUBLANES = 8
PARTS = 3
EDGE = (TAPS - 1) // DEC
CHUNK = 640
CHUNK_OUT = CHUNK // DEC
VMEM_LIMIT = 48 * 1024 * 1024


def forward_table():
    phases = 2.0 * math.pi / NFFT * (np.outer(np.arange(S // 2), np.arange(BINS)) % NFFT)
    return np.concatenate([np.cos(phases), -np.sin(phases)], axis=1).astype(np.float32)


def split_table(table):
    high = table.astype(jnp.bfloat16)
    low = (table - high.astype(np.float32)).astype(jnp.bfloat16)
    return high, low


def band_table():
    bins = np.arange(3 * LANES)[:, None] - LANES
    return (np.abs(bins - np.arange(LANES)[None, :]) <= HALF).astype(jnp.bfloat16)


def lag_table():
    bins = np.arange(BINS)[:, None]
    shift = np.arange(LAGS)[None, :] - LAGS // 2
    phases = 2.0 * math.pi / NFFT * (bins * shift % NFFT)
    weight = np.where(bins == 0, 0.5, 1.0) / math.sqrt(BINS)
    table = np.concatenate([weight * np.cos(phases), -weight * np.sin(phases)], axis=0)
    return table.astype(np.float32).astype(jnp.bfloat16)


def split(value):
    high = value.astype(jnp.bfloat16)
    return high, (value - high.astype(jnp.float32)).astype(jnp.bfloat16)


def dot(a, b):
    return jnp.dot(a, b, preferred_element_type=jnp.float32)


def column(row):
    count = row.shape[1]
    at = [lax.broadcasted_iota(jnp.int32, (count, count), axis) for axis in range(2)]
    rows = jnp.broadcast_to(row, (count, count))
    return jnp.sum(jnp.where(at[0] == at[1], rows, 0.0), axis=1, keepdims=True)


def start_copies(pairs, sems):
    copies = [
        pltpu.make_async_copy(source, target, sems.at[at])
        for at, (source, target) in enumerate(pairs)
    ]
    for copy in copies:
        copy.start()
    return copies


def decimate_kernel(
    paired, raw_hbm, taps_hbm, alive_hbm, picks_hbm, out_ref, pieces_hbm,
    raw_ref, taps_ref, alive_ref, picks_ref, source_ref, pieces_ref, sems,
):
    rows = raw_hbm.shape[0]
    chunks = raw_hbm.shape[1] // CHUNK
    slots = picks_ref.shape[1]
    per_tile = LANES // CHUNK_OUT
    tiles = -(-chunks // per_tile)
    pairs = [(taps_hbm, taps_ref), (picks_hbm, picks_ref), (alive_hbm, alive_ref)]
    for at in range(0, rows, SUBLANES):
        span = slice(at, at + SUBLANES)
        pairs.append((raw_hbm.at[span], raw_ref.at[span]))
    copies = start_copies(pairs, sems)
    source_ref[...] = jnp.zeros_like(source_ref)
    copies[0].wait()
    taps = jnp.broadcast_to(taps_ref[...], (SUBLANES, TAPS))
    eight = jnp.concatenate([taps, jnp.zeros((SUBLANES, CHUNK - TAPS), jnp.float32)], axis=1)
    for _ in range(2):
        eight = pltpu.roll(eight, 0, 1, stride=DEC // 2, stride_axis=0)
    wrapped = jnp.concatenate(
        [eight]
        + [pltpu.roll(eight, DEC * at, 1) for at in range(SUBLANES, CHUNK_OUT, SUBLANES)],
        axis=0,
    )
    lane = lax.broadcasted_iota(jnp.int32, (CHUNK_OUT, CHUNK), 1)
    row = lax.broadcasted_iota(jnp.int32, (CHUNK_OUT, CHUNK), 0)
    main = jnp.where(lane >= DEC * row, wrapped, 0.0)
    rim = wrapped - main
    gap = jnp.zeros((LANES - 2 * CHUNK_OUT, CHUNK), jnp.float32)
    weights_hi, weights_lo = split(jnp.concatenate([main, gap, rim], axis=0).T)
    weights = jnp.concatenate([weights_hi, weights_lo], axis=1)

    def filtered(stacked):
        high, low = split(stacked)
        both = dot(high, weights)
        return both[:, :LANES] + both[:, LANES:] + dot(low, weights_hi)

    for copy in copies[1:]:
        copy.wait()
    for slot in range(slots):
        pick = picks_ref[0, slot]
        alive = alive_ref[0, pick].astype(jnp.float32)
        for j in range(chunks):
            at = SUBLANES * slot + j
            span = slice(CHUNK * j, CHUNK * (j + 1))
            source_ref[at : at + 1, :] = raw_ref[pl.ds(pick, 1), span] * alive
    high, low = split(source_ref[...])
    count = slots * SUBLANES
    both = dot(jnp.concatenate([high, low], axis=0), weights)
    sources = both[:count, :LANES] + both[:count, LANES:] + both[count:, :LANES]
    lane = lax.broadcasted_iota(jnp.int32, (SUBLANES, LANES), 1)
    row = lax.broadcasted_iota(jnp.int32, (SUBLANES, LANES), 0)
    leads = row % per_tile == 0
    wraps = lane >= LANES - EDGE
    piece = []
    rims = jnp.zeros((1, LANES), jnp.float32)
    for slot in range(slots):
        source = sources[SUBLANES * slot : SUBLANES * (slot + 1)]
        placed = source
        for step in range(1, per_tile):
            rolled = pltpu.roll(source, CHUNK_OUT * step, 1)
            placed = jnp.where(row % per_tile == step, rolled, placed)
        own = jnp.where(leads & wraps, 0.0, placed)
        rim = placed - own
        for tile in range(tiles):
            first = per_tile * tile
            inside = jnp.where((row >= first) & (row < first + per_tile), own, 0.0)
            before = jnp.where(row == first + per_tile, rim, 0.0)
            piece.append(jnp.sum(inside + before, axis=0, keepdims=True))
        rims = rims + pltpu.roll(rim[:1], LANES - EDGE * slot if slot else 0, 1)
    piece.append(rims)
    size = len(piece)
    spread = [jnp.broadcast_to(value, (SUBLANES, LANES)) for value in piece]
    eight = []
    for group in range(size):
        place = (row + SUBLANES * group) % size
        total = spread[0]
        for at in range(1, size):
            total = jnp.where(place == at, spread[at], total)
        eight.append(total)
    eight = jnp.concatenate(eight, axis=0)
    for at in range(0, pieces_ref.shape[0], SUBLANES * size):
        pieces_ref[at : at + SUBLANES * size, :] = eight
    sending = pltpu.make_async_copy(pieces_ref, pieces_hbm, sems.at[0])
    sending.start()

    @pl.when(lax.axis_index("blk") >= 0)
    def _():
        result = filtered(
            jnp.concatenate(
                [raw_ref[:, CHUNK * j : CHUNK * (j + 1)] for j in range(chunks)], axis=0
            )
        )
        part = [result[rows * j : rows * (j + 1)] for j in range(chunks)]
        is_main = lax.broadcasted_iota(jnp.int32, (rows, LANES), 1) < LANES // 2
        values = []
        for first in range(0, chunks, per_tile):
            total = jnp.where(is_main, part[first], 0.0)
            for step in range(1, min(per_tile, chunks - first)):
                total = total + pltpu.roll(part[first + step], CHUNK_OUT * step, 1)
            if first + per_tile < chunks:
                total = total + jnp.where(is_main, 0.0, part[first + per_tile])
            values.append(total)
        rim = jnp.where(is_main, 0.0, part[0])
        if paired:
            packed = rim[:SUBLANES]
            for at in range(1, rows // SUBLANES):
                group = rim[SUBLANES * at : SUBLANES * (at + 1)]
                packed = packed + pltpu.roll(group, LANES - EDGE * at, 1)
            for at, value in enumerate(values):
                out_ref[rows * at : rows * (at + 1), :] = value
            out_ref[rows * tiles :, :] = packed
        else:
            for at, value in enumerate(values + [rim]):
                out_ref[:, LANES * at : LANES * (at + 1)] = value

    sending.wait()


def unpack(packed, rows):
    tiles = [packed[at : at + rows] for at in range(0, packed.shape[0] - SUBLANES, rows)]
    rims = packed[packed.shape[0] - SUBLANES :]
    rim = jnp.concatenate(
        [rims]
        + [pltpu.roll(rims, EDGE * at, 1) for at in range(1, rows // SUBLANES)],
        axis=0,
    )
    lane = lax.broadcasted_iota(jnp.int32, rim.shape, 1)
    return tiles + [jnp.where(lane >= LANES - EDGE, rim, 0.0)]


def transform(early, late, table_hi, table_lo):
    rows = early.shape[0]
    high, low = split(jnp.concatenate([early, late], axis=0))
    first = dot(jnp.concatenate([high, low], axis=0), table_hi)
    both = first[: 2 * rows] + first[2 * rows :] + dot(high, table_lo)
    quarter = lax.broadcasted_iota(jnp.int32, (1, BINS), 1) & 3
    cosine = jnp.where(quarter == 0, 1.0, 0.0) - jnp.where(quarter == 2, 1.0, 0.0)
    sine = jnp.where(quarter == 1, 1.0, 0.0) - jnp.where(quarter == 3, 1.0, 0.0)
    early_re, early_im = both[:rows, :BINS], both[:rows, BINS:]
    late_re, late_im = both[rows:, :BINS], both[rows:, BINS:]
    return (
        early_re + cosine * late_re + sine * late_im,
        early_im + cosine * late_im - sine * late_re,
    )


def whitening(real_part, imag_part, band):
    rows = real_part.shape[0]
    tiles = BINS // LANES
    stacked = []
    for part in split(real_part * real_part + imag_part * imag_part):
        zero = jnp.zeros((rows, LANES), part.dtype)
        wide = jnp.concatenate([zero, part, zero], axis=1)
        stacked += [wide[:, LANES * tile : LANES * (tile + 3)] for tile in range(tiles)]
    banded = dot(jnp.concatenate(stacked, axis=0), band)
    step = rows * tiles
    summed = banded[:step] + banded[step:]
    total = jnp.concatenate(
        [summed[rows * tile : rows * (tile + 1)] for tile in range(tiles)], axis=1
    )
    bins = lax.broadcasted_iota(jnp.int32, (1, BINS), 1)
    count = jnp.minimum(bins + HALF, BINS - 1) - jnp.maximum(bins - HALF, 0) + 1
    return lax.rsqrt(total * (1.0 / count.astype(jnp.float32)) + 1e-06)


def prepare_kernel(
    _, alive_hbm, picks_hbm, fwd_hi_hbm, fwd_lo_hbm, band_hbm, lag_hbm,
    hi_ref, lo_ref, band_ref, lag_ref, alive_out, picks_out, alive_ref, picks_ref, sems,
):
    copies = start_copies(
        [
            (alive_hbm, alive_ref),
            (picks_hbm, picks_ref),
            (fwd_hi_hbm, hi_ref),
            (fwd_lo_hbm, lo_ref),
            (band_hbm, band_ref),
            (lag_hbm, lag_ref),
        ],
        sems,
    )
    for copy in copies[:2]:
        copy.wait()
    rows = alive_out.shape[0]
    alive_out[...] = jnp.broadcast_to(
        column(alive_ref[...].astype(jnp.float32)), (rows, LANES)
    )
    channel = lax.broadcasted_iota(jnp.int32, (rows, LANES), 0)
    for slot in range(picks_ref.shape[1]):
        pick = jnp.broadcast_to(picks_ref[:, slot : slot + 1], (rows, LANES))
        picks_out[slot] = jnp.where(channel == pick, 1.0, 0.0)
    for copy in copies[2:]:
        copy.wait()


def spectra_kernel(series_ref, hi_ref, lo_ref, band_ref, alive_ref, *refs):
    spectra_ref = refs[-1]
    rows = alive_ref.shape[0]
    half = S // 2
    if len(refs) > 1:
        mine, other = [unpack(ref[...], rows) for ref in (series_ref, refs[0])]
        first = lax.axis_index("src") == 0
        early = [jnp.where(first, a, b) for a, b in zip(mine, other)]
        late = [jnp.where(first, b, a) for a, b in zip(mine, other)]
        early[-2] = early[-2] + late[-1]
        early, late = [jnp.concatenate(tiles[:-1], axis=1) for tiles in (early, late)]
    else:
        early, late = series_ref[:, :half], series_ref[:, half:]
    real_part, imag_part = transform(early, late, hi_ref[...], lo_ref[...])
    factor = alive_ref[:, :1] * whitening(real_part, imag_part, band_ref[...])
    spectra_ref[:, :BINS] = real_part * factor
    spectra_ref[:, BINS:] = imag_part * factor


def part_bounds(total):
    ends = [3 * total // 8, 3 * total // 4, total]
    return [(a, b) for a, b in zip([0] + ends, ends) if b > a]


def correlate_kernel(
    slots, spectra_ref, pieces_ref, picks_ref, hi_ref, lo_ref, band_ref, lag_ref, out_hbm,
    series_ref, rims_ref, source_ref, cross_ref, out_ref, sems,
):
    rows = spectra_ref.shape[0]
    group = out_ref.shape[0] // slots
    half = BINS // LANES
    own = lax.axis_index("blk")
    base = lax.axis_index("src") * group
    tiles = S // 2 // LANES

    for slot in range(slots):
        for block in range(group):
            row = slice(slot * group + block, slot * group + block + 1)
            at = pieces_ref.shape[0] - 1 - 2 * (base + block)
            for tile in range(tiles):
                span = slice(LANES * (slot * tiles + tile), LANES * (slot * tiles + tile + 1))
                early = slice(LANES * tile, LANES * (tile + 1))
                late = slice(S // 2 + LANES * tile, S // 2 + LANES * (tile + 1))
                series_ref[row, early] = pieces_ref[at, :, span]
                series_ref[row, late] = pieces_ref[at - 1, :, span]
            rims_ref[row, :] = pieces_ref[at - 1, :, LANES * slots * tiles :]
    rims = jnp.concatenate(
        [
            pltpu.roll(rims_ref[slot * group : (slot + 1) * group, :], EDGE * slot, 1)
            for slot in range(slots)
        ],
        axis=0,
    )
    lane = lax.broadcasted_iota(jnp.int32, rims.shape, 1)
    seam = slice(S // 2 - LANES, S // 2)
    series_ref[:, seam] = series_ref[:, seam] + jnp.where(lane >= LANES - EDGE, rims, 0.0)
    early, late = series_ref[:, : S // 2], series_ref[:, S // 2 :]
    real_part, imag_part = transform(early, late, hi_ref[...], lo_ref[...])
    factor = whitening(real_part, imag_part, band_ref[...])
    source_ref[:, :BINS] = real_part * factor
    source_ref[:, BINS:] = imag_part * factor
    copies = []
    for part, (first, last) in enumerate(part_bounds(group * slots)):
        per_part = last - first
        for tile in range(half):
            re = slice(LANES * tile, LANES * (tile + 1))
            im = slice(BINS + LANES * tile, BINS + LANES * (tile + 1))
            rec_re, rec_im = spectra_ref[:, re], spectra_ref[:, im]
            for source in range(first, first + per_part):
                block, slot = divmod(source, slots)
                at = slot * group + block
                src_re, src_im = source_ref[at : at + 1, re], source_ref[at : at + 1, im]
                where = slice(rows * source, rows * (source + 1))
                cross_ref[where, re] = (src_re * rec_re + src_im * rec_im).astype(jnp.bfloat16)
                cross_ref[where, im] = (src_re * rec_im - src_im * rec_re).astype(jnp.bfloat16)
        lagged = dot(cross_ref[rows * first : rows * (first + per_part), :], lag_ref[...])
        for source in range(first, first + per_part):
            block, slot = divmod(source, slots)
            keep = 1.0 - jnp.where(own == base + block, 1.0, 0.0) * picks_ref[slot]
            at = source - first
            kept = lagged[rows * at : rows * (at + 1)] * jnp.concatenate(
                [keep] * (LAGS // LANES), axis=1
            )
            out_ref[source] = kept.astype(jnp.bfloat16)
        span = pl.ds(first, per_part)
        copies.append(pltpu.make_async_copy(out_ref.at[span], out_hbm.at[span], sems.at[part]))
        copies[-1].start()
    for copy in copies:
        copy.wait()


HBM = pl.BlockSpec(memory_space=pltpu.HBM)
VMEM = pl.BlockSpec(memory_space=pltpu.VMEM)
PARAMS = pltpu.CompilerParams(vmem_limit_bytes=VMEM_LIMIT)


def in_hbm(*arrays):
    return [pltpu.with_memory_space_constraint(array, pltpu.HBM) for array in arrays]


def shaped(*shape, dtype=jnp.float32):
    return jax.ShapeDtypeStruct(shape, dtype)


def local(raw_records, fir_taps, alive_mask, source_index):
    src_count = lax.axis_size("src")
    blk_count = lax.axis_size("blk")
    rows, raw_count = raw_records.shape
    slots = source_index.shape[1]
    group = blk_count // src_count
    out_count = raw_count // DEC
    width = -(-out_count // LANES) * LANES + LANES
    chunks = raw_count // CHUNK
    paired = src_count == 2 and 2 * out_count == S
    bf16 = jnp.bfloat16
    forward_hi, forward_lo = split_table(forward_table())
    alive_row = alive_mask.reshape(1, rows)

    with jax.named_scope("decimate"):
        device_count = blk_count * src_count
        main = slots * (width - LANES)
        decimated, pieces = pl.pallas_call(
            lambda *refs: decimate_kernel(paired, *refs),
            out_shape=(
                shaped(rows * (S // 2 // LANES) + SUBLANES, LANES)
                if paired
                else shaped(rows, width),
                shaped(device_count * (main // LANES + 1), LANES),
            ),
            in_specs=[HBM] * 4,
            out_specs=(VMEM, HBM),
            scratch_shapes=[
                pltpu.VMEM((rows, raw_count), jnp.float32),
                pltpu.VMEM((1, TAPS), jnp.float32),
                pltpu.SMEM((1, rows), jnp.int32),
                pltpu.SMEM((1, slots), jnp.int32),
                pltpu.VMEM((SUBLANES * slots, CHUNK), jnp.float32),
                pltpu.VMEM((device_count * (main // LANES + 1), LANES), jnp.float32),
                pltpu.SemaphoreType.DMA((rows // SUBLANES + 3,)),
            ],
            compiler_params=PARAMS,
        )(*in_hbm(raw_records, fir_taps.reshape(1, TAPS), alive_row, source_index))

    def whole(shards):
        rims = jnp.pad(shards[1:, :, width - EDGE :], ((0, 1), (0, 0), (out_count - EDGE, 0)))
        series = shards[:, :, :out_count] + rims
        return series.transpose(1, 0, 2).reshape(shards.shape[1], S)

    with jax.named_scope("gather_sources"):
        gathered = lax.all_to_all(
            pieces.reshape(device_count, 1, main + LANES),
            ("blk", "src"),
            split_axis=0,
            concat_axis=0,
            tiled=True,
            axis_index_groups=[list(reversed(range(device_count)))],
        )
        if not paired:
            gathered = gathered[::-1]
            shards = gathered.reshape(blk_count, src_count, main + LANES)
            shards = shards.transpose(1, 0, 2)
            rims = [shards[:, :, main + LANES - EDGE * (slot + 1) :] for slot in range(slots)]
            rims = jnp.stack([rim[:, :, :EDGE] for rim in rims], axis=2)
            rims = jnp.pad(rims, ((0, 0), (0, 0), (0, 0), (LANES - EDGE, 0)))
            series = shards[:, :, :main].reshape(src_count, blk_count, slots, width - LANES)
            series = jnp.concatenate([series, rims], axis=3)
            series = whole(series.reshape(src_count, blk_count * slots, width))
            series = series.reshape(blk_count, slots, 2, S // 2).transpose(0, 2, 1, 3)
            series = series.reshape(blk_count * 2, 1, slots * S // 2)
            gathered = jnp.pad(series, ((0, 0), (0, 0), (0, LANES)))[::-1]

    with jax.named_scope("prepare"):
        out_shape = (
            shaped(S // 2, NFFT, dtype=bf16),
            shaped(S // 2, NFFT, dtype=bf16),
            shaped(3 * LANES, LANES, dtype=bf16),
            shaped(NFFT, LAGS, dtype=bf16),
            shaped(rows, LANES),
            shaped(slots, rows, LANES),
        )
        table_hi, table_lo, band, lag, alive, picks = pl.pallas_call(
            prepare_kernel,
            out_shape=out_shape,
            in_specs=[VMEM] + [HBM] * 6,
            out_specs=(VMEM,) * len(out_shape),
            scratch_shapes=[
                pltpu.VMEM((1, rows), jnp.int32),
                pltpu.VMEM((1, slots), jnp.int32),
                pltpu.SemaphoreType.DMA((6,)),
            ],
            compiler_params=PARAMS,
            cost_estimate=pl.CostEstimate(
                flops=0, bytes_accessed=4 * S * NFFT, transcendentals=0
            ),
        )(
            decimated,
            *in_hbm(
                alive_row,
                source_index,
                jnp.asarray(forward_hi),
                jnp.asarray(forward_lo),
                jnp.asarray(band_table()),
                jnp.asarray(lag_table()),
            ),
        )

    with jax.named_scope("regroup"):
        if paired:
            series = [decimated]
            other = [lax.ppermute(decimated, "src", [(0, 1), (1, 0)])]
        else:
            series = [whole(lax.all_gather(decimated, "src", axis=0))]
            other = []

    with jax.named_scope("spectra"):
        operands = series + [table_hi, table_lo, band, alive] + other
        spectra = pl.pallas_call(
            spectra_kernel,
            out_shape=shaped(rows, NFFT),
            in_specs=[VMEM] * len(operands),
            out_specs=VMEM,
            compiler_params=PARAMS,
        )(*operands)

    with jax.named_scope("correlate"):
        total = group * slots
        return pl.pallas_call(
            lambda *refs: correlate_kernel(slots, *refs),
            out_shape=shaped(total, rows, LAGS, dtype=bf16),
            in_specs=[VMEM] * 7,
            out_specs=HBM,
            scratch_shapes=[
                pltpu.VMEM((total, S), jnp.float32),
                pltpu.VMEM((total, LANES), jnp.float32),
                pltpu.VMEM((total, NFFT), jnp.float32),
                pltpu.VMEM((total * rows, NFFT), bf16),
                pltpu.VMEM((total, rows, LAGS), bf16),
                pltpu.SemaphoreType.DMA((PARTS,)),
            ],
            compiler_params=PARAMS,
        )(spectra, gathered, picks, table_hi, table_lo, band, lag)


def solution(mesh):
    in_specs = (P("blk", "src"), P(), P("blk"), P("blk", None))
    out_specs = P("src", "blk", None)
    return jax.shard_map(local, mesh=mesh, in_specs=in_specs, out_specs=out_specs, check_vma=False)
```

```python
import math

import jax
import jax.numpy as jnp
import numpy as np
from jax import lax
from jax.experimental import pallas as pl
from jax.experimental.pallas import tpu as pltpu
from jax.sharding import PartitionSpec as P

S = 512
NFFT = 1024
BINS = NFFT // 2
LAGS = 512
TAPS = 64
DEC = 20
HALF = 64
LANES = 128
SUBLANES = 8
PARTS = 3
EDGE = (TAPS - 1) // DEC
CHUNK = 640
CHUNK_OUT = CHUNK // DEC
VMEM_LIMIT = 48 * 1024 * 1024


def forward_table():
    phases = 2.0 * math.pi / NFFT * (np.outer(np.arange(S // 2), np.arange(BINS)) % NFFT)
    return np.concatenate([np.cos(phases), -np.sin(phases)], axis=1).astype(np.float32)


def split_table(table):
    high = table.astype(jnp.bfloat16)
    low = (table - high.astype(np.float32)).astype(jnp.bfloat16)
    return high, low


def band_table():
    bins = np.arange(3 * LANES)[:, None] - LANES
    return (np.abs(bins - np.arange(LANES)[None, :]) <= HALF).astype(jnp.bfloat16)


def lag_table():
    bins = np.arange(BINS)[:, None]
    shift = np.arange(LAGS)[None, :] - LAGS // 2
    phases = 2.0 * math.pi / NFFT * (bins * shift % NFFT)
    weight = np.where(bins == 0, 0.5, 1.0) / math.sqrt(BINS)
    table = np.concatenate([weight * np.cos(phases), -weight * np.sin(phases)], axis=0)
    return table.astype(np.float32).astype(jnp.bfloat16)


def split(value):
    high = value.astype(jnp.bfloat16)
    return high, (value - high.astype(jnp.float32)).astype(jnp.bfloat16)


def dot(a, b):
    return jnp.dot(a, b, preferred_element_type=jnp.float32)


def column(row):
    count = row.shape[1]
    at = [lax.broadcasted_iota(jnp.int32, (count, count), axis) for axis in range(2)]
    rows = jnp.broadcast_to(row, (count, count))
    return jnp.sum(jnp.where(at[0] == at[1], rows, 0.0), axis=1, keepdims=True)


def start_copies(pairs, sems):
    copies = [
        pltpu.make_async_copy(source, target, sems.at[at])
        for at, (source, target) in enumerate(pairs)
    ]
    for copy in copies:
        copy.start()
    return copies


def decimate_kernel(
    paired, raw_hbm, taps_hbm, alive_hbm, picks_hbm, out_ref, pieces_hbm,
    raw_ref, taps_ref, alive_ref, picks_ref, source_ref, pieces_ref, sems,
):
    rows = raw_hbm.shape[0]
    chunks = raw_hbm.shape[1] // CHUNK
    slots = picks_ref.shape[1]
    per_tile = LANES // CHUNK_OUT
    tiles = -(-chunks // per_tile)
    pairs = [(taps_hbm, taps_ref), (picks_hbm, picks_ref), (alive_hbm, alive_ref)]
    for at in range(0, rows, SUBLANES):
        span = slice(at, at + SUBLANES)
        pairs.append((raw_hbm.at[span], raw_ref.at[span]))
    copies = start_copies(pairs, sems)
    source_ref[...] = jnp.zeros_like(source_ref)
    copies[0].wait()
    taps = jnp.broadcast_to(taps_ref[...], (SUBLANES, TAPS))
    eight = jnp.concatenate([taps, jnp.zeros((SUBLANES, CHUNK - TAPS), jnp.float32)], axis=1)
    for _ in range(2):
        eight = pltpu.roll(eight, 0, 1, stride=DEC // 2, stride_axis=0)
    wrapped = jnp.concatenate(
        [eight]
        + [pltpu.roll(eight, DEC * at, 1) for at in range(SUBLANES, CHUNK_OUT, SUBLANES)],
        axis=0,
    )
    lane = lax.broadcasted_iota(jnp.int32, (CHUNK_OUT, CHUNK), 1)
    row = lax.broadcasted_iota(jnp.int32, (CHUNK_OUT, CHUNK), 0)
    main = jnp.where(lane >= DEC * row, wrapped, 0.0)
    rim = wrapped - main
    weights = jnp.concatenate(split(jnp.concatenate([main, rim], axis=0).T), axis=1)

    def filtered(stacked):
        count = stacked.shape[0]
        high, low = split(stacked)
        both = dot(jnp.concatenate([high, low], axis=0), weights)
        both = both[:count] + both[count:]
        both = both + pltpu.roll(both, LANES // 2, 1)
        lane = lax.broadcasted_iota(jnp.int32, both.shape, 1)
        return jnp.where((lane < CHUNK_OUT) | (lane >= LANES - EDGE), both, 0.0)

    for copy in copies[1:]:
        copy.wait()
    for slot in range(slots):
        pick = picks_ref[0, slot]
        alive = alive_ref[0, pick].astype(jnp.float32)
        for j in range(chunks):
            at = SUBLANES * slot + j
            span = slice(CHUNK * j, CHUNK * (j + 1))
            source_ref[at : at + 1, :] = raw_ref[pl.ds(pick, 1), span] * alive
    sources = filtered(source_ref[...])
    lane = lax.broadcasted_iota(jnp.int32, (SUBLANES, LANES), 1)
    row = lax.broadcasted_iota(jnp.int32, (SUBLANES, LANES), 0)
    leads = row % per_tile == 0
    wraps = lane >= LANES - EDGE
    piece = []
    rims = jnp.zeros((1, LANES), jnp.float32)
    for slot in range(slots):
        source = sources[SUBLANES * slot : SUBLANES * (slot + 1)]
        placed = source
        for step in range(1, per_tile):
            rolled = pltpu.roll(source, CHUNK_OUT * step, 1)
            placed = jnp.where(row % per_tile == step, rolled, placed)
        own = jnp.where(leads & wraps, 0.0, placed)
        rim = placed - own
        for tile in range(tiles):
            first = per_tile * tile
            inside = jnp.where((row >= first) & (row < first + per_tile), own, 0.0)
            before = jnp.where(row == first + per_tile, rim, 0.0)
            piece.append(jnp.sum(inside + before, axis=0, keepdims=True))
        rims = rims + pltpu.roll(rim[:1], LANES - EDGE * slot if slot else 0, 1)
    piece.append(rims)
    size = len(piece)
    spread = [jnp.broadcast_to(value, (SUBLANES, LANES)) for value in piece]
    eight = []
    for group in range(size):
        place = (row + SUBLANES * group) % size
        total = spread[0]
        for at in range(1, size):
            total = jnp.where(place == at, spread[at], total)
        eight.append(total)
    eight = jnp.concatenate(eight, axis=0)
    for at in range(0, pieces_ref.shape[0], SUBLANES * size):
        pieces_ref[at : at + SUBLANES * size, :] = eight
    sending = pltpu.make_async_copy(pieces_ref, pieces_hbm, sems.at[0])
    sending.start()

    @pl.when(lax.axis_index("blk") >= 0)
    def _():
        result = filtered(
            jnp.concatenate(
                [raw_ref[:, CHUNK * j : CHUNK * (j + 1)] for j in range(chunks)], axis=0
            )
        )
        part = [result[rows * j : rows * (j + 1)] for j in range(chunks)]
        is_main = lax.broadcasted_iota(jnp.int32, (rows, LANES), 1) < LANES // 2
        values = []
        for first in range(0, chunks, per_tile):
            total = jnp.where(is_main, part[first], 0.0)
            for step in range(1, min(per_tile, chunks - first)):
                total = total + pltpu.roll(part[first + step], CHUNK_OUT * step, 1)
            if first + per_tile < chunks:
                total = total + jnp.where(is_main, 0.0, part[first + per_tile])
            values.append(total)
        rim = jnp.where(is_main, 0.0, part[0])
        if paired:
            packed = rim[:SUBLANES]
            for at in range(1, rows // SUBLANES):
                group = rim[SUBLANES * at : SUBLANES * (at + 1)]
                packed = packed + pltpu.roll(group, LANES - EDGE * at, 1)
            for at, value in enumerate(values):
                out_ref[rows * at : rows * (at + 1), :] = value
            out_ref[rows * tiles :, :] = packed
        else:
            for at, value in enumerate(values + [rim]):
                out_ref[:, LANES * at : LANES * (at + 1)] = value

    sending.wait()


def unpack(packed, rows):
    tiles = [packed[at : at + rows] for at in range(0, packed.shape[0] - SUBLANES, rows)]
    rims = packed[packed.shape[0] - SUBLANES :]
    rim = jnp.concatenate(
        [rims]
        + [pltpu.roll(rims, EDGE * at, 1) for at in range(1, rows // SUBLANES)],
        axis=0,
    )
    lane = lax.broadcasted_iota(jnp.int32, rim.shape, 1)
    return tiles + [jnp.where(lane >= LANES - EDGE, rim, 0.0)]


def transform(early, late, table_hi, table_lo):
    rows = early.shape[0]
    high, low = split(jnp.concatenate([early, late], axis=0))
    first = dot(jnp.concatenate([high, low], axis=0), table_hi)
    both = first[: 2 * rows] + first[2 * rows :] + dot(high, table_lo)
    quarter = lax.broadcasted_iota(jnp.int32, (1, BINS), 1) & 3
    cosine = jnp.where(quarter == 0, 1.0, 0.0) - jnp.where(quarter == 2, 1.0, 0.0)
    sine = jnp.where(quarter == 1, 1.0, 0.0) - jnp.where(quarter == 3, 1.0, 0.0)
    early_re, early_im = both[:rows, :BINS], both[:rows, BINS:]
    late_re, late_im = both[rows:, :BINS], both[rows:, BINS:]
    return (
        early_re + cosine * late_re + sine * late_im,
        early_im + cosine * late_im - sine * late_re,
    )


def whitening(real_part, imag_part, band):
    rows = real_part.shape[0]
    tiles = BINS // LANES
    stacked = []
    for part in split(real_part * real_part + imag_part * imag_part):
        zero = jnp.zeros((rows, LANES), part.dtype)
        wide = jnp.concatenate([zero, part, zero], axis=1)
        stacked += [wide[:, LANES * tile : LANES * (tile + 3)] for tile in range(tiles)]
    banded = dot(jnp.concatenate(stacked, axis=0), band)
    step = rows * tiles
    summed = banded[:step] + banded[step:]
    total = jnp.concatenate(
        [summed[rows * tile : rows * (tile + 1)] for tile in range(tiles)], axis=1
    )
    bins = lax.broadcasted_iota(jnp.int32, (1, BINS), 1)
    count = jnp.minimum(bins + HALF, BINS - 1) - jnp.maximum(bins - HALF, 0) + 1
    return lax.rsqrt(total * (1.0 / count.astype(jnp.float32)) + 1e-06)


def prepare_kernel(
    _, alive_hbm, picks_hbm, fwd_hi_hbm, fwd_lo_hbm, band_hbm, lag_hbm,
    hi_ref, lo_ref, band_ref, lag_ref, alive_out, picks_out, alive_ref, picks_ref, sems,
):
    copies = start_copies(
        [
            (alive_hbm, alive_ref),
            (picks_hbm, picks_ref),
            (fwd_hi_hbm, hi_ref),
            (fwd_lo_hbm, lo_ref),
            (band_hbm, band_ref),
            (lag_hbm, lag_ref),
        ],
        sems,
    )
    for copy in copies[:2]:
        copy.wait()
    rows = alive_out.shape[0]
    alive_out[...] = jnp.broadcast_to(
        column(alive_ref[...].astype(jnp.float32)), (rows, LANES)
    )
    channel = lax.broadcasted_iota(jnp.int32, (rows, LANES), 0)
    for slot in range(picks_ref.shape[1]):
        pick = jnp.broadcast_to(picks_ref[:, slot : slot + 1], (rows, LANES))
        picks_out[slot] = jnp.where(channel == pick, 1.0, 0.0)
    for copy in copies[2:]:
        copy.wait()


def spectra_kernel(series_ref, hi_ref, lo_ref, band_ref, alive_ref, *refs):
    spectra_ref = refs[-1]
    rows = alive_ref.shape[0]
    half = S // 2
    if len(refs) > 1:
        mine, other = [unpack(ref[...], rows) for ref in (series_ref, refs[0])]
        first = lax.axis_index("src") == 0
        early = [jnp.where(first, a, b) for a, b in zip(mine, other)]
        late = [jnp.where(first, b, a) for a, b in zip(mine, other)]
        early[-2] = early[-2] + late[-1]
        early, late = [jnp.concatenate(tiles[:-1], axis=1) for tiles in (early, late)]
    else:
        early, late = series_ref[:, :half], series_ref[:, half:]
    real_part, imag_part = transform(early, late, hi_ref[...], lo_ref[...])
    factor = alive_ref[:, :1] * whitening(real_part, imag_part, band_ref[...])
    spectra_ref[:, :BINS] = real_part * factor
    spectra_ref[:, BINS:] = imag_part * factor


def part_bounds(total):
    ends = [3 * total // 8, 3 * total // 4, total]
    return [(a, b) for a, b in zip([0] + ends, ends) if b > a]


def correlate_kernel(
    slots, spectra_ref, pieces_ref, picks_ref, hi_ref, lo_ref, band_ref, lag_ref, out_hbm,
    series_ref, rims_ref, source_ref, cross_ref, out_ref, sems,
):
    rows = spectra_ref.shape[0]
    group = out_ref.shape[0] // slots
    half = BINS // LANES
    own = lax.axis_index("blk")
    base = lax.axis_index("src") * group
    tiles = S // 2 // LANES

    for slot in range(slots):
        for block in range(group):
            row = slice(slot * group + block, slot * group + block + 1)
            at = pieces_ref.shape[0] - 1 - 2 * (base + block)
            for tile in range(tiles):
                span = slice(LANES * (slot * tiles + tile), LANES * (slot * tiles + tile + 1))
                early = slice(LANES * tile, LANES * (tile + 1))
                late = slice(S // 2 + LANES * tile, S // 2 + LANES * (tile + 1))
                series_ref[row, early] = pieces_ref[at, :, span]
                series_ref[row, late] = pieces_ref[at - 1, :, span]
            rims_ref[row, :] = pieces_ref[at - 1, :, LANES * slots * tiles :]
    rims = jnp.concatenate(
        [
            pltpu.roll(rims_ref[slot * group : (slot + 1) * group, :], EDGE * slot, 1)
            for slot in range(slots)
        ],
        axis=0,
    )
    lane = lax.broadcasted_iota(jnp.int32, rims.shape, 1)
    seam = slice(S // 2 - LANES, S // 2)
    series_ref[:, seam] = series_ref[:, seam] + jnp.where(lane >= LANES - EDGE, rims, 0.0)
    early, late = series_ref[:, : S // 2], series_ref[:, S // 2 :]
    real_part, imag_part = transform(early, late, hi_ref[...], lo_ref[...])
    factor = whitening(real_part, imag_part, band_ref[...])
    source_ref[:, :BINS] = real_part * factor
    source_ref[:, BINS:] = imag_part * factor
    copies = []
    for part, (first, last) in enumerate(part_bounds(group * slots)):
        per_part = last - first
        for tile in range(half):
            re = slice(LANES * tile, LANES * (tile + 1))
            im = slice(BINS + LANES * tile, BINS + LANES * (tile + 1))
            rec_re, rec_im = spectra_ref[:, re], spectra_ref[:, im]
            for source in range(first, first + per_part):
                block, slot = divmod(source, slots)
                at = slot * group + block
                src_re, src_im = source_ref[at : at + 1, re], source_ref[at : at + 1, im]
                where = slice(rows * source, rows * (source + 1))
                cross_ref[where, re] = (src_re * rec_re + src_im * rec_im).astype(jnp.bfloat16)
                cross_ref[where, im] = (src_re * rec_im - src_im * rec_re).astype(jnp.bfloat16)
        lagged = dot(cross_ref[rows * first : rows * (first + per_part), :], lag_ref[...])
        for source in range(first, first + per_part):
            block, slot = divmod(source, slots)
            keep = 1.0 - jnp.where(own == base + block, 1.0, 0.0) * picks_ref[slot]
            at = source - first
            kept = lagged[rows * at : rows * (at + 1)] * jnp.concatenate(
                [keep] * (LAGS // LANES), axis=1
            )
            out_ref[source] = kept.astype(jnp.bfloat16)
        span = pl.ds(first, per_part)
        copies.append(pltpu.make_async_copy(out_ref.at[span], out_hbm.at[span], sems.at[part]))
        copies[-1].start()
    for copy in copies:
        copy.wait()


HBM = pl.BlockSpec(memory_space=pltpu.HBM)
VMEM = pl.BlockSpec(memory_space=pltpu.VMEM)
PARAMS = pltpu.CompilerParams(vmem_limit_bytes=VMEM_LIMIT)


def in_hbm(*arrays):
    return [pltpu.with_memory_space_constraint(array, pltpu.HBM) for array in arrays]


def shaped(*shape, dtype=jnp.float32):
    return jax.ShapeDtypeStruct(shape, dtype)


def local(raw_records, fir_taps, alive_mask, source_index):
    src_count = lax.axis_size("src")
    blk_count = lax.axis_size("blk")
    rows, raw_count = raw_records.shape
    slots = source_index.shape[1]
    group = blk_count // src_count
    out_count = raw_count // DEC
    width = -(-out_count // LANES) * LANES + LANES
    chunks = raw_count // CHUNK
    paired = src_count == 2 and 2 * out_count == S
    bf16 = jnp.bfloat16
    forward_hi, forward_lo = split_table(forward_table())
    alive_row = alive_mask.reshape(1, rows)

    with jax.named_scope("decimate"):
        device_count = blk_count * src_count
        main = slots * (width - LANES)
        decimated, pieces = pl.pallas_call(
            lambda *refs: decimate_kernel(paired, *refs),
            out_shape=(
                shaped(rows * (S // 2 // LANES) + SUBLANES, LANES)
                if paired
                else shaped(rows, width),
                shaped(device_count * (main // LANES + 1), LANES),
            ),
            in_specs=[HBM] * 4,
            out_specs=(VMEM, HBM),
            scratch_shapes=[
                pltpu.VMEM((rows, raw_count), jnp.float32),
                pltpu.VMEM((1, TAPS), jnp.float32),
                pltpu.SMEM((1, rows), jnp.int32),
                pltpu.SMEM((1, slots), jnp.int32),
                pltpu.VMEM((SUBLANES * slots, CHUNK), jnp.float32),
                pltpu.VMEM((device_count * (main // LANES + 1), LANES), jnp.float32),
                pltpu.SemaphoreType.DMA((rows // SUBLANES + 3,)),
            ],
            compiler_params=PARAMS,
        )(*in_hbm(raw_records, fir_taps.reshape(1, TAPS), alive_row, source_index))

    def whole(shards):
        rims = jnp.pad(shards[1:, :, width - EDGE :], ((0, 1), (0, 0), (out_count - EDGE, 0)))
        series = shards[:, :, :out_count] + rims
        return series.transpose(1, 0, 2).reshape(shards.shape[1], S)

    with jax.named_scope("gather_sources"):
        gathered = lax.all_to_all(
            pieces.reshape(device_count, 1, main + LANES),
            ("blk", "src"),
            split_axis=0,
            concat_axis=0,
            tiled=True,
            axis_index_groups=[list(reversed(range(device_count)))],
        )
        if not paired:
            gathered = gathered[::-1]
            shards = gathered.reshape(blk_count, src_count, main + LANES)
            shards = shards.transpose(1, 0, 2)
            rims = [shards[:, :, main + LANES - EDGE * (slot + 1) :] for slot in range(slots)]
            rims = jnp.stack([rim[:, :, :EDGE] for rim in rims], axis=2)
            rims = jnp.pad(rims, ((0, 0), (0, 0), (0, 0), (LANES - EDGE, 0)))
            series = shards[:, :, :main].reshape(src_count, blk_count, slots, width - LANES)
            series = jnp.concatenate([series, rims], axis=3)
            series = whole(series.reshape(src_count, blk_count * slots, width))
            series = series.reshape(blk_count, slots, 2, S // 2).transpose(0, 2, 1, 3)
            series = series.reshape(blk_count * 2, 1, slots * S // 2)
            gathered = jnp.pad(series, ((0, 0), (0, 0), (0, LANES)))[::-1]

    with jax.named_scope("prepare"):
        out_shape = (
            shaped(S // 2, NFFT, dtype=bf16),
            shaped(S // 2, NFFT, dtype=bf16),
            shaped(3 * LANES, LANES, dtype=bf16),
            shaped(NFFT, LAGS, dtype=bf16),
            shaped(rows, LANES),
            shaped(slots, rows, LANES),
        )
        table_hi, table_lo, band, lag, alive, picks = pl.pallas_call(
            prepare_kernel,
            out_shape=out_shape,
            in_specs=[VMEM] + [HBM] * 6,
            out_specs=(VMEM,) * len(out_shape),
            scratch_shapes=[
                pltpu.VMEM((1, rows), jnp.int32),
                pltpu.VMEM((1, slots), jnp.int32),
                pltpu.SemaphoreType.DMA((6,)),
            ],
            compiler_params=PARAMS,
            cost_estimate=pl.CostEstimate(
                flops=0, bytes_accessed=4 * S * NFFT, transcendentals=0
            ),
        )(
            decimated,
            *in_hbm(
                alive_row,
                source_index,
                jnp.asarray(forward_hi),
                jnp.asarray(forward_lo),
                jnp.asarray(band_table()),
                jnp.asarray(lag_table()),
            ),
        )

    with jax.named_scope("regroup"):
        if paired:
            series = [decimated]
            other = [lax.ppermute(decimated, "src", [(0, 1), (1, 0)])]
        else:
            series = [whole(lax.all_gather(decimated, "src", axis=0))]
            other = []

    with jax.named_scope("spectra"):
        operands = series + [table_hi, table_lo, band, alive] + other
        spectra = pl.pallas_call(
            spectra_kernel,
            out_shape=shaped(rows, NFFT),
            in_specs=[VMEM] * len(operands),
            out_specs=VMEM,
            compiler_params=PARAMS,
        )(*operands)

    with jax.named_scope("correlate"):
        total = group * slots
        return pl.pallas_call(
            lambda *refs: correlate_kernel(slots, *refs),
            out_shape=shaped(total, rows, LAGS, dtype=bf16),
            in_specs=[VMEM] * 7,
            out_specs=HBM,
            scratch_shapes=[
                pltpu.VMEM((total, S), jnp.float32),
                pltpu.VMEM((total, LANES), jnp.float32),
                pltpu.VMEM((total, NFFT), jnp.float32),
                pltpu.VMEM((total * rows, NFFT), bf16),
                pltpu.VMEM((total, rows, LAGS), bf16),
                pltpu.SemaphoreType.DMA((PARTS,)),
            ],
            compiler_params=PARAMS,
        )(spectra, gathered, picks, table_hi, table_lo, band, lag)


def solution(mesh):
    in_specs = (P("blk", "src"), P(), P("blk"), P("blk", None))
    out_specs = P("src", "blk", None)
    return jax.shard_map(local, mesh=mesh, in_specs=in_specs, out_specs=out_specs, check_vma=False)
```

```python
import math

import jax
import jax.numpy as jnp
import numpy as np
from jax import lax
from jax.experimental import pallas as pl
from jax.experimental.pallas import tpu as pltpu
from jax.sharding import PartitionSpec as P

S = 512
NFFT = 1024
BINS = NFFT // 2
LAGS = 512
TAPS = 64
DEC = 20
HALF = 64
LANES = 128
SUBLANES = 8
PARTS = 3
EDGE = (TAPS - 1) // DEC
CHUNK = 640
CHUNK_OUT = CHUNK // DEC
VMEM_LIMIT = 48 * 1024 * 1024


def forward_table():
    phases = 2.0 * math.pi / NFFT * (np.outer(np.arange(S // 2), np.arange(BINS)) % NFFT)
    return np.concatenate([np.cos(phases), -np.sin(phases)], axis=1).astype(np.float32)


def split_table(table):
    high = table.astype(jnp.bfloat16)
    low = (table - high.astype(np.float32)).astype(jnp.bfloat16)
    return high, low


def band_table():
    bins = np.arange(3 * LANES)[:, None] - LANES
    return (np.abs(bins - np.arange(LANES)[None, :]) <= HALF).astype(jnp.bfloat16)


def lag_table():
    bins = np.arange(BINS)[:, None]
    shift = np.arange(LAGS)[None, :] - LAGS // 2
    phases = 2.0 * math.pi / NFFT * (bins * shift % NFFT)
    weight = np.where(bins == 0, 0.5, 1.0) / math.sqrt(BINS)
    table = np.concatenate([weight * np.cos(phases), -weight * np.sin(phases)], axis=0)
    return table.astype(np.float32).astype(jnp.bfloat16)


def split(value):
    high = value.astype(jnp.bfloat16)
    return high, (value - high.astype(jnp.float32)).astype(jnp.bfloat16)


def dot(a, b):
    return jnp.dot(a, b, preferred_element_type=jnp.float32)


def column(row):
    count = row.shape[1]
    at = [lax.broadcasted_iota(jnp.int32, (count, count), axis) for axis in range(2)]
    rows = jnp.broadcast_to(row, (count, count))
    return jnp.sum(jnp.where(at[0] == at[1], rows, 0.0), axis=1, keepdims=True)


def start_copies(pairs, sems):
    copies = [
        pltpu.make_async_copy(source, target, sems.at[at])
        for at, (source, target) in enumerate(pairs)
    ]
    for copy in copies:
        copy.start()
    return copies


def decimate_kernel(
    paired, raw_hbm, taps_hbm, alive_hbm, picks_hbm, out_ref, pieces_hbm,
    raw_ref, taps_ref, alive_ref, picks_ref, source_ref, pieces_ref, sems,
):
    rows = raw_hbm.shape[0]
    chunks = raw_hbm.shape[1] // CHUNK
    slots = picks_ref.shape[1]
    per_tile = LANES // CHUNK_OUT
    tiles = -(-chunks // per_tile)
    pairs = [(taps_hbm, taps_ref), (picks_hbm, picks_ref), (alive_hbm, alive_ref)]
    for at in range(0, rows, SUBLANES):
        span = slice(at, at + SUBLANES)
        pairs.append((raw_hbm.at[span], raw_ref.at[span]))
    copies = start_copies(pairs, sems)
    source_ref[...] = jnp.zeros_like(source_ref)
    copies[0].wait()
    taps = jnp.broadcast_to(taps_ref[...], (SUBLANES, TAPS))
    eight = jnp.concatenate([taps, jnp.zeros((SUBLANES, CHUNK - TAPS), jnp.float32)], axis=1)
    for _ in range(2):
        eight = pltpu.roll(eight, 0, 1, stride=DEC // 2, stride_axis=0)
    wrapped = jnp.concatenate(
        [eight]
        + [pltpu.roll(eight, DEC * at, 1) for at in range(SUBLANES, CHUNK_OUT, SUBLANES)],
        axis=0,
    )
    lane = lax.broadcasted_iota(jnp.int32, (CHUNK_OUT, CHUNK), 1)
    row = lax.broadcasted_iota(jnp.int32, (CHUNK_OUT, CHUNK), 0)
    main = jnp.where(lane >= DEC * row, wrapped, 0.0)
    rim = wrapped - main
    weights = jnp.concatenate(split(jnp.concatenate([main, rim], axis=0).T), axis=1)

    def filtered(stacked):
        count = stacked.shape[0]
        high, low = split(stacked)
        both = dot(jnp.concatenate([high, low], axis=0), weights)
        both = both[:count] + both[count:]
        both = both + pltpu.roll(both, LANES // 2, 1)
        lane = lax.broadcasted_iota(jnp.int32, both.shape, 1)
        return jnp.where((lane < CHUNK_OUT) | (lane >= LANES - EDGE), both, 0.0)

    for copy in copies[1:]:
        copy.wait()
    for slot in range(slots):
        pick = picks_ref[0, slot]
        alive = alive_ref[0, pick].astype(jnp.float32)
        for j in range(chunks):
            at = SUBLANES * slot + j
            span = slice(CHUNK * j, CHUNK * (j + 1))
            source_ref[at : at + 1, :] = raw_ref[pl.ds(pick, 1), span] * alive
    sources = filtered(source_ref[...])
    lane = lax.broadcasted_iota(jnp.int32, (SUBLANES, LANES), 1)
    row = lax.broadcasted_iota(jnp.int32, (SUBLANES, LANES), 0)
    leads = row % per_tile == 0
    wraps = lane >= LANES - EDGE
    piece = []
    rims = jnp.zeros((1, LANES), jnp.float32)
    for slot in range(slots):
        source = sources[SUBLANES * slot : SUBLANES * (slot + 1)]
        placed = source
        for step in range(1, per_tile):
            rolled = pltpu.roll(source, CHUNK_OUT * step, 1)
            placed = jnp.where(row % per_tile == step, rolled, placed)
        own = jnp.where(leads & wraps, 0.0, placed)
        rim = placed - own
        for tile in range(tiles):
            first = per_tile * tile
            inside = jnp.where((row >= first) & (row < first + per_tile), own, 0.0)
            before = jnp.where(row == first + per_tile, rim, 0.0)
            piece.append(jnp.sum(inside + before, axis=0, keepdims=True))
        rims = rims + pltpu.roll(rim[:1], LANES - EDGE * slot if slot else 0, 1)
    piece.append(rims)
    size = len(piece)
    spread = [jnp.broadcast_to(value, (SUBLANES, LANES)) for value in piece]
    eight = []
    for group in range(size):
        place = (row + SUBLANES * group) % size
        total = spread[0]
        for at in range(1, size):
            total = jnp.where(place == at, spread[at], total)
        eight.append(total)
    eight = jnp.concatenate(eight, axis=0)
    for at in range(0, pieces_ref.shape[0], SUBLANES * size):
        pieces_ref[at : at + SUBLANES * size, :] = eight
    sending = pltpu.make_async_copy(pieces_ref, pieces_hbm, sems.at[0])
    sending.start()

    @pl.when(lax.axis_index("blk") >= 0)
    def _():
        result = filtered(
            jnp.concatenate(
                [raw_ref[:, CHUNK * j : CHUNK * (j + 1)] for j in range(chunks)], axis=0
            )
        )
        part = [result[rows * j : rows * (j + 1)] for j in range(chunks)]
        is_main = lax.broadcasted_iota(jnp.int32, (rows, LANES), 1) < LANES // 2
        values = []
        for first in range(0, chunks, per_tile):
            total = jnp.where(is_main, part[first], 0.0)
            for step in range(1, min(per_tile, chunks - first)):
                total = total + pltpu.roll(part[first + step], CHUNK_OUT * step, 1)
            if first + per_tile < chunks:
                total = total + jnp.where(is_main, 0.0, part[first + per_tile])
            values.append(total)
        rim = jnp.where(is_main, 0.0, part[0])
        if paired:
            packed = rim[:SUBLANES]
            for at in range(1, rows // SUBLANES):
                group = rim[SUBLANES * at : SUBLANES * (at + 1)]
                packed = packed + pltpu.roll(group, LANES - EDGE * at, 1)
            for at, value in enumerate(values):
                out_ref[rows * at : rows * (at + 1), :] = value
            out_ref[rows * tiles :, :] = packed
        else:
            for at, value in enumerate(values + [rim]):
                out_ref[:, LANES * at : LANES * (at + 1)] = value

    sending.wait()


def unpack(packed, rows):
    tiles = [packed[at : at + rows] for at in range(0, packed.shape[0] - SUBLANES, rows)]
    rims = packed[packed.shape[0] - SUBLANES :]
    rim = jnp.concatenate(
        [rims]
        + [pltpu.roll(rims, EDGE * at, 1) for at in range(1, rows // SUBLANES)],
        axis=0,
    )
    lane = lax.broadcasted_iota(jnp.int32, rim.shape, 1)
    return tiles + [jnp.where(lane >= LANES - EDGE, rim, 0.0)]


def transform(early, late, table_hi, table_lo):
    rows = early.shape[0]
    high, low = split(jnp.concatenate([early, late], axis=0))
    first = dot(jnp.concatenate([high, low], axis=0), table_hi)
    both = first[: 2 * rows] + first[2 * rows :] + dot(high, table_lo)
    quarter = lax.broadcasted_iota(jnp.int32, (1, BINS), 1) & 3
    cosine = jnp.where(quarter == 0, 1.0, 0.0) - jnp.where(quarter == 2, 1.0, 0.0)
    sine = jnp.where(quarter == 1, 1.0, 0.0) - jnp.where(quarter == 3, 1.0, 0.0)
    early_re, early_im = both[:rows, :BINS], both[:rows, BINS:]
    late_re, late_im = both[rows:, :BINS], both[rows:, BINS:]
    return (
        early_re + cosine * late_re + sine * late_im,
        early_im + cosine * late_im - sine * late_re,
    )


def whitening(real_part, imag_part, band):
    rows = real_part.shape[0]
    tiles = BINS // LANES
    stacked = []
    for part in split(real_part * real_part + imag_part * imag_part):
        zero = jnp.zeros((rows, LANES), part.dtype)
        wide = jnp.concatenate([zero, part, zero], axis=1)
        stacked += [wide[:, LANES * tile : LANES * (tile + 3)] for tile in range(tiles)]
    banded = dot(jnp.concatenate(stacked, axis=0), band)
    step = rows * tiles
    summed = banded[:step] + banded[step:]
    total = jnp.concatenate(
        [summed[rows * tile : rows * (tile + 1)] for tile in range(tiles)], axis=1
    )
    bins = lax.broadcasted_iota(jnp.int32, (1, BINS), 1)
    count = jnp.minimum(bins + HALF, BINS - 1) - jnp.maximum(bins - HALF, 0) + 1
    return lax.rsqrt(total * (1.0 / count.astype(jnp.float32)) + 1e-06)


def prepare_kernel(
    _, alive_hbm, picks_hbm, fwd_hi_hbm, fwd_lo_hbm, band_hbm, lag_hbm,
    hi_ref, lo_ref, band_ref, lag_ref, alive_out, picks_out, alive_ref, picks_ref, sems,
):
    copies = start_copies(
        [
            (alive_hbm, alive_ref),
            (picks_hbm, picks_ref),
            (fwd_hi_hbm, hi_ref),
            (fwd_lo_hbm, lo_ref),
            (band_hbm, band_ref),
            (lag_hbm, lag_ref),
        ],
        sems,
    )
    for copy in copies[:2]:
        copy.wait()
    rows = alive_out.shape[0]
    alive_out[...] = jnp.broadcast_to(
        column(alive_ref[...].astype(jnp.float32)), (rows, LANES)
    )
    channel = lax.broadcasted_iota(jnp.int32, (rows, LANES), 0)
    for slot in range(picks_ref.shape[1]):
        pick = jnp.broadcast_to(picks_ref[:, slot : slot + 1], (rows, LANES))
        picks_out[slot] = jnp.where(channel == pick, 1.0, 0.0)
    for copy in copies[2:]:
        copy.wait()


def spectra_kernel(series_ref, hi_ref, lo_ref, band_ref, alive_ref, *refs):
    spectra_ref = refs[-1]
    rows = alive_ref.shape[0]
    half = S // 2
    if len(refs) > 1:
        mine, other = [unpack(ref[...], rows) for ref in (series_ref, refs[0])]
        first = lax.axis_index("src") == 0
        early = [jnp.where(first, a, b) for a, b in zip(mine, other)]
        late = [jnp.where(first, b, a) for a, b in zip(mine, other)]
        early[-2] = early[-2] + late[-1]
        early, late = [jnp.concatenate(tiles[:-1], axis=1) for tiles in (early, late)]
    else:
        early, late = series_ref[:, :half], series_ref[:, half:]
    real_part, imag_part = transform(early, late, hi_ref[...], lo_ref[...])
    factor = alive_ref[:, :1] * whitening(real_part, imag_part, band_ref[...])
    spectra_ref[:, :BINS] = real_part * factor
    spectra_ref[:, BINS:] = imag_part * factor


def part_bounds(total):
    ends = [3 * total // 8, 3 * total // 4, total]
    return [(a, b) for a, b in zip([0] + ends, ends) if b > a]


def correlate_kernel(
    slots, spectra_ref, pieces_ref, picks_ref, hi_ref, lo_ref, band_ref, lag_ref, out_hbm,
    series_ref, rims_ref, source_ref, cross_ref, out_ref, sems,
):
    rows = spectra_ref.shape[0]
    group = out_ref.shape[0] // slots
    half = BINS // LANES
    own = lax.axis_index("blk")
    base = lax.axis_index("src") * group
    tiles = S // 2 // LANES

    for slot in range(slots):
        for block in range(group):
            row = slice(slot * group + block, slot * group + block + 1)
            after = pieces_ref.shape[0] // 2 - 1 - (base + block)
            at = after + pieces_ref.shape[0] // 2
            for tile in range(tiles):
                span = slice(LANES * (slot * tiles + tile), LANES * (slot * tiles + tile + 1))
                early = slice(LANES * tile, LANES * (tile + 1))
                late = slice(S // 2 + LANES * tile, S // 2 + LANES * (tile + 1))
                series_ref[row, early] = pieces_ref[at, :, span]
                series_ref[row, late] = pieces_ref[after, :, span]
            rims_ref[row, :] = pieces_ref[after, :, LANES * slots * tiles :]
    rims = jnp.concatenate(
        [
            pltpu.roll(rims_ref[slot * group : (slot + 1) * group, :], EDGE * slot, 1)
            for slot in range(slots)
        ],
        axis=0,
    )
    lane = lax.broadcasted_iota(jnp.int32, rims.shape, 1)
    seam = slice(S // 2 - LANES, S // 2)
    series_ref[:, seam] = series_ref[:, seam] + jnp.where(lane >= LANES - EDGE, rims, 0.0)
    early, late = series_ref[:, : S // 2], series_ref[:, S // 2 :]
    real_part, imag_part = transform(early, late, hi_ref[...], lo_ref[...])
    factor = whitening(real_part, imag_part, band_ref[...])
    source_ref[:, :BINS] = real_part * factor
    source_ref[:, BINS:] = imag_part * factor
    copies = []
    for part, (first, last) in enumerate(part_bounds(group * slots)):
        per_part = last - first
        for tile in range(half):
            re = slice(LANES * tile, LANES * (tile + 1))
            im = slice(BINS + LANES * tile, BINS + LANES * (tile + 1))
            rec_re, rec_im = spectra_ref[:, re], spectra_ref[:, im]
            for source in range(first, first + per_part):
                block, slot = divmod(source, slots)
                at = slot * group + block
                src_re, src_im = source_ref[at : at + 1, re], source_ref[at : at + 1, im]
                where = slice(rows * source, rows * (source + 1))
                cross_ref[where, re] = (src_re * rec_re + src_im * rec_im).astype(jnp.bfloat16)
                cross_ref[where, im] = (src_re * rec_im - src_im * rec_re).astype(jnp.bfloat16)
        lagged = dot(cross_ref[rows * first : rows * (first + per_part), :], lag_ref[...])
        for source in range(first, first + per_part):
            block, slot = divmod(source, slots)
            keep = 1.0 - jnp.where(own == base + block, 1.0, 0.0) * picks_ref[slot]
            at = source - first
            kept = lagged[rows * at : rows * (at + 1)] * jnp.concatenate(
                [keep] * (LAGS // LANES), axis=1
            )
            out_ref[source] = kept.astype(jnp.bfloat16)
        span = pl.ds(first, per_part)
        copies.append(pltpu.make_async_copy(out_ref.at[span], out_hbm.at[span], sems.at[part]))
        copies[-1].start()
    for copy in copies:
        copy.wait()


HBM = pl.BlockSpec(memory_space=pltpu.HBM)
VMEM = pl.BlockSpec(memory_space=pltpu.VMEM)
PARAMS = pltpu.CompilerParams(vmem_limit_bytes=VMEM_LIMIT)


def in_hbm(*arrays):
    return [pltpu.with_memory_space_constraint(array, pltpu.HBM) for array in arrays]


def shaped(*shape, dtype=jnp.float32):
    return jax.ShapeDtypeStruct(shape, dtype)


def exchange_order(count):
    return [at for start in (count - 1, count - 2) for at in range(start, -1, -2)]


def local(raw_records, fir_taps, alive_mask, source_index):
    src_count = lax.axis_size("src")
    blk_count = lax.axis_size("blk")
    rows, raw_count = raw_records.shape
    slots = source_index.shape[1]
    group = blk_count // src_count
    out_count = raw_count // DEC
    width = -(-out_count // LANES) * LANES + LANES
    chunks = raw_count // CHUNK
    paired = src_count == 2 and 2 * out_count == S
    bf16 = jnp.bfloat16
    forward_hi, forward_lo = split_table(forward_table())
    alive_row = alive_mask.reshape(1, rows)

    with jax.named_scope("decimate"):
        device_count = blk_count * src_count
        main = slots * (width - LANES)
        decimated, pieces = pl.pallas_call(
            lambda *refs: decimate_kernel(paired, *refs),
            out_shape=(
                shaped(rows * (S // 2 // LANES) + SUBLANES, LANES)
                if paired
                else shaped(rows, width),
                shaped(device_count * (main // LANES + 1), LANES),
            ),
            in_specs=[HBM] * 4,
            out_specs=(VMEM, HBM),
            scratch_shapes=[
                pltpu.VMEM((rows, raw_count), jnp.float32),
                pltpu.VMEM((1, TAPS), jnp.float32),
                pltpu.SMEM((1, rows), jnp.int32),
                pltpu.SMEM((1, slots), jnp.int32),
                pltpu.VMEM((SUBLANES * slots, CHUNK), jnp.float32),
                pltpu.VMEM((device_count * (main // LANES + 1), LANES), jnp.float32),
                pltpu.SemaphoreType.DMA((rows // SUBLANES + 3,)),
            ],
            compiler_params=PARAMS,
        )(*in_hbm(raw_records, fir_taps.reshape(1, TAPS), alive_row, source_index))

    def whole(shards):
        rims = jnp.pad(shards[1:, :, width - EDGE :], ((0, 1), (0, 0), (out_count - EDGE, 0)))
        series = shards[:, :, :out_count] + rims
        return series.transpose(1, 0, 2).reshape(shards.shape[1], S)

    with jax.named_scope("gather_sources"):
        gathered = lax.all_to_all(
            pieces.reshape(device_count, 1, main + LANES),
            ("blk", "src"),
            split_axis=0,
            concat_axis=0,
            tiled=True,
            axis_index_groups=[exchange_order(device_count)],
        )
        if not paired:
            gathered = gathered[np.argsort(exchange_order(device_count))]
            shards = gathered.reshape(blk_count, src_count, main + LANES)
            shards = shards.transpose(1, 0, 2)
            rims = [shards[:, :, main + LANES - EDGE * (slot + 1) :] for slot in range(slots)]
            rims = jnp.stack([rim[:, :, :EDGE] for rim in rims], axis=2)
            rims = jnp.pad(rims, ((0, 0), (0, 0), (0, 0), (LANES - EDGE, 0)))
            series = shards[:, :, :main].reshape(src_count, blk_count, slots, width - LANES)
            series = jnp.concatenate([series, rims], axis=3)
            series = whole(series.reshape(src_count, blk_count * slots, width))
            series = series.reshape(blk_count, slots, 2, S // 2).transpose(0, 2, 1, 3)
            series = series.reshape(blk_count * 2, 1, slots * S // 2)
            gathered = jnp.pad(series, ((0, 0), (0, 0), (0, LANES)))
            gathered = gathered[np.array(exchange_order(blk_count * 2))]

    with jax.named_scope("prepare"):
        out_shape = (
            shaped(S // 2, NFFT, dtype=bf16),
            shaped(S // 2, NFFT, dtype=bf16),
            shaped(3 * LANES, LANES, dtype=bf16),
            shaped(NFFT, LAGS, dtype=bf16),
            shaped(rows, LANES),
            shaped(slots, rows, LANES),
        )
        table_hi, table_lo, band, lag, alive, picks = pl.pallas_call(
            prepare_kernel,
            out_shape=out_shape,
            in_specs=[VMEM] + [HBM] * 6,
            out_specs=(VMEM,) * len(out_shape),
            scratch_shapes=[
                pltpu.VMEM((1, rows), jnp.int32),
                pltpu.VMEM((1, slots), jnp.int32),
                pltpu.SemaphoreType.DMA((6,)),
            ],
            compiler_params=PARAMS,
            cost_estimate=pl.CostEstimate(
                flops=0, bytes_accessed=4 * S * NFFT, transcendentals=0
            ),
        )(
            decimated,
            *in_hbm(
                alive_row,
                source_index,
                jnp.asarray(forward_hi),
                jnp.asarray(forward_lo),
                jnp.asarray(band_table()),
                jnp.asarray(lag_table()),
            ),
        )

    with jax.named_scope("regroup"):
        if paired:
            series = [decimated]
            other = [lax.ppermute(decimated, "src", [(0, 1), (1, 0)])]
        else:
            series = [whole(lax.all_gather(decimated, "src", axis=0))]
            other = []

    with jax.named_scope("spectra"):
        operands = series + [table_hi, table_lo, band, alive] + other
        spectra = pl.pallas_call(
            spectra_kernel,
            out_shape=shaped(rows, NFFT),
            in_specs=[VMEM] * len(operands),
            out_specs=VMEM,
            compiler_params=PARAMS,
        )(*operands)

    with jax.named_scope("correlate"):
        total = group * slots
        return pl.pallas_call(
            lambda *refs: correlate_kernel(slots, *refs),
            out_shape=shaped(total, rows, LAGS, dtype=bf16),
            in_specs=[VMEM] * 7,
            out_specs=HBM,
            scratch_shapes=[
                pltpu.VMEM((total, S), jnp.float32),
                pltpu.VMEM((total, LANES), jnp.float32),
                pltpu.VMEM((total, NFFT), jnp.float32),
                pltpu.VMEM((total * rows, NFFT), bf16),
                pltpu.VMEM((total, rows, LAGS), bf16),
                pltpu.SemaphoreType.DMA((PARTS,)),
            ],
            compiler_params=PARAMS,
        )(spectra, gathered, picks, table_hi, table_lo, band, lag)


def solution(mesh):
    in_specs = (P("blk", "src"), P(), P("blk"), P("blk", None))
    out_specs = P("src", "blk", None)
    return jax.shard_map(local, mesh=mesh, in_specs=in_specs, out_specs=out_specs, check_vma=False)
```

```python
import math

import jax
import jax.numpy as jnp
import numpy as np
from jax import lax
from jax.experimental import pallas as pl
from jax.experimental.pallas import tpu as pltpu
from jax.sharding import PartitionSpec as P

S = 512
NFFT = 1024
BINS = NFFT // 2
LAGS = 512
TAPS = 64
DEC = 20
HALF = 64
LANES = 128
SUBLANES = 8
PARTS = 3
EDGE = (TAPS - 1) // DEC
CHUNK = 640
CHUNK_OUT = CHUNK // DEC
VMEM_LIMIT = 48 * 1024 * 1024


def forward_table():
    phases = 2.0 * math.pi / NFFT * (np.outer(np.arange(S // 2), np.arange(BINS)) % NFFT)
    return np.concatenate([np.cos(phases), -np.sin(phases)], axis=1).astype(np.float32)


def split_table(table):
    high = table.astype(jnp.bfloat16)
    low = (table - high.astype(np.float32)).astype(jnp.bfloat16)
    return high, low


def band_table():
    bins = np.arange(3 * LANES)[:, None] - LANES
    return (np.abs(bins - np.arange(LANES)[None, :]) <= HALF).astype(jnp.bfloat16)


def lag_table():
    bins = np.arange(BINS)[:, None]
    shift = np.arange(LAGS)[None, :] - LAGS // 2
    phases = 2.0 * math.pi / NFFT * (bins * shift % NFFT)
    weight = np.where(bins == 0, 0.5, 1.0) / math.sqrt(BINS)
    table = np.concatenate([weight * np.cos(phases), -weight * np.sin(phases)], axis=0)
    return table.astype(np.float32).astype(jnp.bfloat16)


def split(value):
    high = value.astype(jnp.bfloat16)
    return high, (value - high.astype(jnp.float32)).astype(jnp.bfloat16)


def dot(a, b):
    return jnp.dot(a, b, preferred_element_type=jnp.float32)


def column(row):
    count = row.shape[1]
    at = [lax.broadcasted_iota(jnp.int32, (count, count), axis) for axis in range(2)]
    rows = jnp.broadcast_to(row, (count, count))
    return jnp.sum(jnp.where(at[0] == at[1], rows, 0.0), axis=1, keepdims=True)


def start_copies(pairs, sems):
    copies = [
        pltpu.make_async_copy(source, target, sems.at[at])
        for at, (source, target) in enumerate(pairs)
    ]
    for copy in copies:
        copy.start()
    return copies


def decimate_kernel(
    paired, raw_hbm, taps_hbm, alive_hbm, picks_hbm, out_ref, pieces_hbm,
    raw_ref, taps_ref, alive_ref, picks_ref, source_ref, pieces_ref, sems,
):
    rows = raw_hbm.shape[0]
    chunks = raw_hbm.shape[1] // CHUNK
    slots = picks_ref.shape[1]
    per_tile = LANES // CHUNK_OUT
    tiles = -(-chunks // per_tile)
    pairs = [(taps_hbm, taps_ref), (picks_hbm, picks_ref), (alive_hbm, alive_ref)]
    for at in range(0, rows, SUBLANES):
        span = slice(at, at + SUBLANES)
        pairs.append((raw_hbm.at[span], raw_ref.at[span]))
    copies = start_copies(pairs, sems)
    source_ref[...] = jnp.zeros_like(source_ref)
    copies[0].wait()
    taps = jnp.broadcast_to(taps_ref[...], (SUBLANES, TAPS))
    eight = jnp.concatenate([taps, jnp.zeros((SUBLANES, CHUNK - TAPS), jnp.float32)], axis=1)
    for _ in range(2):
        eight = pltpu.roll(eight, 0, 1, stride=DEC // 2, stride_axis=0)
    wrapped = jnp.concatenate(
        [eight]
        + [pltpu.roll(eight, DEC * at, 1) for at in range(SUBLANES, CHUNK_OUT, SUBLANES)],
        axis=0,
    )
    lane = lax.broadcasted_iota(jnp.int32, (CHUNK_OUT, CHUNK), 1)
    row = lax.broadcasted_iota(jnp.int32, (CHUNK_OUT, CHUNK), 0)
    main = jnp.where(lane >= DEC * row, wrapped, 0.0)
    rim = wrapped - main
    weights = jnp.concatenate(split(jnp.concatenate([main, rim], axis=0).T), axis=1)

    def filtered(stacked):
        count = stacked.shape[0]
        high, low = split(stacked)
        both = dot(jnp.concatenate([high, low], axis=0), weights)
        both = both[:count] + both[count:]
        both = both + pltpu.roll(both, LANES // 2, 1)
        lane = lax.broadcasted_iota(jnp.int32, both.shape, 1)
        return jnp.where((lane < CHUNK_OUT) | (lane >= LANES - EDGE), both, 0.0)

    for copy in copies[1:]:
        copy.wait()
    for slot in range(slots):
        pick = picks_ref[0, slot]
        alive = alive_ref[0, pick].astype(jnp.float32)
        for j in range(chunks):
            at = SUBLANES * slot + j
            span = slice(CHUNK * j, CHUNK * (j + 1))
            source_ref[at : at + 1, :] = raw_ref[pl.ds(pick, 1), span] * alive
    sources = filtered(source_ref[...])
    lane = lax.broadcasted_iota(jnp.int32, (SUBLANES, LANES), 1)
    row = lax.broadcasted_iota(jnp.int32, (SUBLANES, LANES), 0)
    leads = row % per_tile == 0
    wraps = lane >= LANES - EDGE
    piece = []
    rims = jnp.zeros((1, LANES), jnp.float32)
    for slot in range(slots):
        source = sources[SUBLANES * slot : SUBLANES * (slot + 1)]
        placed = source
        for step in range(1, per_tile):
            rolled = pltpu.roll(source, CHUNK_OUT * step, 1)
            placed = jnp.where(row % per_tile == step, rolled, placed)
        own = jnp.where(leads & wraps, 0.0, placed)
        rim = placed - own
        for tile in range(tiles):
            first = per_tile * tile
            inside = jnp.where((row >= first) & (row < first + per_tile), own, 0.0)
            before = jnp.where(row == first + per_tile, rim, 0.0)
            piece.append(jnp.sum(inside + before, axis=0, keepdims=True))
        rims = rims + pltpu.roll(rim[:1], LANES - EDGE * slot if slot else 0, 1)
    piece.append(rims)
    size = len(piece)
    spread = [jnp.broadcast_to(value, (SUBLANES, LANES)) for value in piece]
    eight = []
    for group in range(size):
        place = (row + SUBLANES * group) % size
        total = spread[0]
        for at in range(1, size):
            total = jnp.where(place == at, spread[at], total)
        eight.append(total)
    eight = jnp.concatenate(eight, axis=0)
    for at in range(0, pieces_ref.shape[0], SUBLANES * size):
        pieces_ref[at : at + SUBLANES * size, :] = eight
    sending = pltpu.make_async_copy(pieces_ref, pieces_hbm, sems.at[0])
    sending.start()

    @pl.when(lax.axis_index("blk") >= 0)
    def _():
        result = filtered(
            jnp.concatenate(
                [raw_ref[:, CHUNK * j : CHUNK * (j + 1)] for j in range(chunks)], axis=0
            )
        )
        part = [result[rows * j : rows * (j + 1)] for j in range(chunks)]
        is_main = lax.broadcasted_iota(jnp.int32, (rows, LANES), 1) < LANES // 2
        values = []
        for first in range(0, chunks, per_tile):
            total = jnp.where(is_main, part[first], 0.0)
            for step in range(1, min(per_tile, chunks - first)):
                total = total + pltpu.roll(part[first + step], CHUNK_OUT * step, 1)
            if first + per_tile < chunks:
                total = total + jnp.where(is_main, 0.0, part[first + per_tile])
            values.append(total)
        rim = jnp.where(is_main, 0.0, part[0])
        if paired:
            packed = rim[:SUBLANES]
            for at in range(1, rows // SUBLANES):
                group = rim[SUBLANES * at : SUBLANES * (at + 1)]
                packed = packed + pltpu.roll(group, LANES - EDGE * at, 1)
            for at, value in enumerate(values):
                out_ref[rows * at : rows * (at + 1), :] = value
            out_ref[rows * tiles :, :] = packed
        else:
            for at, value in enumerate(values + [rim]):
                out_ref[:, LANES * at : LANES * (at + 1)] = value

    sending.wait()


def unpack(packed, rows):
    tiles = [packed[at : at + rows] for at in range(0, packed.shape[0] - SUBLANES, rows)]
    rims = packed[packed.shape[0] - SUBLANES :]
    rim = jnp.concatenate(
        [rims]
        + [pltpu.roll(rims, EDGE * at, 1) for at in range(1, rows // SUBLANES)],
        axis=0,
    )
    lane = lax.broadcasted_iota(jnp.int32, rim.shape, 1)
    return tiles + [jnp.where(lane >= LANES - EDGE, rim, 0.0)]


def transform(early, late, table_hi, table_lo):
    rows = early.shape[0]
    high, low = split(jnp.concatenate([early, late], axis=0))
    first = dot(jnp.concatenate([high, low], axis=0), table_hi)
    both = first[: 2 * rows] + first[2 * rows :] + dot(high, table_lo)
    quarter = lax.broadcasted_iota(jnp.int32, (1, BINS), 1) & 3
    cosine = jnp.where(quarter == 0, 1.0, 0.0) - jnp.where(quarter == 2, 1.0, 0.0)
    sine = jnp.where(quarter == 1, 1.0, 0.0) - jnp.where(quarter == 3, 1.0, 0.0)
    early_re, early_im = both[:rows, :BINS], both[:rows, BINS:]
    late_re, late_im = both[rows:, :BINS], both[rows:, BINS:]
    return (
        early_re + cosine * late_re + sine * late_im,
        early_im + cosine * late_im - sine * late_re,
    )


def whitening(real_part, imag_part, band):
    rows = real_part.shape[0]
    tiles = BINS // LANES
    stacked = []
    for part in split(real_part * real_part + imag_part * imag_part):
        zero = jnp.zeros((rows, LANES), part.dtype)
        wide = jnp.concatenate([zero, part, zero], axis=1)
        stacked += [wide[:, LANES * tile : LANES * (tile + 3)] for tile in range(tiles)]
    banded = dot(jnp.concatenate(stacked, axis=0), band)
    step = rows * tiles
    summed = banded[:step] + banded[step:]
    total = jnp.concatenate(
        [summed[rows * tile : rows * (tile + 1)] for tile in range(tiles)], axis=1
    )
    bins = lax.broadcasted_iota(jnp.int32, (1, BINS), 1)
    count = jnp.minimum(bins + HALF, BINS - 1) - jnp.maximum(bins - HALF, 0) + 1
    return lax.rsqrt(total * (1.0 / count.astype(jnp.float32)) + 1e-06)


def prepare_kernel(
    _, alive_hbm, picks_hbm, fwd_hi_hbm, fwd_lo_hbm, band_hbm, lag_hbm,
    hi_ref, lo_ref, band_ref, lag_ref, alive_out, picks_out, alive_ref, picks_ref, sems,
):
    copies = start_copies(
        [
            (alive_hbm, alive_ref),
            (picks_hbm, picks_ref),
            (fwd_hi_hbm, hi_ref),
            (fwd_lo_hbm, lo_ref),
            (band_hbm, band_ref),
            (lag_hbm, lag_ref),
        ],
        sems,
    )
    for copy in copies[:2]:
        copy.wait()
    rows = alive_out.shape[0]
    alive_out[...] = jnp.broadcast_to(
        column(alive_ref[...].astype(jnp.float32)), (rows, LANES)
    )
    channel = lax.broadcasted_iota(jnp.int32, (rows, LANES), 0)
    for slot in range(picks_ref.shape[1]):
        pick = jnp.broadcast_to(picks_ref[:, slot : slot + 1], (rows, LANES))
        picks_out[slot] = jnp.where(channel == pick, 1.0, 0.0)
    for copy in copies[2:]:
        copy.wait()


def spectra_kernel(series_ref, hi_ref, lo_ref, band_ref, alive_ref, *refs):
    spectra_ref = refs[-1]
    rows = alive_ref.shape[0]
    half = S // 2
    if len(refs) > 1:
        mine, other = [unpack(ref[...], rows) for ref in (series_ref, refs[0])]
        first = lax.axis_index("src") == 0
        early = [jnp.where(first, a, b) for a, b in zip(mine, other)]
        late = [jnp.where(first, b, a) for a, b in zip(mine, other)]
        early[-2] = early[-2] + late[-1]
        early, late = [jnp.concatenate(tiles[:-1], axis=1) for tiles in (early, late)]
    else:
        early, late = series_ref[:, :half], series_ref[:, half:]
    real_part, imag_part = transform(early, late, hi_ref[...], lo_ref[...])
    factor = alive_ref[:, :1] * whitening(real_part, imag_part, band_ref[...])
    spectra_ref[:, :BINS] = real_part * factor
    spectra_ref[:, BINS:] = imag_part * factor


def part_bounds(total):
    ends = [3 * total // 8, 3 * total // 4, total]
    return [(a, b) for a, b in zip([0] + ends, ends) if b > a]


def correlate_kernel(
    slots, spectra_ref, pieces_ref, picks_ref, hi_ref, lo_ref, band_ref, lag_ref, out_hbm,
    series_ref, rims_ref, source_ref, cross_ref, out_ref, sems,
):
    rows = spectra_ref.shape[0]
    group = out_ref.shape[0] // slots
    half = BINS // LANES
    own = lax.axis_index("blk")
    base = lax.axis_index("src") * group
    tiles = S // 2 // LANES

    for slot in range(slots):
        for block in range(group):
            row = slice(slot * group + block, slot * group + block + 1)
            count = pieces_ref.shape[0]
            at, after = [
                lax.rem(3 * count // 2 - 1 - 2 * (base + block) - half_at, count)
                for half_at in range(2)
            ]
            for tile in range(tiles):
                span = slice(LANES * (slot * tiles + tile), LANES * (slot * tiles + tile + 1))
                early = slice(LANES * tile, LANES * (tile + 1))
                late = slice(S // 2 + LANES * tile, S // 2 + LANES * (tile + 1))
                series_ref[row, early] = pieces_ref[at, :, span]
                series_ref[row, late] = pieces_ref[after, :, span]
            rims_ref[row, :] = pieces_ref[after, :, LANES * slots * tiles :]
    rims = jnp.concatenate(
        [
            pltpu.roll(rims_ref[slot * group : (slot + 1) * group, :], EDGE * slot, 1)
            for slot in range(slots)
        ],
        axis=0,
    )
    lane = lax.broadcasted_iota(jnp.int32, rims.shape, 1)
    seam = slice(S // 2 - LANES, S // 2)
    series_ref[:, seam] = series_ref[:, seam] + jnp.where(lane >= LANES - EDGE, rims, 0.0)
    early, late = series_ref[:, : S // 2], series_ref[:, S // 2 :]
    real_part, imag_part = transform(early, late, hi_ref[...], lo_ref[...])
    factor = whitening(real_part, imag_part, band_ref[...])
    source_ref[:, :BINS] = real_part * factor
    source_ref[:, BINS:] = imag_part * factor
    copies = []
    for part, (first, last) in enumerate(part_bounds(group * slots)):
        per_part = last - first
        for tile in range(half):
            re = slice(LANES * tile, LANES * (tile + 1))
            im = slice(BINS + LANES * tile, BINS + LANES * (tile + 1))
            rec_re, rec_im = spectra_ref[:, re], spectra_ref[:, im]
            for source in range(first, first + per_part):
                block, slot = divmod(source, slots)
                at = slot * group + block
                src_re, src_im = source_ref[at : at + 1, re], source_ref[at : at + 1, im]
                where = slice(rows * source, rows * (source + 1))
                cross_ref[where, re] = (src_re * rec_re + src_im * rec_im).astype(jnp.bfloat16)
                cross_ref[where, im] = (src_re * rec_im - src_im * rec_re).astype(jnp.bfloat16)
        lagged = dot(cross_ref[rows * first : rows * (first + per_part), :], lag_ref[...])
        for source in range(first, first + per_part):
            block, slot = divmod(source, slots)
            keep = 1.0 - jnp.where(own == base + block, 1.0, 0.0) * picks_ref[slot]
            at = source - first
            kept = lagged[rows * at : rows * (at + 1)] * jnp.concatenate(
                [keep] * (LAGS // LANES), axis=1
            )
            out_ref[source] = kept.astype(jnp.bfloat16)
        span = pl.ds(first, per_part)
        copies.append(pltpu.make_async_copy(out_ref.at[span], out_hbm.at[span], sems.at[part]))
        copies[-1].start()
    for copy in copies:
        copy.wait()


HBM = pl.BlockSpec(memory_space=pltpu.HBM)
VMEM = pl.BlockSpec(memory_space=pltpu.VMEM)
PARAMS = pltpu.CompilerParams(vmem_limit_bytes=VMEM_LIMIT)


def in_hbm(*arrays):
    return [pltpu.with_memory_space_constraint(array, pltpu.HBM) for array in arrays]


def shaped(*shape, dtype=jnp.float32):
    return jax.ShapeDtypeStruct(shape, dtype)


def exchange_order(count):
    return [(count // 2 - 1 - at) % count for at in range(count)]


def local(raw_records, fir_taps, alive_mask, source_index):
    src_count = lax.axis_size("src")
    blk_count = lax.axis_size("blk")
    rows, raw_count = raw_records.shape
    slots = source_index.shape[1]
    group = blk_count // src_count
    out_count = raw_count // DEC
    width = -(-out_count // LANES) * LANES + LANES
    chunks = raw_count // CHUNK
    paired = src_count == 2 and 2 * out_count == S
    bf16 = jnp.bfloat16
    forward_hi, forward_lo = split_table(forward_table())
    alive_row = alive_mask.reshape(1, rows)

    with jax.named_scope("decimate"):
        device_count = blk_count * src_count
        main = slots * (width - LANES)
        decimated, pieces = pl.pallas_call(
            lambda *refs: decimate_kernel(paired, *refs),
            out_shape=(
                shaped(rows * (S // 2 // LANES) + SUBLANES, LANES)
                if paired
                else shaped(rows, width),
                shaped(device_count * (main // LANES + 1), LANES),
            ),
            in_specs=[HBM] * 4,
            out_specs=(VMEM, HBM),
            scratch_shapes=[
                pltpu.VMEM((rows, raw_count), jnp.float32),
                pltpu.VMEM((1, TAPS), jnp.float32),
                pltpu.SMEM((1, rows), jnp.int32),
                pltpu.SMEM((1, slots), jnp.int32),
                pltpu.VMEM((SUBLANES * slots, CHUNK), jnp.float32),
                pltpu.VMEM((device_count * (main // LANES + 1), LANES), jnp.float32),
                pltpu.SemaphoreType.DMA((rows // SUBLANES + 3,)),
            ],
            compiler_params=PARAMS,
        )(*in_hbm(raw_records, fir_taps.reshape(1, TAPS), alive_row, source_index))

    def whole(shards):
        rims = jnp.pad(shards[1:, :, width - EDGE :], ((0, 1), (0, 0), (out_count - EDGE, 0)))
        series = shards[:, :, :out_count] + rims
        return series.transpose(1, 0, 2).reshape(shards.shape[1], S)

    with jax.named_scope("gather_sources"):
        gathered = lax.all_to_all(
            pieces.reshape(device_count, 1, main + LANES),
            ("blk", "src"),
            split_axis=0,
            concat_axis=0,
            tiled=True,
            axis_index_groups=[exchange_order(device_count)],
        )
        if not paired:
            gathered = gathered[np.argsort(exchange_order(device_count))]
            shards = gathered.reshape(blk_count, src_count, main + LANES)
            shards = shards.transpose(1, 0, 2)
            rims = [shards[:, :, main + LANES - EDGE * (slot + 1) :] for slot in range(slots)]
            rims = jnp.stack([rim[:, :, :EDGE] for rim in rims], axis=2)
            rims = jnp.pad(rims, ((0, 0), (0, 0), (0, 0), (LANES - EDGE, 0)))
            series = shards[:, :, :main].reshape(src_count, blk_count, slots, width - LANES)
            series = jnp.concatenate([series, rims], axis=3)
            series = whole(series.reshape(src_count, blk_count * slots, width))
            series = series.reshape(blk_count, slots, 2, S // 2).transpose(0, 2, 1, 3)
            series = series.reshape(blk_count * 2, 1, slots * S // 2)
            gathered = jnp.pad(series, ((0, 0), (0, 0), (0, LANES)))
            gathered = gathered[np.array(exchange_order(blk_count * 2))]

    with jax.named_scope("prepare"):
        out_shape = (
            shaped(S // 2, NFFT, dtype=bf16),
            shaped(S // 2, NFFT, dtype=bf16),
            shaped(3 * LANES, LANES, dtype=bf16),
            shaped(NFFT, LAGS, dtype=bf16),
            shaped(rows, LANES),
            shaped(slots, rows, LANES),
        )
        table_hi, table_lo, band, lag, alive, picks = pl.pallas_call(
            prepare_kernel,
            out_shape=out_shape,
            in_specs=[VMEM] + [HBM] * 6,
            out_specs=(VMEM,) * len(out_shape),
            scratch_shapes=[
                pltpu.VMEM((1, rows), jnp.int32),
                pltpu.VMEM((1, slots), jnp.int32),
                pltpu.SemaphoreType.DMA((6,)),
            ],
            compiler_params=PARAMS,
            cost_estimate=pl.CostEstimate(
                flops=0, bytes_accessed=4 * S * NFFT, transcendentals=0
            ),
        )(
            decimated,
            *in_hbm(
                alive_row,
                source_index,
                jnp.asarray(forward_hi),
                jnp.asarray(forward_lo),
                jnp.asarray(band_table()),
                jnp.asarray(lag_table()),
            ),
        )

    with jax.named_scope("regroup"):
        if paired:
            series = [decimated]
            other = [lax.ppermute(decimated, "src", [(0, 1), (1, 0)])]
        else:
            series = [whole(lax.all_gather(decimated, "src", axis=0))]
            other = []

    with jax.named_scope("spectra"):
        operands = series + [table_hi, table_lo, band, alive] + other
        spectra = pl.pallas_call(
            spectra_kernel,
            out_shape=shaped(rows, NFFT),
            in_specs=[VMEM] * len(operands),
            out_specs=VMEM,
            compiler_params=PARAMS,
        )(*operands)

    with jax.named_scope("correlate"):
        total = group * slots
        return pl.pallas_call(
            lambda *refs: correlate_kernel(slots, *refs),
            out_shape=shaped(total, rows, LAGS, dtype=bf16),
            in_specs=[VMEM] * 7,
            out_specs=HBM,
            scratch_shapes=[
                pltpu.VMEM((total, S), jnp.float32),
                pltpu.VMEM((total, LANES), jnp.float32),
                pltpu.VMEM((total, NFFT), jnp.float32),
                pltpu.VMEM((total * rows, NFFT), bf16),
                pltpu.VMEM((total, rows, LAGS), bf16),
                pltpu.SemaphoreType.DMA((PARTS,)),
            ],
            compiler_params=PARAMS,
        )(spectra, gathered, picks, table_hi, table_lo, band, lag)


def solution(mesh):
    in_specs = (P("blk", "src"), P(), P("blk"), P("blk", None))
    out_specs = P("src", "blk", None)
    return jax.shard_map(local, mesh=mesh, in_specs=in_specs, out_specs=out_specs, check_vma=False)
```

```python
import math

import jax
import jax.numpy as jnp
import numpy as np
from jax import lax
from jax.experimental import pallas as pl
from jax.experimental.pallas import tpu as pltpu
from jax.sharding import PartitionSpec as P

S = 512
NFFT = 1024
BINS = NFFT // 2
LAGS = 512
TAPS = 64
DEC = 20
HALF = 64
LANES = 128
SUBLANES = 8
PARTS = 3
EDGE = (TAPS - 1) // DEC
CHUNK = 640
CHUNK_OUT = CHUNK // DEC
VMEM_LIMIT = 48 * 1024 * 1024


def forward_table():
    phases = 2.0 * math.pi / NFFT * (np.outer(np.arange(S // 2), np.arange(BINS)) % NFFT)
    return np.concatenate([np.cos(phases), -np.sin(phases)], axis=1).astype(np.float32)


def split_table(table):
    high = table.astype(jnp.bfloat16)
    low = (table - high.astype(np.float32)).astype(jnp.bfloat16)
    return high, low


def band_table():
    bins = np.arange(3 * LANES)[:, None] - LANES
    return (np.abs(bins - np.arange(LANES)[None, :]) <= HALF).astype(jnp.bfloat16)


def lag_table():
    bins = np.arange(BINS)[:, None]
    shift = np.arange(LAGS)[None, :] - LAGS // 2
    phases = 2.0 * math.pi / NFFT * (bins * shift % NFFT)
    weight = np.where(bins == 0, 0.5, 1.0) / math.sqrt(BINS)
    table = np.concatenate([weight * np.cos(phases), -weight * np.sin(phases)], axis=0)
    return table.astype(np.float32).astype(jnp.bfloat16)


def split(value):
    high = value.astype(jnp.bfloat16)
    return high, (value - high.astype(jnp.float32)).astype(jnp.bfloat16)


def dot(a, b):
    return jnp.dot(a, b, preferred_element_type=jnp.float32)


def column(row):
    count = row.shape[1]
    at = [lax.broadcasted_iota(jnp.int32, (count, count), axis) for axis in range(2)]
    rows = jnp.broadcast_to(row, (count, count))
    return jnp.sum(jnp.where(at[0] == at[1], rows, 0.0), axis=1, keepdims=True)


def start_copies(pairs, sems):
    copies = [
        pltpu.make_async_copy(source, target, sems.at[at])
        for at, (source, target) in enumerate(pairs)
    ]
    for copy in copies:
        copy.start()
    return copies


def decimate_kernel(
    paired, raw_hbm, taps_hbm, alive_hbm, picks_hbm, out_ref, pieces_hbm,
    raw_ref, taps_ref, alive_ref, picks_ref, source_ref, pieces_ref, sems,
):
    rows = raw_hbm.shape[0]
    chunks = raw_hbm.shape[1] // CHUNK
    slots = picks_ref.shape[1]
    per_tile = LANES // CHUNK_OUT
    tiles = -(-chunks // per_tile)
    pairs = [(taps_hbm, taps_ref), (picks_hbm, picks_ref), (alive_hbm, alive_ref)]
    for at in range(0, rows, SUBLANES):
        span = slice(at, at + SUBLANES)
        pairs.append((raw_hbm.at[span], raw_ref.at[span]))
    copies = start_copies(pairs, sems)
    source_ref[...] = jnp.zeros_like(source_ref)
    copies[0].wait()
    taps = jnp.broadcast_to(taps_ref[...], (SUBLANES, TAPS))
    eight = jnp.concatenate([taps, jnp.zeros((SUBLANES, CHUNK - TAPS), jnp.float32)], axis=1)
    for _ in range(2):
        eight = pltpu.roll(eight, 0, 1, stride=DEC // 2, stride_axis=0)
    wrapped = jnp.concatenate(
        [eight]
        + [pltpu.roll(eight, DEC * at, 1) for at in range(SUBLANES, CHUNK_OUT, SUBLANES)],
        axis=0,
    )
    lane = lax.broadcasted_iota(jnp.int32, (CHUNK_OUT, CHUNK), 1)
    row = lax.broadcasted_iota(jnp.int32, (CHUNK_OUT, CHUNK), 0)
    main = jnp.where(lane >= DEC * row, wrapped, 0.0)
    rim = wrapped - main
    weights = jnp.concatenate(split(jnp.concatenate([main, rim], axis=0).T), axis=1)

    def filtered(stacked):
        count = stacked.shape[0]
        high, low = split(stacked)
        both = dot(jnp.concatenate([high, low], axis=0), weights)
        both = both[:count] + both[count:]
        both = both + pltpu.roll(both, LANES // 2, 1)
        lane = lax.broadcasted_iota(jnp.int32, both.shape, 1)
        return jnp.where((lane < CHUNK_OUT) | (lane >= LANES - EDGE), both, 0.0)

    for copy in copies[1:]:
        copy.wait()
    for slot in range(slots):
        pick = picks_ref[0, slot]
        alive = alive_ref[0, pick].astype(jnp.float32)
        for j in range(chunks):
            at = SUBLANES * slot + j
            span = slice(CHUNK * j, CHUNK * (j + 1))
            source_ref[at : at + 1, :] = raw_ref[pl.ds(pick, 1), span] * alive
    sources = filtered(source_ref[...])
    lane = lax.broadcasted_iota(jnp.int32, (SUBLANES, LANES), 1)
    row = lax.broadcasted_iota(jnp.int32, (SUBLANES, LANES), 0)
    leads = row % per_tile == 0
    wraps = lane >= LANES - EDGE
    piece = []
    rims = jnp.zeros((1, LANES), jnp.float32)
    for slot in range(slots):
        source = sources[SUBLANES * slot : SUBLANES * (slot + 1)]
        placed = source
        for step in range(1, per_tile):
            rolled = pltpu.roll(source, CHUNK_OUT * step, 1)
            placed = jnp.where(row % per_tile == step, rolled, placed)
        own = jnp.where(leads & wraps, 0.0, placed)
        rim = placed - own
        for tile in range(tiles):
            first = per_tile * tile
            inside = jnp.where((row >= first) & (row < first + per_tile), own, 0.0)
            before = jnp.where(row == first + per_tile, rim, 0.0)
            piece.append(jnp.sum(inside + before, axis=0, keepdims=True))
        rims = rims + pltpu.roll(rim[:1], LANES - EDGE * slot if slot else 0, 1)
    piece.append(rims)
    size = len(piece)
    spread = [jnp.broadcast_to(value, (SUBLANES, LANES)) for value in piece]
    eight = []
    for group in range(size):
        place = (row + SUBLANES * group) % size
        total = spread[0]
        for at in range(1, size):
            total = jnp.where(place == at, spread[at], total)
        eight.append(total)
    eight = jnp.concatenate(eight, axis=0)
    for at in range(0, pieces_ref.shape[0], SUBLANES * size):
        pieces_ref[at : at + SUBLANES * size, :] = eight
    sending = pltpu.make_async_copy(pieces_ref, pieces_hbm, sems.at[0])
    sending.start()

    @pl.when(lax.axis_index("blk") >= 0)
    def _():
        result = filtered(
            jnp.concatenate(
                [raw_ref[:, CHUNK * j : CHUNK * (j + 1)] for j in range(chunks)], axis=0
            )
        )
        part = [result[rows * j : rows * (j + 1)] for j in range(chunks)]
        is_main = lax.broadcasted_iota(jnp.int32, (rows, LANES), 1) < LANES // 2
        values = []
        for first in range(0, chunks, per_tile):
            total = jnp.where(is_main, part[first], 0.0)
            for step in range(1, min(per_tile, chunks - first)):
                total = total + pltpu.roll(part[first + step], CHUNK_OUT * step, 1)
            if first + per_tile < chunks:
                total = total + jnp.where(is_main, 0.0, part[first + per_tile])
            values.append(total)
        rim = jnp.where(is_main, 0.0, part[0])
        if paired:
            packed = rim[:SUBLANES]
            for at in range(1, rows // SUBLANES):
                group = rim[SUBLANES * at : SUBLANES * (at + 1)]
                packed = packed + pltpu.roll(group, LANES - EDGE * at, 1)
            for at, value in enumerate(values):
                out_ref[rows * at : rows * (at + 1), :] = value
            out_ref[rows * tiles :, :] = packed
        else:
            for at, value in enumerate(values + [rim]):
                out_ref[:, LANES * at : LANES * (at + 1)] = value

    sending.wait()


def unpack(packed, rows):
    tiles = [packed[at : at + rows] for at in range(0, packed.shape[0] - SUBLANES, rows)]
    rims = packed[packed.shape[0] - SUBLANES :]
    rim = jnp.concatenate(
        [rims]
        + [pltpu.roll(rims, EDGE * at, 1) for at in range(1, rows // SUBLANES)],
        axis=0,
    )
    lane = lax.broadcasted_iota(jnp.int32, rim.shape, 1)
    return tiles + [jnp.where(lane >= LANES - EDGE, rim, 0.0)]


def transform(early, late, table_hi, table_lo):
    rows = early.shape[0]
    high, low = split(jnp.concatenate([early, late], axis=0))
    first = dot(jnp.concatenate([high, low], axis=0), table_hi)
    both = first[: 2 * rows] + first[2 * rows :] + dot(high, table_lo)
    quarter = lax.broadcasted_iota(jnp.int32, (1, BINS), 1) & 3
    cosine = jnp.where(quarter == 0, 1.0, 0.0) - jnp.where(quarter == 2, 1.0, 0.0)
    sine = jnp.where(quarter == 1, 1.0, 0.0) - jnp.where(quarter == 3, 1.0, 0.0)
    early_re, early_im = both[:rows, :BINS], both[:rows, BINS:]
    late_re, late_im = both[rows:, :BINS], both[rows:, BINS:]
    return (
        early_re + cosine * late_re + sine * late_im,
        early_im + cosine * late_im - sine * late_re,
    )


def whitening(real_part, imag_part, band):
    rows = real_part.shape[0]
    tiles = BINS // LANES
    stacked = []
    for part in split(real_part * real_part + imag_part * imag_part):
        zero = jnp.zeros((rows, LANES), part.dtype)
        wide = jnp.concatenate([zero, part, zero], axis=1)
        stacked += [wide[:, LANES * tile : LANES * (tile + 3)] for tile in range(tiles)]
    banded = dot(jnp.concatenate(stacked, axis=0), band)
    step = rows * tiles
    summed = banded[:step] + banded[step:]
    total = jnp.concatenate(
        [summed[rows * tile : rows * (tile + 1)] for tile in range(tiles)], axis=1
    )
    bins = lax.broadcasted_iota(jnp.int32, (1, BINS), 1)
    count = jnp.minimum(bins + HALF, BINS - 1) - jnp.maximum(bins - HALF, 0) + 1
    return lax.rsqrt(total * (1.0 / count.astype(jnp.float32)) + 1e-06)


def prepare_kernel(
    _, alive_hbm, picks_hbm, fwd_hi_hbm, fwd_lo_hbm, band_hbm, lag_hbm,
    hi_ref, lo_ref, band_ref, lag_ref, alive_out, picks_out, alive_ref, picks_ref, sems,
):
    copies = start_copies(
        [
            (alive_hbm, alive_ref),
            (picks_hbm, picks_ref),
            (fwd_hi_hbm, hi_ref),
            (fwd_lo_hbm, lo_ref),
            (band_hbm, band_ref),
            (lag_hbm, lag_ref),
        ],
        sems,
    )
    for copy in copies[:2]:
        copy.wait()
    rows = alive_out.shape[0]
    alive_out[...] = jnp.broadcast_to(
        column(alive_ref[...].astype(jnp.float32)), (rows, LANES)
    )
    channel = lax.broadcasted_iota(jnp.int32, (rows, LANES), 0)
    for slot in range(picks_ref.shape[1]):
        pick = jnp.broadcast_to(picks_ref[:, slot : slot + 1], (rows, LANES))
        picks_out[slot] = jnp.where(channel == pick, 1.0, 0.0)
    for copy in copies[2:]:
        copy.wait()


def spectra_kernel(series_ref, hi_ref, lo_ref, band_ref, alive_ref, *refs):
    spectra_ref = refs[-1]
    rows = alive_ref.shape[0]
    half = S // 2
    if len(refs) > 1:
        mine, other = [unpack(ref[...], rows) for ref in (series_ref, refs[0])]
        first = lax.axis_index("src") == 0
        early = [jnp.where(first, a, b) for a, b in zip(mine, other)]
        late = [jnp.where(first, b, a) for a, b in zip(mine, other)]
        early[-2] = early[-2] + late[-1]
        early, late = [jnp.concatenate(tiles[:-1], axis=1) for tiles in (early, late)]
    else:
        early, late = series_ref[:, :half], series_ref[:, half:]
    real_part, imag_part = transform(early, late, hi_ref[...], lo_ref[...])
    factor = alive_ref[:, :1] * whitening(real_part, imag_part, band_ref[...])
    spectra_ref[:, :BINS] = real_part * factor
    spectra_ref[:, BINS:] = imag_part * factor


def part_bounds(total):
    ends = [3 * total // 8, 3 * total // 4, total]
    return [(a, b) for a, b in zip([0] + ends, ends) if b > a]


def correlate_kernel(
    slots, spectra_ref, pieces_ref, picks_ref, hi_ref, lo_ref, band_ref, lag_ref, out_hbm,
    series_ref, rims_ref, source_ref, cross_ref, out_ref, sems,
):
    rows = spectra_ref.shape[0]
    group = out_ref.shape[0] // slots
    half = BINS // LANES
    own = lax.axis_index("blk")
    base = lax.axis_index("src") * group
    tiles = S // 2 // LANES

    for slot in range(slots):
        for block in range(group):
            row = slice(slot * group + block, slot * group + block + 1)
            step = pieces_ref.shape[0] // 8
            at = pieces_ref.shape[0] - 1 - 2 * (base + block) + ((base + block) & (step - 1))
            after = at - step
            for tile in range(tiles):
                span = slice(LANES * (slot * tiles + tile), LANES * (slot * tiles + tile + 1))
                early = slice(LANES * tile, LANES * (tile + 1))
                late = slice(S // 2 + LANES * tile, S // 2 + LANES * (tile + 1))
                series_ref[row, early] = pieces_ref[at, :, span]
                series_ref[row, late] = pieces_ref[after, :, span]
            rims_ref[row, :] = pieces_ref[after, :, LANES * slots * tiles :]
    rims = jnp.concatenate(
        [
            pltpu.roll(rims_ref[slot * group : (slot + 1) * group, :], EDGE * slot, 1)
            for slot in range(slots)
        ],
        axis=0,
    )
    lane = lax.broadcasted_iota(jnp.int32, rims.shape, 1)
    seam = slice(S // 2 - LANES, S // 2)
    series_ref[:, seam] = series_ref[:, seam] + jnp.where(lane >= LANES - EDGE, rims, 0.0)
    early, late = series_ref[:, : S // 2], series_ref[:, S // 2 :]
    real_part, imag_part = transform(early, late, hi_ref[...], lo_ref[...])
    factor = whitening(real_part, imag_part, band_ref[...])
    source_ref[:, :BINS] = real_part * factor
    source_ref[:, BINS:] = imag_part * factor
    copies = []
    for part, (first, last) in enumerate(part_bounds(group * slots)):
        per_part = last - first
        for tile in range(half):
            re = slice(LANES * tile, LANES * (tile + 1))
            im = slice(BINS + LANES * tile, BINS + LANES * (tile + 1))
            rec_re, rec_im = spectra_ref[:, re], spectra_ref[:, im]
            for source in range(first, first + per_part):
                block, slot = divmod(source, slots)
                at = slot * group + block
                src_re, src_im = source_ref[at : at + 1, re], source_ref[at : at + 1, im]
                where = slice(rows * source, rows * (source + 1))
                cross_ref[where, re] = (src_re * rec_re + src_im * rec_im).astype(jnp.bfloat16)
                cross_ref[where, im] = (src_re * rec_im - src_im * rec_re).astype(jnp.bfloat16)
        lagged = dot(cross_ref[rows * first : rows * (first + per_part), :], lag_ref[...])
        for source in range(first, first + per_part):
            block, slot = divmod(source, slots)
            keep = 1.0 - jnp.where(own == base + block, 1.0, 0.0) * picks_ref[slot]
            at = source - first
            kept = lagged[rows * at : rows * (at + 1)] * jnp.concatenate(
                [keep] * (LAGS // LANES), axis=1
            )
            out_ref[source] = kept.astype(jnp.bfloat16)
        span = pl.ds(first, per_part)
        copies.append(pltpu.make_async_copy(out_ref.at[span], out_hbm.at[span], sems.at[part]))
        copies[-1].start()
    for copy in copies:
        copy.wait()


HBM = pl.BlockSpec(memory_space=pltpu.HBM)
VMEM = pl.BlockSpec(memory_space=pltpu.VMEM)
PARAMS = pltpu.CompilerParams(vmem_limit_bytes=VMEM_LIMIT)


def in_hbm(*arrays):
    return [pltpu.with_memory_space_constraint(array, pltpu.HBM) for array in arrays]


def shaped(*shape, dtype=jnp.float32):
    return jax.ShapeDtypeStruct(shape, dtype)


def exchange_order(count):
    quarter = count // 4
    places = sorted(range(quarter), key=lambda place: (place & 1, place))
    return [start + at for start in range(0, count, quarter) for at in places][::-1]


def local(raw_records, fir_taps, alive_mask, source_index):
    src_count = lax.axis_size("src")
    blk_count = lax.axis_size("blk")
    rows, raw_count = raw_records.shape
    slots = source_index.shape[1]
    group = blk_count // src_count
    out_count = raw_count // DEC
    width = -(-out_count // LANES) * LANES + LANES
    chunks = raw_count // CHUNK
    paired = src_count == 2 and 2 * out_count == S
    bf16 = jnp.bfloat16
    forward_hi, forward_lo = split_table(forward_table())
    alive_row = alive_mask.reshape(1, rows)

    with jax.named_scope("decimate"):
        device_count = blk_count * src_count
        main = slots * (width - LANES)
        decimated, pieces = pl.pallas_call(
            lambda *refs: decimate_kernel(paired, *refs),
            out_shape=(
                shaped(rows * (S // 2 // LANES) + SUBLANES, LANES)
                if paired
                else shaped(rows, width),
                shaped(device_count * (main // LANES + 1), LANES),
            ),
            in_specs=[HBM] * 4,
            out_specs=(VMEM, HBM),
            scratch_shapes=[
                pltpu.VMEM((rows, raw_count), jnp.float32),
                pltpu.VMEM((1, TAPS), jnp.float32),
                pltpu.SMEM((1, rows), jnp.int32),
                pltpu.SMEM((1, slots), jnp.int32),
                pltpu.VMEM((SUBLANES * slots, CHUNK), jnp.float32),
                pltpu.VMEM((device_count * (main // LANES + 1), LANES), jnp.float32),
                pltpu.SemaphoreType.DMA((rows // SUBLANES + 3,)),
            ],
            compiler_params=PARAMS,
        )(*in_hbm(raw_records, fir_taps.reshape(1, TAPS), alive_row, source_index))

    def whole(shards):
        rims = jnp.pad(shards[1:, :, width - EDGE :], ((0, 1), (0, 0), (out_count - EDGE, 0)))
        series = shards[:, :, :out_count] + rims
        return series.transpose(1, 0, 2).reshape(shards.shape[1], S)

    with jax.named_scope("gather_sources"):
        gathered = lax.all_to_all(
            pieces.reshape(device_count, 1, main + LANES),
            ("blk", "src"),
            split_axis=0,
            concat_axis=0,
            tiled=True,
            axis_index_groups=[exchange_order(device_count)],
        )
        if not paired:
            gathered = gathered[np.argsort(exchange_order(device_count))]
            shards = gathered.reshape(blk_count, src_count, main + LANES)
            shards = shards.transpose(1, 0, 2)
            rims = [shards[:, :, main + LANES - EDGE * (slot + 1) :] for slot in range(slots)]
            rims = jnp.stack([rim[:, :, :EDGE] for rim in rims], axis=2)
            rims = jnp.pad(rims, ((0, 0), (0, 0), (0, 0), (LANES - EDGE, 0)))
            series = shards[:, :, :main].reshape(src_count, blk_count, slots, width - LANES)
            series = jnp.concatenate([series, rims], axis=3)
            series = whole(series.reshape(src_count, blk_count * slots, width))
            series = series.reshape(blk_count, slots, 2, S // 2).transpose(0, 2, 1, 3)
            series = series.reshape(blk_count * 2, 1, slots * S // 2)
            gathered = jnp.pad(series, ((0, 0), (0, 0), (0, LANES)))
            gathered = gathered[np.array(exchange_order(blk_count * 2))]

    with jax.named_scope("prepare"):
        out_shape = (
            shaped(S // 2, NFFT, dtype=bf16),
            shaped(S // 2, NFFT, dtype=bf16),
            shaped(3 * LANES, LANES, dtype=bf16),
            shaped(NFFT, LAGS, dtype=bf16),
            shaped(rows, LANES),
            shaped(slots, rows, LANES),
        )
        table_hi, table_lo, band, lag, alive, picks = pl.pallas_call(
            prepare_kernel,
            out_shape=out_shape,
            in_specs=[VMEM] + [HBM] * 6,
            out_specs=(VMEM,) * len(out_shape),
            scratch_shapes=[
                pltpu.VMEM((1, rows), jnp.int32),
                pltpu.VMEM((1, slots), jnp.int32),
                pltpu.SemaphoreType.DMA((6,)),
            ],
            compiler_params=PARAMS,
            cost_estimate=pl.CostEstimate(
                flops=0, bytes_accessed=4 * S * NFFT, transcendentals=0
            ),
        )(
            decimated,
            *in_hbm(
                alive_row,
                source_index,
                jnp.asarray(forward_hi),
                jnp.asarray(forward_lo),
                jnp.asarray(band_table()),
                jnp.asarray(lag_table()),
            ),
        )

    with jax.named_scope("regroup"):
        if paired:
            series = [decimated]
            other = [lax.ppermute(decimated, "src", [(0, 1), (1, 0)])]
        else:
            series = [whole(lax.all_gather(decimated, "src", axis=0))]
            other = []

    with jax.named_scope("spectra"):
        operands = series + [table_hi, table_lo, band, alive] + other
        spectra = pl.pallas_call(
            spectra_kernel,
            out_shape=shaped(rows, NFFT),
            in_specs=[VMEM] * len(operands),
            out_specs=VMEM,
            compiler_params=PARAMS,
        )(*operands)

    with jax.named_scope("correlate"):
        total = group * slots
        return pl.pallas_call(
            lambda *refs: correlate_kernel(slots, *refs),
            out_shape=shaped(total, rows, LAGS, dtype=bf16),
            in_specs=[VMEM] * 7,
            out_specs=HBM,
            scratch_shapes=[
                pltpu.VMEM((total, S), jnp.float32),
                pltpu.VMEM((total, LANES), jnp.float32),
                pltpu.VMEM((total, NFFT), jnp.float32),
                pltpu.VMEM((total * rows, NFFT), bf16),
                pltpu.VMEM((total, rows, LAGS), bf16),
                pltpu.SemaphoreType.DMA((PARTS,)),
            ],
            compiler_params=PARAMS,
        )(spectra, gathered, picks, table_hi, table_lo, band, lag)


def solution(mesh):
    in_specs = (P("blk", "src"), P(), P("blk"), P("blk", None))
    out_specs = P("src", "blk", None)
    return jax.shard_map(local, mesh=mesh, in_specs=in_specs, out_specs=out_specs, check_vma=False)
```

```python
import math

import jax
import jax.numpy as jnp
import numpy as np
from jax import lax
from jax.experimental import pallas as pl
from jax.experimental.pallas import tpu as pltpu
from jax.sharding import PartitionSpec as P

S = 512
NFFT = 1024
BINS = NFFT // 2
LAGS = 512
TAPS = 64
DEC = 20
HALF = 64
LANES = 128
SUBLANES = 8
PARTS = 3
EDGE = (TAPS - 1) // DEC
CHUNK = 640
CHUNK_OUT = CHUNK // DEC
VMEM_LIMIT = 48 * 1024 * 1024


def forward_table():
    phases = 2.0 * math.pi / NFFT * (np.outer(np.arange(S // 2), np.arange(BINS)) % NFFT)
    return np.concatenate([np.cos(phases), -np.sin(phases)], axis=1).astype(np.float32)


def split_table(table):
    high = table.astype(jnp.bfloat16)
    low = (table - high.astype(np.float32)).astype(jnp.bfloat16)
    return high, low


def band_table():
    bins = np.arange(3 * LANES)[:, None] - LANES
    return (np.abs(bins - np.arange(LANES)[None, :]) <= HALF).astype(jnp.bfloat16)


def lag_table():
    bins = np.arange(BINS)[:, None]
    shift = np.arange(LAGS)[None, :] - LAGS // 2
    phases = 2.0 * math.pi / NFFT * (bins * shift % NFFT)
    weight = np.where(bins == 0, 0.5, 1.0) / math.sqrt(BINS)
    table = np.concatenate([weight * np.cos(phases), -weight * np.sin(phases)], axis=0)
    return table.astype(np.float32).astype(jnp.bfloat16)


def split(value):
    high = value.astype(jnp.bfloat16)
    return high, (value - high.astype(jnp.float32)).astype(jnp.bfloat16)


def dot(a, b):
    return jnp.dot(a, b, preferred_element_type=jnp.float32)


def column(row):
    count = row.shape[1]
    at = [lax.broadcasted_iota(jnp.int32, (count, count), axis) for axis in range(2)]
    rows = jnp.broadcast_to(row, (count, count))
    return jnp.sum(jnp.where(at[0] == at[1], rows, 0.0), axis=1, keepdims=True)


def start_copies(pairs, sems):
    copies = [
        pltpu.make_async_copy(source, target, sems.at[at])
        for at, (source, target) in enumerate(pairs)
    ]
    for copy in copies:
        copy.start()
    return copies


def decimate_kernel(
    paired, raw_hbm, taps_hbm, alive_hbm, picks_hbm, out_ref, pieces_hbm,
    raw_ref, taps_ref, alive_ref, picks_ref, source_ref, pieces_ref, sems,
):
    rows = raw_hbm.shape[0]
    chunks = raw_hbm.shape[1] // CHUNK
    slots = picks_ref.shape[1]
    per_tile = LANES // CHUNK_OUT
    tiles = -(-chunks // per_tile)
    pairs = [(taps_hbm, taps_ref)]
    for at in range(0, rows, SUBLANES):
        span = slice(at, at + SUBLANES)
        pairs.append((raw_hbm.at[span], raw_ref.at[span]))
    pairs += [(picks_hbm, picks_ref), (alive_hbm, alive_ref)]
    copies = start_copies(pairs, sems)
    source_ref[...] = jnp.zeros_like(source_ref)
    copies[0].wait()
    taps = jnp.broadcast_to(taps_ref[...], (SUBLANES, TAPS))
    eight = jnp.concatenate([taps, jnp.zeros((SUBLANES, CHUNK - TAPS), jnp.float32)], axis=1)
    for _ in range(2):
        eight = pltpu.roll(eight, 0, 1, stride=DEC // 2, stride_axis=0)
    wrapped = jnp.concatenate(
        [eight]
        + [pltpu.roll(eight, DEC * at, 1) for at in range(SUBLANES, CHUNK_OUT, SUBLANES)],
        axis=0,
    )
    lane = lax.broadcasted_iota(jnp.int32, (CHUNK_OUT, CHUNK), 1)
    row = lax.broadcasted_iota(jnp.int32, (CHUNK_OUT, CHUNK), 0)
    main = jnp.where(lane >= DEC * row, wrapped, 0.0)
    rim = wrapped - main
    weights = jnp.concatenate(split(jnp.concatenate([main, rim], axis=0).T), axis=1)

    def filtered(stacked):
        count = stacked.shape[0]
        high, low = split(stacked)
        both = dot(jnp.concatenate([high, low], axis=0), weights)
        both = both[:count] + both[count:]
        both = both + pltpu.roll(both, LANES // 2, 1)
        lane = lax.broadcasted_iota(jnp.int32, both.shape, 1)
        return jnp.where((lane < CHUNK_OUT) | (lane >= LANES - EDGE), both, 0.0)

    for copy in copies[1:]:
        copy.wait()
    for slot in range(slots):
        pick = picks_ref[0, slot]
        alive = alive_ref[0, pick].astype(jnp.float32)
        for j in range(chunks):
            at = SUBLANES * slot + j
            span = slice(CHUNK * j, CHUNK * (j + 1))
            source_ref[at : at + 1, :] = raw_ref[pl.ds(pick, 1), span] * alive
    sources = filtered(source_ref[...])
    lane = lax.broadcasted_iota(jnp.int32, (SUBLANES, LANES), 1)
    row = lax.broadcasted_iota(jnp.int32, (SUBLANES, LANES), 0)
    leads = row % per_tile == 0
    wraps = lane >= LANES - EDGE
    piece = []
    rims = jnp.zeros((1, LANES), jnp.float32)
    for slot in range(slots):
        source = sources[SUBLANES * slot : SUBLANES * (slot + 1)]
        placed = source
        for step in range(1, per_tile):
            rolled = pltpu.roll(source, CHUNK_OUT * step, 1)
            placed = jnp.where(row % per_tile == step, rolled, placed)
        own = jnp.where(leads & wraps, 0.0, placed)
        rim = placed - own
        for tile in range(tiles):
            first = per_tile * tile
            inside = jnp.where((row >= first) & (row < first + per_tile), own, 0.0)
            before = jnp.where(row == first + per_tile, rim, 0.0)
            piece.append(jnp.sum(inside + before, axis=0, keepdims=True))
        rims = rims + pltpu.roll(rim[:1], LANES - EDGE * slot if slot else 0, 1)
    piece.append(rims)
    size = len(piece)
    spread = [jnp.broadcast_to(value, (SUBLANES, LANES)) for value in piece]
    eight = []
    for group in range(size):
        place = (row + SUBLANES * group) % size
        total = spread[0]
        for at in range(1, size):
            total = jnp.where(place == at, spread[at], total)
        eight.append(total)
    eight = jnp.concatenate(eight, axis=0)
    for at in range(0, pieces_ref.shape[0], SUBLANES * size):
        pieces_ref[at : at + SUBLANES * size, :] = eight
    sending = pltpu.make_async_copy(pieces_ref, pieces_hbm, sems.at[0])
    sending.start()

    @pl.when(lax.axis_index("blk") >= 0)
    def _():
        result = filtered(
            jnp.concatenate(
                [raw_ref[:, CHUNK * j : CHUNK * (j + 1)] for j in range(chunks)], axis=0
            )
        )
        part = [result[rows * j : rows * (j + 1)] for j in range(chunks)]
        is_main = lax.broadcasted_iota(jnp.int32, (rows, LANES), 1) < LANES // 2
        values = []
        for first in range(0, chunks, per_tile):
            total = jnp.where(is_main, part[first], 0.0)
            for step in range(1, min(per_tile, chunks - first)):
                total = total + pltpu.roll(part[first + step], CHUNK_OUT * step, 1)
            if first + per_tile < chunks:
                total = total + jnp.where(is_main, 0.0, part[first + per_tile])
            values.append(total)
        rim = jnp.where(is_main, 0.0, part[0])
        if paired:
            packed = rim[:SUBLANES]
            for at in range(1, rows // SUBLANES):
                group = rim[SUBLANES * at : SUBLANES * (at + 1)]
                packed = packed + pltpu.roll(group, LANES - EDGE * at, 1)
            for at, value in enumerate(values):
                out_ref[rows * at : rows * (at + 1), :] = value
            out_ref[rows * tiles :, :] = packed
        else:
            for at, value in enumerate(values + [rim]):
                out_ref[:, LANES * at : LANES * (at + 1)] = value

    sending.wait()


def unpack(packed, rows):
    tiles = [packed[at : at + rows] for at in range(0, packed.shape[0] - SUBLANES, rows)]
    rims = packed[packed.shape[0] - SUBLANES :]
    rim = jnp.concatenate(
        [rims]
        + [pltpu.roll(rims, EDGE * at, 1) for at in range(1, rows // SUBLANES)],
        axis=0,
    )
    lane = lax.broadcasted_iota(jnp.int32, rim.shape, 1)
    return tiles + [jnp.where(lane >= LANES - EDGE, rim, 0.0)]


def transform(early, late, table_hi, table_lo):
    rows = early.shape[0]
    high, low = split(jnp.concatenate([early, late], axis=0))
    first = dot(jnp.concatenate([high, low], axis=0), table_hi)
    both = first[: 2 * rows] + first[2 * rows :] + dot(high, table_lo)
    quarter = lax.broadcasted_iota(jnp.int32, (1, BINS), 1) & 3
    cosine = jnp.where(quarter == 0, 1.0, 0.0) - jnp.where(quarter == 2, 1.0, 0.0)
    sine = jnp.where(quarter == 1, 1.0, 0.0) - jnp.where(quarter == 3, 1.0, 0.0)
    early_re, early_im = both[:rows, :BINS], both[:rows, BINS:]
    late_re, late_im = both[rows:, :BINS], both[rows:, BINS:]
    return (
        early_re + cosine * late_re + sine * late_im,
        early_im + cosine * late_im - sine * late_re,
    )


def whitening(real_part, imag_part, band):
    rows = real_part.shape[0]
    tiles = BINS // LANES
    stacked = []
    for part in split(real_part * real_part + imag_part * imag_part):
        zero = jnp.zeros((rows, LANES), part.dtype)
        wide = jnp.concatenate([zero, part, zero], axis=1)
        stacked += [wide[:, LANES * tile : LANES * (tile + 3)] for tile in range(tiles)]
    banded = dot(jnp.concatenate(stacked, axis=0), band)
    step = rows * tiles
    summed = banded[:step] + banded[step:]
    total = jnp.concatenate(
        [summed[rows * tile : rows * (tile + 1)] for tile in range(tiles)], axis=1
    )
    bins = lax.broadcasted_iota(jnp.int32, (1, BINS), 1)
    count = jnp.minimum(bins + HALF, BINS - 1) - jnp.maximum(bins - HALF, 0) + 1
    return lax.rsqrt(total * (1.0 / count.astype(jnp.float32)) + 1e-06)


def prepare_kernel(
    _, alive_hbm, picks_hbm, fwd_hi_hbm, fwd_lo_hbm, band_hbm, lag_hbm,
    hi_ref, lo_ref, band_ref, lag_ref, alive_out, picks_out, alive_ref, picks_ref, sems,
):
    copies = start_copies(
        [
            (alive_hbm, alive_ref),
            (picks_hbm, picks_ref),
            (fwd_hi_hbm, hi_ref),
            (fwd_lo_hbm, lo_ref),
            (band_hbm, band_ref),
            (lag_hbm, lag_ref),
        ],
        sems,
    )
    for copy in copies[:2]:
        copy.wait()
    rows = alive_out.shape[0]
    alive_out[...] = jnp.broadcast_to(
        column(alive_ref[...].astype(jnp.float32)), (rows, LANES)
    )
    channel = lax.broadcasted_iota(jnp.int32, (rows, LANES), 0)
    for slot in range(picks_ref.shape[1]):
        pick = jnp.broadcast_to(picks_ref[:, slot : slot + 1], (rows, LANES))
        picks_out[slot] = jnp.where(channel == pick, 1.0, 0.0)
    for copy in copies[2:]:
        copy.wait()


def spectra_kernel(series_ref, hi_ref, lo_ref, band_ref, alive_ref, *refs):
    spectra_ref = refs[-1]
    rows = alive_ref.shape[0]
    half = S // 2
    if len(refs) > 1:
        mine, other = [unpack(ref[...], rows) for ref in (series_ref, refs[0])]
        first = lax.axis_index("src") == 0
        early = [jnp.where(first, a, b) for a, b in zip(mine, other)]
        late = [jnp.where(first, b, a) for a, b in zip(mine, other)]
        early[-2] = early[-2] + late[-1]
        early, late = [jnp.concatenate(tiles[:-1], axis=1) for tiles in (early, late)]
    else:
        early, late = series_ref[:, :half], series_ref[:, half:]
    real_part, imag_part = transform(early, late, hi_ref[...], lo_ref[...])
    factor = alive_ref[:, :1] * whitening(real_part, imag_part, band_ref[...])
    spectra_ref[:, :BINS] = real_part * factor
    spectra_ref[:, BINS:] = imag_part * factor


def part_bounds(total):
    ends = [3 * total // 8, 3 * total // 4, total]
    return [(a, b) for a, b in zip([0] + ends, ends) if b > a]


def correlate_kernel(
    slots, spectra_ref, pieces_ref, picks_ref, hi_ref, lo_ref, band_ref, lag_ref, out_hbm,
    series_ref, rims_ref, source_ref, difference_ref, sum_ref, cross_ref, out_ref, sems,
):
    rows = spectra_ref.shape[0]
    group = out_ref.shape[0] // slots
    half = BINS // LANES
    own = lax.axis_index("blk")
    base = lax.axis_index("src") * group
    tiles = S // 2 // LANES

    for slot in range(slots):
        for block in range(group):
            row = slice(slot * group + block, slot * group + block + 1)
            at = pieces_ref.shape[0] - 1 - 2 * (base + block)
            for tile in range(tiles):
                span = slice(LANES * (slot * tiles + tile), LANES * (slot * tiles + tile + 1))
                early = slice(LANES * tile, LANES * (tile + 1))
                late = slice(S // 2 + LANES * tile, S // 2 + LANES * (tile + 1))
                series_ref[row, early] = pieces_ref[at, :, span]
                series_ref[row, late] = pieces_ref[at - 1, :, span]
            rims_ref[row, :] = pieces_ref[at - 1, :, LANES * slots * tiles :]
    rims = jnp.concatenate(
        [
            pltpu.roll(rims_ref[slot * group : (slot + 1) * group, :], EDGE * slot, 1)
            for slot in range(slots)
        ],
        axis=0,
    )
    lane = lax.broadcasted_iota(jnp.int32, rims.shape, 1)
    seam = slice(S // 2 - LANES, S // 2)
    series_ref[:, seam] = series_ref[:, seam] + jnp.where(lane >= LANES - EDGE, rims, 0.0)
    early, late = series_ref[:, : S // 2], series_ref[:, S // 2 :]
    real_part, imag_part = transform(early, late, hi_ref[...], lo_ref[...])
    factor = whitening(real_part, imag_part, band_ref[...])
    real_part, imag_part = real_part * factor, imag_part * factor
    source_ref[...] = real_part
    difference_ref[...] = imag_part - real_part
    sum_ref[...] = imag_part + real_part
    copies = []
    for part, (first, last) in enumerate(part_bounds(group * slots)):
        per_part = last - first
        for tile in range(half):
            re = slice(LANES * tile, LANES * (tile + 1))
            im = slice(BINS + LANES * tile, BINS + LANES * (tile + 1))
            rec_re, rec_im = spectra_ref[:, re], spectra_ref[:, im]
            rec_sum = rec_re + rec_im
            for source in range(first, last):
                block, slot = divmod(source, slots)
                at = slot * group + block
                common = source_ref[at : at + 1, re] * rec_sum
                where = slice(rows * source, rows * (source + 1))
                cross_ref[where, re] = (common + difference_ref[at : at + 1, re] * rec_im).astype(
                    jnp.bfloat16
                )
                cross_ref[where, im] = (common - sum_ref[at : at + 1, re] * rec_re).astype(
                    jnp.bfloat16
                )
        lagged = dot(cross_ref[rows * first : rows * (first + per_part), :], lag_ref[...])
        for source in range(first, last):
            at = source - first
            out_ref[source] = lagged[rows * at : rows * (at + 1)].astype(jnp.bfloat16)
        for slot in range(slots):
            mine = (own - base) * slots + slot
            inside = (mine >= first) & (mine < last)
            at = jnp.where(inside, mine, first)
            keep = 1.0 - jnp.where(inside, 1.0, 0.0) * picks_ref[slot]
            keep = jnp.concatenate([keep] * (LAGS // LANES), axis=1)
            out_ref[at] = (out_ref[at].astype(jnp.float32) * keep).astype(jnp.bfloat16)
        span = pl.ds(first, per_part)
        copies.append(pltpu.make_async_copy(out_ref.at[span], out_hbm.at[span], sems.at[part]))
        copies[-1].start()
    for copy in copies:
        copy.wait()


HBM = pl.BlockSpec(memory_space=pltpu.HBM)
VMEM = pl.BlockSpec(memory_space=pltpu.VMEM)
PARAMS = pltpu.CompilerParams(vmem_limit_bytes=VMEM_LIMIT)


def in_hbm(*arrays):
    return [pltpu.with_memory_space_constraint(array, pltpu.HBM) for array in arrays]


def shaped(*shape, dtype=jnp.float32):
    return jax.ShapeDtypeStruct(shape, dtype)


def local(raw_records, fir_taps, alive_mask, source_index):
    src_count = lax.axis_size("src")
    blk_count = lax.axis_size("blk")
    rows, raw_count = raw_records.shape
    slots = source_index.shape[1]
    group = blk_count // src_count
    out_count = raw_count // DEC
    width = -(-out_count // LANES) * LANES + LANES
    chunks = raw_count // CHUNK
    paired = src_count == 2 and 2 * out_count == S
    bf16 = jnp.bfloat16
    forward_hi, forward_lo = split_table(forward_table())
    alive_row = alive_mask.reshape(1, rows)

    with jax.named_scope("decimate"):
        device_count = blk_count * src_count
        main = slots * (width - LANES)
        decimated, pieces = pl.pallas_call(
            lambda *refs: decimate_kernel(paired, *refs),
            out_shape=(
                shaped(rows * (S // 2 // LANES) + SUBLANES, LANES)
                if paired
                else shaped(rows, width),
                shaped(device_count * (main // LANES + 1), LANES),
            ),
            in_specs=[HBM] * 4,
            out_specs=(VMEM, HBM),
            scratch_shapes=[
                pltpu.VMEM((rows, raw_count), jnp.float32),
                pltpu.VMEM((1, TAPS), jnp.float32),
                pltpu.SMEM((1, rows), jnp.int32),
                pltpu.SMEM((1, slots), jnp.int32),
                pltpu.VMEM((SUBLANES * slots, CHUNK), jnp.float32),
                pltpu.VMEM((device_count * (main // LANES + 1), LANES), jnp.float32),
                pltpu.SemaphoreType.DMA((rows // SUBLANES + 3,)),
            ],
            compiler_params=PARAMS,
        )(*in_hbm(raw_records, fir_taps.reshape(1, TAPS), alive_row, source_index))

    def whole(shards):
        rims = jnp.pad(shards[1:, :, width - EDGE :], ((0, 1), (0, 0), (out_count - EDGE, 0)))
        series = shards[:, :, :out_count] + rims
        return series.transpose(1, 0, 2).reshape(shards.shape[1], S)

    with jax.named_scope("gather_sources"):
        gathered = lax.all_to_all(
            pieces.reshape(device_count, 1, main + LANES),
            ("blk", "src"),
            split_axis=0,
            concat_axis=0,
            tiled=True,
            axis_index_groups=[list(reversed(range(device_count)))],
        )
        if not paired:
            gathered = gathered[::-1]
            shards = gathered.reshape(blk_count, src_count, main + LANES)
            shards = shards.transpose(1, 0, 2)
            rims = [shards[:, :, main + LANES - EDGE * (slot + 1) :] for slot in range(slots)]
            rims = jnp.stack([rim[:, :, :EDGE] for rim in rims], axis=2)
            rims = jnp.pad(rims, ((0, 0), (0, 0), (0, 0), (LANES - EDGE, 0)))
            series = shards[:, :, :main].reshape(src_count, blk_count, slots, width - LANES)
            series = jnp.concatenate([series, rims], axis=3)
            series = whole(series.reshape(src_count, blk_count * slots, width))
            series = series.reshape(blk_count, slots, 2, S // 2).transpose(0, 2, 1, 3)
            series = series.reshape(blk_count * 2, 1, slots * S // 2)
            gathered = jnp.pad(series, ((0, 0), (0, 0), (0, LANES)))[::-1]

    with jax.named_scope("prepare"):
        out_shape = (
            shaped(S // 2, NFFT, dtype=bf16),
            shaped(S // 2, NFFT, dtype=bf16),
            shaped(3 * LANES, LANES, dtype=bf16),
            shaped(NFFT, LAGS, dtype=bf16),
            shaped(rows, LANES),
            shaped(slots, rows, LANES),
        )
        table_hi, table_lo, band, lag, alive, picks = pl.pallas_call(
            prepare_kernel,
            out_shape=out_shape,
            in_specs=[VMEM] + [HBM] * 6,
            out_specs=(VMEM,) * len(out_shape),
            scratch_shapes=[
                pltpu.VMEM((1, rows), jnp.int32),
                pltpu.VMEM((1, slots), jnp.int32),
                pltpu.SemaphoreType.DMA((6,)),
            ],
            compiler_params=PARAMS,
            cost_estimate=pl.CostEstimate(
                flops=0, bytes_accessed=4 * S * NFFT, transcendentals=0
            ),
        )(
            decimated,
            *in_hbm(
                alive_row,
                source_index,
                jnp.asarray(forward_hi),
                jnp.asarray(forward_lo),
                jnp.asarray(band_table()),
                jnp.asarray(lag_table()),
            ),
        )

    with jax.named_scope("regroup"):
        if paired:
            series = [decimated]
            other = [lax.ppermute(decimated, "src", [(0, 1), (1, 0)])]
        else:
            series = [whole(lax.all_gather(decimated, "src", axis=0))]
            other = []

    with jax.named_scope("spectra"):
        operands = series + [table_hi, table_lo, band, alive] + other
        spectra = pl.pallas_call(
            spectra_kernel,
            out_shape=shaped(rows, NFFT),
            in_specs=[VMEM] * len(operands),
            out_specs=VMEM,
            compiler_params=PARAMS,
        )(*operands)

    with jax.named_scope("correlate"):
        total = group * slots
        return pl.pallas_call(
            lambda *refs: correlate_kernel(slots, *refs),
            out_shape=shaped(total, rows, LAGS, dtype=bf16),
            in_specs=[VMEM] * 7,
            out_specs=HBM,
            scratch_shapes=[
                pltpu.VMEM((total, S), jnp.float32),
                pltpu.VMEM((total, LANES), jnp.float32),
                pltpu.VMEM((total, BINS), jnp.float32),
                pltpu.VMEM((total, BINS), jnp.float32),
                pltpu.VMEM((total, BINS), jnp.float32),
                pltpu.VMEM((total * rows, NFFT), bf16),
                pltpu.VMEM((total, rows, LAGS), bf16),
                pltpu.SemaphoreType.DMA((PARTS,)),
            ],
            compiler_params=PARAMS,
        )(spectra, gathered, picks, table_hi, table_lo, band, lag)


def solution(mesh):
    in_specs = (P("blk", "src"), P(), P("blk"), P("blk", None))
    out_specs = P("src", "blk", None)
    return jax.shard_map(local, mesh=mesh, in_specs=in_specs, out_specs=out_specs, check_vma=False)
```

```python
import math

import jax
import jax.numpy as jnp
import numpy as np
from jax import lax
from jax.experimental import pallas as pl
from jax.experimental.pallas import tpu as pltpu
from jax.sharding import PartitionSpec as P

S = 512
NFFT = 1024
BINS = NFFT // 2
LAGS = 512
TAPS = 64
DEC = 20
HALF = 64
LANES = 128
SUBLANES = 8
PARTS = 3
EDGE = (TAPS - 1) // DEC
CHUNK = 640
CHUNK_OUT = CHUNK // DEC
VMEM_LIMIT = 48 * 1024 * 1024


def forward_table():
    phases = 2.0 * math.pi / NFFT * (np.outer(np.arange(S // 2), np.arange(BINS)) % NFFT)
    return np.concatenate([np.cos(phases), -np.sin(phases)], axis=1).astype(np.float32)


def split_table(table):
    high = table.astype(jnp.bfloat16)
    low = (table - high.astype(np.float32)).astype(jnp.bfloat16)
    return high, low


def band_table():
    bins = np.arange(3 * LANES)[:, None] - LANES
    return (np.abs(bins - np.arange(LANES)[None, :]) <= HALF).astype(jnp.bfloat16)


def lag_table():
    bins = np.arange(BINS)[:, None]
    shift = np.arange(LAGS)[None, :] - LAGS // 2
    phases = 2.0 * math.pi / NFFT * (bins * shift % NFFT)
    weight = np.where(bins == 0, 0.5, 1.0) / math.sqrt(BINS)
    table = np.concatenate([weight * np.cos(phases), -weight * np.sin(phases)], axis=0)
    return table.astype(np.float32).astype(jnp.bfloat16)


def split(value):
    high = value.astype(jnp.bfloat16)
    return high, (value - high.astype(jnp.float32)).astype(jnp.bfloat16)


def dot(a, b):
    return jnp.dot(a, b, preferred_element_type=jnp.float32)


def column(row):
    count = row.shape[1]
    at = [lax.broadcasted_iota(jnp.int32, (count, count), axis) for axis in range(2)]
    rows = jnp.broadcast_to(row, (count, count))
    return jnp.sum(jnp.where(at[0] == at[1], rows, 0.0), axis=1, keepdims=True)


def start_copies(pairs, sems):
    copies = [
        pltpu.make_async_copy(source, target, sems.at[at])
        for at, (source, target) in enumerate(pairs)
    ]
    for copy in copies:
        copy.start()
    return copies


def decimate_kernel(
    paired, raw_hbm, taps_hbm, alive_hbm, picks_hbm, out_ref, pieces_hbm,
    raw_ref, taps_ref, alive_ref, picks_ref, source_ref, pieces_ref, sems,
):
    rows = raw_hbm.shape[0]
    chunks = raw_hbm.shape[1] // CHUNK
    slots = picks_ref.shape[1]
    per_tile = LANES // CHUNK_OUT
    tiles = -(-chunks // per_tile)
    pairs = [(taps_hbm, taps_ref), (picks_hbm, picks_ref), (alive_hbm, alive_ref)]
    for at in range(0, rows, SUBLANES):
        span = slice(at, at + SUBLANES)
        pairs.append((raw_hbm.at[span], raw_ref.at[span]))
    copies = start_copies(pairs, sems)
    source_ref[...] = jnp.zeros_like(source_ref)
    copies[0].wait()
    taps = jnp.broadcast_to(taps_ref[...], (SUBLANES, TAPS))
    eight = jnp.concatenate([taps, jnp.zeros((SUBLANES, CHUNK - TAPS), jnp.float32)], axis=1)
    for _ in range(2):
        eight = pltpu.roll(eight, 0, 1, stride=DEC // 2, stride_axis=0)
    wrapped = jnp.concatenate(
        [eight]
        + [pltpu.roll(eight, DEC * at, 1) for at in range(SUBLANES, CHUNK_OUT, SUBLANES)],
        axis=0,
    )
    lane = lax.broadcasted_iota(jnp.int32, (CHUNK_OUT, CHUNK), 1)
    row = lax.broadcasted_iota(jnp.int32, (CHUNK_OUT, CHUNK), 0)
    main = jnp.where(lane >= DEC * row, wrapped, 0.0)
    rim = wrapped - main
    weights = jnp.concatenate(split(jnp.concatenate([main, rim], axis=0).T), axis=1)

    def filtered(stacked):
        count = stacked.shape[0]
        high, low = split(stacked)
        both = dot(jnp.concatenate([high, low], axis=0), weights)
        both = both[:count] + both[count:]
        both = both + pltpu.roll(both, LANES // 2, 1)
        lane = lax.broadcasted_iota(jnp.int32, both.shape, 1)
        return jnp.where((lane < CHUNK_OUT) | (lane >= LANES - EDGE), both, 0.0)

    for copy in copies[1:]:
        copy.wait()
    for slot in range(slots):
        pick = picks_ref[0, slot]
        alive = alive_ref[0, pick].astype(jnp.float32)
        for j in range(chunks):
            at = SUBLANES * slot + j
            span = slice(CHUNK * j, CHUNK * (j + 1))
            source_ref[at : at + 1, :] = raw_ref[pl.ds(pick, 1), span] * alive
    sources = filtered(source_ref[...])
    lane = lax.broadcasted_iota(jnp.int32, (SUBLANES, LANES), 1)
    row = lax.broadcasted_iota(jnp.int32, (SUBLANES, LANES), 0)
    leads = row % per_tile == 0
    wraps = lane >= LANES - EDGE
    piece = []
    rims = jnp.zeros((1, LANES), jnp.float32)
    for slot in range(slots):
        source = sources[SUBLANES * slot : SUBLANES * (slot + 1)]
        placed = source
        for step in range(1, per_tile):
            rolled = pltpu.roll(source, CHUNK_OUT * step, 1)
            placed = jnp.where(row % per_tile == step, rolled, placed)
        own = jnp.where(leads & wraps, 0.0, placed)
        rim = placed - own
        for tile in range(tiles):
            first = per_tile * tile
            inside = jnp.where((row >= first) & (row < first + per_tile), own, 0.0)
            before = jnp.where(row == first + per_tile, rim, 0.0)
            piece.append(jnp.sum(inside + before, axis=0, keepdims=True))
        rims = rims + pltpu.roll(rim[:1], LANES - EDGE * slot if slot else 0, 1)
    piece.append(rims)
    size = len(piece)
    spread = [jnp.broadcast_to(value, (SUBLANES, LANES)) for value in piece]
    eight = []
    for group in range(size):
        place = (row + SUBLANES * group) % size
        total = spread[0]
        for at in range(1, size):
            total = jnp.where(place == at, spread[at], total)
        eight.append(total)
    eight = jnp.concatenate(eight, axis=0)
    for at in range(0, pieces_ref.shape[0], SUBLANES * size):
        pieces_ref[at : at + SUBLANES * size, :] = eight
    sending = pltpu.make_async_copy(pieces_ref, pieces_hbm, sems.at[0])
    sending.start()

    result = filtered(
        jnp.concatenate(
            [raw_ref[:, CHUNK * j : CHUNK * (j + 1)] for j in range(chunks)], axis=0
        )
    )
    part = [result[rows * j : rows * (j + 1)] for j in range(chunks)]
    is_main = lax.broadcasted_iota(jnp.int32, (rows, LANES), 1) < LANES // 2
    values = []
    for first in range(0, chunks, per_tile):
        total = jnp.where(is_main, part[first], 0.0)
        for step in range(1, min(per_tile, chunks - first)):
            total = total + pltpu.roll(part[first + step], CHUNK_OUT * step, 1)
        if first + per_tile < chunks:
            total = total + jnp.where(is_main, 0.0, part[first + per_tile])
        values.append(total)
    rim = jnp.where(is_main, 0.0, part[0])
    if paired:
        packed = rim[:SUBLANES]
        for at in range(1, rows // SUBLANES):
            group = rim[SUBLANES * at : SUBLANES * (at + 1)]
            packed = packed + pltpu.roll(group, LANES - EDGE * at, 1)
        for at, value in enumerate(values):
            out_ref[rows * at : rows * (at + 1), :] = value
        out_ref[rows * tiles :, :] = packed
    else:
        for at, value in enumerate(values + [rim]):
            out_ref[:, LANES * at : LANES * (at + 1)] = value
    sending.wait()


def unpack(packed, rows):
    tiles = [packed[at : at + rows] for at in range(0, packed.shape[0] - SUBLANES, rows)]
    rims = packed[packed.shape[0] - SUBLANES :]
    rim = jnp.concatenate(
        [rims]
        + [pltpu.roll(rims, EDGE * at, 1) for at in range(1, rows // SUBLANES)],
        axis=0,
    )
    lane = lax.broadcasted_iota(jnp.int32, rim.shape, 1)
    return tiles + [jnp.where(lane >= LANES - EDGE, rim, 0.0)]


def transform(early, late, table_hi, table_lo):
    rows = early.shape[0]
    high, low = split(jnp.concatenate([early, late], axis=0))
    first = dot(jnp.concatenate([high, low], axis=0), table_hi)
    both = first[: 2 * rows] + first[2 * rows :] + dot(high, table_lo)
    quarter = lax.broadcasted_iota(jnp.int32, (1, BINS), 1) & 3
    cosine = jnp.where(quarter == 0, 1.0, 0.0) - jnp.where(quarter == 2, 1.0, 0.0)
    sine = jnp.where(quarter == 1, 1.0, 0.0) - jnp.where(quarter == 3, 1.0, 0.0)
    early_re, early_im = both[:rows, :BINS], both[:rows, BINS:]
    late_re, late_im = both[rows:, :BINS], both[rows:, BINS:]
    return (
        early_re + cosine * late_re + sine * late_im,
        early_im + cosine * late_im - sine * late_re,
    )


def whitening(real_part, imag_part, band):
    rows = real_part.shape[0]
    tiles = BINS // LANES
    stacked = []
    for part in split(real_part * real_part + imag_part * imag_part):
        zero = jnp.zeros((rows, LANES), part.dtype)
        wide = jnp.concatenate([zero, part, zero], axis=1)
        stacked += [wide[:, LANES * tile : LANES * (tile + 3)] for tile in range(tiles)]
    banded = dot(jnp.concatenate(stacked, axis=0), band)
    step = rows * tiles
    summed = banded[:step] + banded[step:]
    total = jnp.concatenate(
        [summed[rows * tile : rows * (tile + 1)] for tile in range(tiles)], axis=1
    )
    bins = lax.broadcasted_iota(jnp.int32, (1, BINS), 1)
    count = jnp.minimum(bins + HALF, BINS - 1) - jnp.maximum(bins - HALF, 0) + 1
    return lax.rsqrt(total * (1.0 / count.astype(jnp.float32)) + 1e-06)


def prepare_kernel(
    _, alive_hbm, picks_hbm, fwd_hi_hbm, fwd_lo_hbm, band_hbm, lag_hbm,
    hi_ref, lo_ref, band_ref, lag_ref, alive_out, picks_out, alive_ref, picks_ref, sems,
):
    copies = start_copies(
        [
            (alive_hbm, alive_ref),
            (picks_hbm, picks_ref),
            (fwd_hi_hbm, hi_ref),
            (fwd_lo_hbm, lo_ref),
            (band_hbm, band_ref),
            (lag_hbm, lag_ref),
        ],
        sems,
    )
    for copy in copies[:2]:
        copy.wait()
    rows = alive_out.shape[0]
    alive_out[...] = jnp.broadcast_to(
        column(alive_ref[...].astype(jnp.float32)), (rows, LANES)
    )
    channel = lax.broadcasted_iota(jnp.int32, (rows, LANES), 0)
    for slot in range(picks_ref.shape[1]):
        pick = jnp.broadcast_to(picks_ref[:, slot : slot + 1], (rows, LANES))
        picks_out[slot] = jnp.where(channel == pick, 1.0, 0.0)
    for copy in copies[2:]:
        copy.wait()


def spectra_kernel(series_ref, hi_ref, lo_ref, band_ref, alive_ref, *refs):
    spectra_ref = refs[-1]
    rows = alive_ref.shape[0]
    half = S // 2
    if len(refs) > 1:
        mine, other = [unpack(ref[...], rows) for ref in (series_ref, refs[0])]
        first = lax.axis_index("src") == 0
        early = [jnp.where(first, a, b) for a, b in zip(mine, other)]
        late = [jnp.where(first, b, a) for a, b in zip(mine, other)]
        early[-2] = early[-2] + late[-1]
        early, late = [jnp.concatenate(tiles[:-1], axis=1) for tiles in (early, late)]
    else:
        early, late = series_ref[:, :half], series_ref[:, half:]
    real_part, imag_part = transform(early, late, hi_ref[...], lo_ref[...])
    factor = alive_ref[:, :1] * whitening(real_part, imag_part, band_ref[...])
    spectra_ref[:, :BINS] = real_part * factor
    spectra_ref[:, BINS:] = imag_part * factor


def part_bounds(total):
    ends = [3 * total // 8, 3 * total // 4, total]
    return [(a, b) for a, b in zip([0] + ends, ends) if b > a]


def correlate_kernel(
    slots, spectra_ref, pieces_ref, picks_ref, hi_ref, lo_ref, band_ref, lag_ref, out_hbm,
    series_ref, rims_ref, source_ref, cross_ref, out_ref, sems,
):
    rows = spectra_ref.shape[0]
    group = out_ref.shape[0] // slots
    half = BINS // LANES
    own = lax.axis_index("blk")
    base = lax.axis_index("src") * group
    tiles = S // 2 // LANES

    for slot in range(slots):
        for block in range(group):
            row = slice(slot * group + block, slot * group + block + 1)
            at = pieces_ref.shape[0] - 1 - 2 * (base + block)
            for tile in range(tiles):
                span = slice(LANES * (slot * tiles + tile), LANES * (slot * tiles + tile + 1))
                early = slice(LANES * tile, LANES * (tile + 1))
                late = slice(S // 2 + LANES * tile, S // 2 + LANES * (tile + 1))
                series_ref[row, early] = pieces_ref[at, :, span]
                series_ref[row, late] = pieces_ref[at - 1, :, span]
            rims_ref[row, :] = pieces_ref[at - 1, :, LANES * slots * tiles :]
    rims = jnp.concatenate(
        [
            pltpu.roll(rims_ref[slot * group : (slot + 1) * group, :], EDGE * slot, 1)
            for slot in range(slots)
        ],
        axis=0,
    )
    lane = lax.broadcasted_iota(jnp.int32, rims.shape, 1)
    seam = slice(S // 2 - LANES, S // 2)
    series_ref[:, seam] = series_ref[:, seam] + jnp.where(lane >= LANES - EDGE, rims, 0.0)
    early, late = series_ref[:, : S // 2], series_ref[:, S // 2 :]
    real_part, imag_part = transform(early, late, hi_ref[...], lo_ref[...])
    factor = whitening(real_part, imag_part, band_ref[...])
    source_ref[:, :BINS] = real_part * factor
    source_ref[:, BINS:] = imag_part * factor
    copies = []
    for part, (first, last) in enumerate(part_bounds(group * slots)):
        per_part = last - first
        for tile in range(half):
            re = slice(LANES * tile, LANES * (tile + 1))
            im = slice(BINS + LANES * tile, BINS + LANES * (tile + 1))
            rec_re, rec_im = spectra_ref[:, re], spectra_ref[:, im]
            for source in range(first, first + per_part):
                block, slot = divmod(source, slots)
                at = slot * group + block
                src_re, src_im = source_ref[at : at + 1, re], source_ref[at : at + 1, im]
                where = slice(rows * source, rows * (source + 1))
                cross_ref[where, re] = (src_re * rec_re + src_im * rec_im).astype(jnp.bfloat16)
                cross_ref[where, im] = (src_re * rec_im - src_im * rec_re).astype(jnp.bfloat16)
        lagged = dot(cross_ref[rows * first : rows * (first + per_part), :], lag_ref[...])
        for source in range(first, first + per_part):
            block, slot = divmod(source, slots)
            keep = 1.0 - jnp.where(own == base + block, 1.0, 0.0) * picks_ref[slot]
            at = source - first
            kept = lagged[rows * at : rows * (at + 1)] * jnp.concatenate(
                [keep] * (LAGS // LANES), axis=1
            )
            out_ref[source] = kept.astype(jnp.bfloat16)
        span = pl.ds(first, per_part)
        copies.append(pltpu.make_async_copy(out_ref.at[span], out_hbm.at[span], sems.at[part]))
        copies[-1].start()
    for copy in copies:
        copy.wait()


HBM = pl.BlockSpec(memory_space=pltpu.HBM)
VMEM = pl.BlockSpec(memory_space=pltpu.VMEM)
PARAMS = pltpu.CompilerParams(vmem_limit_bytes=VMEM_LIMIT)


def in_hbm(*arrays):
    return [pltpu.with_memory_space_constraint(array, pltpu.HBM) for array in arrays]


def shaped(*shape, dtype=jnp.float32):
    return jax.ShapeDtypeStruct(shape, dtype)


def local(raw_records, fir_taps, alive_mask, source_index):
    src_count = lax.axis_size("src")
    blk_count = lax.axis_size("blk")
    rows, raw_count = raw_records.shape
    slots = source_index.shape[1]
    group = blk_count // src_count
    out_count = raw_count // DEC
    width = -(-out_count // LANES) * LANES + LANES
    chunks = raw_count // CHUNK
    paired = src_count == 2 and 2 * out_count == S
    bf16 = jnp.bfloat16
    forward_hi, forward_lo = split_table(forward_table())
    alive_row = alive_mask.reshape(1, rows)

    with jax.named_scope("decimate"):
        device_count = blk_count * src_count
        main = slots * (width - LANES)
        decimated, pieces = pl.pallas_call(
            lambda *refs: decimate_kernel(paired, *refs),
            out_shape=(
                shaped(rows * (S // 2 // LANES) + SUBLANES, LANES)
                if paired
                else shaped(rows, width),
                shaped(device_count * (main // LANES + 1), LANES),
            ),
            in_specs=[HBM] * 4,
            out_specs=(VMEM, HBM),
            scratch_shapes=[
                pltpu.VMEM((rows, raw_count), jnp.float32),
                pltpu.VMEM((1, TAPS), jnp.float32),
                pltpu.SMEM((1, rows), jnp.int32),
                pltpu.SMEM((1, slots), jnp.int32),
                pltpu.VMEM((SUBLANES * slots, CHUNK), jnp.float32),
                pltpu.VMEM((device_count * (main // LANES + 1), LANES), jnp.float32),
                pltpu.SemaphoreType.DMA((rows // SUBLANES + 3,)),
            ],
            compiler_params=PARAMS,
        )(*in_hbm(raw_records, fir_taps.reshape(1, TAPS), alive_row, source_index))

    def whole(shards):
        rims = jnp.pad(shards[1:, :, width - EDGE :], ((0, 1), (0, 0), (out_count - EDGE, 0)))
        series = shards[:, :, :out_count] + rims
        return series.transpose(1, 0, 2).reshape(shards.shape[1], S)

    with jax.named_scope("gather_sources"):
        gathered = lax.all_to_all(
            pieces.reshape(device_count, 1, main + LANES),
            ("blk", "src"),
            split_axis=0,
            concat_axis=0,
            tiled=True,
            axis_index_groups=[list(reversed(range(device_count)))],
        )
        if not paired:
            gathered = gathered[::-1]
            shards = gathered.reshape(blk_count, src_count, main + LANES)
            shards = shards.transpose(1, 0, 2)
            rims = [shards[:, :, main + LANES - EDGE * (slot + 1) :] for slot in range(slots)]
            rims = jnp.stack([rim[:, :, :EDGE] for rim in rims], axis=2)
            rims = jnp.pad(rims, ((0, 0), (0, 0), (0, 0), (LANES - EDGE, 0)))
            series = shards[:, :, :main].reshape(src_count, blk_count, slots, width - LANES)
            series = jnp.concatenate([series, rims], axis=3)
            series = whole(series.reshape(src_count, blk_count * slots, width))
            series = series.reshape(blk_count, slots, 2, S // 2).transpose(0, 2, 1, 3)
            series = series.reshape(blk_count * 2, 1, slots * S // 2)
            gathered = jnp.pad(series, ((0, 0), (0, 0), (0, LANES)))[::-1]

    with jax.named_scope("prepare"):
        out_shape = (
            shaped(S // 2, NFFT, dtype=bf16),
            shaped(S // 2, NFFT, dtype=bf16),
            shaped(3 * LANES, LANES, dtype=bf16),
            shaped(NFFT, LAGS, dtype=bf16),
            shaped(rows, LANES),
            shaped(slots, rows, LANES),
        )
        table_hi, table_lo, band, lag, alive, picks = pl.pallas_call(
            prepare_kernel,
            out_shape=out_shape,
            in_specs=[VMEM] + [HBM] * 6,
            out_specs=(VMEM,) * len(out_shape),
            scratch_shapes=[
                pltpu.VMEM((1, rows), jnp.int32),
                pltpu.VMEM((1, slots), jnp.int32),
                pltpu.SemaphoreType.DMA((6,)),
            ],
            compiler_params=PARAMS,
            cost_estimate=pl.CostEstimate(
                flops=0, bytes_accessed=4 * S * NFFT, transcendentals=0
            ),
        )(
            decimated,
            *in_hbm(
                alive_row,
                source_index,
                jnp.asarray(forward_hi),
                jnp.asarray(forward_lo),
                jnp.asarray(band_table()),
                jnp.asarray(lag_table()),
            ),
        )

    with jax.named_scope("regroup"):
        if paired:
            series = [decimated]
            other = [lax.ppermute(decimated, "src", [(0, 1), (1, 0)])]
        else:
            series = [whole(lax.all_gather(decimated, "src", axis=0))]
            other = []

    with jax.named_scope("spectra"):
        operands = series + [table_hi, table_lo, band, alive] + other
        spectra = pl.pallas_call(
            spectra_kernel,
            out_shape=shaped(rows, NFFT),
            in_specs=[VMEM] * len(operands),
            out_specs=VMEM,
            compiler_params=PARAMS,
        )(*operands)

    with jax.named_scope("correlate"):
        total = group * slots
        return pl.pallas_call(
            lambda *refs: correlate_kernel(slots, *refs),
            out_shape=shaped(total, rows, LAGS, dtype=bf16),
            in_specs=[VMEM] * 7,
            out_specs=HBM,
            scratch_shapes=[
                pltpu.VMEM((total, S), jnp.float32),
                pltpu.VMEM((total, LANES), jnp.float32),
                pltpu.VMEM((total, NFFT), jnp.float32),
                pltpu.VMEM((total * rows, NFFT), bf16),
                pltpu.VMEM((total, rows, LAGS), bf16),
                pltpu.SemaphoreType.DMA((PARTS,)),
            ],
            compiler_params=PARAMS,
        )(spectra, gathered, picks, table_hi, table_lo, band, lag)


def solution(mesh):
    in_specs = (P("blk", "src"), P(), P("blk"), P("blk", None))
    out_specs = P("src", "blk", None)
    return jax.shard_map(local, mesh=mesh, in_specs=in_specs, out_specs=out_specs, check_vma=False)
```
